32 devices in a mesh: section: 2 (over core), dp: 4 (over y, x), tensor: 4 (over z).
Axes of the slice: x: 2, y: 2, z: 4, core: 2. Of those that a mesh axis runs over, the one named last changes fastest.
Arguments:
- tokens_in: bfloat16 [2, 1024, 1536], P(None, ('dp', 'tensor')), may hold values from -6 to 6
- out_cotangent: bfloat16 [2, 1024, 1536], P(None, ('dp', 'tensor')), may hold values from -6 to 6
- attn_gain: float32 [2, 1536], P('section'), may hold values from 0.25 to 1.75
- query_weight: bfloat16 [2, 1536, 1536], P('section', None, 'tensor'), may hold values from -0.15625 to 0.15625
- key_weight: bfloat16 [2, 1536, 512], P('section', None, 'tensor'), may hold values from -0.15625 to 0.15625
- value_weight: bfloat16 [2, 1536, 512], P('section', None, 'tensor'), may hold values from -0.15625 to 0.15625
- output_weight: bfloat16 [2, 1536, 1536], P('section', 'tensor'), may hold values from -1.25 to 1.25
- expert_gain: float32 [2, 1536], P('section'), may hold values from 0.25 to 1.75
- router_weight: bfloat16 [2, 1536, 16], P('section'), may hold values from -0.078125 to 0.078125
- gate_weight: bfloat16 [2, 16, 1536, 512], P('section', None, None, 'tensor'), may hold values from -0.15625 to 0.15625
- up_weight: bfloat16 [2, 16, 1536, 512], P('section', None, None, 'tensor'), may hold values from -0.15625 to 0.15625
- down_weight: bfloat16 [2, 16, 512, 1536], P('section', None, 'tensor'), may hold values from -1.5 to 1.5
- lengths: int32 [2, 4, 3], P(None, 'dp'), may hold values from 1 to 192, 256 in all within a row
- dealing: int32 [2, 4, 3], P(None, 'dp'), may hold values from 0 to 2, each once within a row
- slot_order: int32 [2, 2, 4, 256], P('section', None, 'dp'), may hold values from 0 to 255, each once within a row
- routes: int32 [2, 2, 1024, 8], P('section', None, 'dp'), may hold values from 0 to 15, all different within a row
Outputs:
- layer_outputs: float32 [2, 2, 1024, 1536], P('section', None, ('dp', 'tensor'))
- input_grads: float32 [2, 2, 1024, 1536], P('section', None, ('dp', 'tensor'))
- attn_gain_grad: float32 [2, 1536], P('section')
- query_weight_grad: float32 [2, 1536, 1536], P('section', None, 'tensor')
- key_weight_grad: float32 [2, 1536, 512], P('section', None, 'tensor')
- value_weight_grad: float32 [2, 1536, 512], P('section', None, 'tensor')
- output_weight_grad: float32 [2, 1536, 1536], P('section', 'tensor')
- expert_gain_grad: float32 [2, 1536], P('section')
- router_weight_grad: float32 [2, 1536, 16], P('section')
- gate_weight_grad: float32 [2, 16, 1536, 512], P('section', 'dp', None, 'tensor')
- up_weight_grad: float32 [2, 16, 1536, 512], P('section', 'dp', None, 'tensor')
- down_weight_grad: float32 [2, 16, 512, 1536], P('section', 'dp', 'tensor')
The draws below stay inside these ranges and needn't reach their ends.
Inputs may be any that keep to these rules, and one draw needn't show every extreme that they name: `lengths`: each row sums to 256; its largest entry is 192. `dealing`: each row is a permutation. `slot_order`: each row is a permutation. `routes`: the 8 entries of a row are different.
All inputs are finite; a program needn't handle non-finite values.
Results may differ from the reference program's by a relative error of at most 0.03.
Values may be sent and summed in bfloat16 or wider, within the bound.
A program may use at most 320 MiB of HBM per device.

```python
import math
import jax
import jax.numpy as jnp
import numpy as np
from jax import lax

D = 1536
H = 24
KV = 8
HD = 64
F = 512
TOPK = 8
E = 16
M = 2
SEQ_MB = 3
TM = 256
LMOST = 192
CAP = 160
N_DP = 4


def level_of(own_key, extent, pieces, low, top_value):
    factor_of, own = 1.0, jax.random.fold_in(own_key, 6)
    for dim, shards_of in pieces:
        draws = jnp.exp(jax.random.uniform(jax.random.fold_in(own, dim), (shards_of,), jnp.float32, low / len(pieces), top_value / len(pieces)))
        factor_of = factor_of * jnp.repeat(draws, extent[dim] // shards_of).reshape([-1 if axis == dim else 1 for axis in range(len(extent))])
    return factor_of


def picks_of(own_key, rows, number_of, top, lift):
    sequence = jax.random.permutation(jax.random.fold_in(own_key, 1), number_of)
    pull = sequence
    for power in range(3):
        pull = pull * pull // number_of
    pull = pull * lift // number_of
    chance = jax.random.randint(jax.random.fold_in(own_key, 2), (rows, number_of), 0, 4096) + pull
    sure = jax.random.permutation(jax.random.fold_in(own_key, 3), rows)[jnp.arange(number_of) % rows]
    chance = jnp.where(jnp.arange(rows)[:, None] == sure[None, :], 1 << 14, chance)
    merit = chance * number_of + jnp.arange(number_of)
    return lax.top_k(merit.astype(jnp.int32), top)[1].astype(jnp.int32)


def split_up(number_of, total, most, lean):
    loads = [(1 << 20) // math.isqrt(grade ** lean) + 1 for grade in range(2, number_of + 1)]
    surplus, given = total - most - (number_of - 1), [1] * (number_of - 1)
    while surplus > 0:
        free = [i for i in range(number_of - 1) if given[i] < most]
        whole, budget = sum([loads[i] for i in free]), surplus
        for i in free:
            extra = min(most - given[i], max(1, budget * loads[i] // whole), surplus)
            given[i] = given[i] + extra
            surplus = surplus - extra
    return np.array([most] + given)


def ragged(own_key, count, total, bound, slope):
    if count == 2:
        one = jax.random.randint(own_key, (), max(1, total - bound), min(bound, total - 1) + 1)
        return jnp.stack([one, total - one])
    sizes = jnp.asarray(split_up(count, total, bound, slope), jnp.int32)
    pairs = (count - 1) // 2
    giver, taker = sizes[1:1 + 2 * pairs:2], sizes[2:2 + 2 * pairs:2]
    margin = jnp.minimum(giver - 1, bound - taker)
    moved = jax.random.randint(jax.random.fold_in(own_key, 1), (pairs,), 0, 1 << 20) % (margin + 1)
    sizes = sizes.at[1:1 + 2 * pairs:2].set(giver - moved).at[2:2 + 2 * pairs:2].set(taker + moved)
    return sizes[jax.random.permutation(jax.random.fold_in(own_key, 2), count)]


def centred(key, dims, deviation, most, cuts=(), kind=jnp.bfloat16):
    factor_of = level_of(key, dims, cuts, -0.22, 0.18) if cuts else 1.0
    values = jax.random.normal(key, dims, jnp.float32) * deviation * factor_of
    return jnp.minimum(jnp.maximum(values, -most), most).astype(kind)


def setup_inputs(seed: int = 0) -> dict:
    arg_keys = jax.random.split(jax.random.key(seed), 17)
    tokens_in = centred(arg_keys[0], (M, N_DP * TM, D), 1.0, 6.0, ((1, 16),))
    out_cotangent = centred(arg_keys[1], (M, N_DP * TM, D), 1.0, 6.0, ((1, 16),))
    attn_gain = jnp.clip(1.0 + 0.15 * jax.random.normal(arg_keys[2], (2, D), jnp.float32), 0.25, 1.75)
    query_weight = centred(arg_keys[3], (2, D, H * HD), D ** -0.5, 0.15625, ((0, 2), (2, 4)))
    key_weight = centred(arg_keys[4], (2, D, KV * HD), D ** -0.5, 0.15625, ((0, 2), (2, 4)))
    value_weight = centred(arg_keys[5], (2, D, KV * HD), D ** -0.5, 0.15625, ((0, 2), (2, 4)))
    output_weight = centred(arg_keys[6], (2, H * HD, D), (H * HD // 64) ** -0.5, 1.25, ((0, 2), (1, 4)))
    expert_gain = jnp.clip(1.0 + 0.15 * jax.random.normal(arg_keys[7], (2, D), jnp.float32), 0.25, 1.75)
    router_weight = centred(arg_keys[8], (2, D, E), (4 * D) ** -0.5, 0.078125, ((0, 2),))
    gate_weight = centred(arg_keys[9], (2, E, D, F), D ** -0.5, 0.15625, ((0, 2), (3, 4)))
    up_weight = centred(arg_keys[10], (2, E, D, F), D ** -0.5, 0.15625, ((0, 2), (3, 4)))
    down_weight = centred(arg_keys[11], (2, E, F, D), (F // 32) ** -0.5, 1.5, ((0, 2), (2, 4)))
    lengths = jax.vmap(lambda own: ragged(own, SEQ_MB, TM, LMOST, 2))(jax.random.split(arg_keys[12], M * N_DP)).reshape((M, N_DP, SEQ_MB)).astype(jnp.int32)
    dealing = jax.vmap(lambda own: jax.random.permutation(own, SEQ_MB))(jax.random.split(arg_keys[13], M * N_DP)).reshape((M, N_DP, SEQ_MB)).astype(jnp.int32)
    slot_order = jax.vmap(lambda own: jax.random.permutation(own, TM))(jax.random.split(arg_keys[14], 2 * M * N_DP)).reshape((2, M, N_DP, TM)).astype(jnp.int32)
    routes = picks_of(arg_keys[15], 2 * M * (N_DP * TM), E, TOPK, 4096).reshape((2, M, N_DP * TM, TOPK))
    return dict(tokens_in=tokens_in, out_cotangent=out_cotangent, attn_gain=attn_gain, query_weight=query_weight, key_weight=key_weight, value_weight=value_weight, output_weight=output_weight, expert_gain=expert_gain, router_weight=router_weight, gate_weight=gate_weight, up_weight=up_weight, down_weight=down_weight, lengths=lengths, dealing=dealing, slot_order=slot_order, routes=routes)


@jax.custom_vjp
def low(v):
    return lax.optimization_barrier(v.astype(jnp.bfloat16)).astype(jnp.float32)

@jax.custom_vjp
def low_back(v):
    return v

def low_keep(v):
    return (low(v), None)

def low_pass(kept, grad):
    return (grad,)

def back_keep(v):
    return (v, None)

def back_low(kept, grad):
    return (low(grad),)
low.defvjp(low_keep, low_pass)
low_back.defvjp(back_keep, back_low)
epsilon = 1e-05
rope_base = 10000.0
masked_score = -1e+30
highest = lax.Precision.HIGHEST

def rms_scale(stream, gain):
    return stream * lax.rsqrt(lax.optimization_barrier(jnp.mean(stream * stream, axis=-1, keepdims=True)) + epsilon) * gain

def rotate_half(rows_in):
    half_width = rows_in.shape[-1] // 2
    return jnp.concatenate([-rows_in[..., half_width:], rows_in[..., :half_width]], axis=-1)

def rope_tables(position, head_dim):
    half_width = head_dim // 2
    freqs = rope_base ** (-2.0 * jnp.arange(half_width, dtype=jnp.float32) / head_dim)
    angles = position.astype(jnp.float32)[:, None] * freqs[None, :]
    return (jnp.concatenate([jnp.cos(angles)] * 2, axis=1), jnp.concatenate([jnp.sin(angles)] * 2, axis=1))

def rope_apply(rows_in, cosine_table, sine_table):
    return rows_in * cosine_table[:, None, :] + rotate_half(rows_in) * sine_table[:, None, :]

def pack_layout(lengths, dealing, order, routes, experts, capacity):
    tokens_pack = order.shape[0]
    seq_count = lengths.shape[0]
    top_count = routes.shape[1]
    token_index = jnp.arange(tokens_pack, dtype=jnp.int32)
    seq_index = jnp.arange(seq_count, dtype=jnp.int32)
    seq_ends = jnp.cumsum(lengths).astype(jnp.int32)
    seq_starts = (seq_ends - lengths).astype(jnp.int32)
    segment = lax.optimization_barrier(jnp.sum((token_index[:, None] >= seq_ends[None, :]).astype(jnp.int32), axis=1)).astype(jnp.int32)
    seg_onehot = (segment[:, None] == seq_index[None, :]).astype(jnp.int32)
    position = (token_index - lax.optimization_barrier(jnp.sum(seg_onehot * seq_starts[None, :], axis=1))).astype(jnp.int32)
    dealt_rank = lax.optimization_barrier(jnp.sum(jnp.where(dealing[:, None] == seq_index[None, :], seq_index[:, None], 0), axis=0)).astype(jnp.int32)
    dealt_start = lax.optimization_barrier(jnp.sum(jnp.where(dealt_rank[:, None] < dealt_rank[None, :], lengths[:, None], 0), axis=0)).astype(jnp.int32)
    dealt_place = (lax.optimization_barrier(jnp.sum(seg_onehot * dealt_start[None, :], axis=1)) + position).astype(jnp.int32)
    priority = order[dealt_place]
    served = jnp.zeros((tokens_pack,), jnp.int32).at[priority].set(token_index)
    expert_index = jnp.arange(experts, dtype=jnp.int32)
    picked = lax.optimization_barrier(jnp.sum((routes[:, :, None] == expert_index[None, None, :]).astype(jnp.int32), axis=1)).astype(jnp.int32)
    ordered = picked[served]
    earlier = (jnp.cumsum(ordered, axis=0) - ordered).astype(jnp.int32)
    slot_rank = jnp.take_along_axis(earlier[priority], routes, axis=1).astype(jnp.int32)
    slot_id = jnp.where(slot_rank < capacity, routes * capacity + slot_rank, experts * capacity).astype(jnp.int32)
    slot_token = jnp.full((experts * capacity + 1,), tokens_pack, jnp.int32).at[slot_id.reshape(-1)].set(jnp.repeat(token_index, top_count))
    return (segment, position, slot_id, slot_token[:experts * capacity])

def layer(stream, weights, route_rows, segment, position, slot_id, slot_token):
    attn_gain, query_weight, key_weight, value_weight, output_weight, expert_gain, router_weight, gate_weight, up_weight, down_weight = weights
    tokens_pack = stream.shape[0]
    group_size = H // KV
    attn_in = low(rms_scale(stream, attn_gain))
    queries = low_back(jnp.dot(attn_in, query_weight, precision=highest)).reshape(tokens_pack, H, HD)
    keys_pre = low_back(jnp.dot(attn_in, key_weight, precision=highest)).reshape(tokens_pack, KV, HD)
    values_b = low(low_back(jnp.dot(attn_in, value_weight, precision=highest))).reshape(tokens_pack, KV, HD)
    cosine_table, sine_table = rope_tables(position, HD)
    queries_rot = low(rope_apply(queries, cosine_table, sine_table))
    keys_rot = low(rope_apply(keys_pre, cosine_table, sine_table))
    keys_all = jnp.repeat(keys_rot, group_size, axis=1)
    values_all = jnp.repeat(values_b, group_size, axis=1)
    scores = low_back(0.125 * jnp.einsum('qhd,khd->hqk', queries_rot, keys_all, precision=highest))
    token_index = jnp.arange(tokens_pack, dtype=jnp.int32)
    allowed = (segment[:, None] == segment[None, :]) & (token_index[None, :] <= token_index[:, None])
    soft_scores = jax.nn.softmax(jnp.where(allowed[None], scores, masked_score), axis=-1)
    attended = jnp.einsum('hqk,khd->qhd', low(soft_scores), values_all, precision=highest).reshape(tokens_pack, H * HD)
    attended = low(low_back(attended))
    mid_stream = stream + low_back(jnp.dot(attended, output_weight, precision=highest))
    expert_in = low(rms_scale(mid_stream, expert_gain))
    logits = low_back(jnp.dot(expert_in, router_weight, precision=highest))
    gate = jax.nn.softmax(jnp.take_along_axis(logits, route_rows, axis=1), axis=-1)
    padded = jnp.concatenate([expert_in, jnp.zeros((1, D), jnp.float32)], axis=0)
    slot_in = padded[slot_token].reshape(E, CAP, D)
    gate_pre = low_back(jnp.einsum('ecd,edf->ecf', slot_in, gate_weight, precision=highest))
    up_pre = low_back(jnp.einsum('ecd,edf->ecf', slot_in, up_weight, precision=highest))
    hidden = low(jax.nn.silu(gate_pre) * up_pre)
    expert_out = low_back(jnp.einsum('ecf,efd->ecd', hidden, down_weight, precision=highest)).reshape(E * CAP, D)
    expert_pad = jnp.concatenate([expert_out, jnp.zeros((1, D), jnp.float32)], axis=0)
    return mid_stream + jnp.einsum('tk,tkd->td', gate, expert_pad[slot_id], precision=highest)

def two_layers(params, pack_data):
    stream_in, probe_pack, lengths, dealing, order, routes = pack_data
    stream = stream_in
    first_out = stream_in
    second_out = stream_in
    for layer_index in range(2):
        weights = tuple((weight_arr[layer_index] for weight_arr in params))
        segment, position, slot_id, slot_token = pack_layout(lengths, dealing, order[layer_index], routes[layer_index], E, CAP)
        result = layer(stream, weights, routes[layer_index], segment, position, slot_id, slot_token)
        if layer_index == 0:
            first_out = result
            stream = low_back(low(result)) + probe_pack
        else:
            second_out = result
    return (first_out, second_out)

def reference(tokens_in, out_cotangent, attn_gain, query_weight, key_weight, value_weight, output_weight, expert_gain, router_weight, gate_weight, up_weight, down_weight, lengths, dealing, slot_order, routes):
    pack_count = M * N_DP
    params = tuple((weight_arr.astype(jnp.float32) for weight_arr in (attn_gain, query_weight, key_weight, value_weight, output_weight, expert_gain, router_weight, gate_weight, up_weight, down_weight)))
    stream_packs = tokens_in.astype(jnp.float32).reshape(pack_count, TM, D)
    probes = jnp.zeros((pack_count, TM, D), jnp.float32)
    length_packs = lengths.reshape(pack_count, SEQ_MB)
    deal_packs = dealing.reshape(pack_count, SEQ_MB)
    order_packs = jnp.moveaxis(slot_order.reshape(2, pack_count, TM), 0, 1)
    route_packs = jnp.moveaxis(routes.reshape(2, pack_count, TM, TOPK), 0, 1)

    def forward(params, stream_packs, probes):

        def run_pack(pack_data):
            return two_layers(params, pack_data)
        return lax.map(jax.checkpoint(run_pack), (stream_packs, probes, length_packs, deal_packs, order_packs, route_packs))
    (first_out, second_out), pullback = jax.vjp(forward, params, stream_packs, probes)
    cotangent = out_cotangent.astype(jnp.float32).reshape(pack_count, TM, D)
    param_grads, stream_grad, probe_grad = pullback((jnp.zeros_like(first_out), cotangent))
    layer_outputs = jnp.stack([first_out, second_out]).reshape(2, M, N_DP * TM, D).astype(jnp.float32)
    input_grads = jnp.stack([stream_grad, probe_grad]).reshape(2, M, N_DP * TM, D).astype(jnp.float32)
    return (layer_outputs, input_grads, param_grads[0], param_grads[1], param_grads[2], param_grads[3], param_grads[4], param_grads[5], param_grads[6], param_grads[7], param_grads[8], param_grads[9])
```

```python
import jax
import jax.numpy as jnp
from jax import lax
from jax.sharding import PartitionSpec as P

H = 24
KV = 8
HD = 64
E = 16
CAP = 160

epsilon = 1e-05
rope_base = 10000.0
masked_score = -1e30
bf16 = jnp.bfloat16
f32 = jnp.float32


def dot(a, b, dims):
    return lax.dot_general(a, b, (dims, ((), ())), preferred_element_type=f32)


NN = ((1,), (0,))
NT = ((1,), (1,))
TN = ((0,), (0,))


def swapped(value):
    return lax.ppermute(value, "section", [(0, 1), (1, 0)])


def rotate_half(rows_in):
    half_width = rows_in.shape[-1] // 2
    return jnp.concatenate([-rows_in[..., half_width:], rows_in[..., :half_width]], axis=-1)


def rope_tables(position, head_dim):
    half_width = head_dim // 2
    freqs = rope_base ** (-2.0 * jnp.arange(half_width, dtype=f32) / head_dim)
    angles = position.astype(f32)[:, None] * freqs[None, :]
    return (
        jnp.concatenate([jnp.cos(angles)] * 2, axis=1),
        jnp.concatenate([jnp.sin(angles)] * 2, axis=1),
    )


def token_places(lengths, dealing, tokens_pack):
    seq_count = lengths.shape[0]
    token_index = jnp.arange(tokens_pack, dtype=jnp.int32)
    seq_index = jnp.arange(seq_count, dtype=jnp.int32)
    before = seq_index[None, :] <= seq_index[:, None]
    seq_ends = jnp.sum(jnp.where(before, lengths[None, :], 0), axis=1)
    seq_starts = seq_ends - lengths
    segment = jnp.sum((token_index[:, None] >= seq_ends[None, :]).astype(jnp.int32), axis=1)
    seg_onehot = (segment[:, None] == seq_index[None, :]).astype(jnp.int32)
    position = token_index - jnp.sum(seg_onehot * seq_starts[None, :], axis=1)
    dealt_rank = jnp.sum(
        jnp.where(dealing[:, None] == seq_index[None, :], seq_index[:, None], 0), axis=0
    )
    dealt_start = jnp.sum(
        jnp.where(dealt_rank[:, None] < dealt_rank[None, :], lengths[:, None], 0), axis=0
    )
    dealt_place = jnp.sum(seg_onehot * dealt_start[None, :], axis=1) + position
    return segment, position, dealt_place


def expert_masks(dealt_place, order, routes):
    tokens_pack = order.shape[0]
    token_index = jnp.arange(tokens_pack, dtype=jnp.int32)
    priority = jnp.sum(
        jnp.where(dealt_place[:, None] == token_index[None, :], order[None, :], 0), axis=1
    )
    expert_index = jnp.arange(E, dtype=jnp.int32)
    picked = jnp.any(routes[:, :, None] == expert_index[None, None, :], axis=1)
    earlier = (priority[None, :] < priority[:, None]).astype(bf16)
    rank = dot(earlier, picked.astype(bf16), NN)
    kept = picked & (rank < CAP)
    return picked.astype(f32), kept.astype(f32)


def norm_scale(rows_in):
    return lax.rsqrt(jnp.mean(rows_in * rows_in, axis=-1, keepdims=True) + epsilon)


def norm_back(rows_in, gain, out_grad):
    scaled = rows_in * norm_scale(rows_in)
    gain_grad = jnp.sum(out_grad * scaled, axis=0)
    inner = out_grad * gain
    value_grad = norm_scale(rows_in) * (
        inner - scaled * jnp.mean(inner * scaled, axis=-1, keepdims=True)
    )
    return value_grad, gain_grad


def gathered(rows_in):
    return lax.all_gather(rows_in, "tensor", axis=0, tiled=True)


def scattered(partial):
    return lax.psum_scatter(
        partial.astype(bf16), "tensor", scatter_dimension=0, tiled=True
    ).astype(f32)


def layer_forward(weights, stream, tables, masks, allowed):
    attn_gain, joint_weight, output_weight, expert_gain, router_weight, gw, uw, dw = weights
    cosine, sine = tables
    picked, kept = masks
    tokens_pack = allowed.shape[0]
    tensor_size = lax.axis_size("tensor")
    key_heads = KV // tensor_size
    group = H // KV
    qw = H // tensor_size * HD
    kw = key_heads * HD
    attn_in = gathered((stream * norm_scale(stream) * attn_gain).astype(bf16))
    proj = dot(attn_in, joint_weight, NN)

    def rope(block):
        block = block.reshape(tokens_pack, -1, HD)
        return (
            (block * cosine[:, None, :] + rotate_half(block) * sine[:, None, :])
            .astype(bf16)
            .reshape(tokens_pack, -1)
        )

    queries = rope(proj[:, :qw])
    keys = rope(proj[:, qw : qw + kw])
    values = proj[:, qw + kw :].astype(bf16)
    q4 = queries.reshape(tokens_pack, key_heads, group, HD)
    k3 = keys.reshape(tokens_pack, key_heads, HD)
    v3 = values.reshape(tokens_pack, key_heads, HD)
    scores = jnp.einsum("qgnd,kgd->gnqk", q4, k3, preferred_element_type=f32) * 0.125
    scores = jnp.where(allowed, scores, masked_score)
    row_max = jnp.max(scores, axis=-1, keepdims=True)
    weighed = jnp.exp(scores - row_max)
    row_total = jnp.sum(weighed, axis=-1, keepdims=True)
    probs = weighed / row_total
    log_total = row_max + jnp.log(row_total)
    attended = jnp.einsum("gnqk,kgd->qgnd", probs.astype(bf16), v3, preferred_element_type=f32)
    attended = attended.reshape(tokens_pack, qw).astype(bf16)
    mid = stream + scattered(dot(attended, output_weight, NN))
    expert_in = gathered((mid * norm_scale(mid) * expert_gain).astype(bf16))
    logits = dot(expert_in, router_weight, NN)
    top = jnp.max(jnp.where(picked > 0, logits, masked_score), axis=1, keepdims=True)
    weighed = jnp.where(picked > 0, jnp.exp(logits - top), 0.0)
    gate = weighed / jnp.sum(weighed, axis=1, keepdims=True)
    gate_kept = gate * kept
    gate_pre = jnp.einsum("td,edf->tef", expert_in, gw, preferred_element_type=f32)
    up_pre = jnp.einsum("td,edf->tef", expert_in, uw, preferred_element_type=f32)
    hidden = (jax.nn.silu(gate_pre) * up_pre).astype(bf16).astype(f32)
    gated = (hidden * gate_kept[:, :, None]).astype(bf16).reshape(tokens_pack, -1)
    out = mid + scattered(dot(gated, dw.reshape(-1, dw.shape[2]), NN))
    state = (stream, attn_in, mid, queries, keys, values, log_total, attended, expert_in,
             gate_pre, up_pre, gate, gated)
    return out, state


def layer_backward(weights, state, tables, masks, allowed, out_grad):
    attn_gain, joint_weight, output_weight, expert_gain, router_weight, gw, uw, dw = weights
    (stream, attn_in, mid, queries, keys, values, log_total, attended, expert_in,
     gate_pre, up_pre, gate, gated) = state
    cosine, sine = tables
    picked, kept = masks
    tokens_pack = allowed.shape[0]
    rows = stream.shape[0]
    tensor_size = lax.axis_size("tensor")
    key_heads = KV // tensor_size
    group = H // KV
    qw = H // tensor_size * HD
    kw = key_heads * HD
    own = lax.axis_index("tensor") * rows
    grad_full = gathered(out_grad)
    plain = jnp.einsum("td,efd->tef", grad_full, dw, preferred_element_type=f32)
    sig = 1.0 / (1.0 + jnp.exp(-gate_pre))
    act = gate_pre * sig
    hidden = (act * up_pre).astype(bf16).astype(f32)
    gate_part = jnp.sum(hidden * plain, axis=2) * kept
    hidden_grad = plain * (gate * kept)[:, :, None]
    gpg = (hidden_grad * up_pre * (sig * (1.0 + gate_pre * (1.0 - sig)))).astype(bf16)
    upg = (hidden_grad * act).astype(bf16)
    in_part = jnp.einsum("tef,edf->td", gpg, gw, preferred_element_type=f32) + jnp.einsum(
        "tef,edf->td", upg, uw, preferred_element_type=f32
    )
    in_grad = scattered(in_part)
    gate_grad = lax.psum_scatter(gate_part, "tensor", scatter_dimension=0, tiled=True)
    gate_rows = lax.dynamic_slice_in_dim(gate, own, rows, 0)
    expert_rows = lax.dynamic_slice_in_dim(expert_in, own, rows, 0)
    logits_grad = (
        gate_rows * (gate_grad - jnp.sum(gate_rows * gate_grad, axis=1, keepdims=True))
    ).astype(bf16)
    router_grad = dot(expert_rows, logits_grad, TN)
    in_grad = in_grad + dot(logits_grad, router_weight, NT)
    mid_part, expert_gain_grad = norm_back(mid, expert_gain, in_grad)
    mid_grad = out_grad.astype(f32) + mid_part
    attn_out_grad = gathered(mid_grad.astype(bf16))
    attended_grad = dot(attn_out_grad, output_weight, NT).astype(bf16)
    q4 = queries.reshape(tokens_pack, key_heads, group, HD)
    k3 = keys.reshape(tokens_pack, key_heads, HD)
    v3 = values.reshape(tokens_pack, key_heads, HD)
    ag4 = attended_grad.reshape(tokens_pack, key_heads, group, HD)
    scores = jnp.einsum("qgnd,kgd->gnqk", q4, k3, preferred_element_type=f32) * 0.125
    probs = jnp.exp(jnp.where(allowed, scores, masked_score) - log_total)
    probs_grad = jnp.einsum("qgnd,kgd->gnqk", ag4, v3, preferred_element_type=f32)
    inner = jnp.sum(probs * probs_grad, axis=-1, keepdims=True)
    score_grad = (probs * (probs_grad - inner)).astype(bf16)
    value_grad = jnp.einsum("gnqk,qgnd->kgd", probs.astype(bf16), ag4, preferred_element_type=f32)
    value_grad = value_grad.astype(bf16).reshape(tokens_pack, kw)
    query_grad = jnp.einsum("gnqk,kgd->qgnd", score_grad, k3, preferred_element_type=f32) * 0.125
    key_grad = jnp.einsum("gnqk,qgnd->kgd", score_grad, q4, preferred_element_type=f32) * 0.125

    def unrope(block):
        block = block.reshape(tokens_pack, -1, HD)
        return (
            (block * cosine[:, None, :] - rotate_half(block) * sine[:, None, :])
            .astype(bf16)
            .reshape(tokens_pack, -1)
        )

    joint_rows = jnp.concatenate([unrope(query_grad), unrope(key_grad), value_grad], axis=1)
    attn_in_grad = scattered(dot(joint_rows, joint_weight, NT))
    stream_part, attn_gain_grad = norm_back(stream, attn_gain, attn_in_grad)
    stream_grad = mid_grad + stream_part
    small = (attn_gain_grad, expert_gain_grad, router_grad)
    acts = (expert_in, grad_full, attn_in, attn_out_grad,
            gpg.reshape(tokens_pack, -1), upg.reshape(tokens_pack, -1), gated, joint_rows, attended)
    return stream_grad, small, acts


def weight_grads(acts, section):
    expert_in, grad_full, attn_in, attn_out_grad, gpg, upg, gated, joint_rows, attended = acts
    half = expert_in.shape[1] // 2
    wide = (expert_in, grad_full, attn_in, attn_out_grad)
    mine = [lax.dynamic_slice_in_dim(v, section * half, half, 1) for v in wide]
    sent = [lax.dynamic_slice_in_dim(v, (1 - section) * half, half, 1) for v in wide]
    theirs = [swapped(v) for v in sent]
    x, og, ai, ao = [jnp.concatenate([a, b], axis=0) for a, b in zip(mine, theirs)]
    gpg, upg, gated, joint_rows, attended = [
        jnp.concatenate([v, swapped(v)], axis=0) for v in (gpg, upg, gated, joint_rows, attended)
    ]
    tokens = x.shape[0]
    gpg3, upg3, gated3 = [v.reshape(tokens, E, -1) for v in (gpg, upg, gated)]
    gate = jnp.einsum("td,tef->edf", x, gpg3, preferred_element_type=f32).astype(bf16)
    up = jnp.einsum("td,tef->edf", x, upg3, preferred_element_type=f32).astype(bf16)
    down = jnp.einsum("tef,td->efd", gated3, og, preferred_element_type=f32).astype(bf16)
    joint = dot(ai, joint_rows, TN).astype(bf16)
    output = dot(attended, ao, TN).astype(bf16)
    return gate, up, down, joint, output


def shards(
    tokens_in, out_cotangent, attn_gain, query_weight, key_weight, value_weight, output_weight,
    expert_gain, router_weight, gate_weight, up_weight, down_weight, lengths, dealing,
    slot_order, routes,
):
    section = lax.axis_index("section")
    first = section == 0

    def pick(pair):
        return lax.dynamic_index_in_dim(pair, section, 0, keepdims=False)

    qw = query_weight.shape[2]
    kw = key_weight.shape[2]
    joint_weight = jnp.concatenate([query_weight[0], key_weight[0], value_weight[0]], axis=1)
    held = (attn_gain[0], joint_weight, output_weight[0], expert_gain[0], router_weight[0],
            gate_weight[0], up_weight[0], down_weight[0])
    other = [swapped(v) for v in held]
    weights = (
        [jnp.where(first, a, b) for a, b in zip(held, other)],
        [jnp.where(first, b, a) for a, b in zip(held, other)],
    )
    tokens_pack = slot_order.shape[3]
    segment, position, dealt = token_places(pick(lengths)[0], pick(dealing)[0], tokens_pack)
    tables = rope_tables(position, HD)
    token_index = jnp.arange(tokens_pack, dtype=jnp.int32)
    allowed = (segment[:, None] == segment[None, :]) & (token_index[None, :] <= token_index[:, None])
    orders = slot_order[0, :, 0]
    order_own, order_sent = pick(orders), pick(orders[::-1])
    routes_own, routes_sent = pick(routes[0]), pick(routes[0][::-1])
    order_other, routes_other = swapped(order_sent), swapped(routes_sent)
    masks = (
        expert_masks(dealt, jnp.where(first, order_own, order_other),
                     jnp.where(first, routes_own, routes_other)),
        expert_masks(dealt, jnp.where(first, order_other, order_own),
                     jnp.where(first, routes_other, routes_own)),
    )
    stream = pick(tokens_in).astype(f32)
    out0, state0 = layer_forward(weights[0], stream, tables, masks[0], allowed)
    out1, state1 = layer_forward(weights[1], out0.astype(bf16).astype(f32), tables, masks[1], allowed)
    grad1, small1, acts1 = layer_backward(weights[1], state1, tables, masks[1], allowed,
                                          pick(out_cotangent))
    sums1 = weight_grads(acts1, section)
    grad0, small0, acts0 = layer_backward(weights[0], state0, tables, masks[0], allowed,
                                          grad1.astype(bf16))
    sums0 = weight_grads(acts0, section)

    def by_layer(zero, one):
        mine = jnp.where(first, zero, one)
        theirs = swapped(jnp.where(first, one, zero))
        return jnp.where(first, jnp.stack([mine, theirs]), jnp.stack([theirs, mine]))[None]

    layer_outputs = by_layer(out0, out1)
    input_grads = by_layer(grad0, grad1)

    def reduced(sums):
        gate, up, down, joint, output = sums
        gate, up, down = [
            lax.psum_scatter(v, "dp", scatter_dimension=0, tiled=True) for v in (gate, up, down)
        ]
        joint, output = lax.psum((joint, output), "dp")
        return gate, up, down, joint, output

    red1 = reduced(sums1)
    red0 = reduced(sums0)

    def joined(zero, one, axis):
        mine = jnp.where(first, zero, one)
        theirs = swapped(jnp.where(first, one, zero))
        return jnp.where(
            first,
            jnp.concatenate([mine, theirs], axis=axis),
            jnp.concatenate([theirs, mine], axis=axis),
        ).astype(f32)

    gate, up, down, joint, output = [
        joined(a, b, axis) for a, b, axis in zip(red0, red1, (1, 1, 2, 0, 1))
    ]
    gains = [lax.psum((a, b), ("section", "dp", "tensor")) for a, b in zip(small0, small1)]
    attn_gain_grad, expert_gain_grad, router_grad = [jnp.where(first, a, b) for a, b in gains]
    return (
        layer_outputs,
        input_grads,
        attn_gain_grad[None],
        joint[:, :qw][None],
        joint[:, qw : qw + kw][None],
        joint[:, qw + kw :][None],
        output[None],
        expert_gain_grad[None],
        router_grad[None],
        gate[None],
        up[None],
        down[None],
    )


def solution(mesh):
    return jax.shard_map(
        shards,
        mesh=mesh,
        in_specs=(
            P(None, ("dp", "tensor"), None),
            P(None, ("dp", "tensor"), None),
            P("section", None),
            P("section", None, "tensor"),
            P("section", None, "tensor"),
            P("section", None, "tensor"),
            P("section", "tensor", None),
            P("section", None),
            P("section", None, None),
            P("section", None, None, "tensor"),
            P("section", None, None, "tensor"),
            P("section", None, "tensor", None),
            P(None, "dp", None),
            P(None, "dp", None),
            P("section", None, "dp", None),
            P("section", None, "dp", None),
        ),
        out_specs=(
            P("section", None, ("dp", "tensor"), None),
            P("section", None, ("dp", "tensor"), None),
            P("section", None),
            P("section", None, "tensor"),
            P("section", None, "tensor"),
            P("section", None, "tensor"),
            P("section", "tensor", None),
            P("section", None),
            P("section", None, None),
            P("section", "dp", None, "tensor"),
            P("section", "dp", None, "tensor"),
            P("section", "dp", "tensor", None),
        ),
        check_vma=False,
    )
```

```python
import functools
import math

import jax
import jax.numpy as jnp
from jax import lax
from jax.experimental import pallas as pl
from jax.experimental.pallas import tpu as pltpu
from jax.sharding import PartitionSpec as P

H = 24
KV = 8
HD = 64
E = 16
CAP = 160

epsilon = 1e-05
rope_base = 10000.0
masked_score = -1e30
bf16 = jnp.bfloat16
f32 = jnp.float32
MESH = pl.DeviceIdType.MESH


def dot(a, b, dims):
    return lax.dot_general(a, b, (dims, ((), ())), preferred_element_type=f32)


NN = ((1,), (0,))
NT = ((1,), (1,))
TN = ((0,), (0,))


def swapped(value):
    return lax.ppermute(value, "section", [(0, 1), (1, 0)])


def rotate_half(rows_in):
    half_width = rows_in.shape[-1] // 2
    return jnp.concatenate([-rows_in[..., half_width:], rows_in[..., :half_width]], axis=-1)


def rope_tables(position, head_dim):
    half_width = head_dim // 2
    freqs = rope_base ** (-2.0 * jnp.arange(half_width, dtype=f32) / head_dim)
    angles = position.astype(f32)[:, None] * freqs[None, :]
    return (
        jnp.concatenate([jnp.cos(angles)] * 2, axis=1),
        jnp.concatenate([jnp.sin(angles)] * 2, axis=1),
    )


def token_places(lengths, dealing, tokens_pack):
    seq_count = lengths.shape[0]
    token_index = jnp.arange(tokens_pack, dtype=jnp.int32)
    seq_index = jnp.arange(seq_count, dtype=jnp.int32)
    before = seq_index[None, :] <= seq_index[:, None]
    seq_ends = jnp.sum(jnp.where(before, lengths[None, :], 0), axis=1)
    seq_starts = seq_ends - lengths
    segment = jnp.sum((token_index[:, None] >= seq_ends[None, :]).astype(jnp.int32), axis=1)
    seg_onehot = (segment[:, None] == seq_index[None, :]).astype(jnp.int32)
    position = token_index - jnp.sum(seg_onehot * seq_starts[None, :], axis=1)
    dealt_rank = jnp.sum(
        jnp.where(dealing[:, None] == seq_index[None, :], seq_index[:, None], 0), axis=0
    )
    dealt_start = jnp.sum(
        jnp.where(dealt_rank[:, None] < dealt_rank[None, :], lengths[:, None], 0), axis=0
    )
    dealt_place = jnp.sum(seg_onehot * dealt_start[None, :], axis=1) + position
    return segment, position, dealt_place


def expert_masks(dealt_place, order, routes):
    tokens_pack = order.shape[0]
    token_index = jnp.arange(tokens_pack, dtype=jnp.int32)
    priority = jnp.sum(
        jnp.where(dealt_place[:, None] == token_index[None, :], order[None, :], 0), axis=1
    )
    expert_index = jnp.arange(E, dtype=jnp.int32)
    picked = jnp.any(routes[:, :, None] == expert_index[None, None, :], axis=1)
    earlier = (priority[None, :] < priority[:, None]).astype(bf16)
    rank = dot(earlier, picked.astype(bf16), NN)
    kept = picked & (rank < CAP)
    return picked.astype(f32), kept.astype(f32)


def norm_scale(rows_in):
    return lax.rsqrt(jnp.mean(rows_in * rows_in, axis=-1, keepdims=True) + epsilon)


def params(collective_id):
    return pltpu.CompilerParams(
        collective_id=collective_id, has_side_effects=True, vmem_limit_bytes=56 * 2**20
    )


def tensor_peers(count):
    me = lax.axis_index("tensor")
    return [{"tensor": lax.rem(me + step, count)} for step in range(1, count)]


def greet(peers):
    barrier = pltpu.get_barrier_semaphore()
    for peer in peers:
        pl.semaphore_signal(barrier, inc=1, device_id=peer, device_id_type=MESH)
    pl.semaphore_wait(barrier, len(peers))


def factors(count):
    inner = math.isqrt(count)
    while count % inner:
        inner -= 1
    return count // inner, inner


def group_place(count):
    outer, inner = factors(count)
    me = lax.axis_index("dp")
    return outer, inner, me // inner, lax.rem(me, inner)


def near_groups(count):
    outer, inner, mo, mi = group_place(count)
    across = [lax.rem(mi + step, inner) for step in range(1, inner)]
    along = [lax.rem(mo + step, outer) for step in range(1, outer)]
    return (
        [(place, {"dp": mo * inner + place}) for place in across],
        [(place, {"dp": place * inner + mi}) for place in along],
    )


class FirstStage:
    def __init__(self, value, axis):
        self.count = lax.axis_size("dp")
        outer, inner = factors(self.count)
        self.inputs = [value.reshape((outer, inner, value.shape[0] // self.count) + value.shape[1:])]
        self.axis = axis
        shape = list(self.inputs[0].shape[2:])
        shape[axis] //= 2
        self.half = shape[axis]
        self.outputs = [
            jax.ShapeDtypeStruct((inner - 1, outer, *shape), value.dtype),
            jax.ShapeDtypeStruct((outer - 1, inner, *shape), value.dtype),
        ]
        self.copies = inner + outer - 2

    def pairs(self, inputs, outputs):
        across, along = near_groups(self.count)
        value = inputs[0]
        cut = [slice(None)] * 3
        first, second = list(cut), list(cut)
        first[self.axis], second[self.axis] = pl.ds(0, self.half), pl.ds(self.half, self.half)
        found = []
        for slot, (place, device) in enumerate(across):
            found.append((value.at[(slice(None), place, *first)], outputs[0].at[slot], device))
        for slot, (place, device) in enumerate(along):
            found.append((value.at[(place, slice(None), *second)], outputs[1].at[slot], device))
        return found

    def peers(self):
        across, along = near_groups(self.count)
        return [device for _, device in across + along]

    def sums(self, outputs):
        outer, inner, mo, mi = group_place(self.count)
        value = self.inputs[0]
        first, second = jnp.split(value, 2, axis=2 + self.axis)
        row = lax.dynamic_index_in_dim(first, mi, 1, keepdims=False).astype(f32)
        col = lax.dynamic_index_in_dim(second, mo, 0, keepdims=False).astype(f32)
        for slot in range(inner - 1):
            row = row + outputs[0][slot].astype(f32)
        for slot in range(outer - 1):
            col = col + outputs[1][slot].astype(f32)
        return row.astype(bf16), col.astype(bf16)


class SecondStage:
    def __init__(self, row, col, axis):
        self.count = lax.axis_size("dp")
        outer, inner = factors(self.count)
        self.inputs = [row, col]
        self.axis = axis
        self.outputs = [
            jax.ShapeDtypeStruct((outer - 1, *row.shape[1:]), row.dtype),
            jax.ShapeDtypeStruct((inner - 1, *col.shape[1:]), col.dtype),
        ]
        self.copies = inner + outer - 2

    def pairs(self, inputs, outputs):
        across, along = near_groups(self.count)
        found = []
        for slot, (place, device) in enumerate(along):
            found.append((inputs[0].at[place], outputs[0].at[slot], device))
        for slot, (place, device) in enumerate(across):
            found.append((inputs[1].at[place], outputs[1].at[slot], device))
        return found

    def peers(self):
        across, along = near_groups(self.count)
        return [device for _, device in across + along]

    def sums(self, outputs):
        outer, inner, mo, mi = group_place(self.count)
        row = lax.dynamic_index_in_dim(self.inputs[0], mo, 0, keepdims=False).astype(f32)
        col = lax.dynamic_index_in_dim(self.inputs[1], mi, 0, keepdims=False).astype(f32)
        for slot in range(outer - 1):
            row = row + outputs[0][slot].astype(f32)
        for slot in range(inner - 1):
            col = col + outputs[1][slot].astype(f32)
        return jnp.concatenate([row, col], axis=self.axis)


class Scatter:
    def __init__(self, value):
        self.count = lax.axis_size("dp")
        block = (value.shape[0] // self.count,) + value.shape[1:]
        self.inputs = [value.reshape((self.count, *block))]
        self.outputs = [jax.ShapeDtypeStruct((self.count - 1, *block), value.dtype)]
        self.copies = self.count - 1

    def pairs(self, inputs, outputs):
        me = lax.axis_index("dp")
        found = []
        for step in range(1, self.count):
            place = lax.rem(me + step, self.count)
            found.append((inputs[0].at[place], outputs[0].at[step - 1], {"dp": place}))
        return found

    def peers(self):
        me = lax.axis_index("dp")
        return [{"dp": lax.rem(me + step, self.count)} for step in range(1, self.count)]

    def sums(self, outputs):
        me = lax.axis_index("dp")
        total = lax.dynamic_index_in_dim(self.inputs[0], me, 0, keepdims=False).astype(f32)
        for slot in range(self.count - 1):
            total = total + outputs[0][slot].astype(f32)
        return total.astype(bf16)


class Gather:
    def __init__(self, block):
        self.count = lax.axis_size("dp")
        self.inputs = [block]
        self.outputs = [jax.ShapeDtypeStruct((self.count, *block.shape), block.dtype)]
        self.copies = self.count - 1

    def pairs(self, inputs, outputs):
        me = lax.axis_index("dp")
        return [
            (inputs[0], outputs[0].at[me], {"dp": lax.rem(me + step, self.count)})
            for step in range(1, self.count)
        ]

    def peers(self):
        me = lax.axis_index("dp")
        return [{"dp": lax.rem(me + step, self.count)} for step in range(1, self.count)]

    def sums(self, outputs):
        me = lax.axis_index("dp")
        whole = lax.dynamic_update_index_in_dim(outputs[0], self.inputs[0], me, 0)
        return whole.reshape((-1, *self.inputs[0].shape[1:]))


class Beside:
    def __init__(self, jobs):
        self.jobs = jobs
        self.inputs = [v for job in jobs for v in job.inputs]
        self.outputs = [v for job in jobs for v in job.outputs]
        self.total = sum(job.copies for job in jobs)
        self.sems = [pltpu.SemaphoreType.DMA((max(1, self.total),)) for _ in range(2)]

    def peers(self):
        if any(isinstance(job, (Scatter, Gather)) for job in self.jobs):
            count = lax.axis_size("dp")
            me = lax.axis_index("dp")
            return [{"dp": lax.rem(me + step, count)} for step in range(1, count)]
        return self.jobs[0].peers() if self.jobs else []

    def make(self, inputs, outputs, sends, recvs):
        copies = []
        for job in self.jobs:
            mine, inputs = inputs[: len(job.inputs)], inputs[len(job.inputs) :]
            theirs, outputs = outputs[: len(job.outputs)], outputs[len(job.outputs) :]
            for src, dst, device in job.pairs(mine, theirs):
                index = len(copies)
                copies.append(
                    pltpu.make_async_remote_copy(
                        src_ref=src, dst_ref=dst, send_sem=sends.at[index], recv_sem=recvs.at[index],
                        device_id=device, device_id_type=MESH,
                    )
                )
        return copies

    def results(self, outputs):
        found = []
        for job in self.jobs:
            found.append(job.sums(outputs[: len(job.outputs)]))
            outputs = outputs[len(job.outputs) :]
        return found


def spread(count, buf, rows, sends, recvs):
    me = lax.axis_index("tensor")
    own = buf.at[pl.ds(pl.multiple_of(me * rows, rows), rows)]
    copies = []
    for step in range(1, count):
        copies.append(
            pltpu.make_async_remote_copy(
                src_ref=own,
                dst_ref=own,
                send_sem=sends.at[step - 1],
                recv_sem=recvs.at[step - 1],
                device_id={"tensor": lax.rem(me + step, count)},
                device_id_type=MESH,
            )
        )
    for copy in copies:
        copy.start()
    return copies


def deal_out(count, part, rows, columns, landing, sends, recvs):
    me = lax.axis_index("tensor")
    copies = []
    for step in range(1, count):
        peer = lax.rem(me + step, count)
        copies.append(
            pltpu.make_async_remote_copy(
                src_ref=part.at[pl.ds(pl.multiple_of(peer * rows, rows), rows), columns],
                dst_ref=landing.at[step - 1, :, columns],
                send_sem=sends.at[step - 1],
                recv_sem=recvs.at[step - 1],
                device_id={"tensor": peer},
                device_id_type=MESH,
            )
        )
    for copy in copies:
        copy.start()
    return copies


def core_peer():
    return {"section": 1 - lax.axis_index("section")}


def hand_over(own, sent, kept, received, sems, index):
    copies = [
        pltpu.make_async_copy(own, kept, sems[0].at[index]),
        pltpu.make_async_remote_copy(
            src_ref=sent, dst_ref=received, send_sem=sems[1].at[index], recv_sem=sems[2].at[index],
            device_id=core_peer(), device_id_type=MESH,
        ),
    ]
    for copy in copies:
        copy.start()
    return copies


def hand_rows(value, pair, sems, index):
    tokens = value.shape[0]
    return hand_over(value, value, pair.at[pl.ds(0, tokens)], pair.at[pl.ds(tokens, tokens)], sems, index)


def hand_halves(value, pair, sems, index):
    section = lax.axis_index("section")
    tokens, half = value.shape[0], value.shape[1] // 2
    mine = value.at[:, pl.ds(pl.multiple_of(section * half, half), half)]
    other = value.at[:, pl.ds(pl.multiple_of((1 - section) * half, half), half)]
    return hand_over(mine, other, pair.at[pl.ds(0, tokens)], pair.at[pl.ds(tokens, tokens)], sems, index)


def wait_all(copies):
    for copy in copies:
        copy.wait()


def either(use_own, own, other, run):
    @pl.when(use_own)
    def _():
        run(own)

    @pl.when(jnp.logical_not(use_own))
    def _():
        run(other)


def weight_copies(refs, scratch, sems, expert):
    gate, up, down = refs
    gu_s, down_s = scratch
    width = gate.shape[2]
    return (
        pltpu.make_async_copy(gate.at[expert], gu_s.at[expert, :, pl.ds(0, width)], sems.at[0, expert]),
        pltpu.make_async_copy(up.at[expert], gu_s.at[expert, :, pl.ds(width, width)], sems.at[1, expert]),
        pltpu.make_async_copy(
            down.at[expert], down_s.at[pl.ds(pl.multiple_of(expert * width, width), width)], sems.at[2, expert]
        ),
    )


def attn_copies(refs, scratch, sems):
    query, key, value, output = refs
    joint_s, output_s = scratch
    qw, kw = query.shape[1], key.shape[1]
    return (
        pltpu.make_async_copy(query, joint_s.at[:, pl.ds(0, qw)], sems.at[0]),
        pltpu.make_async_copy(key, joint_s.at[:, pl.ds(qw, kw)], sems.at[1]),
        pltpu.make_async_copy(value, joint_s.at[:, pl.ds(qw + kw, kw)], sems.at[2]),
        pltpu.make_async_copy(output, output_s, sems.at[3]),
    )


def turned(block):
    lane = lax.broadcasted_iota(jnp.int32, block.shape, 1)
    half = HD // 2
    return jnp.where(
        lane % HD < half, pltpu.roll(block, block.shape[1] - half, 1), pltpu.roll(block, half, 1)
    )


def column(table, index):
    lane = lax.broadcasted_iota(jnp.int32, table.shape, 1)
    return jnp.sum(jnp.where(lane == index, table, 0.0), axis=1, keepdims=True)


def swap_copies(own, other, sems, piece):
    sends, recvs = sems
    names = len(own)
    if isinstance(piece, tuple):
        name, expert = piece
        source, target = own[name].at[expert], other[name].at[expert]
        index = 4 + (name - 4) * own[4].shape[0] + expert
    else:
        source, target, index = own[piece], other[piece], piece
    return pltpu.make_async_remote_copy(
        src_ref=source, dst_ref=target, send_sem=sends.at[index], recv_sem=recvs.at[index],
        device_id=core_peer(), device_id_type=MESH,
    )


def forward_kernel(layer, count, swap, *refs):
    refs = list(refs)

    def take(number):
        taken = refs[:number]
        del refs[:number]
        return taken

    stream, attn_gain, expert_gain, router, cosine, sine, bias, picked, kept = take(9)
    own = take(7)
    other = None if swap else take(7)
    (out, mid_out, expert_rows_out, qs_out, keys_out, values_out, probs_out, gate_out,
     attn_in_out, expert_in_out, gated_out, attended_out, pre_out) = take(13)
    if swap:
        other = take(7)
    scratch = take(4)
    joint_s, output_s, gu_s, down_s = scratch
    (ag1, ag2, part, landing1, landing2, pre_s, gated_s, attended_s, send_s, recv_s, attn_sems,
     expert_sems, pre_sems, *core_sems) = refs[:16]
    swap_sems = refs[16:]
    rows, width = stream.shape
    tokens = ag1.shape[0]
    experts = gu_s.shape[0]
    hidden_width = gu_s.shape[2] // 2
    kw = keys_out.shape[1]
    qw = attended_s.shape[1]
    heads, key_heads = qw // HD, kw // HD
    group = heads // key_heads
    me = lax.axis_index("tensor")
    own_rows = pl.ds(pl.multiple_of(me * rows, rows), rows)
    use_own = lax.axis_index("section") == layer

    def start_attn(w):
        for copy in attn_copies(w[:4], scratch[:2], attn_sems):
            copy.start()

    def wait_attn(w):
        for copy in attn_copies(w[:4], scratch[:2], attn_sems):
            copy.wait()

    def start_expert(w, expert):
        for copy in weight_copies(w[4:], scratch[2:], expert_sems, expert):
            copy.start()

    def wait_expert(w, expert):
        for copy in weight_copies(w[4:], scratch[2:], expert_sems, expert):
            copy.wait()

    def each_expert(run):
        def step(expert, carry):
            run(expert)
            return carry

        lax.fori_loop(0, experts, step, 0)

    def swap_expert(expert):
        return [swap_copies(own, other, swap_sems, (name, expert)) for name in (4, 5, 6)]

    value = stream[...].astype(bf16).astype(f32)
    ag1[own_rows, :] = (value * norm_scale(value) * attn_gain[...]).astype(bf16)
    greet(tensor_peers(count) + [core_peer()])
    first = spread(count, ag1, rows, send_s.at[0], recv_s.at[0])
    if swap:
        for piece in range(4):
            swap_copies(own, other, swap_sems, piece).start()
        each_expert(lambda expert: [c.start() for c in swap_expert(expert)] and None)

        @pl.when(use_own)
        def _():
            start_attn(own)
            each_expert(lambda expert: start_expert(own, expert))

        @pl.when(jnp.logical_not(use_own))
        def _():
            for piece in range(4):
                swap_copies(own, other, swap_sems, piece).wait_recv()
            start_attn(other)
    else:
        either(use_own, own, other, start_attn)
        either(use_own, own, other, lambda w: each_expert(lambda expert: start_expert(w, expert)))
    wait_all(first)
    handed = hand_halves(ag1, attn_in_out, core_sems, 0)
    either(use_own, own, other, wait_attn)
    proj = dot(ag1[...], joint_s[...], NN)
    for chunk in range(qw // 128):
        block = proj[:, chunk * 128 : chunk * 128 + 128]
        block = (block * cosine[...] + turned(block) * sine[...]).astype(bf16)
        for part_index in range(128 // HD):
            head = chunk * (128 // HD) + part_index
            qs_out[pl.ds(head * tokens, tokens), :] = block[:, part_index * HD : part_index * HD + HD]
    for chunk in range(kw // 128):
        block = proj[:, qw + chunk * 128 : qw + chunk * 128 + 128]
        keys_out[:, pl.ds(chunk * 128, 128)] = (
            block * cosine[...] + turned(block) * sine[...]
        ).astype(bf16)
    values_out[...] = proj[:, qw + kw :].astype(bf16)
    for g in range(key_heads):
        lanes = pl.ds(g * HD, HD)
        span = pl.ds(g * group * tokens, group * tokens)
        scores = dot(qs_out[span, :], keys_out[:, lanes], NT) * 0.125
        scores = (scores.reshape(group, tokens, tokens) + bias[...][None]).reshape(
            group * tokens, tokens
        )
        top = jnp.max(scores, axis=1, keepdims=True)
        weighed = jnp.exp(scores - top)
        probs = (weighed / jnp.sum(weighed, axis=1, keepdims=True)).astype(bf16)
        probs_out[span, :] = probs
        attended = dot(probs, values_out[:, lanes], NN).astype(bf16)
        for h in range(group):
            attended_s[:, pl.ds((g * group + h) * HD, HD)] = attended[h * tokens : (h + 1) * tokens]
    handed += hand_rows(attended_s, attended_out, core_sems, 1)
    part[...] = dot(attended_s[...], output_s[...], NN).astype(bf16)
    dealt = deal_out(count, part, rows, slice(None), landing1, send_s.at[1], recv_s.at[1])
    if swap:
        lead = min(4, experts)

        @pl.when(jnp.logical_not(use_own))
        def _():
            for expert in range(lead):
                for copy in swap_expert(expert):
                    copy.wait_recv()
                start_expert(other, expert)

    wait_all(dealt)
    mid = value + part[own_rows, :].astype(f32)
    for step in range(count - 1):
        mid = mid + landing1[step].astype(f32)
    mid_out[...] = mid
    expert_rows = (mid * norm_scale(mid) * expert_gain[...]).astype(bf16)
    expert_rows_out[...] = expert_rows
    ag2[own_rows, :] = expert_rows
    wait_all(spread(count, ag2, rows, send_s.at[2], recv_s.at[2]))
    handed += hand_halves(ag2, expert_in_out, core_sems, 2)
    logits = dot(ag2[...], router[...], NN)
    chosen = picked[...] > 0
    top = jnp.max(jnp.where(chosen, logits, masked_score), axis=1, keepdims=True)
    weighed = jnp.where(chosen, jnp.exp(logits - top), 0.0)
    gate_out[...] = weighed / jnp.sum(weighed, axis=1, keepdims=True)

    def expert_step(expert, carry):
        if swap:

            @pl.when(jnp.logical_not(use_own) & (expert + lead < experts))
            def _():
                for copy in swap_expert(expert + lead):
                    copy.wait_recv()
                start_expert(other, expert + lead)

        either(use_own, own, other, lambda w: wait_expert(w, expert))
        pre = dot(ag2[...], gu_s[expert], NN)
        pre_s[expert] = pre
        pltpu.make_async_copy(pre_s.at[expert], pre_out.at[expert], pre_sems.at[expert]).start()
        gate_pre, up_pre = pre[:, :hidden_width], pre[:, hidden_width:]
        hidden = (gate_pre / (1.0 + jnp.exp(-gate_pre)) * up_pre).astype(bf16).astype(f32)
        weight = column(gate_out[...] * kept[...], expert)
        gated_s[:, pl.ds(pl.multiple_of(expert * hidden_width, hidden_width), hidden_width)] = (
            hidden * weight
        ).astype(bf16)
        return carry

    lax.fori_loop(0, experts, expert_step, 0)
    handed += hand_rows(gated_s, gated_out, core_sems, 3)
    copies = []
    tile = width // 4
    for t in range(4):
        columns = pl.ds(t * tile, tile)
        part[:, columns] = dot(gated_s[...], down_s[:, columns], NN).astype(bf16)
        copies += deal_out(count, part, rows, columns, landing2, send_s.at[3 + t], recv_s.at[3 + t])
    wait_all(copies)
    total = mid_out[...] + part[own_rows, :].astype(f32)
    for step in range(count - 1):
        total = total + landing2[step].astype(f32)
    out[...] = total
    wait_all(handed)
    if swap:
        for piece in range(4):
            swap_copies(own, other, swap_sems, piece).wait_send()
        each_expert(lambda expert: [c.wait_send() for c in swap_expert(expert)] and None)

        @pl.when(use_own)
        def _():
            for piece in range(4):
                swap_copies(own, other, swap_sems, piece).wait_recv()
            each_expert(lambda expert: [c.wait_recv() for c in swap_expert(expert)] and None)

    def finish(expert, carry):
        pltpu.make_async_copy(pre_s.at[expert], pre_out.at[expert], pre_sems.at[expert]).wait()
        return carry

    lax.fori_loop(0, experts, finish, 0)


def weight_scratch(own):
    query, key, value, output, gate, up, down = own
    depth = query.shape[0]
    experts, _, hidden_width = gate.shape
    return [
        pltpu.VMEM((depth, query.shape[1] + 2 * key.shape[1]), bf16),
        pltpu.VMEM(output.shape, bf16),
        pltpu.VMEM((experts, depth, 2 * hidden_width), bf16),
        pltpu.VMEM((experts * hidden_width, depth), bf16),
    ]


def layer_forward(layer, gains, own, other, stream, tables, masks, bias):
    count = lax.axis_size("tensor")
    attn_gain, expert_gain, router = gains
    picked, kept = masks
    rows, width = stream.shape
    tokens = bias.shape[0]
    qw, kw = own[0].shape[1], own[1].shape[1]
    experts, _, hidden_width = own[4].shape
    heads = qw // HD
    swap = other is None
    vmem = pl.BlockSpec(memory_space=pltpu.VMEM)
    hbm = pl.BlockSpec(memory_space=pl.ANY)
    shape = jax.ShapeDtypeStruct
    dma = pltpu.SemaphoreType.DMA
    pieces = 4 + 3 * experts
    found = pl.pallas_call(
        functools.partial(forward_kernel, layer, count, swap),
        name=f"layer_forward_{layer}",
        out_shape=(
            shape((rows, width), f32),
            shape((rows, width), f32),
            shape((rows, width), bf16),
            shape((heads * tokens, HD), bf16),
            shape((tokens, kw), bf16),
            shape((tokens, kw), bf16),
            shape((heads * tokens, tokens), bf16),
            shape((tokens, experts), f32),
            shape((2 * tokens, width // 2), bf16),
            shape((2 * tokens, width // 2), bf16),
            shape((2 * tokens, experts * hidden_width), bf16),
            shape((2 * tokens, qw), bf16),
            shape((experts, tokens, 2 * hidden_width), f32),
        )
        + (tuple(shape(w.shape, w.dtype) for w in own) if swap else ()),
        in_specs=[vmem] * 9 + [hbm] * (7 if swap else 14),
        out_specs=(vmem,) * 8 + (hbm,) * (12 if swap else 5),
        scratch_shapes=weight_scratch(own)
        + [
            pltpu.VMEM((tokens, width), bf16),
            pltpu.VMEM((tokens, width), bf16),
            pltpu.VMEM((tokens, width), bf16),
            pltpu.VMEM((count - 1, rows, width), bf16),
            pltpu.VMEM((count - 1, rows, width), bf16),
            pltpu.VMEM((experts, tokens, 2 * hidden_width), f32),
            pltpu.VMEM((tokens, experts * hidden_width), bf16),
            pltpu.VMEM((tokens, qw), bf16),
            dma((7, count - 1)),
            dma((7, count - 1)),
            dma((4,)),
            dma((3, experts)),
            dma((experts,)),
            dma((4,)),
            dma((4,)),
            dma((4,)),
        ]
        + ([dma((pieces,)), dma((pieces,))] if swap else []),
        compiler_params=params(1 + layer),
    )(stream, attn_gain, expert_gain, router, *tables, bias, picked, kept, *own,
      *(() if swap else other))
    return found[:13], found[13:]


def norm_back(value, gain, out_grad):
    scale = norm_scale(value)
    scaled = value * scale
    gain_grad = jnp.sum(out_grad * scaled, axis=0, keepdims=True)
    inner = out_grad * gain
    value_grad = scale * (inner - scaled * jnp.mean(inner * scaled, axis=-1, keepdims=True))
    return value_grad, gain_grad


def experts_back_kernel(layer, count, beside, *refs):
    refs = list(refs)

    def take(number):
        taken = refs[:number]
        del refs[:number]
        return taken

    out_grad, mid, expert_gain, router, kept, gate, expert_rows, pre_in = take(8)
    own, other = take(3), take(3)
    beside_in = take(len(beside.inputs))
    mid_grad_out, router_out, expert_gain_out, og_out, gpu_out = take(5)
    beside_out = take(len(beside.outputs))
    scratch = take(2)
    gu_s, down_s = scratch
    (ag1, part, landing1, pre_s, gpu_s, acc, gate_part, gate_land, send_s, recv_s, expert_sems,
     pre_sems, beside_send, beside_recv, *core_sems) = refs
    rows, width = mid.shape
    experts = gu_s.shape[0]
    hidden_width = gu_s.shape[2] // 2
    me = lax.axis_index("tensor")
    own_rows = pl.ds(pl.multiple_of(me * rows, rows), rows)
    use_own = lax.axis_index("section") == layer

    def start_expert(expert, carry):
        either(use_own, own, other,
               lambda w: [c.start() for c in weight_copies(w, scratch, expert_sems, expert)])
        pltpu.make_async_copy(pre_in.at[expert], pre_s.at[expert], pre_sems.at[expert]).start()
        return carry

    ag1[own_rows, :] = out_grad[...].astype(bf16)
    greet(tensor_peers(count) + [core_peer()] + beside.peers())
    first = spread(count, ag1, rows, send_s.at[0], recv_s.at[0])
    lax.fori_loop(0, experts, start_expert, 0)
    behind = beside.make(beside_in, beside_out, beside_send, beside_recv)
    for copy in behind:
        copy.start()
    gate_part[...] = jnp.zeros_like(gate_part)
    wait_all(first)
    handed = hand_halves(ag1, og_out, core_sems, 0)

    def expert_step(expert, carry):
        either(use_own, own, other,
               lambda w: [c.wait() for c in weight_copies(w, scratch, expert_sems, expert)])
        pltpu.make_async_copy(pre_in.at[expert], pre_s.at[expert], pre_sems.at[expert]).wait()
        lanes = pl.ds(pl.multiple_of(expert * hidden_width, hidden_width), hidden_width)
        plain = dot(ag1[...], down_s[lanes, :], NT)
        gate_pre = pre_s[expert, :, pl.ds(0, hidden_width)]
        up_pre = pre_s[expert, :, pl.ds(hidden_width, hidden_width)]
        sig = 1.0 / (1.0 + jnp.exp(-gate_pre))
        act = gate_pre * sig
        hidden = (act * up_pre).astype(bf16).astype(f32)
        held = column(kept[...], expert)
        weight = column(gate[...], expert) * held
        summed = jnp.sum(hidden * plain, axis=1, keepdims=True) * held
        lane = lax.broadcasted_iota(jnp.int32, gate_part.shape, 1)
        gate_part[...] += jnp.where(lane == expert, summed, 0.0)
        hidden_grad = plain * weight
        gpu_s[expert, :, pl.ds(0, hidden_width)] = (
            hidden_grad * up_pre * (sig * (1.0 + gate_pre * (1.0 - sig)))
        ).astype(bf16)
        gpu_s[expert, :, pl.ds(hidden_width, hidden_width)] = (hidden_grad * act).astype(bf16)
        back = dot(gpu_s[expert], gu_s[expert], NT)

        @pl.when(expert == 0)
        def _():
            acc[...] = back

        @pl.when(expert > 0)
        def _():
            acc[...] += back

        return carry

    lax.fori_loop(0, experts, expert_step, 0)
    tokens = ag1.shape[0]
    handed += hand_over(
        gpu_s, gpu_s, gpu_out.at[:, pl.ds(0, tokens)], gpu_out.at[:, pl.ds(tokens, tokens)], core_sems, 1
    )
    part[...] = acc[...].astype(bf16)
    copies = deal_out(count, part, rows, slice(None), landing1, send_s.at[1], recv_s.at[1])
    copies += deal_out(count, gate_part, rows, slice(None), gate_land, send_s.at[2], recv_s.at[2])
    wait_all(copies)
    in_grad = acc[own_rows, :]
    gate_grad = gate_part[own_rows, :]
    for step in range(count - 1):
        in_grad = in_grad + landing1[step].astype(f32)
        gate_grad = gate_grad + gate_land[step]
    gate_grad = gate_grad[:, :experts]
    gate_rows = gate[own_rows, :]
    logits_grad = (
        gate_rows * (gate_grad - jnp.sum(gate_rows * gate_grad, axis=1, keepdims=True))
    ).astype(bf16)
    router_out[...] = dot(logits_grad, expert_rows[...], TN)
    in_grad = in_grad + dot(logits_grad, router[...], NT)
    mid_part, expert_gain_grad = norm_back(mid[...], expert_gain[...], in_grad)
    expert_gain_out[...] = expert_gain_grad
    mid_grad_out[...] = ag1[own_rows, :].astype(f32) + mid_part
    wait_all(handed)
    wait_all(behind)


def experts_back(layer, gains, own, other, out_grad, state, masks, beside):
    count = lax.axis_size("tensor")
    _, expert_gain, router = gains
    mid, gate, expert_rows, pre = state
    rows, width = mid.shape
    tokens = gate.shape[0]
    own, other = own[4:], other[4:]
    experts, depth, hidden_width = own[0].shape
    vmem = pl.BlockSpec(memory_space=pltpu.VMEM)
    hbm = pl.BlockSpec(memory_space=pl.ANY)
    shape = jax.ShapeDtypeStruct
    found = pl.pallas_call(
        functools.partial(experts_back_kernel, layer, count, beside),
        name=f"experts_back_{layer}",
        out_shape=(
            shape((rows, width), f32),
            shape((experts, width), f32),
            shape((1, width), f32),
            shape((2 * tokens, width // 2), bf16),
            shape((experts, 2 * tokens, 2 * hidden_width), bf16),
            *beside.outputs,
        ),
        in_specs=[vmem] * 7 + [hbm] * (7 + len(beside.inputs)),
        out_specs=(vmem, vmem, vmem, hbm, hbm) + (hbm,) * len(beside.outputs),
        scratch_shapes=[
            pltpu.VMEM((experts, depth, 2 * hidden_width), bf16),
            pltpu.VMEM((experts * hidden_width, depth), bf16),
            pltpu.VMEM((tokens, width), bf16),
            pltpu.VMEM((tokens, width), bf16),
            pltpu.VMEM((count - 1, rows, width), bf16),
            pltpu.VMEM((experts, tokens, 2 * hidden_width), f32),
            pltpu.VMEM((experts, tokens, 2 * hidden_width), bf16),
            pltpu.VMEM((tokens, width), f32),
            pltpu.VMEM((tokens, 128), f32),
            pltpu.VMEM((count - 1, rows, 128), f32),
            pltpu.SemaphoreType.DMA((3, count - 1)),
            pltpu.SemaphoreType.DMA((3, count - 1)),
            pltpu.SemaphoreType.DMA((3, experts)),
            pltpu.SemaphoreType.DMA((experts,)),
            *beside.sems,
            *[pltpu.SemaphoreType.DMA((2,)) for _ in range(3)],
        ],
        compiler_params=params(3 + layer),
    )(out_grad, mid, expert_gain, router, masks[1], gate, expert_rows, pre, *own, *other,
      *beside.inputs)
    return found[:5], beside.results(found[5:])


def attention_back_kernel(layer, count, beside, *refs):
    refs = list(refs)

    def take(number):
        taken = refs[:number]
        del refs[:number]
        return taken

    mid_grad, stream, attn_gain, cosine, sine, qs, keys, values, probs = take(9)
    own, other = take(4), take(4)
    beside_in = take(len(beside.inputs))
    grad_out, attn_gain_out, ao_out, joint_out = take(4)
    beside_out = take(len(beside.outputs))
    scratch = take(2)
    joint_s, output_s = scratch
    (ag2, part, landing2, ag_stack, dq_s, joint_rows, send_s, recv_s, attn_sems, beside_send,
     beside_recv, *core_sems) = refs
    rows, width = stream.shape
    tokens = ag2.shape[0]
    kw = keys.shape[1]
    qw = output_s.shape[0]
    heads, key_heads = qw // HD, kw // HD
    group = heads // key_heads
    me = lax.axis_index("tensor")
    own_rows = pl.ds(pl.multiple_of(me * rows, rows), rows)
    use_own = lax.axis_index("section") == layer
    ag2[own_rows, :] = mid_grad[...].astype(bf16)
    greet(tensor_peers(count) + [core_peer()] + beside.peers())
    first = spread(count, ag2, rows, send_s.at[0], recv_s.at[0])
    either(use_own, own, other, lambda w: [c.start() for c in attn_copies(w, scratch, attn_sems)])
    behind = beside.make(beside_in, beside_out, beside_send, beside_recv)
    for copy in behind:
        copy.start()
    wait_all(first)
    handed = hand_halves(ag2, ao_out, core_sems, 0)
    either(use_own, own, other, lambda w: [c.wait() for c in attn_copies(w, scratch, attn_sems)])
    attended_grad = dot(ag2[...], output_s[...], NT).astype(bf16)
    for h in range(heads):
        ag_stack[pl.ds(h * tokens, tokens), :] = attended_grad[:, h * HD : (h + 1) * HD]
    for g in range(key_heads):
        lanes = pl.ds(g * HD, HD)
        span = pl.ds(g * group * tokens, group * tokens)
        soft_b = probs[span, :]
        soft = soft_b.astype(f32)
        soft_grad = dot(ag_stack[span, :], values[:, lanes], NT)
        inner = jnp.sum(soft * soft_grad, axis=1, keepdims=True)
        score_grad = (soft * (soft_grad - inner)).astype(bf16)
        dq = dot(score_grad, keys[:, lanes], NN) * 0.125
        for h in range(group):
            dq_s[:, pl.ds((g * group + h) * HD, HD)] = dq[h * tokens : (h + 1) * tokens]
        dq_s[:, pl.ds(qw + g * HD, HD)] = dot(score_grad, qs[span, :], TN) * 0.125
        joint_rows[:, pl.ds(qw + kw + g * HD, HD)] = dot(soft_b, ag_stack[span, :], TN).astype(bf16)
    for chunk in range((qw + kw) // 128):
        lanes = pl.ds(chunk * 128, 128)
        block = dq_s[:, lanes]
        joint_rows[:, lanes] = (block * cosine[...] - turned(block) * sine[...]).astype(bf16)
    handed += hand_rows(joint_rows, joint_out, core_sems, 1)
    copies = []
    tile = width // 2
    for t in range(2):
        columns = pl.ds(t * tile, tile)
        part[:, columns] = dot(joint_rows[...], joint_s[columns, :], NT).astype(bf16)
        copies += deal_out(count, part, rows, columns, landing2, send_s.at[1 + t], recv_s.at[1 + t])
    wait_all(copies)
    in_grad = part[own_rows, :].astype(f32)
    for step in range(count - 1):
        in_grad = in_grad + landing2[step].astype(f32)
    stream_part, attn_gain_grad = norm_back(
        stream[...].astype(bf16).astype(f32), attn_gain[...], in_grad
    )
    attn_gain_out[...] = attn_gain_grad
    grad_out[...] = mid_grad[...] + stream_part
    wait_all(handed)
    wait_all(behind)


def attention_back(layer, gains, own, other, mid_grad, stream, state, tables, beside):
    count = lax.axis_size("tensor")
    attn_gain = gains[0]
    qs, keys, values, probs = state
    rows, width = stream.shape
    tokens = keys.shape[0]
    own, other = own[:4], other[:4]
    qw, kw = own[0].shape[1], own[1].shape[1]
    heads = qw // HD
    vmem = pl.BlockSpec(memory_space=pltpu.VMEM)
    hbm = pl.BlockSpec(memory_space=pl.ANY)
    shape = jax.ShapeDtypeStruct
    found = pl.pallas_call(
        functools.partial(attention_back_kernel, layer, count, beside),
        name=f"attention_back_{layer}",
        out_shape=(
            shape((rows, width), f32),
            shape((1, width), f32),
            shape((2 * tokens, width // 2), bf16),
            shape((2 * tokens, qw + 2 * kw), bf16),
            *beside.outputs,
        ),
        in_specs=[vmem] * 9 + [hbm] * (8 + len(beside.inputs)),
        out_specs=(vmem, vmem, hbm, hbm) + (hbm,) * len(beside.outputs),
        scratch_shapes=[
            pltpu.VMEM((width, qw + 2 * kw), bf16),
            pltpu.VMEM((qw, width), bf16),
            pltpu.VMEM((tokens, width), bf16),
            pltpu.VMEM((tokens, width), bf16),
            pltpu.VMEM((count - 1, rows, width), bf16),
            pltpu.VMEM((heads * tokens, HD), bf16),
            pltpu.VMEM((tokens, qw + kw), f32),
            pltpu.VMEM((tokens, qw + 2 * kw), bf16),
            pltpu.SemaphoreType.DMA((3, count - 1)),
            pltpu.SemaphoreType.DMA((3, count - 1)),
            pltpu.SemaphoreType.DMA((4,)),
            *beside.sems,
            *[pltpu.SemaphoreType.DMA((2,)) for _ in range(3)],
        ],
        compiler_params=params(5 + layer),
    )(mid_grad, stream, attn_gain, *tables, qs, keys, values, probs, *own, *other, *beside.inputs)
    return found[:4], beside.results(found[4:])


def finish_kernel(beside, *refs):
    refs = list(refs)

    def take(number):
        taken = refs[:number]
        del refs[:number]
        return taken

    small, dense, *beside_in = take(2 + len(beside.inputs))
    small_out, whole_out, *beside_out = take(2 + len(beside.outputs))
    (landing, block, small_z, small_dp, small_core, small_sum, small_mid, small_last, small_whole,
     sends, recvs, local_sems, z_sends, z_recvs, dp_sends, dp_recvs, core_sends, core_recvs,
     beside_send, beside_recv) = refs
    count = dense.shape[0]
    tensor = small_z.shape[0] + 1
    lanes = small_z.shape[2]
    me = lax.axis_index("dp")
    here = lax.axis_index("tensor")
    groups = [{"dp": lax.rem(me + step, count)} for step in range(1, count)]
    greet(groups + tensor_peers(tensor) + [core_peer()])

    def remote(src, dst, send, recv, device):
        copy = pltpu.make_async_remote_copy(
            src_ref=src, dst_ref=dst, send_sem=send, recv_sem=recv, device_id=device, device_id_type=MESH
        )
        copy.start()
        return copy

    def columns(place):
        return pl.ds(pl.multiple_of(place * lanes, lanes), lanes)

    first = []
    for step in range(1, tensor):
        place = lax.rem(here + step, tensor)
        first.append(
            remote(small.at[:, columns(place)], small_z.at[step - 1], z_sends.at[0, step - 1],
                   z_recvs.at[0, step - 1], {"tensor": place})
        )
    copies = []
    for step in range(1, count):
        place = lax.rem(me + step, count)
        copies.append(
            remote(dense.at[place], landing.at[step - 1], sends.at[0, step - 1],
                   recvs.at[0, step - 1], {"dp": place})
        )
    behind = beside.make(beside_in, beside_out, beside_send, beside_recv)
    for copy in behind:
        copy.start()
    mine = pltpu.make_async_copy(dense.at[me], block, local_sems.at[0])
    mine.start()
    wait_all(first)
    total = small[:, columns(here)]
    for step in range(tensor - 1):
        total = total + small_z[step]
    small_sum[...] = total
    second = [
        remote(small_sum, small_dp.at[step], dp_sends.at[step], dp_recvs.at[step], groups[step])
        for step in range(count - 1)
    ]
    mine.wait()
    wait_all(copies)
    total = block[...].astype(f32)
    for step in range(count - 1):
        total = total + landing[step].astype(f32)
    block[...] = total.astype(bf16)
    copies = [
        remote(block, whole_out.at[me], sends.at[1, step], recvs.at[1, step], groups[step])
        for step in range(count - 1)
    ]
    mine = pltpu.make_async_copy(block, whole_out.at[me], local_sems.at[1])
    mine.start()
    wait_all(second)
    total = small_sum[...]
    for step in range(count - 1):
        total = total + small_dp[step]
    small_mid[...] = total
    third = remote(small_mid, small_core, core_sends.at[0], core_recvs.at[0], core_peer())
    third.wait()
    small_last[...] = small_mid[...] + small_core[...]
    last = [
        remote(small_last, small_whole.at[:, columns(here)], z_sends.at[1, step - 1],
               z_recvs.at[1, step - 1], {"tensor": lax.rem(here + step, tensor)})
        for step in range(1, tensor)
    ]
    small_whole[:, columns(here)] = small_last[...]
    wait_all(last)
    small_out[...] = small_whole[...]
    mine.wait()
    wait_all(copies)
    wait_all(behind)


def finish(small, dense, beside):
    count = lax.axis_size("dp")
    tensor = lax.axis_size("tensor")
    rows = dense.shape[0] // count
    lanes = small.shape[1] // tensor
    hbm = pl.BlockSpec(memory_space=pl.ANY)
    vmem = pl.BlockSpec(memory_space=pltpu.VMEM)
    dma = pltpu.SemaphoreType.DMA
    found = pl.pallas_call(
        functools.partial(finish_kernel, beside),
        name="finish",
        out_shape=(
            jax.ShapeDtypeStruct(small.shape, f32),
            jax.ShapeDtypeStruct((count, rows, dense.shape[1]), bf16),
            *beside.outputs,
        ),
        in_specs=[vmem] + [hbm] * (1 + len(beside.inputs)),
        out_specs=(vmem,) + (hbm,) * (1 + len(beside.outputs)),
        scratch_shapes=[
            pltpu.VMEM((count - 1, rows, dense.shape[1]), bf16),
            pltpu.VMEM((rows, dense.shape[1]), bf16),
            pltpu.VMEM((tensor - 1, small.shape[0], lanes), f32),
            pltpu.VMEM((count - 1, small.shape[0], lanes), f32),
            pltpu.VMEM((small.shape[0], lanes), f32),
            pltpu.VMEM((small.shape[0], lanes), f32),
            pltpu.VMEM((small.shape[0], lanes), f32),
            pltpu.VMEM((small.shape[0], lanes), f32),
            pltpu.VMEM(small.shape, f32),
            dma((2, count - 1)),
            dma((2, count - 1)),
            dma((2,)),
            dma((2, tensor - 1)),
            dma((2, tensor - 1)),
            dma((count - 1,)),
            dma((count - 1,)),
            dma((1,)),
            dma((1,)),
            *beside.sems,
        ],
        compiler_params=params(7),
    )(small, dense.reshape(count, rows, dense.shape[1]), *beside.inputs)
    return found[0], found[1].reshape(dense.shape), beside.results(found[2:])


def expert_grads_kernel(x, og, gpu, gated, pair, down, turned_x):
    @pl.when(pl.program_id(0) == 0)
    def _():
        turned_x[...] = x[...].T

    pair[0] = dot(turned_x[...], gpu[0], NN).astype(bf16)
    down[0] = dot(gated[...], og[...], TN).astype(bf16)


def expert_grads(x, og, gpu, gated):
    tokens, half = x.shape
    experts, _, wide = gpu.shape
    hidden_width = wide // 2
    return pl.pallas_call(
        expert_grads_kernel,
        name="expert_grads",
        grid=(experts,),
        out_shape=(
            jax.ShapeDtypeStruct((experts, half, wide), bf16),
            jax.ShapeDtypeStruct((experts, hidden_width, half), bf16),
        ),
        in_specs=[
            pl.BlockSpec((tokens, half), lambda e: (0, 0)),
            pl.BlockSpec((tokens, half), lambda e: (0, 0)),
            pl.BlockSpec((1, tokens, wide), lambda e: (e, 0, 0)),
            pl.BlockSpec((tokens, hidden_width), lambda e: (0, e)),
        ],
        out_specs=(
            pl.BlockSpec((1, half, wide), lambda e: (e, 0, 0)),
            pl.BlockSpec((1, hidden_width, half), lambda e: (e, 0, 0)),
        ),
        scratch_shapes=[pltpu.VMEM((half, tokens), bf16)],
        compiler_params=pltpu.CompilerParams(vmem_limit_bytes=32 * 2**20),
    )(x, og, gpu, gated)


def dense_grads_kernel(ai, ao, joint_rows, attended, grads):
    wide = joint_rows.shape[1]
    grads[:, :wide] = dot(ai[...], joint_rows[...], TN).astype(bf16)
    grads[:, wide:] = dot(ao[...], attended[...], TN).astype(bf16)


def dense_grads(ai, ao, joint_rows, attended):
    return pl.pallas_call(
        dense_grads_kernel,
        name="dense_grads",
        out_shape=jax.ShapeDtypeStruct((ai.shape[1], joint_rows.shape[1] + attended.shape[1]), bf16),
        compiler_params=pltpu.CompilerParams(vmem_limit_bytes=32 * 2**20),
    )(ai, ao, joint_rows, attended)


def shards(
    tokens_in, out_cotangent, attn_gain, query_weight, key_weight, value_weight, output_weight,
    expert_gain, router_weight, gate_weight, up_weight, down_weight, lengths, dealing,
    slot_order, routes,
):
    section = lax.axis_index("section")
    first = section == 0

    def pick(pair):
        return lax.dynamic_index_in_dim(pair, section, 0, keepdims=False)

    qw = query_weight.shape[2]
    kw = key_weight.shape[2]
    own = (query_weight[0], key_weight[0], value_weight[0], output_weight[0], gate_weight[0],
           up_weight[0], down_weight[0])
    held = (attn_gain, expert_gain, router_weight[0])
    held_other = [swapped(v) for v in held]
    gains = (
        [jnp.where(first, a, b) for a, b in zip(held, held_other)],
        [jnp.where(first, b, a) for a, b in zip(held, held_other)],
    )
    tokens_pack = slot_order.shape[3]
    segment, position, dealt = token_places(pick(lengths)[0], pick(dealing)[0], tokens_pack)
    cosine, sine = rope_tables(position, HD)
    low_half = jnp.arange(HD) < HD // 2
    tables = tuple(jnp.tile(v, (1, 128 // HD)) for v in (cosine, jnp.where(low_half, -sine, sine)))
    token_index = jnp.arange(tokens_pack, dtype=jnp.int32)
    allowed = (segment[:, None] == segment[None, :]) & (token_index[None, :] <= token_index[:, None])
    bias = jnp.where(allowed, 0.0, masked_score).astype(f32)
    orders = slot_order[0, :, 0]
    order_own, order_sent = pick(orders), pick(orders[::-1])
    routes_own, routes_sent = pick(routes[0]), pick(routes[0][::-1])
    order_other, routes_other = swapped(order_sent), swapped(routes_sent)
    masks = (
        expert_masks(dealt, jnp.where(first, order_own, order_other),
                     jnp.where(first, routes_own, routes_other)),
        expert_masks(dealt, jnp.where(first, order_other, order_own),
                     jnp.where(first, routes_other, routes_own)),
    )
    stream = pick(tokens_in).astype(f32)
    (out0, *state0), other = layer_forward(0, gains[0], own, None, stream, tables, masks[0], bias)
    (out1, *state1), _ = layer_forward(1, gains[1], own, other, out0, tables, masks[1], bias)
    saved = (state0, state1)
    streams = (stream, out0)

    def experts(layer, out_grad, jobs):
        mid, expert_rows, qs, keys, values, probs, gate, ai, x, gated, attended, pre = saved[layer]
        (mid_grad, router_part, gain_part, og, gpu), done = experts_back(
            layer, gains[layer], own, other, out_grad, (mid, gate, expert_rows, pre), masks[layer],
            Beside(jobs)
        )
        return mid_grad, (gain_part, router_part), expert_grads(x, og, gpu, gated), done

    def attention(layer, mid_grad, jobs):
        mid, expert_rows, qs, keys, values, probs, gate, ai, x, gated, attended, pre = saved[layer]
        (grad, gain_part, ao, joint_rows), done = attention_back(
            layer, gains[layer], own, other, mid_grad, streams[layer], (qs, keys, values, probs),
            tables, Beside(jobs)
        )
        return grad, gain_part, dense_grads(ai, ao, joint_rows, attended), done

    mid_grad, small1, (pair, down), _ = experts(1, pick(out_cotangent), [])
    grad1, gain1, dense1, (pair, down) = attention(
        1, mid_grad, [FirstStage(pair, 1), FirstStage(down, 2)]
    )
    mid_grad, small0, (pair0, down0), (pair1, down1, dense1) = experts(
        0, grad1.astype(bf16), [SecondStage(*pair, 1), SecondStage(*down, 2), Scatter(dense1)]
    )
    grad0, gain0, dense0, (pair, down, dense1) = attention(
        0, mid_grad, [FirstStage(pair0, 1), FirstStage(down0, 2), Gather(dense1)]
    )
    blank = jnp.zeros((6, gain0.shape[1]), f32)
    small = jnp.concatenate([small0[1], gain0, small0[0], blank, small1[1], gain1, small1[0], blank])
    small, dense0, (pair0, down0) = finish(
        small, dense0, Beside([SecondStage(*pair, 1), SecondStage(*down, 2)])
    )

    def by_layer(zero, one):
        mine = jnp.where(first, zero, one)
        theirs = swapped(jnp.where(first, one, zero))
        return jnp.where(first, jnp.stack([mine, theirs]), jnp.stack([theirs, mine]))[None]

    layer_outputs = by_layer(out0, out1)
    input_grads = by_layer(grad0, grad1)

    def joined(zero, one, axis):
        mine = jnp.where(first, zero, one).astype(bf16)
        theirs = swapped(jnp.where(first, one, zero).astype(bf16))
        return jnp.where(
            first,
            jnp.concatenate([mine, theirs], axis=axis),
            jnp.concatenate([theirs, mine], axis=axis),
        ).astype(f32)

    pair = joined(pair0, pair1, 1)
    down = joined(down0, down1, 2)
    dense = joined(dense0, dense1, 0)
    hidden_width = pair.shape[2] // 2
    small = jnp.where(first, small[: small.shape[0] // 2], small[small.shape[0] // 2 :])
    router_grad, attn_gain_grad, expert_gain_grad = small[:E].T, small[E : E + 1], small[E + 1 : E + 2]
    joint, output = dense[:, : qw + 2 * kw], dense[:, qw + 2 * kw :].T
    gate, up = pair[:, :, :hidden_width], pair[:, :, hidden_width:]
    return (
        layer_outputs,
        input_grads,
        attn_gain_grad,
        joint[:, :qw][None],
        joint[:, qw : qw + kw][None],
        joint[:, qw + kw :][None],
        output[None],
        expert_gain_grad,
        router_grad[None],
        gate[None],
        up[None],
        down[None],
    )


def solution(mesh):
    return jax.shard_map(
        shards,
        mesh=mesh,
        in_specs=(
            P(None, ("dp", "tensor"), None),
            P(None, ("dp", "tensor"), None),
            P("section", None),
            P("section", None, "tensor"),
            P("section", None, "tensor"),
            P("section", None, "tensor"),
            P("section", "tensor", None),
            P("section", None),
            P("section", None, None),
            P("section", None, None, "tensor"),
            P("section", None, None, "tensor"),
            P("section", None, "tensor", None),
            P(None, "dp", None),
            P(None, "dp", None),
            P("section", None, "dp", None),
            P("section", None, "dp", None),
        ),
        out_specs=(
            P("section", None, ("dp", "tensor"), None),
            P("section", None, ("dp", "tensor"), None),
            P("section", None),
            P("section", None, "tensor"),
            P("section", None, "tensor"),
            P("section", None, "tensor"),
            P("section", "tensor", None),
            P("section", None),
            P("section", None, None),
            P("section", "dp", None, "tensor"),
            P("section", "dp", None, "tensor"),
            P("section", "dp", "tensor", None),
        ),
        check_vma=False,
    )
```

```python
import functools
import math

import jax
import jax.numpy as jnp
from jax import lax
from jax.experimental import pallas as pl
from jax.experimental.pallas import tpu as pltpu
from jax.sharding import PartitionSpec as P

H = 24
KV = 8
HD = 64
E = 16
CAP = 160

epsilon = 1e-05
rope_base = 10000.0
masked_score = -1e30
bf16 = jnp.bfloat16
f32 = jnp.float32
MESH = pl.DeviceIdType.MESH


def dot(a, b, dims):
    return lax.dot_general(a, b, (dims, ((), ())), preferred_element_type=f32)


NN = ((1,), (0,))
NT = ((1,), (1,))
TN = ((0,), (0,))


def swapped(value):
    return lax.ppermute(value, "section", [(0, 1), (1, 0)])


def norm_scale(rows_in):
    return lax.rsqrt(jnp.mean(rows_in * rows_in, axis=-1, keepdims=True) + epsilon)


def params(collective_id):
    return pltpu.CompilerParams(
        collective_id=collective_id, has_side_effects=True, vmem_limit_bytes=56 * 2**20
    )


def tensor_peers(count):
    me = lax.axis_index("tensor")
    return [{"tensor": lax.rem(me + step, count)} for step in range(1, count)]


def greet(peers):
    barrier = pltpu.get_barrier_semaphore()
    for peer in peers:
        pl.semaphore_signal(barrier, inc=1, device_id=peer, device_id_type=MESH)
    pl.semaphore_wait(barrier, len(peers))


def factors(count):
    inner = math.isqrt(count)
    while count % inner:
        inner -= 1
    return count // inner, inner


def group_place(count):
    outer, inner = factors(count)
    me = lax.axis_index("dp")
    return outer, inner, me // inner, lax.rem(me, inner)


def near_groups(count):
    outer, inner, mo, mi = group_place(count)
    across = [lax.rem(mi + step, inner) for step in range(1, inner)]
    along = [lax.rem(mo + step, outer) for step in range(1, outer)]
    return (
        [(place, {"dp": mo * inner + place}) for place in across],
        [(place, {"dp": place * inner + mi}) for place in along],
    )


dma = pltpu.SemaphoreType.DMA


def remote(src, dst, send, recv, device):
    return pltpu.make_async_remote_copy(
        src_ref=src, dst_ref=dst, send_sem=send, recv_sem=recv, device_id=device, device_id_type=MESH
    )


class FirstStage:
    def __init__(self, value, axis):
        self.count = lax.axis_size("dp")
        outer, inner = factors(self.count)
        self.inputs = [value.reshape((outer, inner, value.shape[0] // self.count) + value.shape[1:])]
        self.axis = axis
        shape = list(self.inputs[0].shape[2:])
        shape[axis] //= 2
        self.shape = shape
        self.outputs = [
            jax.ShapeDtypeStruct((inner - 1, outer, *shape), value.dtype),
            jax.ShapeDtypeStruct((outer - 1, inner, *shape), value.dtype),
        ]
        self.sems = [dma((inner + outer - 2,)), dma((inner + outer - 2,))]

    def copies(self, inputs, outputs, sems):
        across, along = near_groups(self.count)
        value = inputs[0]
        half = self.shape[self.axis]
        cut = [slice(None)] * 3
        first, second = list(cut), list(cut)
        first[self.axis], second[self.axis] = pl.ds(0, half), pl.ds(half, half)
        found = []
        for slot, (place, device) in enumerate(across):
            found.append((value.at[(slice(None), place, *first)], outputs[0].at[slot], device))
        for slot, (place, device) in enumerate(along):
            found.append((value.at[(place, slice(None), *second)], outputs[1].at[slot], device))
        return [
            remote(src, dst, sems[0].at[index], sems[1].at[index], device)
            for index, (src, dst, device) in enumerate(found)
        ]

    def start(self, inputs, outputs, sems):
        for copy in self.copies(inputs, outputs, sems):
            copy.start()

    def wait(self, inputs, outputs, sems):
        for copy in self.copies(inputs, outputs, sems):
            copy.wait()

    def results(self, outputs):
        outer, inner, mo, mi = group_place(self.count)
        value = self.inputs[0]
        half = self.shape[self.axis]
        later = [0] * 5
        later[2 + self.axis] = half
        row = lax.dynamic_slice(value, (0, mi, 0, 0, 0), (outer, 1, *self.shape))[:, 0].astype(f32)
        later[0] = mo
        col = lax.dynamic_slice(value, later, (1, inner, *self.shape))[0].astype(f32)
        for slot in range(inner - 1):
            row = row + outputs[0][slot].astype(f32)
        for slot in range(outer - 1):
            col = col + outputs[1][slot].astype(f32)
        return row.astype(bf16), col.astype(bf16)


class Bring:
    def __init__(self, layer, kind, value, in_vmem=False):
        self.layer, self.kind, self.in_vmem = layer, kind, in_vmem
        count = lax.axis_size("dp")
        outer, inner = factors(count)
        self.size = {"column": outer, "row": inner, "all": count}[kind]
        block = value.shape if kind == "all" else value.shape[1:]
        self.inputs = [value]
        self.outputs = [jax.ShapeDtypeStruct((2, self.size, *block), value.dtype)]
        self.sems = [dma((self.size,)), dma((2, self.size)), dma((2,))]
        if not in_vmem:
            self.sems.append(pltpu.VMEM(block, value.dtype))

    def place(self, step):
        count = lax.axis_size("dp")
        outer, inner, mo, mi = group_place(count)
        if self.kind == "column":
            place = lax.rem(mo + step, outer)
            return place, place * inner + mi
        if self.kind == "row":
            place = lax.rem(mi + step, inner)
            return place, mo * inner + place
        place = lax.rem(lax.axis_index("dp") + step, count)
        return place, place

    def parts(self, inputs, outputs, sems):
        core = lax.axis_index("section")
        mine, _ = self.place(0)
        target = outputs[0].at[core, mine]
        recv = sems[1].at[core, mine]

        def source(place):
            return inputs[0] if self.kind == "all" else inputs[0].at[place]

        sent = []
        for step in range(1, self.size):
            place, group = self.place(step)
            sent.append(
                remote(source(place), target, sems[0].at[step - 1], recv,
                       {"dp": group, "section": self.layer})
            )
        across = remote(source(mine), target, sems[0].at[self.size - 1], recv, core_peer())
        if self.in_vmem:
            local = [pltpu.make_async_copy(source(mine), target, sems[2].at[0])]
        else:
            local = [
                pltpu.make_async_copy(source(mine), sems[3], sems[2].at[0]),
                pltpu.make_async_copy(sems[3], target, sems[2].at[1]),
            ]
        return sent, across, local

    def start(self, inputs, outputs, sems):
        sent, across, local = self.parts(inputs, outputs, sems)
        for copy in sent:
            copy.start()
        here = lax.axis_index("section") == self.layer

        @pl.when(here)
        def _():
            local[0].start()

        @pl.when(jnp.logical_not(here))
        def _():
            across.start()

    def wait(self, inputs, outputs, sems):
        sent, across, local = self.parts(inputs, outputs, sems)
        core = lax.axis_index("section")
        here = core == self.layer
        block = inputs[0] if self.kind == "all" else inputs[0].at[0]

        def arrived(which, place):
            remote(block, outputs[0].at[which, place], sems[0].at[0], sems[1].at[which, place],
                   core_peer()).wait_recv()

        for copy in sent:
            copy.wait_send()

        @pl.when(here)
        def _():
            local[0].wait()
            for copy in local[1:]:
                copy.start()
                copy.wait()
            for step in range(self.size):
                place, _ = self.place(step)
                if step:
                    arrived(core, place)
                arrived(1 - core, place)

        @pl.when(jnp.logical_not(here))
        def _():
            across.wait_send()

    def results(self, outputs):
        return outputs[0]


class Scatter:
    def __init__(self, value):
        self.count = lax.axis_size("dp")
        block = (value.shape[0] // self.count,) + value.shape[1:]
        self.inputs = [value.reshape((self.count, *block))]
        self.outputs = [jax.ShapeDtypeStruct((self.count - 1, *block), value.dtype)]
        self.sems = [dma((self.count - 1,)), dma((self.count - 1,))]

    def copies(self, inputs, outputs, sems):
        me = lax.axis_index("dp")
        found = []
        for step in range(1, self.count):
            place = lax.rem(me + step, self.count)
            found.append(
                remote(inputs[0].at[place], outputs[0].at[step - 1], sems[0].at[step - 1],
                       sems[1].at[step - 1], {"dp": place})
            )
        return found

    def start(self, inputs, outputs, sems):
        for copy in self.copies(inputs, outputs, sems):
            copy.start()

    def wait(self, inputs, outputs, sems):
        for copy in self.copies(inputs, outputs, sems):
            copy.wait()

    def results(self, outputs):
        me = lax.axis_index("dp")
        total = lax.dynamic_index_in_dim(self.inputs[0], me, 0, keepdims=False).astype(f32)
        for slot in range(self.count - 1):
            total = total + outputs[0][slot].astype(f32)
        return total.astype(bf16)


def both_cores(groups):
    core = lax.axis_index("section")
    return [{"dp": group, "section": which} for group in groups for which in (core, 1 - core)]


class Beside:
    def __init__(self, jobs):
        self.jobs = jobs
        self.inputs = [v for job in jobs for v in job.inputs]
        self.outputs = [v for job in jobs for v in job.outputs]
        self.sems = [v for job in jobs for v in job.sems]

    def peers(self):
        count = lax.axis_size("dp")
        if any(isinstance(job, Scatter) or getattr(job, "kind", "") == "all" for job in self.jobs):
            me = lax.axis_index("dp")
            return both_cores([lax.rem(me + step, count) for step in range(1, count)])
        if not self.jobs:
            return []
        across, along = near_groups(count)
        return both_cores([device["dp"] for _, device in across + along])

    def each(self, refs, run):
        inputs, outputs, sems = refs
        for job in self.jobs:
            mine, inputs = inputs[: len(job.inputs)], inputs[len(job.inputs) :]
            theirs, outputs = outputs[: len(job.outputs)], outputs[len(job.outputs) :]
            own, sems = sems[: len(job.sems)], sems[len(job.sems) :]
            run(job)(mine, theirs, own)

    def start(self, *refs):
        self.each(refs, lambda job: job.start)

    def wait(self, *refs):
        self.each(refs, lambda job: job.wait)

    def results(self, outputs):
        found = []
        for job in self.jobs:
            found.append(job.results(outputs[: len(job.outputs)]))
            outputs = outputs[len(job.outputs) :]
        return found


def spread(count, buf, rows, sends, recvs):
    me = lax.axis_index("tensor")
    own = buf.at[pl.ds(pl.multiple_of(me * rows, rows), rows)]
    copies = []
    for step in range(1, count):
        copies.append(
            pltpu.make_async_remote_copy(
                src_ref=own,
                dst_ref=own,
                send_sem=sends.at[step - 1],
                recv_sem=recvs.at[step - 1],
                device_id={"tensor": lax.rem(me + step, count)},
                device_id_type=MESH,
            )
        )
    return copies


def deal_out(count, part, rows, columns, landing, sends, recvs):
    me = lax.axis_index("tensor")
    copies = []
    for step in range(1, count):
        peer = lax.rem(me + step, count)
        copies.append(
            pltpu.make_async_remote_copy(
                src_ref=part.at[pl.ds(pl.multiple_of(peer * rows, rows), rows), columns],
                dst_ref=landing.at[step - 1, :, columns],
                send_sem=sends.at[step - 1],
                recv_sem=recvs.at[step - 1],
                device_id={"tensor": peer},
                device_id_type=MESH,
            )
        )
    for copy in copies:
        copy.start()
    return copies


def core_peer():
    return {"section": 1 - lax.axis_index("section")}


def hand_rows(value, pair, sems):
    tokens = value.shape[0]
    return [
        pltpu.make_async_copy(value, pair.at[pl.ds(0, tokens)], sems[0]),
        remote(value, pair.at[pl.ds(tokens, tokens)], sems[1], sems[2], core_peer()),
    ]


def hand_halves(value, pair, sems):
    section = lax.axis_index("section")
    tokens, half = value.shape[0], value.shape[1] // 2
    mine = value.at[:, pl.ds(pl.multiple_of(section * half, half), half)]
    other = value.at[:, pl.ds(pl.multiple_of((1 - section) * half, half), half)]
    return [
        pltpu.make_async_copy(mine, pair.at[pl.ds(0, tokens)], sems[0]),
        remote(other, pair.at[pl.ds(tokens, tokens)], sems[1], sems[2], core_peer()),
    ]


def start_all(copies):
    for copy in copies:
        copy.start()


def wait_all(copies):
    for copy in copies:
        copy.wait()


def either(use_own, own, other, run):
    @pl.when(use_own)
    def _():
        run(own)

    @pl.when(jnp.logical_not(use_own))
    def _():
        run(other)


def weight_copies(refs, scratch, sems, expert):
    gate, up, down = refs
    gu_s, down_s = scratch
    width = gate.shape[2]
    return (
        pltpu.make_async_copy(gate.at[expert], gu_s.at[expert, :, pl.ds(0, width)], sems.at[0, expert]),
        pltpu.make_async_copy(up.at[expert], gu_s.at[expert, :, pl.ds(width, width)], sems.at[1, expert]),
        pltpu.make_async_copy(
            down.at[expert], down_s.at[pl.ds(pl.multiple_of(expert * width, width), width)], sems.at[2, expert]
        ),
    )


def attn_copies(refs, scratch, sems):
    query, key, value, output = refs
    joint_s, output_s = scratch
    qw, kw = query.shape[1], key.shape[1]
    return (
        pltpu.make_async_copy(query, joint_s.at[:, pl.ds(0, qw)], sems.at[0]),
        pltpu.make_async_copy(key, joint_s.at[:, pl.ds(qw, kw)], sems.at[1]),
        pltpu.make_async_copy(value, joint_s.at[:, pl.ds(qw + kw, kw)], sems.at[2]),
        pltpu.make_async_copy(output, output_s, sems.at[3]),
    )


def turned(block):
    lane = lax.broadcasted_iota(jnp.int32, block.shape, 1)
    half = HD // 2
    return jnp.where(
        lane % HD < half, pltpu.roll(block, block.shape[1] - half, 1), pltpu.roll(block, half, 1)
    )


def column(table, index):
    lane = lax.broadcasted_iota(jnp.int32, table.shape, 1)
    return jnp.sum(jnp.where(lane == index, table, 0.0), axis=1, keepdims=True)


def swap_copies(own, other, sems, piece):
    sends, recvs = sems
    names = len(own)
    if isinstance(piece, tuple):
        name, expert = piece
        source, target = own[name].at[expert], other[name].at[expert]
        index = 4 + (name - 4) * own[4].shape[0] + expert
    else:
        source, target, index = own[piece], other[piece], piece
    return pltpu.make_async_remote_copy(
        src_ref=source, dst_ref=target, send_sem=sends.at[index], recv_sem=recvs.at[index],
        device_id=core_peer(), device_id_type=MESH,
    )


def forward_kernel(layer, count, swap, *refs):
    refs = list(refs)

    def take(number):
        taken = refs[:number]
        del refs[:number]
        return taken

    (stream_in, attn_gains, expert_gains, routers, cosine, sine, bias, pickeds, kepts) = take(9)
    attn_gain, expert_gain, router = attn_gains.at[layer], expert_gains.at[layer], routers.at[layer]
    picked, kept = pickeds.at[layer], kepts.at[layer]
    stream = stream_in.at[lax.axis_index("section")] if layer == 0 else stream_in
    own = take(7)
    other = None if swap else take(7)
    (out, mid_out, expert_rows_out, qs_out, keys_out, values_out, probs_out, gate_out,
     attn_in_out, expert_in_out, gated_out, attended_out, pre_out) = take(13)
    if swap:
        other = take(7)
    scratch = take(4)
    joint_s, output_s, gu_s, down_s = scratch
    (ag1, ag2, part, landing1, landing2, pre_s, gated_s, attended_s, send_s, recv_s, attn_sems,
     expert_sems, pre_sems, save_sems) = refs[:14]
    swap_sems = refs[14:]
    rows, width = stream.shape
    tokens = ag1.shape[0]
    experts = gu_s.shape[0]
    hidden_width = gu_s.shape[2] // 2
    kw = keys_out.shape[1]
    qw = attended_s.shape[1]
    heads, key_heads = qw // HD, kw // HD
    group = heads // key_heads
    me = lax.axis_index("tensor")
    own_rows = pl.ds(pl.multiple_of(me * rows, rows), rows)
    use_own = lax.axis_index("section") == layer

    def start_attn(w):
        for copy in attn_copies(w[:4], scratch[:2], attn_sems):
            copy.start()

    def wait_attn(w):
        for copy in attn_copies(w[:4], scratch[:2], attn_sems):
            copy.wait()

    def start_expert(w, expert):
        for copy in weight_copies(w[4:], scratch[2:], expert_sems, expert):
            copy.start()

    def wait_expert(w, expert):
        for copy in weight_copies(w[4:], scratch[2:], expert_sems, expert):
            copy.wait()

    def each_expert(run):
        def step(expert, carry):
            run(expert)
            return carry

        lax.fori_loop(0, experts, step, 0)

    def swap_expert(expert):
        return [swap_copies(own, other, swap_sems, (name, expert)) for name in (4, 5, 6)]

    value = stream[...].astype(bf16).astype(f32)
    ag1[own_rows, :] = (value * norm_scale(value) * attn_gain[...]).astype(bf16)
    greet(tensor_peers(count) + ([core_peer()] if swap else []))
    first = spread(count, ag1, rows, send_s.at[0], recv_s.at[0])
    if swap:
        lead = min(2, experts)
        for piece in range(4):
            swap_copies(own, other, swap_sems, piece).start()
        each_expert(lambda expert: [c.start() for c in swap_expert(expert)] and None)

        @pl.when(use_own)
        def _():
            start_all(first)
            start_attn(own)
            each_expert(lambda expert: start_expert(own, expert))

        @pl.when(jnp.logical_not(use_own))
        def _():
            for piece in range(4):
                swap_copies(own, other, swap_sems, piece).wait_recv()
            start_attn(other)
            for expert in range(lead):
                for copy in swap_expert(expert):
                    copy.wait_recv()
                start_expert(other, expert)
            start_all(first)
    else:
        start_all(first)
        either(use_own, own, other, start_attn)
        either(use_own, own, other, lambda w: each_expert(lambda expert: start_expert(w, expert)))
    wait_all(first)
    saved = [pltpu.make_async_copy(ag1, attn_in_out, save_sems.at[0])]
    saved[0].start()
    either(use_own, own, other, wait_attn)
    proj = dot(ag1[...], joint_s[...], NN)
    for chunk in range(qw // 128):
        block = proj[:, chunk * 128 : chunk * 128 + 128]
        block = (block * cosine[...] + turned(block) * sine[...]).astype(bf16)
        for part_index in range(128 // HD):
            head = chunk * (128 // HD) + part_index
            qs_out[pl.ds(head * tokens, tokens), :] = block[:, part_index * HD : part_index * HD + HD]
    for chunk in range(kw // 128):
        block = proj[:, qw + chunk * 128 : qw + chunk * 128 + 128]
        keys_out[:, pl.ds(chunk * 128, 128)] = (
            block * cosine[...] + turned(block) * sine[...]
        ).astype(bf16)
    values_out[...] = proj[:, qw + kw :].astype(bf16)
    for g in range(key_heads):
        lanes = pl.ds(g * HD, HD)
        span = pl.ds(g * group * tokens, group * tokens)
        scores = dot(qs_out[span, :], keys_out[:, lanes], NT) * 0.125
        scores = (scores.reshape(group, tokens, tokens) + bias[...][None]).reshape(
            group * tokens, tokens
        )
        top = jnp.max(scores, axis=1, keepdims=True)
        weighed = jnp.exp(scores - top)
        probs = (weighed / jnp.sum(weighed, axis=1, keepdims=True)).astype(bf16)
        probs_out[span, :] = probs
        attended = dot(probs, values_out[:, lanes], NN).astype(bf16)
        for h in range(group):
            attended_s[:, pl.ds((g * group + h) * HD, HD)] = attended[h * tokens : (h + 1) * tokens]
    saved.append(pltpu.make_async_copy(attended_s, attended_out, save_sems.at[1]))
    saved[1].start()
    part[...] = dot(attended_s[...], output_s[...], NN).astype(bf16)
    dealt = deal_out(count, part, rows, slice(None), landing1, send_s.at[1], recv_s.at[1])
    wait_all(dealt)
    mid = value + part[own_rows, :].astype(f32)
    for step in range(count - 1):
        mid = mid + landing1[step].astype(f32)
    mid_out[...] = mid
    expert_rows = (mid * norm_scale(mid) * expert_gain[...]).astype(bf16)
    expert_rows_out[...] = expert_rows
    ag2[own_rows, :] = expert_rows
    second = spread(count, ag2, rows, send_s.at[2], recv_s.at[2])
    start_all(second)
    wait_all(second)
    saved.append(pltpu.make_async_copy(ag2, expert_in_out, save_sems.at[2]))
    saved[2].start()
    logits = dot(ag2[...], router[...], NN)
    chosen = picked[...] > 0
    top = jnp.max(jnp.where(chosen, logits, masked_score), axis=1, keepdims=True)
    weighed = jnp.where(chosen, jnp.exp(logits - top), 0.0)
    gate_out[...] = weighed / jnp.sum(weighed, axis=1, keepdims=True)

    def expert_step(expert, carry):
        if swap:

            @pl.when(jnp.logical_not(use_own) & (expert + lead < experts))
            def _():
                for copy in swap_expert(expert + lead):
                    copy.wait_recv()
                start_expert(other, expert + lead)

        either(use_own, own, other, lambda w: wait_expert(w, expert))
        pre = dot(ag2[...], gu_s[expert], NN)
        pre_s[expert] = pre
        pltpu.make_async_copy(pre_s.at[expert], pre_out.at[expert], pre_sems.at[expert]).start()
        gate_pre, up_pre = pre[:, :hidden_width], pre[:, hidden_width:]
        hidden = (gate_pre / (1.0 + jnp.exp(-gate_pre)) * up_pre).astype(bf16).astype(f32)
        weight = column(gate_out[...] * kept[...], expert)
        gated_s[:, pl.ds(pl.multiple_of(expert * hidden_width, hidden_width), hidden_width)] = (
            hidden * weight
        ).astype(bf16)
        return carry

    lax.fori_loop(0, experts, expert_step, 0)
    saved.append(pltpu.make_async_copy(gated_s, gated_out, save_sems.at[3]))
    saved[3].start()
    copies = []
    tile = width // 4
    for t in range(4):
        columns = pl.ds(t * tile, tile)
        part[:, columns] = dot(gated_s[...], down_s[:, columns], NN).astype(bf16)
        copies += deal_out(count, part, rows, columns, landing2, send_s.at[3 + t], recv_s.at[3 + t])
    wait_all(copies)
    total = mid_out[...] + part[own_rows, :].astype(f32)
    for step in range(count - 1):
        total = total + landing2[step].astype(f32)
    out[...] = total
    wait_all(saved)
    if swap:
        for piece in range(4):
            swap_copies(own, other, swap_sems, piece).wait_send()
        each_expert(lambda expert: [c.wait_send() for c in swap_expert(expert)] and None)

        @pl.when(use_own)
        def _():
            for piece in range(4):
                swap_copies(own, other, swap_sems, piece).wait_recv()
            each_expert(lambda expert: [c.wait_recv() for c in swap_expert(expert)] and None)

    def finish(expert, carry):
        pltpu.make_async_copy(pre_s.at[expert], pre_out.at[expert], pre_sems.at[expert]).wait()
        return carry

    lax.fori_loop(0, experts, finish, 0)


def weight_scratch(own):
    query, key, value, output, gate, up, down = own
    depth = query.shape[0]
    experts, _, hidden_width = gate.shape
    return [
        pltpu.VMEM((depth, query.shape[1] + 2 * key.shape[1]), bf16),
        pltpu.VMEM(output.shape, bf16),
        pltpu.VMEM((experts, depth, 2 * hidden_width), bf16),
        pltpu.VMEM((experts * hidden_width, depth), bf16),
    ]


def layer_forward(layer, gains, own, other, stream, tables, masks):
    count = lax.axis_size("tensor")
    rows, width = stream.shape[-2:]
    tokens = tables[2].shape[0]
    qw, kw = own[0].shape[1], own[1].shape[1]
    experts, _, hidden_width = own[4].shape
    heads = qw // HD
    swap = other is None
    vmem = pl.BlockSpec(memory_space=pltpu.VMEM)
    hbm = pl.BlockSpec(memory_space=pl.ANY)
    shape = jax.ShapeDtypeStruct
    pieces = 4 + 3 * experts
    found = pl.pallas_call(
        functools.partial(forward_kernel, layer, count, swap),
        name=f"layer_forward_{layer}",
        out_shape=(
            shape((rows, width), f32),
            shape((rows, width), f32),
            shape((rows, width), bf16),
            shape((heads * tokens, HD), bf16),
            shape((tokens, kw), bf16),
            shape((tokens, kw), bf16),
            shape((heads * tokens, tokens), bf16),
            shape((tokens, experts), f32),
            shape((tokens, width), bf16),
            shape((tokens, width), bf16),
            shape((tokens, experts * hidden_width), bf16),
            shape((tokens, qw), bf16),
            shape((experts, tokens, 2 * hidden_width), f32),
        )
        + (tuple(shape(w.shape, w.dtype) for w in own) if swap else ()),
        in_specs=[vmem] * 9 + [hbm] * (7 if swap else 14),
        out_specs=(vmem,) * 8 + (hbm,) * (12 if swap else 5),
        scratch_shapes=weight_scratch(own)
        + [
            pltpu.VMEM((tokens, width), bf16),
            pltpu.VMEM((tokens, width), bf16),
            pltpu.VMEM((tokens, width), bf16),
            pltpu.VMEM((count - 1, rows, width), bf16),
            pltpu.VMEM((count - 1, rows, width), bf16),
            pltpu.VMEM((experts, tokens, 2 * hidden_width), f32),
            pltpu.VMEM((tokens, experts * hidden_width), bf16),
            pltpu.VMEM((tokens, qw), bf16),
            dma((7, count - 1)),
            dma((7, count - 1)),
            dma((4,)),
            dma((3, experts)),
            dma((experts,)),
            dma((4,)),
        ]
        + ([dma((pieces,)), dma((pieces,))] if swap else []),
        compiler_params=params(1 + layer),
    )(stream, *gains, *tables, *masks, *own,
      *(() if swap else other))
    return found[:13], found[13:]


def norm_back(value, gain, out_grad):
    scale = norm_scale(value)
    scaled = value * scale
    gain_grad = jnp.sum(out_grad * scaled, axis=0, keepdims=True)
    inner = out_grad * gain
    value_grad = scale * (inner - scaled * jnp.mean(inner * scaled, axis=-1, keepdims=True))
    return value_grad, gain_grad


def experts_back_kernel(layer, count, beside, *refs):
    refs = list(refs)

    def take(number):
        taken = refs[:number]
        del refs[:number]
        return taken

    out_grad_in, mid, expert_gains, routers, kepts, gate, expert_rows, pre_in = take(8)
    expert_gain, router, kept = expert_gains.at[layer], routers.at[layer], kepts.at[layer]
    out_grad = out_grad_in if layer == 0 else out_grad_in.at[lax.axis_index("section")]
    x_in, gated_in = take(2)
    own, other = take(3), take(3)
    beside_in = take(len(beside.inputs))
    mid_grad_out, router_out, expert_gain_out, pair_out, down_out = take(5)
    beside_out = take(len(beside.outputs))
    scratch = take(2)
    gu_s, down_s = scratch
    (ag1, part, landing1, pre_s, gpu_s, acc, gate_part, gate_land, og_s, gpu_peer, x_s, turned_x,
     gated_s, turned_gated, pair_s, down_grad_s, send_s, recv_s, expert_sems, pre_sems, core_send,
     core_recv, local_sems, hand_send, hand_recv, save_sems) = take(26)
    beside_refs = (beside_in, beside_out, refs)
    rows, width = mid.shape
    experts = gu_s.shape[0]
    hidden_width = gu_s.shape[2] // 2
    me = lax.axis_index("tensor")
    own_rows = pl.ds(pl.multiple_of(me * rows, rows), rows)
    use_own = lax.axis_index("section") == layer

    def start_expert(expert, carry):
        either(use_own, own, other,
               lambda w: [c.start() for c in weight_copies(w, scratch, expert_sems, expert)])
        pltpu.make_async_copy(pre_in.at[expert], pre_s.at[expert], pre_sems.at[expert]).start()
        return carry

    ag1[own_rows, :] = out_grad[...].astype(bf16)
    greet(tensor_peers(count) + [core_peer()] + beside.peers())
    first = spread(count, ag1, rows, send_s.at[0], recv_s.at[0])
    start_all(first)
    lax.fori_loop(0, experts, start_expert, 0)
    loads = hand_halves(x_in, x_s, [v.at[0] for v in (local_sems, hand_send, hand_recv)])
    loads += hand_rows(gated_in, gated_s, [v.at[1] for v in (local_sems, hand_send, hand_recv)])
    for copy in loads:
        copy.start()
    beside.start(*beside_refs)
    gate_part[...] = jnp.zeros_like(gate_part)
    wait_all(loads)
    turned_x[...] = x_s[...].T
    tokens = ag1.shape[0]

    def turn_gated(expert, carry):
        lanes = pl.ds(pl.multiple_of(expert * hidden_width, hidden_width), hidden_width)
        turned_gated[lanes, :] = gated_s[:, lanes].T
        return carry

    lax.fori_loop(0, experts, turn_gated, 0)
    wait_all(first)
    core = lax.axis_index("section")
    half = width // 2
    og_s[pl.ds(0, tokens), :] = ag1[:, pl.ds(pl.multiple_of(core * half, half), half)]
    handed = [
        remote(ag1.at[:, pl.ds(pl.multiple_of((1 - core) * half, half), half)],
               og_s.at[pl.ds(tokens, tokens)], core_send.at[0], core_recv.at[0], core_peer())
    ]
    handed[0].start()

    def expert_step(expert, carry):
        either(use_own, own, other,
               lambda w: [c.wait() for c in weight_copies(w, scratch, expert_sems, expert)])
        pltpu.make_async_copy(pre_in.at[expert], pre_s.at[expert], pre_sems.at[expert]).wait()
        lanes = pl.ds(pl.multiple_of(expert * hidden_width, hidden_width), hidden_width)
        plain = dot(ag1[...], down_s[lanes, :], NT)
        gate_pre = pre_s[expert, :, pl.ds(0, hidden_width)]
        up_pre = pre_s[expert, :, pl.ds(hidden_width, hidden_width)]
        sig = 1.0 / (1.0 + jnp.exp(-gate_pre))
        act = gate_pre * sig
        hidden = (act * up_pre).astype(bf16).astype(f32)
        held = column(kept[...], expert)
        weight = column(gate[...], expert) * held
        summed = jnp.sum(hidden * plain, axis=1, keepdims=True) * held
        lane = lax.broadcasted_iota(jnp.int32, gate_part.shape, 1)
        gate_part[...] += jnp.where(lane == expert, summed, 0.0)
        hidden_grad = plain * weight
        gpu_s[expert, :, pl.ds(0, hidden_width)] = (
            hidden_grad * up_pre * (sig * (1.0 + gate_pre * (1.0 - sig)))
        ).astype(bf16)
        gpu_s[expert, :, pl.ds(hidden_width, hidden_width)] = (hidden_grad * act).astype(bf16)
        back = dot(gpu_s[expert], gu_s[expert], NT)

        @pl.when(expert == 0)
        def _():
            acc[...] = back

        @pl.when(expert > 0)
        def _():
            acc[...] += back

        return carry

    lax.fori_loop(0, experts, expert_step, 0)
    handed.append(remote(gpu_s, gpu_peer, core_send.at[1], core_recv.at[1], core_peer()))
    handed[1].start()
    part[...] = acc[...].astype(bf16)
    copies = deal_out(count, part, rows, slice(None), landing1, send_s.at[1], recv_s.at[1])
    copies += deal_out(count, gate_part, rows, slice(None), gate_land, send_s.at[2], recv_s.at[2])
    wait_all(handed)

    def saves(expert):
        lanes = pl.ds(pl.multiple_of(expert * hidden_width, hidden_width), hidden_width)
        return (
            pltpu.make_async_copy(pair_s.at[expert], pair_out.at[expert], save_sems.at[0, expert]),
            pltpu.make_async_copy(down_grad_s.at[lanes], down_out.at[expert], save_sems.at[1, expert]),
        )

    def grads_step(expert, carry):
        lanes = pl.ds(pl.multiple_of(expert * hidden_width, hidden_width), hidden_width)
        pair_s[expert] = (
            dot(turned_x[:, :tokens], gpu_s[expert], NN)
            + dot(turned_x[:, tokens:], gpu_peer[expert], NN)
        ).astype(bf16)
        down_grad_s[lanes, :] = dot(turned_gated[lanes, :], og_s[...], NN).astype(bf16)
        for copy in saves(expert):
            copy.start()
        return carry

    lax.fori_loop(0, experts, grads_step, 0)
    wait_all(copies)
    in_grad = acc[own_rows, :]
    gate_grad = gate_part[own_rows, :]
    for step in range(count - 1):
        in_grad = in_grad + landing1[step].astype(f32)
        gate_grad = gate_grad + gate_land[step]
    gate_grad = gate_grad[:, :experts]
    gate_rows = gate[own_rows, :]
    logits_grad = (
        gate_rows * (gate_grad - jnp.sum(gate_rows * gate_grad, axis=1, keepdims=True))
    ).astype(bf16)
    router_out[...] = dot(logits_grad, expert_rows[...], TN)
    in_grad = in_grad + dot(logits_grad, router[...], NT)
    mid_part, expert_gain_grad = norm_back(mid[...], expert_gain[...], in_grad)
    expert_gain_out[...] = expert_gain_grad
    mid_grad_out[...] = ag1[own_rows, :].astype(f32) + mid_part

    def finish_save(expert, carry):
        for copy in saves(expert):
            copy.wait()
        return carry

    lax.fori_loop(0, experts, finish_save, 0)
    beside.wait(*beside_refs)


def experts_back(layer, gains, own, other, out_grad, state, pairs, masks, beside):
    count = lax.axis_size("tensor")
    mid, gate, expert_rows, pre = state
    rows, width = mid.shape
    tokens = gate.shape[0]
    own, other = own[4:], other[4:]
    experts, depth, hidden_width = own[0].shape
    vmem = pl.BlockSpec(memory_space=pltpu.VMEM)
    hbm = pl.BlockSpec(memory_space=pl.ANY)
    shape = jax.ShapeDtypeStruct
    found = pl.pallas_call(
        functools.partial(experts_back_kernel, layer, count, beside),
        name=f"experts_back_{layer}",
        out_shape=(
            shape((rows, width), f32),
            shape((experts, width), f32),
            shape((1, width), f32),
            shape((experts, width // 2, 2 * hidden_width), bf16),
            shape((experts, hidden_width, width // 2), bf16),
            *beside.outputs,
        ),
        in_specs=[vmem] * 7 + [hbm] * (9 + len(beside.inputs)),
        out_specs=(vmem, vmem, vmem, hbm, hbm) + (hbm,) * len(beside.outputs),
        scratch_shapes=[
            pltpu.VMEM((experts, depth, 2 * hidden_width), bf16),
            pltpu.VMEM((experts * hidden_width, depth), bf16),
            pltpu.VMEM((tokens, width), bf16),
            pltpu.VMEM((tokens, width), bf16),
            pltpu.VMEM((count - 1, rows, width), bf16),
            pltpu.VMEM((experts, tokens, 2 * hidden_width), f32),
            pltpu.VMEM((experts, tokens, 2 * hidden_width), bf16),
            pltpu.VMEM((tokens, width), f32),
            pltpu.VMEM((tokens, 128), f32),
            pltpu.VMEM((count - 1, rows, 128), f32),
            pltpu.VMEM((2 * tokens, width // 2), bf16),
            pltpu.VMEM((experts, tokens, 2 * hidden_width), bf16),
            pltpu.VMEM((2 * tokens, width // 2), bf16),
            pltpu.VMEM((width // 2, 2 * tokens), bf16),
            pltpu.VMEM((2 * tokens, experts * hidden_width), bf16),
            pltpu.VMEM((experts * hidden_width, 2 * tokens), bf16),
            pltpu.VMEM((experts, width // 2, 2 * hidden_width), bf16),
            pltpu.VMEM((experts * hidden_width, width // 2), bf16),
            pltpu.SemaphoreType.DMA((3, count - 1)),
            pltpu.SemaphoreType.DMA((3, count - 1)),
            pltpu.SemaphoreType.DMA((3, experts)),
            pltpu.SemaphoreType.DMA((experts,)),
            *[pltpu.SemaphoreType.DMA((2,)) for _ in range(5)],
            pltpu.SemaphoreType.DMA((2, experts)),
            *beside.sems,
        ],
        compiler_params=params(3 + layer),
    )(out_grad, mid, *gains[1:], masks[1], gate, expert_rows, pre, *pairs, *own, *other,
      *beside.inputs)
    return found[:5], beside.results(found[5:])


def attention_back_kernel(layer, count, beside, *refs):
    refs = list(refs)

    def take(number):
        taken = refs[:number]
        del refs[:number]
        return taken

    mid_grad, stream_in, attn_gains, cosine, sine, qs, keys, values, probs = take(9)
    attn_gain = attn_gains.at[layer]
    stream = stream_in.at[lax.axis_index("section")] if layer == 0 else stream_in
    ai_in, attended_in = take(2)
    own, other = take(4), take(4)
    beside_in = take(len(beside.inputs))
    grad_out, attn_gain_out, dense_out = take(3)
    beside_out = take(len(beside.outputs))
    scratch = take(2)
    joint_s, output_s = scratch
    (ag2, part, landing2, ag_stack, dq_s, joint_rows, joint_peer, ao_s, ai_s, turned_ai, attended_s,
     dense_s, send_s, recv_s, attn_sems, core_send, core_recv, local_sems,
     hand_send, hand_recv) = take(20)
    beside_refs = (beside_in, beside_out, refs)
    rows, width = stream.shape
    tokens = ag2.shape[0]
    kw = keys.shape[1]
    qw = output_s.shape[0]
    heads, key_heads = qw // HD, kw // HD
    group = heads // key_heads
    me = lax.axis_index("tensor")
    own_rows = pl.ds(pl.multiple_of(me * rows, rows), rows)
    use_own = lax.axis_index("section") == layer
    ag2[own_rows, :] = mid_grad[...].astype(bf16)
    greet(tensor_peers(count) + [core_peer()] + beside.peers())
    first = spread(count, ag2, rows, send_s.at[0], recv_s.at[0])
    start_all(first)
    either(use_own, own, other, lambda w: [c.start() for c in attn_copies(w, scratch, attn_sems)])
    loads = hand_halves(ai_in, ai_s, [v.at[0] for v in (local_sems, hand_send, hand_recv)])
    loads += hand_rows(attended_in, attended_s, [v.at[1] for v in (local_sems, hand_send, hand_recv)])
    for copy in loads:
        copy.start()
    beside.start(*beside_refs)
    wait_all(loads)
    turned_ai[...] = ai_s[...].T
    wait_all(first)
    core = lax.axis_index("section")
    half = width // 2
    ao_s[pl.ds(0, tokens), :] = ag2[:, pl.ds(pl.multiple_of(core * half, half), half)]
    handed = [
        remote(ag2.at[:, pl.ds(pl.multiple_of((1 - core) * half, half), half)],
               ao_s.at[pl.ds(tokens, tokens)], core_send.at[0], core_recv.at[0], core_peer())
    ]
    handed[0].start()
    either(use_own, own, other, lambda w: [c.wait() for c in attn_copies(w, scratch, attn_sems)])
    attended_grad = dot(ag2[...], output_s[...], NT).astype(bf16)
    for h in range(heads):
        ag_stack[pl.ds(h * tokens, tokens), :] = attended_grad[:, h * HD : (h + 1) * HD]
    for g in range(key_heads):
        lanes = pl.ds(g * HD, HD)
        span = pl.ds(g * group * tokens, group * tokens)
        soft_b = probs[span, :]
        soft = soft_b.astype(f32)
        soft_grad = dot(ag_stack[span, :], values[:, lanes], NT)
        inner = jnp.sum(soft * soft_grad, axis=1, keepdims=True)
        score_grad = (soft * (soft_grad - inner)).astype(bf16)
        dq = dot(score_grad, keys[:, lanes], NN) * 0.125
        for h in range(group):
            dq_s[:, pl.ds((g * group + h) * HD, HD)] = dq[h * tokens : (h + 1) * tokens]
        dq_s[:, pl.ds(qw + g * HD, HD)] = dot(score_grad, qs[span, :], TN) * 0.125
        joint_rows[:, pl.ds(qw + kw + g * HD, HD)] = dot(soft_b, ag_stack[span, :], TN).astype(bf16)
    for chunk in range((qw + kw) // 128):
        lanes = pl.ds(chunk * 128, 128)
        block = dq_s[:, lanes]
        joint_rows[:, lanes] = (block * cosine[...] - turned(block) * sine[...]).astype(bf16)
    handed.append(remote(joint_rows, joint_peer, core_send.at[1], core_recv.at[1], core_peer()))
    handed[1].start()
    copies = []
    tile = width // 2
    for t in range(2):
        columns = pl.ds(t * tile, tile)
        part[:, columns] = dot(joint_rows[...], joint_s[columns, :], NT).astype(bf16)
        copies += deal_out(count, part, rows, columns, landing2, send_s.at[1 + t], recv_s.at[1 + t])
    wait_all(handed)
    wide = qw + 2 * kw
    dense_s[:, :wide] = (
        dot(turned_ai[:, :tokens], joint_rows[...], NN) + dot(turned_ai[:, tokens:], joint_peer[...], NN)
    ).astype(bf16)
    dense_s[:, wide:] = dot(ao_s[...], attended_s[...], TN).astype(bf16)
    save = pltpu.make_async_copy(dense_s, dense_out, local_sems.at[0])
    save.start()
    wait_all(copies)
    in_grad = part[own_rows, :].astype(f32)
    for step in range(count - 1):
        in_grad = in_grad + landing2[step].astype(f32)
    stream_part, attn_gain_grad = norm_back(
        stream[...].astype(bf16).astype(f32), attn_gain[...], in_grad
    )
    attn_gain_out[...] = attn_gain_grad
    grad_out[...] = mid_grad[...] + stream_part
    save.wait()
    beside.wait(*beside_refs)


def attention_back(layer, gains, own, other, mid_grad, stream, state, pairs, tables, beside):
    count = lax.axis_size("tensor")
    qs, keys, values, probs = state
    rows, width = mid_grad.shape
    tokens = keys.shape[0]
    own, other = own[:4], other[:4]
    qw, kw = own[0].shape[1], own[1].shape[1]
    heads = qw // HD
    vmem = pl.BlockSpec(memory_space=pltpu.VMEM)
    hbm = pl.BlockSpec(memory_space=pl.ANY)
    shape = jax.ShapeDtypeStruct
    found = pl.pallas_call(
        functools.partial(attention_back_kernel, layer, count, beside),
        name=f"attention_back_{layer}",
        out_shape=(
            shape((rows, width), f32),
            shape((1, width), f32),
            shape((width // 2, 2 * qw + 2 * kw), bf16),
            *beside.outputs,
        ),
        in_specs=[vmem] * 9 + [hbm] * (10 + len(beside.inputs)),
        out_specs=(vmem, vmem, hbm) + (hbm,) * len(beside.outputs),
        scratch_shapes=[
            pltpu.VMEM((width, qw + 2 * kw), bf16),
            pltpu.VMEM((qw, width), bf16),
            pltpu.VMEM((tokens, width), bf16),
            pltpu.VMEM((tokens, width), bf16),
            pltpu.VMEM((count - 1, rows, width), bf16),
            pltpu.VMEM((heads * tokens, HD), bf16),
            pltpu.VMEM((tokens, qw + kw), f32),
            pltpu.VMEM((tokens, qw + 2 * kw), bf16),
            pltpu.VMEM((tokens, qw + 2 * kw), bf16),
            pltpu.VMEM((2 * tokens, width // 2), bf16),
            pltpu.VMEM((2 * tokens, width // 2), bf16),
            pltpu.VMEM((width // 2, 2 * tokens), bf16),
            pltpu.VMEM((2 * tokens, qw), bf16),
            pltpu.VMEM((width // 2, 2 * qw + 2 * kw), bf16),
            pltpu.SemaphoreType.DMA((3, count - 1)),
            pltpu.SemaphoreType.DMA((3, count - 1)),
            pltpu.SemaphoreType.DMA((4,)),
            *[pltpu.SemaphoreType.DMA((2,)) for _ in range(5)],
            *beside.sems,
        ],
        compiler_params=params(5 + layer),
    )(mid_grad, stream, gains[0], *tables[:2], qs, keys, values, probs, *pairs, *own, *other,
      *beside.inputs)
    return found[:3], beside.results(found[3:])


def finish_kernel(bring, beside, *refs):
    refs = list(refs)

    def take(number):
        taken = refs[:number]
        del refs[:number]
        return taken

    *small_parts, dense = take(7)
    beside_in = take(len(beside.inputs))
    small_out, whole_out, *beside_out = take(2 + len(beside.outputs))
    (landing, block, small_z, small_dp, small_core, small_sum, small_mid, small_last, small_whole,
     sends, recvs, local_sems, z_sends, z_recvs, dp_sends, dp_recvs, core_sends,
     core_recvs, small) = take(19)
    bring_sems = take(len(bring.sems))
    beside_refs = (beside_in, beside_out, refs)
    count = dense.shape[0]
    tensor = small_z.shape[0] + 1
    lanes = small_z.shape[2]
    me = lax.axis_index("dp")
    here = lax.axis_index("tensor")
    groups = [{"dp": lax.rem(me + step, count)} for step in range(1, count)]
    greet(both_cores([group["dp"] for group in groups]) + tensor_peers(tensor) + [core_peer()])

    def launch(*args):
        copy = remote(*args)
        copy.start()
        return copy

    def columns(place):
        return pl.ds(pl.multiple_of(place * lanes, lanes), lanes)

    place = 0
    for index, value in enumerate(small_parts):
        if index % 3 == 0:
            place = index // 3 * (small.shape[0] // 2)
        small[pl.ds(place, value.shape[0]), :] = value[...]
        place += value.shape[0]
    first = []
    for step in range(1, tensor):
        place = lax.rem(here + step, tensor)
        first.append(
            launch(small.at[:, columns(place)], small_z.at[step - 1], z_sends.at[0, step - 1],
                   z_recvs.at[0, step - 1], {"tensor": place})
        )
    copies = []
    for step in range(1, count):
        place = lax.rem(me + step, count)
        copies.append(
            launch(dense.at[place], landing.at[step - 1], sends.at[0, step - 1],
                   recvs.at[0, step - 1], {"dp": place})
        )
    beside.start(*beside_refs)
    mine = pltpu.make_async_copy(dense.at[me], block, local_sems.at[0])
    mine.start()
    wait_all(first)
    total = small[:, columns(here)]
    for step in range(tensor - 1):
        total = total + small_z[step]
    small_sum[...] = total
    second = [
        launch(small_sum, small_dp.at[step], dp_sends.at[step], dp_recvs.at[step], groups[step])
        for step in range(count - 1)
    ]
    mine.wait()
    wait_all(copies)
    total = block[...].astype(f32)
    for step in range(count - 1):
        total = total + landing[step].astype(f32)
    block[...] = total.astype(bf16)
    bring.start([block], [whole_out], bring_sems)
    wait_all(second)
    total = small_sum[...]
    for step in range(count - 1):
        total = total + small_dp[step]
    small_mid[...] = total
    third = launch(small_mid, small_core, core_sends.at[0], core_recvs.at[0], core_peer())
    third.wait()
    small_last[...] = small_mid[...] + small_core[...]
    last = [
        launch(small_last, small_whole.at[:, columns(here)], z_sends.at[1, step - 1],
               z_recvs.at[1, step - 1], {"tensor": lax.rem(here + step, tensor)})
        for step in range(1, tensor)
    ]
    small_whole[:, columns(here)] = small_last[...]
    wait_all(last)
    small_out[...] = small_whole[...]
    bring.wait([block], [whole_out], bring_sems)
    beside.wait(*beside_refs)


def finish(small_parts, dense, layer, beside):
    count = lax.axis_size("dp")
    tensor = lax.axis_size("tensor")
    rows = dense.shape[0] // count
    depth = -(-sum(v.shape[0] for v in small_parts[:3]) // 8) * 8
    small = jax.ShapeDtypeStruct((2 * depth, small_parts[0].shape[1]), f32)
    lanes = small.shape[1] // tensor
    hbm = pl.BlockSpec(memory_space=pl.ANY)
    vmem = pl.BlockSpec(memory_space=pltpu.VMEM)
    bring = Bring(layer, "all", jax.ShapeDtypeStruct((rows, dense.shape[1]), bf16), True)
    found = pl.pallas_call(
        functools.partial(finish_kernel, bring, beside),
        name="finish",
        out_shape=(
            jax.ShapeDtypeStruct(small.shape, f32),
            *bring.outputs,
            *beside.outputs,
        ),
        in_specs=[vmem] * 6 + [hbm] * (1 + len(beside.inputs)),
        out_specs=(vmem,) + (hbm,) * (1 + len(beside.outputs)),
        scratch_shapes=[
            pltpu.VMEM((count - 1, rows, dense.shape[1]), bf16),
            pltpu.VMEM((rows, dense.shape[1]), bf16),
            pltpu.VMEM((tensor - 1, small.shape[0], lanes), f32),
            pltpu.VMEM((count - 1, small.shape[0], lanes), f32),
            pltpu.VMEM((small.shape[0], lanes), f32),
            pltpu.VMEM((small.shape[0], lanes), f32),
            pltpu.VMEM((small.shape[0], lanes), f32),
            pltpu.VMEM((small.shape[0], lanes), f32),
            pltpu.VMEM(small.shape, f32),
            dma((1, count - 1)),
            dma((1, count - 1)),
            dma((1,)),
            dma((2, tensor - 1)),
            dma((2, tensor - 1)),
            dma((count - 1,)),
            dma((count - 1,)),
            dma((1,)),
            dma((1,)),
            pltpu.VMEM(small.shape, f32),
            *bring.sems,
            *beside.sems,
        ],
        compiler_params=params(7),
    )(*small_parts, dense.reshape(count, rows, dense.shape[1]), *beside.inputs)
    return found[0], found[1], beside.results(found[2:])


def prepare_kernel(lengths, dealing, order, routes, attn_gain, expert_gain, router, freqs,
                   cosine, sine, bias, picked, kept, attn_gains, expert_gains, routers,
                   order_peer, routes_peer, sends, recvs):
    core = lax.axis_index("section")
    attn_gains[core] = attn_gain[...]
    expert_gains[core] = expert_gain[...]
    routers[core] = router[...]
    greet([core_peer()])
    copies = [
        remote(source, target, sends.at[index], recvs.at[index], core_peer())
        for index, (source, target) in enumerate((
            (order.at[1 - core], order_peer),
            (routes.at[1 - core], routes_peer),
            (attn_gain, attn_gains.at[core]),
            (expert_gain, expert_gains.at[core]),
            (router, routers.at[core]),
        ))
    ]
    start_all(copies)
    tokens = bias.shape[0]
    sequences = lengths.shape[1]
    tall = lax.broadcasted_iota(jnp.int32, (tokens, 1), 0)
    wide = lax.broadcasted_iota(jnp.int32, (1, tokens), 1)
    sizes = [lengths[core, index] for index in range(sequences)]
    starts = [sum(sizes[:index], 0) for index in range(sequences)]
    ranks = [
        sum(jnp.where(dealing[core, place] == index, place, 0) for place in range(sequences))
        for index in range(sequences)
    ]
    dealt_starts = [
        sum(jnp.where(ranks[before] < ranks[index], sizes[before], 0) for before in range(sequences))
        for index in range(sequences)
    ]

    def places(token):
        segment = sum((token >= starts[index] + sizes[index]).astype(jnp.int32)
                      for index in range(sequences))
        position, dealt = token, token
        for index in range(sequences):
            inside = segment == index
            position = jnp.where(inside, token - starts[index], position)
            dealt = jnp.where(inside, token - starts[index] + dealt_starts[index], dealt)
        return segment, position, dealt

    segment, position, dealt = places(tall)
    segment_wide, _, dealt_wide = places(wide)
    allowed = (segment == segment_wide) & (wide <= tall)
    bias[...] = jnp.where(allowed, 0.0, masked_score).astype(f32)
    angles = position.astype(f32) * freqs[...]
    cosine[...] = jnp.cos(angles)
    lane = lax.broadcasted_iota(jnp.int32, (1, freqs.shape[1]), 1)
    sine[...] = jnp.sin(angles) * jnp.where(lane % HD < HD // 2, -1.0, 1.0)

    def masks(order_row, route_rows):
        order_wide = order_row.astype(f32)
        order_tall = jnp.sum(jnp.where(tall == wide, order_wide, 0.0), axis=1, keepdims=True)
        first = jnp.sum(jnp.where(dealt == wide, order_wide, 0.0), axis=1, keepdims=True)
        first_wide = jnp.sum(jnp.where(dealt_wide == tall, order_tall, 0.0), axis=0, keepdims=True)
        earlier = jnp.where(first_wide < first, 1.0, 0.0).astype(bf16)
        experts = picked.shape[2]
        index = lax.broadcasted_iota(jnp.int32, (tokens, experts), 1)
        chosen = jnp.zeros((tokens, experts), f32)
        for k in range(route_rows.shape[1]):
            chosen = jnp.where(route_rows[:, k : k + 1] == index, 1.0, chosen)
        rank = dot(earlier, chosen.astype(bf16), NN)
        return chosen, jnp.where(rank < CAP, chosen, 0.0)

    picked[core], kept[core] = masks(order[core], routes[core])
    wait_all(copies)
    picked[1 - core], kept[1 - core] = masks(order_peer[...], routes_peer[...])


def prepare(lengths, dealing, order, routes, attn_gain, expert_gain, router):
    tokens = order.shape[2]
    width = attn_gain.shape[1]
    half = HD // 2
    freqs = jnp.tile(rope_base ** (-2.0 * jnp.arange(half, dtype=f32) / HD), 128 // half)[None]
    vmem = pl.BlockSpec(memory_space=pltpu.VMEM)
    smem = pl.BlockSpec(memory_space=pltpu.SMEM)
    shape = jax.ShapeDtypeStruct
    found = pl.pallas_call(
        prepare_kernel,
        name="prepare",
        out_shape=(
            shape((tokens, 128), f32),
            shape((tokens, 128), f32),
            shape((tokens, tokens), f32),
            shape((2, tokens, E), f32),
            shape((2, tokens, E), f32),
            shape((2, 1, width), f32),
            shape((2, 1, width), f32),
            shape((2, *router.shape), bf16),
        ),
        in_specs=[smem] * 2 + [vmem] * 6,
        out_specs=(vmem,) * 8,
        scratch_shapes=[
            pltpu.VMEM(order.shape[1:], order.dtype),
            pltpu.VMEM(routes.shape[1:], routes.dtype),
            dma((5,)),
            dma((5,)),
        ],
        compiler_params=params(8),
    )(lengths, dealing, order, routes, attn_gain, expert_gain, router, freqs)
    return found[:3], found[3:5], found[5:]


def assemble_kernel(section, *refs):
    expert_refs, dense_refs, outs = (refs[:4], refs[4:8]), refs[8:10], refs[10:]
    query, key, value, output, gate, up, down = outs
    hidden_width = gate.shape[2]
    qw, kw = query.shape[1], key.shape[1]

    def write(parts, dense):
        cores = range(2)
        pair = [[jnp.sum(v[core, :, 0].astype(f32), axis=0) for v in parts[:2]] for core in cores]
        depth = 0
        for block in pair[0] + pair[1]:
            rows = pl.ds(depth, block.shape[0])
            gate[0, rows, :] = block[:, :hidden_width]
            up[0, rows, :] = block[:, hidden_width:]
            depth += block.shape[0]
        depth = 0
        for core in cores:
            for v in parts[2:]:
                block = jnp.sum(v[core, :, 0].astype(f32), axis=0)
                down[0, :, pl.ds(depth, block.shape[1])] = block
                depth += block.shape[1]
        rows = dense[...].astype(f32)
        query[...] = rows[:, :qw]
        key[...] = rows[:, qw : qw + kw]
        value[...] = rows[:, qw + kw : qw + 2 * kw]
        output[...] = rows[:, qw + 2 * kw :].T

    pl.when(section[0] == 0)(lambda: write(expert_refs[0], dense_refs[0]))
    pl.when(section[0] == 1)(lambda: write(expert_refs[1], dense_refs[1]))


def assemble(parts, denses, qw, kw):
    groups = parts[0][0].shape[2]
    hidden_width = parts[0][2].shape[3]
    dense = [v.reshape(-1, v.shape[3]) for v in denses]
    depth = dense[0].shape[0]
    rows = depth // groups

    def part_spec(layer, shape):
        block = (*shape[:2], 1, *shape[3:])
        return pl.BlockSpec(block, lambda e, s: (0, 0, jnp.where(s[0] == layer, e, 0), 0, 0))

    def dense_spec(layer, width):
        return pl.BlockSpec((rows, width), lambda e, s: (jnp.where(s[0] == layer, e, 0), 0))

    shape = jax.ShapeDtypeStruct
    return pl.pallas_call(
        assemble_kernel,
        name="assemble",
        out_shape=(
            shape((depth, qw), f32),
            shape((depth, kw), f32),
            shape((depth, kw), f32),
            shape((qw, depth), f32),
            shape((groups, depth, hidden_width), f32),
            shape((groups, depth, hidden_width), f32),
            shape((groups, hidden_width, depth), f32),
        ),
        grid_spec=pltpu.PrefetchScalarGridSpec(
            num_scalar_prefetch=1,
            grid=(groups,),
            in_specs=[part_spec(layer, v.shape) for layer in range(2) for v in parts[layer]]
            + [dense_spec(layer, dense[layer].shape[1]) for layer in range(2)],
            out_specs=(
                pl.BlockSpec((rows, qw), lambda e, s: (e, 0)),
                pl.BlockSpec((rows, kw), lambda e, s: (e, 0)),
                pl.BlockSpec((rows, kw), lambda e, s: (e, 0)),
                pl.BlockSpec((qw, rows), lambda e, s: (0, e)),
                pl.BlockSpec((1, depth, hidden_width), lambda e, s: (e, 0, 0)),
                pl.BlockSpec((1, depth, hidden_width), lambda e, s: (e, 0, 0)),
                pl.BlockSpec((1, hidden_width, depth), lambda e, s: (e, 0, 0)),
            ),
        ),
        compiler_params=pltpu.CompilerParams(vmem_limit_bytes=48 * 2**20),
    )(lax.axis_index("section").astype(jnp.int32)[None], *parts[0], *parts[1], *dense)


def shards(
    tokens_in, out_cotangent, attn_gain, query_weight, key_weight, value_weight, output_weight,
    expert_gain, router_weight, gate_weight, up_weight, down_weight, lengths, dealing,
    slot_order, routes,
):
    first = lax.axis_index("section") == 0
    qw, kw = query_weight.shape[2], key_weight.shape[2]
    own = (query_weight[0], key_weight[0], value_weight[0], output_weight[0], gate_weight[0],
           up_weight[0], down_weight[0])
    tables, masks, gains = prepare(lengths[:, 0], dealing[:, 0], slot_order[0], routes[0], attn_gain,
                                   expert_gain, router_weight[0])
    (out0, *state0), other = layer_forward(0, gains, own, None, tokens_in, tables, masks)
    (out1, *state1), _ = layer_forward(1, gains, own, other, out0, tables, masks)
    saved = (state0, state1)
    streams = (tokens_in, out0)

    def experts(layer, out_grad, jobs):
        mid, expert_rows, qs, keys, values, probs, gate, ai, x, gated, attended, pre = saved[layer]
        (mid_grad, router_part, gain_part, pair, down), done = experts_back(
            layer, gains, own, other, out_grad, (mid, gate, expert_rows, pre), (x, gated), masks,
            Beside(jobs)
        )
        return mid_grad, (gain_part, router_part), [FirstStage(pair, 1), FirstStage(down, 2)], done

    def attention(layer, mid_grad, jobs):
        mid, expert_rows, qs, keys, values, probs, gate, ai, x, gated, attended, pre = saved[layer]
        (grad, gain_part, dense), done = attention_back(
            layer, gains, own, other, mid_grad, streams[layer], (qs, keys, values, probs),
            (ai, attended), tables, Beside(jobs)
        )
        return grad, gain_part, dense, done

    def second(layer, sums):
        return [Bring(layer, kind, v) for pair in sums for kind, v in zip(("column", "row"), pair)]

    mid_grad, small1, stage, _ = experts(1, out_cotangent, [])
    grad1, gain1, dense1, sums = attention(1, mid_grad, stage)
    mid_grad, small0, stage, (*parts1, dense1) = experts(
        0, grad1.astype(bf16), second(1, sums) + [Scatter(dense1)]
    )
    grad0, gain0, dense0, (*sums, dense1) = attention(
        0, mid_grad, stage + [Bring(1, "all", dense1)]
    )
    small, dense0, parts0 = finish(
        (small0[1], gain0, small0[0], small1[1], gain1, small1[0]), dense0, 0, Beside(second(0, sums))
    )

    def by_layer(zero, one):
        mine = jnp.where(first, zero, one)
        theirs = swapped(jnp.where(first, one, zero))
        return jnp.where(first, jnp.stack([mine, theirs]), jnp.stack([theirs, mine]))[None]

    layer_outputs = by_layer(out0, out1)
    input_grads = by_layer(grad0, grad1)

    query, key, value, output, gate, up, down = assemble((parts0, parts1), (dense0, dense1), qw, kw)
    small = jnp.where(first, small[: small.shape[0] // 2], small[small.shape[0] // 2 :])
    router_grad, attn_gain_grad, expert_gain_grad = small[:E].T, small[E : E + 1], small[E + 1 : E + 2]
    return (
        layer_outputs,
        input_grads,
        attn_gain_grad,
        query[None],
        key[None],
        value[None],
        output[None],
        expert_gain_grad,
        router_grad[None],
        gate[None],
        up[None],
        down[None],
    )


def solution(mesh):
    return jax.shard_map(
        shards,
        mesh=mesh,
        in_specs=(
            P(None, ("dp", "tensor"), None),
            P(None, ("dp", "tensor"), None),
            P("section", None),
            P("section", None, "tensor"),
            P("section", None, "tensor"),
            P("section", None, "tensor"),
            P("section", "tensor", None),
            P("section", None),
            P("section", None, None),
            P("section", None, None, "tensor"),
            P("section", None, None, "tensor"),
            P("section", None, "tensor", None),
            P(None, "dp", None),
            P(None, "dp", None),
            P("section", None, "dp", None),
            P("section", None, "dp", None),
        ),
        out_specs=(
            P("section", None, ("dp", "tensor"), None),
            P("section", None, ("dp", "tensor"), None),
            P("section", None),
            P("section", None, "tensor"),
            P("section", None, "tensor"),
            P("section", None, "tensor"),
            P("section", "tensor", None),
            P("section", None),
            P("section", None, None),
            P("section", "dp", None, "tensor"),
            P("section", "dp", None, "tensor"),
            P("section", "dp", "tensor", None),
        ),
        check_vma=False,
    )
```

```python
import functools
import math

import jax
import jax.numpy as jnp
from jax import lax
from jax.experimental import pallas as pl
from jax.experimental.pallas import tpu as pltpu
from jax.sharding import PartitionSpec as P

H = 24
KV = 8
HD = 64
E = 16
CAP = 160

epsilon = 1e-05
rope_base = 10000.0
masked_score = -1e30
bf16 = jnp.bfloat16
f32 = jnp.float32
MESH = pl.DeviceIdType.MESH


def dot(a, b, dims):
    return lax.dot_general(a, b, (dims, ((), ())), preferred_element_type=f32)


NN = ((1,), (0,))
NT = ((1,), (1,))
TN = ((0,), (0,))


def norm_scale(rows_in):
    return lax.rsqrt(jnp.mean(rows_in * rows_in, axis=-1, keepdims=True) + epsilon)


def params(collective_id):
    return pltpu.CompilerParams(
        collective_id=collective_id, has_side_effects=True, vmem_limit_bytes=56 * 2**20
    )


def tensor_peers(count):
    me = lax.axis_index("tensor")
    return [{"tensor": lax.rem(me + step, count)} for step in range(1, count)]


def greet(peers):
    barrier = pltpu.get_barrier_semaphore()
    for peer in peers:
        pl.semaphore_signal(barrier, inc=1, device_id=peer, device_id_type=MESH)
    pl.semaphore_wait(barrier, len(peers))


def factors(count):
    inner = math.isqrt(count)
    while count % inner:
        inner -= 1
    return count // inner, inner


def group_place(count):
    outer, inner = factors(count)
    me = lax.axis_index("dp")
    return outer, inner, me // inner, lax.rem(me, inner)


def near_groups(count):
    outer, inner, mo, mi = group_place(count)
    across = [lax.rem(mi + step, inner) for step in range(1, inner)]
    along = [lax.rem(mo + step, outer) for step in range(1, outer)]
    return (
        [(place, {"dp": mo * inner + place}) for place in across],
        [(place, {"dp": place * inner + mi}) for place in along],
    )


dma = pltpu.SemaphoreType.DMA


def remote(src, dst, send, recv, device):
    return pltpu.make_async_remote_copy(
        src_ref=src, dst_ref=dst, send_sem=send, recv_sem=recv, device_id=device, device_id_type=MESH
    )


class Bring:
    def __init__(self, layer, kind, value, in_vmem=False):
        self.layer, self.kind, self.in_vmem = layer, kind, in_vmem
        count = lax.axis_size("dp")
        outer, inner = factors(count)
        self.size = {"column": outer, "row": inner, "all": count}[kind]
        block = value.shape if kind == "all" else value.shape[1:]
        self.inputs = [value]
        self.outputs = [jax.ShapeDtypeStruct((2, self.size, *block), value.dtype)]
        self.sems = [dma((self.size,)), dma((2, self.size)), dma((2,))]
        if not in_vmem:
            self.sems.append(pltpu.VMEM(block, value.dtype))

    def place(self, step):
        count = lax.axis_size("dp")
        outer, inner, mo, mi = group_place(count)
        if self.kind == "column":
            place = lax.rem(mo + step, outer)
            return place, place * inner + mi
        if self.kind == "row":
            place = lax.rem(mi + step, inner)
            return place, mo * inner + place
        place = lax.rem(lax.axis_index("dp") + step, count)
        return place, place

    def parts(self, inputs, outputs, sems):
        core = lax.axis_index("section")
        mine, _ = self.place(0)
        target = outputs[0].at[core, mine]
        recv = sems[1].at[core, mine]

        def source(place):
            return inputs[0] if self.kind == "all" else inputs[0].at[place]

        sent = []
        for step in range(1, self.size):
            place, group = self.place(step)
            sent.append(
                remote(source(place), target, sems[0].at[step - 1], recv,
                       {"dp": group, "section": self.layer})
            )
        across = remote(source(mine), target, sems[0].at[self.size - 1], recv, core_peer())
        if self.in_vmem:
            local = [pltpu.make_async_copy(source(mine), target, sems[2].at[0])]
        else:
            local = [
                pltpu.make_async_copy(source(mine), sems[3], sems[2].at[0]),
                pltpu.make_async_copy(sems[3], target, sems[2].at[1]),
            ]
        return sent, across, local

    def start(self, inputs, outputs, sems):
        sent, across, local = self.parts(inputs, outputs, sems)
        for copy in sent:
            copy.start()
        here = lax.axis_index("section") == self.layer

        @pl.when(here)
        def _():
            local[0].start()

        @pl.when(jnp.logical_not(here))
        def _():
            across.start()

    def wait(self, inputs, outputs, sems):
        sent, across, local = self.parts(inputs, outputs, sems)
        core = lax.axis_index("section")
        here = core == self.layer
        block = inputs[0] if self.kind == "all" else inputs[0].at[0]

        def arrived(which, place):
            remote(block, outputs[0].at[which, place], sems[0].at[0], sems[1].at[which, place],
                   core_peer()).wait_recv()

        for copy in sent:
            copy.wait_send()

        @pl.when(here)
        def _():
            local[0].wait()
            for copy in local[1:]:
                copy.start()
                copy.wait()
            for step in range(self.size):
                place, _ = self.place(step)
                if step:
                    arrived(core, place)
                arrived(1 - core, place)

        @pl.when(jnp.logical_not(here))
        def _():
            across.wait_send()

    def results(self, outputs):
        return outputs[0]


class FirstStage:
    def __init__(self, value, axis, layer=None):
        self.count = lax.axis_size("dp")
        outer, inner = factors(self.count)
        self.inputs = [value.reshape((outer, inner, value.shape[0] // self.count) + value.shape[1:])]
        self.axis = axis
        shape = list(self.inputs[0].shape[2:])
        shape[axis] //= 2
        self.shape = shape
        sums = [
            jax.ShapeDtypeStruct((outer, *shape), value.dtype),
            jax.ShapeDtypeStruct((inner, *shape), value.dtype),
        ]
        self.sems = [
            dma((inner + outer - 2,)),
            dma((inner + outer - 2,)),
            pltpu.VMEM((inner - 1, outer, *shape), value.dtype),
            pltpu.VMEM((outer - 1, inner, *shape), value.dtype),
            *[pltpu.VMEM(v.shape, v.dtype) for v in sums],
            dma((2,)),
            dma((2,)),
        ]
        self.outputs = sums
        self.brings = []
        if layer is not None:
            self.brings = [Bring(layer, kind, v, True) for kind, v in zip(("column", "row"), sums)]
            self.outputs = [v for bring in self.brings for v in bring.outputs]
            self.sems += [v for bring in self.brings for v in bring.sems]

    def copies(self, inputs, sems):
        across, along = near_groups(self.count)
        _, _, mo, mi = group_place(self.count)
        value = inputs[0]
        half = self.shape[self.axis]
        cut = [slice(None)] * 3
        first, second = list(cut), list(cut)
        first[self.axis], second[self.axis] = pl.ds(0, half), pl.ds(half, half)
        found = []
        for slot, (place, device) in enumerate(across):
            found.append((value.at[(slice(None), place, *first)], sems[2].at[slot], device))
        for slot, (place, device) in enumerate(along):
            found.append((value.at[(place, slice(None), *second)], sems[3].at[slot], device))
        sent = [
            remote(src, dst, sems[0].at[index], sems[1].at[index], device)
            for index, (src, dst, device) in enumerate(found)
        ]
        loads = [
            pltpu.make_async_copy(value.at[(slice(None), mi, *first)], sems[4], sems[6].at[0]),
            pltpu.make_async_copy(value.at[(mo, slice(None), *second)], sems[5], sems[6].at[1]),
        ]
        return sent + loads

    def onward(self, outputs, sems):
        place = 8
        found = []
        for index, bring in enumerate(self.brings):
            found.append((bring, [sems[4 + index]], [outputs[index]], sems[place : place + len(bring.sems)]))
            place += len(bring.sems)
        return found

    def saves(self, outputs, sems):
        return [pltpu.make_async_copy(sems[4 + k], outputs[k], sems[7].at[k]) for k in range(2)]

    def start(self, inputs, outputs, sems):
        start_all(self.copies(inputs, sems))

    def middle(self, inputs, outputs, sems):
        wait_all(self.copies(inputs, sems))
        for total, landed in ((sems[4], sems[2]), (sems[5], sems[3])):
            depth = total.shape[1]

            def add(index, carry, total=total, landed=landed, depth=depth):
                place, expert = index // depth, lax.rem(index, depth)
                value = total[place, expert].astype(f32)
                for slot in range(landed.shape[0]):
                    value = value + landed[slot, place, expert].astype(f32)
                total[place, expert] = value.astype(bf16)
                return carry

            lax.fori_loop(0, total.shape[0] * depth, add, 0)
        if self.brings:
            for bring, *refs in self.onward(outputs, sems):
                bring.start(*refs)
        else:
            start_all(self.saves(outputs, sems))

    def wait(self, inputs, outputs, sems):
        if self.brings:
            for bring, *refs in self.onward(outputs, sems):
                bring.wait(*refs)
        else:
            wait_all(self.saves(outputs, sems))

    def results(self, outputs):
        return outputs


class DenseSum:
    kind = "all"

    def __init__(self, value, layer):
        count = lax.axis_size("dp")
        self.rows, width = value.shape[0] // count, value.shape[1]
        self.bring = Bring(layer, "all", jax.ShapeDtypeStruct((self.rows, width), bf16), True)
        self.inputs = [value]
        self.outputs = self.bring.outputs
        self.sems = [
            dma((count - 1,)),
            dma((count - 1,)),
            pltpu.VMEM((count - 1, self.rows, width), bf16),
            pltpu.VMEM((self.rows, width), bf16),
            dma((1,)),
            *self.bring.sems,
        ]

    def copies(self, inputs, sems):
        count = lax.axis_size("dp")
        me = lax.axis_index("dp")

        def block(place):
            return inputs[0].at[pl.ds(pl.multiple_of(place * self.rows, self.rows), self.rows)]

        found = [pltpu.make_async_copy(block(me), sems[3], sems[4].at[0])]
        for step in range(1, count):
            place = lax.rem(me + step, count)
            found.append(
                remote(block(place), sems[2].at[step - 1], sems[0].at[step - 1], sems[1].at[step - 1],
                       {"dp": place})
            )
        return found

    def start(self, inputs, outputs, sems):
        start_all(self.copies(inputs, sems))

    def middle(self, inputs, outputs, sems):
        wait_all(self.copies(inputs, sems))
        total = sems[3][...].astype(f32)
        for slot in range(sems[2].shape[0]):
            total = total + sems[2][slot].astype(f32)
        sems[3][...] = total.astype(bf16)
        self.bring.start([sems[3]], outputs, sems[5:])

    def wait(self, inputs, outputs, sems):
        self.bring.wait([sems[3]], outputs, sems[5:])

    def results(self, outputs):
        return outputs[0]


class SmallSum:
    def __init__(self, depth, width):
        self.tensor, self.count = lax.axis_size("tensor"), lax.axis_size("dp")
        self.lanes = width // self.tensor
        self.depth = depth
        part = (depth, self.lanes)
        self.sems = [
            pltpu.VMEM((depth, width), f32),
            pltpu.VMEM((self.tensor - 1, *part), f32),
            pltpu.VMEM((self.count - 1, *part), f32),
            *[pltpu.VMEM(part, f32) for _ in range(4)],
            pltpu.VMEM((depth, width), f32),
            dma((2, self.tensor - 1)),
            dma((2, self.tensor - 1)),
            dma((self.count,)),
            dma((self.count,)),
        ]

    def columns(self, place):
        return pl.ds(pl.multiple_of(place * self.lanes, self.lanes), self.lanes)

    def over_tensor(self, sems):
        here = lax.axis_index("tensor")
        found = []
        for step in range(1, self.tensor):
            place = lax.rem(here + step, self.tensor)
            found.append(
                remote(sems[0].at[:, self.columns(place)], sems[1].at[step - 1],
                       sems[8].at[0, step - 1], sems[9].at[0, step - 1], {"tensor": place})
            )
        return found

    def over_groups(self, sems):
        me = lax.axis_index("dp")
        return [
            remote(sems[3], sems[2].at[step - 1], sems[10].at[step - 1], sems[11].at[step - 1],
                   {"dp": lax.rem(me + step, self.count)})
            for step in range(1, self.count)
        ]

    def over_cores(self, sems):
        last = self.count - 1
        return [remote(sems[4], sems[5], sems[10].at[last], sems[11].at[last], core_peer())]

    def back(self, sems):
        here = lax.axis_index("tensor")
        own = sems[7].at[:, self.columns(here)]
        return [
            remote(sems[6], own, sems[8].at[1, step - 1], sems[9].at[1, step - 1],
                   {"tensor": lax.rem(here + step, self.tensor)})
            for step in range(1, self.tensor)
        ]

    def first(self, sems):
        start_all(self.over_tensor(sems))

    def second(self, sems):
        wait_all(self.over_tensor(sems))
        total = sems[0][:, self.columns(lax.axis_index("tensor"))]
        for slot in range(self.tensor - 1):
            total = total + sems[1][slot]
        sems[3][...] = total
        start_all(self.over_groups(sems))

    def third(self, sems):
        wait_all(self.over_groups(sems))
        total = sems[3][...]
        for slot in range(self.count - 1):
            total = total + sems[2][slot]
        sems[4][...] = total
        copies = self.over_cores(sems)
        start_all(copies)
        wait_all(copies)
        sems[6][...] = sems[4][...] + sems[5][...]
        start_all(self.back(sems))
        sems[7][:, self.columns(lax.axis_index("tensor"))] = sems[6][...]

    def last(self, sems, out):
        wait_all(self.back(sems))
        out[...] = sems[7][...]


class Trade:
    def __init__(self, shape):
        self.sems = [pltpu.VMEM((2, *shape), f32), dma((1,)), dma((1,))]

    def copy(self, value, sems):
        core = lax.axis_index("section")
        return remote(value, sems[0].at[core], sems[1].at[0], sems[2].at[0], core_peer())

    def start(self, zero, one, sems):
        core = lax.axis_index("section")

        @pl.when(core == 0)
        def _():
            self.copy(one, sems).start()
            sems[0][0] = zero[...]

        @pl.when(core == 1)
        def _():
            self.copy(zero, sems).start()
            sems[0][1] = one[...]

    def wait(self, zero, out, sems):
        self.copy(zero, sems).wait()
        out[...] = sems[0][...]


def both_cores(groups):
    core = lax.axis_index("section")
    return [{"dp": group, "section": which} for group in groups for which in (core, 1 - core)]


class Beside:
    def __init__(self, jobs):
        self.jobs = jobs
        self.inputs = [v for job in jobs for v in job.inputs]
        self.outputs = [v for job in jobs for v in job.outputs]
        self.sems = [v for job in jobs for v in job.sems]

    def peers(self):
        count = lax.axis_size("dp")
        if any(getattr(job, "kind", "") == "all" for job in self.jobs):
            me = lax.axis_index("dp")
            return both_cores([lax.rem(me + step, count) for step in range(1, count)])
        if not self.jobs:
            return []
        across, along = near_groups(count)
        return both_cores([device["dp"] for _, device in across + along])

    def each(self, refs, run):
        inputs, outputs, sems = refs
        for job in self.jobs:
            mine, inputs = inputs[: len(job.inputs)], inputs[len(job.inputs) :]
            theirs, outputs = outputs[: len(job.outputs)], outputs[len(job.outputs) :]
            own, sems = sems[: len(job.sems)], sems[len(job.sems) :]
            run(job)(mine, theirs, own)

    def start(self, *refs):
        self.each(refs, lambda job: job.start)

    def middle(self, *refs):
        self.each(refs, lambda job: getattr(job, "middle", lambda *refs: None))

    def wait(self, *refs):
        self.each(refs, lambda job: job.wait)

    def results(self, outputs):
        found = []
        for job in self.jobs:
            found.append(job.results(outputs[: len(job.outputs)]))
            outputs = outputs[len(job.outputs) :]
        return found


def spread(count, buf, rows, sends, recvs):
    me = lax.axis_index("tensor")
    own = buf.at[pl.ds(pl.multiple_of(me * rows, rows), rows)]
    copies = []
    for step in range(1, count):
        copies.append(
            pltpu.make_async_remote_copy(
                src_ref=own,
                dst_ref=own,
                send_sem=sends.at[step - 1],
                recv_sem=recvs.at[step - 1],
                device_id={"tensor": lax.rem(me + step, count)},
                device_id_type=MESH,
            )
        )
    return copies


def deal_out(count, part, rows, columns, landing, sends, recvs):
    me = lax.axis_index("tensor")
    copies = []
    for step in range(1, count):
        peer = lax.rem(me + step, count)
        copies.append(
            pltpu.make_async_remote_copy(
                src_ref=part.at[pl.ds(pl.multiple_of(peer * rows, rows), rows), columns],
                dst_ref=landing.at[step - 1, :, columns],
                send_sem=sends.at[step - 1],
                recv_sem=recvs.at[step - 1],
                device_id={"tensor": peer},
                device_id_type=MESH,
            )
        )
    for copy in copies:
        copy.start()
    return copies


def core_peer():
    return {"section": 1 - lax.axis_index("section")}


def hand_rows(value, pair, sems):
    tokens = value.shape[0]
    return [
        pltpu.make_async_copy(value, pair.at[pl.ds(0, tokens)], sems[0]),
        remote(value, pair.at[pl.ds(tokens, tokens)], sems[1], sems[2], core_peer()),
    ]


def hand_halves(value, pair, sems):
    section = lax.axis_index("section")
    tokens, half = value.shape[0], value.shape[1] // 2
    mine = value.at[:, pl.ds(pl.multiple_of(section * half, half), half)]
    other = value.at[:, pl.ds(pl.multiple_of((1 - section) * half, half), half)]
    return [
        pltpu.make_async_copy(mine, pair.at[pl.ds(0, tokens)], sems[0]),
        remote(other, pair.at[pl.ds(tokens, tokens)], sems[1], sems[2], core_peer()),
    ]


def start_all(copies):
    for copy in copies:
        copy.start()


def wait_all(copies):
    for copy in copies:
        copy.wait()


def either(use_own, own, other, run):
    @pl.when(use_own)
    def _():
        run(own)

    @pl.when(jnp.logical_not(use_own))
    def _():
        run(other)


def weight_copies(refs, scratch, sems, expert):
    gate, up, down = refs
    gu_s, down_s = scratch
    width = gate.shape[2]
    return (
        pltpu.make_async_copy(gate.at[expert], gu_s.at[expert, :, pl.ds(0, width)], sems.at[0, expert]),
        pltpu.make_async_copy(up.at[expert], gu_s.at[expert, :, pl.ds(width, width)], sems.at[1, expert]),
        pltpu.make_async_copy(
            down.at[expert], down_s.at[pl.ds(pl.multiple_of(expert * width, width), width)], sems.at[2, expert]
        ),
    )


def attn_copies(refs, scratch, sems):
    query, key, value, output = refs
    joint_s, output_s = scratch
    qw, kw = query.shape[1], key.shape[1]
    return (
        pltpu.make_async_copy(query, joint_s.at[:, pl.ds(0, qw)], sems.at[0]),
        pltpu.make_async_copy(key, joint_s.at[:, pl.ds(qw, kw)], sems.at[1]),
        pltpu.make_async_copy(value, joint_s.at[:, pl.ds(qw + kw, kw)], sems.at[2]),
        pltpu.make_async_copy(output, output_s, sems.at[3]),
    )


def turned(block):
    lane = lax.broadcasted_iota(jnp.int32, block.shape, 1)
    half = HD // 2
    return jnp.where(
        lane % HD < half, pltpu.roll(block, block.shape[1] - half, 1), pltpu.roll(block, half, 1)
    )


def column(table, index):
    lane = lax.broadcasted_iota(jnp.int32, table.shape, 1)
    return jnp.sum(jnp.where(lane == index, table, 0.0), axis=1, keepdims=True)


def swap_copies(own, other, sems, piece):
    sends, recvs = sems
    names = len(own)
    if isinstance(piece, tuple):
        name, expert = piece
        source, target = own[name].at[expert], other[name].at[expert]
        index = 4 + (name - 4) * own[4].shape[0] + expert
    else:
        source, target, index = own[piece], other[piece], piece
    return pltpu.make_async_remote_copy(
        src_ref=source, dst_ref=target, send_sem=sends.at[index], recv_sem=recvs.at[index],
        device_id=core_peer(), device_id_type=MESH,
    )


def forward_kernel(layer, count, swap, *refs):
    refs = list(refs)

    def take(number):
        taken = refs[:number]
        del refs[:number]
        return taken

    (stream_in, attn_gains, expert_gains, routers, cosine, sine, bias, pickeds, kepts) = take(9)
    attn_gain, expert_gain, router = attn_gains.at[layer], expert_gains.at[layer], routers.at[layer]
    picked, kept = pickeds.at[layer], kepts.at[layer]
    stream = stream_in.at[lax.axis_index("section")] if layer == 0 else stream_in
    own = take(7)
    other = None if swap else take(7)
    (out, mid_out, expert_rows_out, qs_out, keys_out, values_out, probs_out, gate_out,
     attn_in_out, expert_in_out, gated_out, attended_out, pre_out) = take(13)
    if swap:
        other = take(7)
    scratch = take(4)
    joint_s, output_s, gu_s, down_s = scratch
    (ag1, ag2, part, landing1, landing2, pre_s, gated_s, attended_s, send_s, recv_s, attn_sems,
     expert_sems, pre_sems, save_sems) = refs[:14]
    swap_sems = refs[14:]
    rows, width = stream.shape
    tokens = ag1.shape[0]
    experts = gu_s.shape[0]
    hidden_width = gu_s.shape[2] // 2
    kw = keys_out.shape[1]
    qw = attended_s.shape[1]
    heads, key_heads = qw // HD, kw // HD
    group = heads // key_heads
    me = lax.axis_index("tensor")
    own_rows = pl.ds(pl.multiple_of(me * rows, rows), rows)
    use_own = lax.axis_index("section") == layer

    def start_attn(w):
        for copy in attn_copies(w[:4], scratch[:2], attn_sems):
            copy.start()

    def wait_attn(w):
        for copy in attn_copies(w[:4], scratch[:2], attn_sems):
            copy.wait()

    def start_expert(w, expert):
        for copy in weight_copies(w[4:], scratch[2:], expert_sems, expert):
            copy.start()

    def wait_expert(w, expert):
        for copy in weight_copies(w[4:], scratch[2:], expert_sems, expert):
            copy.wait()

    def each_expert(run):
        def step(expert, carry):
            run(expert)
            return carry

        lax.fori_loop(0, experts, step, 0)

    def swap_expert(expert):
        return [swap_copies(own, other, swap_sems, (name, expert)) for name in (4, 5, 6)]

    value = stream[...].astype(bf16).astype(f32)
    ag1[own_rows, :] = (value * norm_scale(value) * attn_gain[...]).astype(bf16)
    greet(tensor_peers(count) + ([core_peer()] if swap else []))
    first = spread(count, ag1, rows, send_s.at[0], recv_s.at[0])
    if swap:
        lead = min(2, experts)
        for piece in range(4):
            swap_copies(own, other, swap_sems, piece).start()
        each_expert(lambda expert: [c.start() for c in swap_expert(expert)] and None)

        @pl.when(use_own)
        def _():
            start_all(first)
            start_attn(own)
            each_expert(lambda expert: start_expert(own, expert))

        @pl.when(jnp.logical_not(use_own))
        def _():
            for piece in range(4):
                swap_copies(own, other, swap_sems, piece).wait_recv()
            start_attn(other)
            for expert in range(lead):
                for copy in swap_expert(expert):
                    copy.wait_recv()
                start_expert(other, expert)
            start_all(first)
    else:
        start_all(first)
        either(use_own, own, other, start_attn)
        either(use_own, own, other, lambda w: each_expert(lambda expert: start_expert(w, expert)))
    wait_all(first)
    saved = [pltpu.make_async_copy(ag1, attn_in_out, save_sems.at[0])]
    saved[0].start()
    either(use_own, own, other, wait_attn)
    proj = dot(ag1[...], joint_s[...], NN)
    for chunk in range(qw // 128):
        block = proj[:, chunk * 128 : chunk * 128 + 128]
        block = (block * cosine[...] + turned(block) * sine[...]).astype(bf16)
        for part_index in range(128 // HD):
            head = chunk * (128 // HD) + part_index
            qs_out[pl.ds(head * tokens, tokens), :] = block[:, part_index * HD : part_index * HD + HD]
    for chunk in range(kw // 128):
        block = proj[:, qw + chunk * 128 : qw + chunk * 128 + 128]
        keys_out[:, pl.ds(chunk * 128, 128)] = (
            block * cosine[...] + turned(block) * sine[...]
        ).astype(bf16)
    values_out[...] = proj[:, qw + kw :].astype(bf16)
    for g in range(key_heads):
        lanes = pl.ds(g * HD, HD)
        span = pl.ds(g * group * tokens, group * tokens)
        scores = dot(qs_out[span, :], keys_out[:, lanes], NT) * 0.125
        scores = (scores.reshape(group, tokens, tokens) + bias[...][None]).reshape(
            group * tokens, tokens
        )
        top = jnp.max(scores, axis=1, keepdims=True)
        weighed = jnp.exp(scores - top)
        probs = (weighed / jnp.sum(weighed, axis=1, keepdims=True)).astype(bf16)
        probs_out[span, :] = probs
        attended = dot(probs, values_out[:, lanes], NN).astype(bf16)
        for h in range(group):
            attended_s[:, pl.ds((g * group + h) * HD, HD)] = attended[h * tokens : (h + 1) * tokens]
    saved.append(pltpu.make_async_copy(attended_s, attended_out, save_sems.at[1]))
    saved[1].start()
    part[...] = dot(attended_s[...], output_s[...], NN).astype(bf16)
    dealt = deal_out(count, part, rows, slice(None), landing1, send_s.at[1], recv_s.at[1])
    wait_all(dealt)
    mid = value + part[own_rows, :].astype(f32)
    for step in range(count - 1):
        mid = mid + landing1[step].astype(f32)
    mid_out[...] = mid
    expert_rows = (mid * norm_scale(mid) * expert_gain[...]).astype(bf16)
    expert_rows_out[...] = expert_rows
    ag2[own_rows, :] = expert_rows
    second = spread(count, ag2, rows, send_s.at[2], recv_s.at[2])
    start_all(second)
    wait_all(second)
    saved.append(pltpu.make_async_copy(ag2, expert_in_out, save_sems.at[2]))
    saved[2].start()
    logits = dot(ag2[...], router[...], NN)
    chosen = picked[...] > 0
    top = jnp.max(jnp.where(chosen, logits, masked_score), axis=1, keepdims=True)
    weighed = jnp.where(chosen, jnp.exp(logits - top), 0.0)
    gate_out[...] = weighed / jnp.sum(weighed, axis=1, keepdims=True)

    def expert_step(expert, carry):
        if swap:

            @pl.when(jnp.logical_not(use_own) & (expert + lead < experts))
            def _():
                for copy in swap_expert(expert + lead):
                    copy.wait_recv()
                start_expert(other, expert + lead)

        either(use_own, own, other, lambda w: wait_expert(w, expert))
        pre = dot(ag2[...], gu_s[expert], NN)
        pre_s[expert] = pre
        pltpu.make_async_copy(pre_s.at[expert], pre_out.at[expert], pre_sems.at[expert]).start()
        gate_pre, up_pre = pre[:, :hidden_width], pre[:, hidden_width:]
        hidden = (gate_pre / (1.0 + jnp.exp(-gate_pre)) * up_pre).astype(bf16).astype(f32)
        weight = column(gate_out[...] * kept[...], expert)
        gated_s[:, pl.ds(pl.multiple_of(expert * hidden_width, hidden_width), hidden_width)] = (
            hidden * weight
        ).astype(bf16)
        return carry

    lax.fori_loop(0, experts, expert_step, 0)
    saved.append(pltpu.make_async_copy(gated_s, gated_out, save_sems.at[3]))
    saved[3].start()
    copies = []
    tile = width // 4
    for t in range(4):
        columns = pl.ds(t * tile, tile)
        part[:, columns] = dot(gated_s[...], down_s[:, columns], NN).astype(bf16)
        copies += deal_out(count, part, rows, columns, landing2, send_s.at[3 + t], recv_s.at[3 + t])
    wait_all(copies)
    total = mid_out[...] + part[own_rows, :].astype(f32)
    for step in range(count - 1):
        total = total + landing2[step].astype(f32)
    out[...] = total
    wait_all(saved)
    if swap:
        for piece in range(4):
            swap_copies(own, other, swap_sems, piece).wait_send()
        each_expert(lambda expert: [c.wait_send() for c in swap_expert(expert)] and None)

        @pl.when(use_own)
        def _():
            for piece in range(4):
                swap_copies(own, other, swap_sems, piece).wait_recv()
            each_expert(lambda expert: [c.wait_recv() for c in swap_expert(expert)] and None)

    def finish(expert, carry):
        pltpu.make_async_copy(pre_s.at[expert], pre_out.at[expert], pre_sems.at[expert]).wait()
        return carry

    lax.fori_loop(0, experts, finish, 0)


def weight_scratch(own):
    query, key, value, output, gate, up, down = own
    depth = query.shape[0]
    experts, _, hidden_width = gate.shape
    return [
        pltpu.VMEM((depth, query.shape[1] + 2 * key.shape[1]), bf16),
        pltpu.VMEM(output.shape, bf16),
        pltpu.VMEM((experts, depth, 2 * hidden_width), bf16),
        pltpu.VMEM((experts * hidden_width, depth), bf16),
    ]


def layer_forward(layer, gains, own, other, stream, tables, masks):
    count = lax.axis_size("tensor")
    rows, width = stream.shape[-2:]
    tokens = tables[2].shape[0]
    qw, kw = own[0].shape[1], own[1].shape[1]
    experts, _, hidden_width = own[4].shape
    heads = qw // HD
    swap = other is None
    vmem = pl.BlockSpec(memory_space=pltpu.VMEM)
    hbm = pl.BlockSpec(memory_space=pl.ANY)
    shape = jax.ShapeDtypeStruct
    pieces = 4 + 3 * experts
    found = pl.pallas_call(
        functools.partial(forward_kernel, layer, count, swap),
        name=f"layer_forward_{layer}",
        out_shape=(
            shape((rows, width), f32),
            shape((rows, width), f32),
            shape((rows, width), bf16),
            shape((heads * tokens, HD), bf16),
            shape((tokens, kw), bf16),
            shape((tokens, kw), bf16),
            shape((heads * tokens, tokens), bf16),
            shape((tokens, experts), f32),
            shape((tokens, width), bf16),
            shape((tokens, width), bf16),
            shape((tokens, experts * hidden_width), bf16),
            shape((tokens, qw), bf16),
            shape((experts, tokens, 2 * hidden_width), f32),
        )
        + (tuple(shape(w.shape, w.dtype) for w in own) if swap else ()),
        in_specs=[vmem] * 9 + [hbm] * (7 if swap else 14),
        out_specs=(vmem,) * 8 + (hbm,) * (12 if swap else 5),
        scratch_shapes=weight_scratch(own)
        + [
            pltpu.VMEM((tokens, width), bf16),
            pltpu.VMEM((tokens, width), bf16),
            pltpu.VMEM((tokens, width), bf16),
            pltpu.VMEM((count - 1, rows, width), bf16),
            pltpu.VMEM((count - 1, rows, width), bf16),
            pltpu.VMEM((experts, tokens, 2 * hidden_width), f32),
            pltpu.VMEM((tokens, experts * hidden_width), bf16),
            pltpu.VMEM((tokens, qw), bf16),
            dma((7, count - 1)),
            dma((7, count - 1)),
            dma((4,)),
            dma((3, experts)),
            dma((experts,)),
            dma((4,)),
        ]
        + ([dma((pieces,)), dma((pieces,))] if swap else []),
        compiler_params=params(1 + layer),
    )(stream, *gains, *tables, *masks, *own,
      *(() if swap else other))
    return found[:13], found[13:]


def norm_back(value, gain, out_grad):
    scale = norm_scale(value)
    scaled = value * scale
    gain_grad = jnp.sum(out_grad * scaled, axis=0, keepdims=True)
    inner = out_grad * gain
    value_grad = scale * (inner - scaled * jnp.mean(inner * scaled, axis=-1, keepdims=True))
    return value_grad, gain_grad


def experts_back_kernel(layer, count, trade, beside, *refs):
    refs = list(refs)

    def take(number):
        taken = refs[:number]
        del refs[:number]
        return taken

    out_grad_in, mid, expert_gains, routers, kepts, gate, expert_rows, pre_in = take(8)
    expert_gain, router, kept = expert_gains.at[layer], routers.at[layer], kepts.at[layer]
    out_grad = out_grad_in if layer == 0 else out_grad_in.at[lax.axis_index("section")]
    x_in, gated_in = take(2)
    own, other = take(3), take(3)
    traded = take(2 if trade else 0)
    beside_in = take(len(beside.inputs))
    mid_grad_out, router_out, expert_gain_out, pair_out, down_out = take(5)
    traded_out = take(1 if trade else 0)
    beside_out = take(len(beside.outputs))
    scratch = take(2)
    gu_s, down_s = scratch
    (ag1, part, landing1, pre_s, gpu_s, acc, gate_part, gate_land, og_s, gpu_peer, x_s, turned_x,
     gated_s, turned_gated, pair_s, down_grad_s, send_s, recv_s, expert_sems, pre_sems, core_send,
     core_recv, local_sems, hand_send, hand_recv, save_sems) = take(26)
    trade_sems = take(len(trade.sems) if trade else 0)
    beside_refs = (beside_in, beside_out, refs)
    rows, width = mid.shape
    experts = gu_s.shape[0]
    hidden_width = gu_s.shape[2] // 2
    me = lax.axis_index("tensor")
    own_rows = pl.ds(pl.multiple_of(me * rows, rows), rows)
    use_own = lax.axis_index("section") == layer

    def start_expert(expert, carry):
        either(use_own, own, other,
               lambda w: [c.start() for c in weight_copies(w, scratch, expert_sems, expert)])
        pltpu.make_async_copy(pre_in.at[expert], pre_s.at[expert], pre_sems.at[expert]).start()
        return carry

    ag1[own_rows, :] = out_grad[...].astype(bf16)
    greet(tensor_peers(count) + [core_peer()] + beside.peers())
    first = spread(count, ag1, rows, send_s.at[0], recv_s.at[0])
    start_all(first)
    lax.fori_loop(0, experts, start_expert, 0)
    loads = hand_halves(x_in, x_s, [v.at[0] for v in (local_sems, hand_send, hand_recv)])
    loads += hand_rows(gated_in, gated_s, [v.at[1] for v in (local_sems, hand_send, hand_recv)])
    for copy in loads:
        copy.start()
    beside.start(*beside_refs)
    if trade:
        trade.start(*traded, trade_sems)
    gate_part[...] = jnp.zeros_like(gate_part)
    wait_all(loads)
    turned_x[...] = x_s[...].T
    tokens = ag1.shape[0]

    def turn_gated(expert, carry):
        lanes = pl.ds(pl.multiple_of(expert * hidden_width, hidden_width), hidden_width)
        turned_gated[lanes, :] = gated_s[:, lanes].T
        return carry

    lax.fori_loop(0, experts, turn_gated, 0)
    wait_all(first)
    core = lax.axis_index("section")
    half = width // 2
    og_s[pl.ds(0, tokens), :] = ag1[:, pl.ds(pl.multiple_of(core * half, half), half)]
    handed = [
        remote(ag1.at[:, pl.ds(pl.multiple_of((1 - core) * half, half), half)],
               og_s.at[pl.ds(tokens, tokens)], core_send.at[0], core_recv.at[0], core_peer())
    ]
    handed[0].start()

    def expert_step(expert, carry):
        either(use_own, own, other,
               lambda w: [c.wait() for c in weight_copies(w, scratch, expert_sems, expert)])
        pltpu.make_async_copy(pre_in.at[expert], pre_s.at[expert], pre_sems.at[expert]).wait()
        lanes = pl.ds(pl.multiple_of(expert * hidden_width, hidden_width), hidden_width)
        plain = dot(ag1[...], down_s[lanes, :], NT)
        gate_pre = pre_s[expert, :, pl.ds(0, hidden_width)]
        up_pre = pre_s[expert, :, pl.ds(hidden_width, hidden_width)]
        sig = 1.0 / (1.0 + jnp.exp(-gate_pre))
        act = gate_pre * sig
        hidden = (act * up_pre).astype(bf16).astype(f32)
        held = column(kept[...], expert)
        weight = column(gate[...], expert) * held
        summed = jnp.sum(hidden * plain, axis=1, keepdims=True) * held
        lane = lax.broadcasted_iota(jnp.int32, gate_part.shape, 1)
        gate_part[...] += jnp.where(lane == expert, summed, 0.0)
        hidden_grad = plain * weight
        gpu_s[expert, :, pl.ds(0, hidden_width)] = (
            hidden_grad * up_pre * (sig * (1.0 + gate_pre * (1.0 - sig)))
        ).astype(bf16)
        gpu_s[expert, :, pl.ds(hidden_width, hidden_width)] = (hidden_grad * act).astype(bf16)
        back = dot(gpu_s[expert], gu_s[expert], NT)

        @pl.when(expert == 0)
        def _():
            acc[...] = back

        @pl.when(expert > 0)
        def _():
            acc[...] += back

        return carry

    lax.fori_loop(0, experts, expert_step, 0)
    handed.append(remote(gpu_s, gpu_peer, core_send.at[1], core_recv.at[1], core_peer()))
    handed[1].start()
    part[...] = acc[...].astype(bf16)
    copies = deal_out(count, part, rows, slice(None), landing1, send_s.at[1], recv_s.at[1])
    copies += deal_out(count, gate_part, rows, slice(None), gate_land, send_s.at[2], recv_s.at[2])
    wait_all(handed)

    def saves(expert):
        lanes = pl.ds(pl.multiple_of(expert * hidden_width, hidden_width), hidden_width)
        return (
            pltpu.make_async_copy(pair_s.at[expert], pair_out.at[expert], save_sems.at[0, expert]),
            pltpu.make_async_copy(down_grad_s.at[lanes], down_out.at[expert], save_sems.at[1, expert]),
        )

    def grads_step(expert, carry):
        lanes = pl.ds(pl.multiple_of(expert * hidden_width, hidden_width), hidden_width)
        pair_s[expert] = (
            dot(turned_x[:, :tokens], gpu_s[expert], NN)
            + dot(turned_x[:, tokens:], gpu_peer[expert], NN)
        ).astype(bf16)
        down_grad_s[lanes, :] = dot(turned_gated[lanes, :], og_s[...], NN).astype(bf16)
        for copy in saves(expert):
            copy.start()
        return carry

    lax.fori_loop(0, experts, grads_step, 0)
    beside.middle(*beside_refs)
    wait_all(copies)
    in_grad = acc[own_rows, :]
    gate_grad = gate_part[own_rows, :]
    for step in range(count - 1):
        in_grad = in_grad + landing1[step].astype(f32)
        gate_grad = gate_grad + gate_land[step]
    gate_grad = gate_grad[:, :experts]
    gate_rows = gate[own_rows, :]
    logits_grad = (
        gate_rows * (gate_grad - jnp.sum(gate_rows * gate_grad, axis=1, keepdims=True))
    ).astype(bf16)
    router_out[...] = dot(logits_grad, expert_rows[...], TN)
    in_grad = in_grad + dot(logits_grad, router[...], NT)
    mid_part, expert_gain_grad = norm_back(mid[...], expert_gain[...], in_grad)
    expert_gain_out[...] = expert_gain_grad
    mid_grad_out[...] = ag1[own_rows, :].astype(f32) + mid_part

    def finish_save(expert, carry):
        for copy in saves(expert):
            copy.wait()
        return carry

    lax.fori_loop(0, experts, finish_save, 0)
    if trade:
        trade.wait(traded[0], traded_out[0], trade_sems)
    beside.wait(*beside_refs)


def experts_back(layer, gains, own, other, out_grad, state, pairs, masks, traded, beside):
    count = lax.axis_size("tensor")
    mid, gate, expert_rows, pre = state
    rows, width = mid.shape
    tokens = gate.shape[0]
    own, other = own[4:], other[4:]
    trade = Trade((rows, width)) if traded else None
    experts, depth, hidden_width = own[0].shape
    vmem = pl.BlockSpec(memory_space=pltpu.VMEM)
    hbm = pl.BlockSpec(memory_space=pl.ANY)
    shape = jax.ShapeDtypeStruct
    found = pl.pallas_call(
        functools.partial(experts_back_kernel, layer, count, trade, beside),
        name=f"experts_back_{layer}",
        out_shape=(
            shape((rows, width), f32),
            shape((experts, width), f32),
            shape((1, width), f32),
            shape((experts, width // 2, 2 * hidden_width), bf16),
            shape((experts, hidden_width, width // 2), bf16),
            *((shape((2, rows, width), f32),) if traded else ()),
            *beside.outputs,
        ),
        in_specs=[vmem] * 7 + [hbm] * 9 + [vmem] * len(traded) + [hbm] * len(beside.inputs),
        out_specs=(vmem, vmem, vmem, hbm, hbm) + (vmem,) * bool(traded) + (hbm,) * len(beside.outputs),
        scratch_shapes=[
            pltpu.VMEM((experts, depth, 2 * hidden_width), bf16),
            pltpu.VMEM((experts * hidden_width, depth), bf16),
            pltpu.VMEM((tokens, width), bf16),
            pltpu.VMEM((tokens, width), bf16),
            pltpu.VMEM((count - 1, rows, width), bf16),
            pltpu.VMEM((experts, tokens, 2 * hidden_width), f32),
            pltpu.VMEM((experts, tokens, 2 * hidden_width), bf16),
            pltpu.VMEM((tokens, width), f32),
            pltpu.VMEM((tokens, 128), f32),
            pltpu.VMEM((count - 1, rows, 128), f32),
            pltpu.VMEM((2 * tokens, width // 2), bf16),
            pltpu.VMEM((experts, tokens, 2 * hidden_width), bf16),
            pltpu.VMEM((2 * tokens, width // 2), bf16),
            pltpu.VMEM((width // 2, 2 * tokens), bf16),
            pltpu.VMEM((2 * tokens, experts * hidden_width), bf16),
            pltpu.VMEM((experts * hidden_width, 2 * tokens), bf16),
            pltpu.VMEM((experts, width // 2, 2 * hidden_width), bf16),
            pltpu.VMEM((experts * hidden_width, width // 2), bf16),
            pltpu.SemaphoreType.DMA((3, count - 1)),
            pltpu.SemaphoreType.DMA((3, count - 1)),
            pltpu.SemaphoreType.DMA((3, experts)),
            pltpu.SemaphoreType.DMA((experts,)),
            *[pltpu.SemaphoreType.DMA((2,)) for _ in range(5)],
            pltpu.SemaphoreType.DMA((2, experts)),
            *(trade.sems if trade else ()),
            *beside.sems,
        ],
        compiler_params=params(3 + layer),
    )(out_grad, mid, *gains[1:], masks[1], gate, expert_rows, pre, *pairs, *own, *other,
      *traded, *beside.inputs)
    kept = 6 if traded else 5
    return found[:kept], beside.results(found[kept:])


def attention_back_kernel(layer, count, last, beside, *refs):
    refs = list(refs)

    def take(number):
        taken = refs[:number]
        del refs[:number]
        return taken

    mid_grad, stream_in, attn_gains, cosine, sine, qs, keys, values, probs = take(9)
    attn_gain = attn_gains.at[layer]
    stream = stream_in.at[lax.axis_index("section")] if layer == 0 else stream_in
    ai_in, attended_in = take(2)
    own, other = take(4), take(4)
    small_parts = take(5 if last else 0)
    later_grad = take(1 if last else 0)
    beside_in = take(len(beside.inputs))
    if last:
        dense_sum, small_sum, trade = last
        traded_out, small_out, whole_out = take(3)
    else:
        grad_out, attn_gain_out, dense_out = take(3)
    beside_out = take(len(beside.outputs))
    scratch = take(2)
    joint_s, output_s = scratch
    (ag2, part, landing2, ag_stack, dq_s, joint_rows, joint_peer, ao_s, ai_s, turned_ai, attended_s,
     dense_s, send_s, recv_s, attn_sems, core_send, core_recv, local_sems,
     hand_send, hand_recv) = take(20)
    if last:
        grad_s, trade_sems = refs.pop(0), take(len(trade.sems))
        dense_sems, small_sems = take(len(dense_sum.sems)), take(len(small_sum.sems))
        dense_refs = ([dense_s], [whole_out], dense_sems)
    beside_refs = (beside_in, beside_out, refs)
    rows, width = stream.shape
    tokens = ag2.shape[0]
    kw = keys.shape[1]
    qw = output_s.shape[0]
    heads, key_heads = qw // HD, kw // HD
    group = heads // key_heads
    me = lax.axis_index("tensor")
    own_rows = pl.ds(pl.multiple_of(me * rows, rows), rows)
    use_own = lax.axis_index("section") == layer
    ag2[own_rows, :] = mid_grad[...].astype(bf16)
    everyone = Beside([*beside.jobs, dense_sum]) if last else beside
    greet(tensor_peers(count) + [core_peer()] + everyone.peers())
    first = spread(count, ag2, rows, send_s.at[0], recv_s.at[0])
    start_all(first)
    either(use_own, own, other, lambda w: [c.start() for c in attn_copies(w, scratch, attn_sems)])
    loads = hand_halves(ai_in, ai_s, [v.at[0] for v in (local_sems, hand_send, hand_recv)])
    loads += hand_rows(attended_in, attended_s, [v.at[1] for v in (local_sems, hand_send, hand_recv)])
    for copy in loads:
        copy.start()
    beside.start(*beside_refs)
    wait_all(loads)
    turned_ai[...] = ai_s[...].T
    wait_all(first)
    core = lax.axis_index("section")
    half = width // 2
    ao_s[pl.ds(0, tokens), :] = ag2[:, pl.ds(pl.multiple_of(core * half, half), half)]
    handed = [
        remote(ag2.at[:, pl.ds(pl.multiple_of((1 - core) * half, half), half)],
               ao_s.at[pl.ds(tokens, tokens)], core_send.at[0], core_recv.at[0], core_peer())
    ]
    handed[0].start()
    either(use_own, own, other, lambda w: [c.wait() for c in attn_copies(w, scratch, attn_sems)])
    attended_grad = dot(ag2[...], output_s[...], NT).astype(bf16)
    for h in range(heads):
        ag_stack[pl.ds(h * tokens, tokens), :] = attended_grad[:, h * HD : (h + 1) * HD]
    for g in range(key_heads):
        lanes = pl.ds(g * HD, HD)
        span = pl.ds(g * group * tokens, group * tokens)
        soft_b = probs[span, :]
        soft = soft_b.astype(f32)
        soft_grad = dot(ag_stack[span, :], values[:, lanes], NT)
        inner = jnp.sum(soft * soft_grad, axis=1, keepdims=True)
        score_grad = (soft * (soft_grad - inner)).astype(bf16)
        dq = dot(score_grad, keys[:, lanes], NN) * 0.125
        for h in range(group):
            dq_s[:, pl.ds((g * group + h) * HD, HD)] = dq[h * tokens : (h + 1) * tokens]
        dq_s[:, pl.ds(qw + g * HD, HD)] = dot(score_grad, qs[span, :], TN) * 0.125
        joint_rows[:, pl.ds(qw + kw + g * HD, HD)] = dot(soft_b, ag_stack[span, :], TN).astype(bf16)
    for chunk in range((qw + kw) // 128):
        lanes = pl.ds(chunk * 128, 128)
        block = dq_s[:, lanes]
        joint_rows[:, lanes] = (block * cosine[...] - turned(block) * sine[...]).astype(bf16)
    handed.append(remote(joint_rows, joint_peer, core_send.at[1], core_recv.at[1], core_peer()))
    handed[1].start()
    copies = []
    tile = width // 2
    for t in range(2):
        columns = pl.ds(t * tile, tile)
        part[:, columns] = dot(joint_rows[...], joint_s[columns, :], NT).astype(bf16)
        copies += deal_out(count, part, rows, columns, landing2, send_s.at[1 + t], recv_s.at[1 + t])
    wait_all(handed)
    wide = qw + 2 * kw
    dense_s[:, :wide] = (
        dot(turned_ai[:, :tokens], joint_rows[...], NN) + dot(turned_ai[:, tokens:], joint_peer[...], NN)
    ).astype(bf16)
    dense_s[:, wide:] = dot(ao_s[...], attended_s[...], TN).astype(bf16)
    if last:
        dense_sum.start(*dense_refs)
    else:
        save = pltpu.make_async_copy(dense_s, dense_out, local_sems.at[0])
        save.start()
    wait_all(copies)
    in_grad = part[own_rows, :].astype(f32)
    for step in range(count - 1):
        in_grad = in_grad + landing2[step].astype(f32)
    stream_part, attn_gain_grad = norm_back(
        stream[...].astype(bf16).astype(f32), attn_gain[...], in_grad
    )
    grad = mid_grad[...] + stream_part
    if not last:
        attn_gain_out[...] = attn_gain_grad
        grad_out[...] = grad
        save.wait()
        beside.middle(*beside_refs)
        beside.wait(*beside_refs)
        return
    small = small_sems[0]
    router0, gain0, router1, attn_gain1, gain1 = small_parts
    place = 0
    for value in (router0[...], attn_gain_grad, gain0[...]):
        small[pl.ds(place, value.shape[0]), :] = value
        place += value.shape[0]
    place = small.shape[0] // 2
    for value in (router1[...], attn_gain1[...], gain1[...]):
        small[pl.ds(place, value.shape[0]), :] = value
        place += value.shape[0]
    small_sum.first(small_sems)
    grad_s[...] = grad
    trade.start(grad_s, later_grad[0], trade_sems)
    beside.middle(*beside_refs)
    small_sum.second(small_sems)
    dense_sum.middle(*dense_refs)
    small_sum.third(small_sems)
    trade.wait(grad_s, traded_out, trade_sems)
    small_sum.last(small_sems, small_out)
    dense_sum.wait(*dense_refs)
    beside.wait(*beside_refs)


def attention_back(layer, gains, own, other, mid_grad, stream, state, pairs, tables, ending, beside):
    count = lax.axis_size("tensor")
    qs, keys, values, probs = state
    rows, width = mid_grad.shape
    tokens = keys.shape[0]
    own, other = own[:4], other[:4]
    qw, kw = own[0].shape[1], own[1].shape[1]
    heads = qw // HD
    vmem = pl.BlockSpec(memory_space=pltpu.VMEM)
    hbm = pl.BlockSpec(memory_space=pl.ANY)
    shape = jax.ShapeDtypeStruct
    dense = shape((width // 2, 2 * qw + 2 * kw), bf16)
    if ending:
        depth = 2 * (-(-(ending[0].shape[0] + 2) // 8) * 8)
        last = (DenseSum(dense, layer), SmallSum(depth, width), Trade((rows, width)))
        own_outs = (shape((2, rows, width), f32), shape((depth, width), f32), *last[0].outputs)
        more = [pltpu.VMEM((rows, width), f32), *last[2].sems, *last[0].sems, *last[1].sems]
    else:
        last, more = None, []
        own_outs = (shape((rows, width), f32), shape((1, width), f32), dense)
    found = pl.pallas_call(
        functools.partial(attention_back_kernel, layer, count, last, beside),
        name=f"attention_back_{layer}",
        out_shape=(*own_outs, *beside.outputs),
        in_specs=[vmem] * 9 + [hbm] * 10 + [vmem] * len(ending) + [hbm] * len(beside.inputs),
        out_specs=(vmem, vmem, hbm) + (hbm,) * len(beside.outputs),
        scratch_shapes=[
            pltpu.VMEM((width, qw + 2 * kw), bf16),
            pltpu.VMEM((qw, width), bf16),
            pltpu.VMEM((tokens, width), bf16),
            pltpu.VMEM((tokens, width), bf16),
            pltpu.VMEM((count - 1, rows, width), bf16),
            pltpu.VMEM((heads * tokens, HD), bf16),
            pltpu.VMEM((tokens, qw + kw), f32),
            pltpu.VMEM((tokens, qw + 2 * kw), bf16),
            pltpu.VMEM((tokens, qw + 2 * kw), bf16),
            pltpu.VMEM((2 * tokens, width // 2), bf16),
            pltpu.VMEM((2 * tokens, width // 2), bf16),
            pltpu.VMEM((width // 2, 2 * tokens), bf16),
            pltpu.VMEM((2 * tokens, qw), bf16),
            pltpu.VMEM((width // 2, 2 * qw + 2 * kw), bf16),
            pltpu.SemaphoreType.DMA((3, count - 1)),
            pltpu.SemaphoreType.DMA((3, count - 1)),
            pltpu.SemaphoreType.DMA((4,)),
            *[pltpu.SemaphoreType.DMA((2,)) for _ in range(5)],
            *more,
            *beside.sems,
        ],
        compiler_params=params(5 + layer),
    )(mid_grad, stream, gains[0], *tables[:2], qs, keys, values, probs, *pairs, *own, *other,
      *ending, *beside.inputs)
    return found[:3], beside.results(found[3:])


def prepare_kernel(lengths, dealing, order, routes, attn_gain, expert_gain, router, freqs,
                   cosine, sine, bias, picked, kept, attn_gains, expert_gains, routers,
                   order_peer, routes_peer, sends, recvs):
    core = lax.axis_index("section")
    attn_gains[core] = attn_gain[...]
    expert_gains[core] = expert_gain[...]
    routers[core] = router[...]
    greet([core_peer()])
    copies = [
        remote(source, target, sends.at[index], recvs.at[index], core_peer())
        for index, (source, target) in enumerate((
            (order.at[1 - core], order_peer),
            (routes.at[1 - core], routes_peer),
            (attn_gain, attn_gains.at[core]),
            (expert_gain, expert_gains.at[core]),
            (router, routers.at[core]),
        ))
    ]
    start_all(copies)
    tokens = bias.shape[0]
    sequences = lengths.shape[1]
    tall = lax.broadcasted_iota(jnp.int32, (tokens, 1), 0)
    wide = lax.broadcasted_iota(jnp.int32, (1, tokens), 1)
    sizes = [lengths[core, index] for index in range(sequences)]
    starts = [sum(sizes[:index], 0) for index in range(sequences)]
    ranks = [
        sum(jnp.where(dealing[core, place] == index, place, 0) for place in range(sequences))
        for index in range(sequences)
    ]
    dealt_starts = [
        sum(jnp.where(ranks[before] < ranks[index], sizes[before], 0) for before in range(sequences))
        for index in range(sequences)
    ]

    def places(token):
        segment = sum((token >= starts[index] + sizes[index]).astype(jnp.int32)
                      for index in range(sequences))
        position, dealt = token, token
        for index in range(sequences):
            inside = segment == index
            position = jnp.where(inside, token - starts[index], position)
            dealt = jnp.where(inside, token - starts[index] + dealt_starts[index], dealt)
        return segment, position, dealt

    segment, position, dealt = places(tall)
    segment_wide, _, dealt_wide = places(wide)
    allowed = (segment == segment_wide) & (wide <= tall)
    bias[...] = jnp.where(allowed, 0.0, masked_score).astype(f32)
    angles = position.astype(f32) * freqs[...]
    cosine[...] = jnp.cos(angles)
    lane = lax.broadcasted_iota(jnp.int32, (1, freqs.shape[1]), 1)
    sine[...] = jnp.sin(angles) * jnp.where(lane % HD < HD // 2, -1.0, 1.0)

    def masks(order_row, route_rows):
        order_wide = order_row.astype(f32)
        order_tall = jnp.sum(jnp.where(tall == wide, order_wide, 0.0), axis=1, keepdims=True)
        first = jnp.sum(jnp.where(dealt == wide, order_wide, 0.0), axis=1, keepdims=True)
        first_wide = jnp.sum(jnp.where(dealt_wide == tall, order_tall, 0.0), axis=0, keepdims=True)
        earlier = jnp.where(first_wide < first, 1.0, 0.0).astype(bf16)
        experts = picked.shape[2]
        index = lax.broadcasted_iota(jnp.int32, (tokens, experts), 1)
        chosen = jnp.zeros((tokens, experts), f32)
        for k in range(route_rows.shape[1]):
            chosen = jnp.where(route_rows[:, k : k + 1] == index, 1.0, chosen)
        rank = dot(earlier, chosen.astype(bf16), NN)
        return chosen, jnp.where(rank < CAP, chosen, 0.0)

    picked[core], kept[core] = masks(order[core], routes[core])
    wait_all(copies)
    picked[1 - core], kept[1 - core] = masks(order_peer[...], routes_peer[...])


def prepare(lengths, dealing, order, routes, attn_gain, expert_gain, router):
    tokens = order.shape[2]
    width = attn_gain.shape[1]
    half = HD // 2
    freqs = jnp.tile(rope_base ** (-2.0 * jnp.arange(half, dtype=f32) / HD), 128 // half)[None]
    vmem = pl.BlockSpec(memory_space=pltpu.VMEM)
    smem = pl.BlockSpec(memory_space=pltpu.SMEM)
    shape = jax.ShapeDtypeStruct
    found = pl.pallas_call(
        prepare_kernel,
        name="prepare",
        out_shape=(
            shape((tokens, 128), f32),
            shape((tokens, 128), f32),
            shape((tokens, tokens), f32),
            shape((2, tokens, E), f32),
            shape((2, tokens, E), f32),
            shape((2, 1, width), f32),
            shape((2, 1, width), f32),
            shape((2, *router.shape), bf16),
        ),
        in_specs=[smem] * 2 + [vmem] * 6,
        out_specs=(vmem,) * 8,
        scratch_shapes=[
            pltpu.VMEM(order.shape[1:], order.dtype),
            pltpu.VMEM(routes.shape[1:], routes.dtype),
            dma((5,)),
            dma((5,)),
        ],
        compiler_params=params(8),
    )(lengths, dealing, order, routes, attn_gain, expert_gain, router, freqs)
    return found[:3], found[3:5], found[5:]


def assemble_kernel(section, *refs):
    expert_refs, dense_refs, outs = (refs[:4], refs[4:8]), refs[8:10], refs[10:]
    query, key, value, output, gate, up, down = outs
    hidden_width = gate.shape[2]
    qw, kw = query.shape[1], key.shape[1]

    def write(parts, dense):
        cores = range(2)
        pair = [[jnp.sum(v[core, :, 0].astype(f32), axis=0) for v in parts[:2]] for core in cores]
        depth = 0
        for block in pair[0] + pair[1]:
            rows = pl.ds(depth, block.shape[0])
            gate[0, rows, :] = block[:, :hidden_width]
            up[0, rows, :] = block[:, hidden_width:]
            depth += block.shape[0]
        depth = 0
        for core in cores:
            for v in parts[2:]:
                block = jnp.sum(v[core, :, 0].astype(f32), axis=0)
                down[0, :, pl.ds(depth, block.shape[1])] = block
                depth += block.shape[1]
        rows = dense[...].astype(f32)
        query[...] = rows[:, :qw]
        key[...] = rows[:, qw : qw + kw]
        value[...] = rows[:, qw + kw : qw + 2 * kw]
        output[...] = rows[:, qw + 2 * kw :].T

    pl.when(section[0] == 0)(lambda: write(expert_refs[0], dense_refs[0]))
    pl.when(section[0] == 1)(lambda: write(expert_refs[1], dense_refs[1]))


def assemble(parts, denses, qw, kw):
    groups = parts[0][0].shape[2]
    hidden_width = parts[0][2].shape[3]
    dense = [v.reshape(-1, v.shape[3]) for v in denses]
    depth = dense[0].shape[0]
    rows = depth // groups

    def part_spec(layer, shape):
        block = (*shape[:2], 1, *shape[3:])
        return pl.BlockSpec(block, lambda e, s: (0, 0, jnp.where(s[0] == layer, e, 0), 0, 0))

    def dense_spec(layer, width):
        return pl.BlockSpec((rows, width), lambda e, s: (jnp.where(s[0] == layer, e, 0), 0))

    shape = jax.ShapeDtypeStruct
    return pl.pallas_call(
        assemble_kernel,
        name="assemble",
        out_shape=(
            shape((depth, qw), f32),
            shape((depth, kw), f32),
            shape((depth, kw), f32),
            shape((qw, depth), f32),
            shape((groups, depth, hidden_width), f32),
            shape((groups, depth, hidden_width), f32),
            shape((groups, hidden_width, depth), f32),
        ),
        grid_spec=pltpu.PrefetchScalarGridSpec(
            num_scalar_prefetch=1,
            grid=(groups,),
            in_specs=[part_spec(layer, v.shape) for layer in range(2) for v in parts[layer]]
            + [dense_spec(layer, dense[layer].shape[1]) for layer in range(2)],
            out_specs=(
                pl.BlockSpec((rows, qw), lambda e, s: (e, 0)),
                pl.BlockSpec((rows, kw), lambda e, s: (e, 0)),
                pl.BlockSpec((rows, kw), lambda e, s: (e, 0)),
                pl.BlockSpec((qw, rows), lambda e, s: (0, e)),
                pl.BlockSpec((1, depth, hidden_width), lambda e, s: (e, 0, 0)),
                pl.BlockSpec((1, depth, hidden_width), lambda e, s: (e, 0, 0)),
                pl.BlockSpec((1, hidden_width, depth), lambda e, s: (e, 0, 0)),
            ),
        ),
        compiler_params=pltpu.CompilerParams(vmem_limit_bytes=48 * 2**20),
    )(lax.axis_index("section").astype(jnp.int32)[None], *parts[0], *parts[1], *dense)


def shards(
    tokens_in, out_cotangent, attn_gain, query_weight, key_weight, value_weight, output_weight,
    expert_gain, router_weight, gate_weight, up_weight, down_weight, lengths, dealing,
    slot_order, routes,
):
    first = lax.axis_index("section") == 0
    qw, kw = query_weight.shape[2], key_weight.shape[2]
    own = (query_weight[0], key_weight[0], value_weight[0], output_weight[0], gate_weight[0],
           up_weight[0], down_weight[0])
    tables, masks, gains = prepare(lengths[:, 0], dealing[:, 0], slot_order[0], routes[0], attn_gain,
                                   expert_gain, router_weight[0])
    (out0, *state0), other = layer_forward(0, gains, own, None, tokens_in, tables, masks)
    (out1, *state1), _ = layer_forward(1, gains, own, other, out0, tables, masks)
    saved = (state0, state1)
    streams = (tokens_in, out0)

    def experts(layer, out_grad, traded, jobs):
        mid, expert_rows, qs, keys, values, probs, gate, ai, x, gated, attended, pre = saved[layer]
        return experts_back(
            layer, gains, own, other, out_grad, (mid, gate, expert_rows, pre), (x, gated), masks,
            traded, Beside(jobs)
        )

    def attention(layer, mid_grad, ending, jobs):
        mid, expert_rows, qs, keys, values, probs, gate, ai, x, gated, attended, pre = saved[layer]
        return attention_back(
            layer, gains, own, other, mid_grad, streams[layer], (qs, keys, values, probs),
            (ai, attended), tables, ending, Beside(jobs)
        )

    (mid_grad, router1, gain1, pair, down, layer_outputs), _ = experts(1, out_cotangent, (out0, out1), [])
    (grad1, attn_gain1, dense1), sums = attention(
        1, mid_grad, (), [FirstStage(pair, 1), FirstStage(down, 2)]
    )
    jobs = [Bring(1, kind, v) for stage in sums for kind, v in zip(("column", "row"), stage)]
    (mid_grad, router0, gain0, pair, down), (*parts1, dense1) = experts(
        0, grad1, (), jobs + [DenseSum(dense1, 1)]
    )
    (input_grads, small, dense0), parts0 = attention(
        0, mid_grad, (router0, gain0, router1, attn_gain1, gain1, grad1),
        [FirstStage(pair, 1, 0), FirstStage(down, 2, 0)]
    )
    parts0 = [v for stage in parts0 for v in stage]
    query, key, value, output, gate, up, down = assemble((parts0, parts1), (dense0, dense1), qw, kw)
    small = jnp.where(first, small[: small.shape[0] // 2], small[small.shape[0] // 2 :])
    router_grad, attn_gain_grad, expert_gain_grad = small[:E].T, small[E : E + 1], small[E + 1 : E + 2]
    return (
        layer_outputs[None],
        input_grads[None],
        attn_gain_grad,
        query[None],
        key[None],
        value[None],
        output[None],
        expert_gain_grad,
        router_grad[None],
        gate[None],
        up[None],
        down[None],
    )


def solution(mesh):
    return jax.shard_map(
        shards,
        mesh=mesh,
        in_specs=(
            P(None, ("dp", "tensor"), None),
            P(None, ("dp", "tensor"), None),
            P("section", None),
            P("section", None, "tensor"),
            P("section", None, "tensor"),
            P("section", None, "tensor"),
            P("section", "tensor", None),
            P("section", None),
            P("section", None, None),
            P("section", None, None, "tensor"),
            P("section", None, None, "tensor"),
            P("section", None, "tensor", None),
            P(None, "dp", None),
            P(None, "dp", None),
            P("section", None, "dp", None),
            P("section", None, "dp", None),
        ),
        out_specs=(
            P("section", None, ("dp", "tensor"), None),
            P("section", None, ("dp", "tensor"), None),
            P("section", None),
            P("section", None, "tensor"),
            P("section", None, "tensor"),
            P("section", None, "tensor"),
            P("section", "tensor", None),
            P("section", None),
            P("section", None, None),
            P("section", "dp", None, "tensor"),
            P("section", "dp", None, "tensor"),
            P("section", "dp", "tensor", None),
        ),
        check_vma=False,
    )
```

```python
import functools
import math

import jax
import jax.numpy as jnp
from jax import lax
from jax.experimental import pallas as pl
from jax.experimental.pallas import tpu as pltpu
from jax.sharding import PartitionSpec as P

H = 24
KV = 8
HD = 64
E = 16
CAP = 160

epsilon = 1e-05
rope_base = 10000.0
masked_score = -1e30
bf16 = jnp.bfloat16
f32 = jnp.float32
MESH = pl.DeviceIdType.MESH


def dot(a, b, dims):
    return lax.dot_general(a, b, (dims, ((), ())), preferred_element_type=f32)


NN = ((1,), (0,))
NT = ((1,), (1,))
TN = ((0,), (0,))


def norm_scale(rows_in):
    return lax.rsqrt(jnp.mean(rows_in * rows_in, axis=-1, keepdims=True) + epsilon)


def params(collective_id):
    return pltpu.CompilerParams(
        collective_id=collective_id, has_side_effects=True, vmem_limit_bytes=56 * 2**20
    )


def tensor_peers(count):
    me = lax.axis_index("tensor")
    return [{"tensor": lax.rem(me + step, count)} for step in range(1, count)]


def greet(peers):
    barrier = pltpu.get_barrier_semaphore()
    for peer in peers:
        pl.semaphore_signal(barrier, inc=1, device_id=peer, device_id_type=MESH)
    pl.semaphore_wait(barrier, len(peers))


def factors(count):
    inner = math.isqrt(count)
    while count % inner:
        inner -= 1
    return count // inner, inner


def group_place(count):
    outer, inner = factors(count)
    me = lax.axis_index("dp")
    return outer, inner, me // inner, lax.rem(me, inner)


def near_groups(count):
    outer, inner, mo, mi = group_place(count)
    across = [lax.rem(mi + step, inner) for step in range(1, inner)]
    along = [lax.rem(mo + step, outer) for step in range(1, outer)]
    return (
        [(place, {"dp": mo * inner + place}) for place in across],
        [(place, {"dp": place * inner + mi}) for place in along],
    )


dma = pltpu.SemaphoreType.DMA


def remote(src, dst, send, recv, device):
    return pltpu.make_async_remote_copy(
        src_ref=src, dst_ref=dst, send_sem=send, recv_sem=recv, device_id=device, device_id_type=MESH
    )


class Bring:
    def __init__(self, layer, kind, value, in_vmem=False, target=None):
        self.layer, self.kind, self.in_vmem = layer, kind, in_vmem
        self.whole = kind == "all" or target is not None
        self.target = target or (lambda outputs, core, place: outputs[0].at[core, place])
        count = lax.axis_size("dp")
        outer, inner = factors(count)
        self.size = {"column": outer, "row": inner, "all": count}[kind]
        block = value.shape if self.whole else value.shape[1:]
        self.inputs = [value]
        self.outputs = [jax.ShapeDtypeStruct((2, self.size, *block), value.dtype)]
        self.sems = [dma((self.size,)), dma((2, self.size)), dma((2,))]
        if not in_vmem:
            self.sems.append(pltpu.VMEM(block, value.dtype))

    def place(self, step):
        count = lax.axis_size("dp")
        outer, inner, mo, mi = group_place(count)
        if self.kind == "column":
            place = lax.rem(mo + step, outer)
            return place, place * inner + mi
        if self.kind == "row":
            place = lax.rem(mi + step, inner)
            return place, mo * inner + place
        place = lax.rem(lax.axis_index("dp") + step, count)
        return place, place

    def parts(self, inputs, outputs, sems):
        core = lax.axis_index("section")
        mine, _ = self.place(0)
        target = self.target(outputs, core, mine)
        recv = sems[1].at[core, mine]

        def source(place):
            return inputs[0] if self.whole else inputs[0].at[place]

        sent = []
        for step in range(1, self.size):
            place, group = self.place(step)
            sent.append(
                remote(source(place), target, sems[0].at[step - 1], recv,
                       {"dp": group, "section": self.layer})
            )
        across = remote(source(mine), target, sems[0].at[self.size - 1], recv, core_peer())
        if self.in_vmem:
            local = [pltpu.make_async_copy(source(mine), target, sems[2].at[0])]
        else:
            local = [
                pltpu.make_async_copy(source(mine), sems[3], sems[2].at[0]),
                pltpu.make_async_copy(sems[3], target, sems[2].at[1]),
            ]
        return sent, across, local

    def start(self, inputs, outputs, sems):
        sent, across, local = self.parts(inputs, outputs, sems)
        for copy in sent:
            copy.start()
        here = lax.axis_index("section") == self.layer

        @pl.when(here)
        def _():
            local[0].start()

        @pl.when(jnp.logical_not(here))
        def _():
            across.start()

    def wait(self, inputs, outputs, sems):
        sent, across, local = self.parts(inputs, outputs, sems)
        core = lax.axis_index("section")
        here = core == self.layer
        block = inputs[0] if self.whole else inputs[0].at[0]

        def arrived(which, place):
            remote(block, self.target(outputs, which, place), sems[0].at[0], sems[1].at[which, place],
                   core_peer()).wait_recv()

        for copy in sent:
            copy.wait_send()

        @pl.when(here)
        def _():
            local[0].wait()
            for copy in local[1:]:
                copy.start()
                copy.wait()
            for step in range(self.size):
                place, _ = self.place(step)
                if step:
                    arrived(core, place)
                arrived(1 - core, place)

        @pl.when(jnp.logical_not(here))
        def _():
            across.wait_send()

    def results(self, outputs):
        return outputs[0]


class FirstStage:
    def __init__(self, value, axis, layer=None):
        self.count = lax.axis_size("dp")
        outer, inner = factors(self.count)
        self.blocks = (outer, inner, value.shape[0] // self.count, *value.shape[1:])
        inside = isinstance(value, jax.ShapeDtypeStruct)
        self.inputs = [] if inside else [value.reshape(self.blocks)]
        self.axis = axis
        shape = list(self.blocks[2:])
        shape[axis] //= 2
        self.shape = shape
        sums = [
            jax.ShapeDtypeStruct((outer, *shape), value.dtype),
            jax.ShapeDtypeStruct((inner, *shape), value.dtype),
        ]
        self.sems = [
            dma((inner + outer - 2,)),
            dma((inner + outer - 2,)),
            pltpu.VMEM((inner - 1, outer, *shape), value.dtype),
            pltpu.VMEM((outer - 1, inner, *shape), value.dtype),
            *[pltpu.VMEM(v.shape, v.dtype) for v in sums],
            dma((2,)),
            dma((2,)),
        ]
        self.outputs = sums
        self.brings = []
        if layer is not None:
            self.brings = [Bring(layer, kind, v, True) for kind, v in zip(("column", "row"), sums)]
            self.outputs = [v for bring in self.brings for v in bring.outputs]
            self.sems += [v for bring in self.brings for v in bring.sems]

    def copies(self, inputs, sems):
        across, along = near_groups(self.count)
        _, _, mo, mi = group_place(self.count)
        value = inputs[0]
        half = self.shape[self.axis]
        cut = [slice(None)] * 3
        first, second = list(cut), list(cut)
        first[self.axis], second[self.axis] = pl.ds(0, half), pl.ds(half, half)
        found = []
        for slot, (place, device) in enumerate(across):
            found.append((value.at[(slice(None), place, *first)], sems[2].at[slot], device))
        for slot, (place, device) in enumerate(along):
            found.append((value.at[(place, slice(None), *second)], sems[3].at[slot], device))
        sent = [
            remote(src, dst, sems[0].at[index], sems[1].at[index], device)
            for index, (src, dst, device) in enumerate(found)
        ]
        loads = [
            pltpu.make_async_copy(value.at[(slice(None), mi, *first)], sems[4], sems[6].at[0]),
            pltpu.make_async_copy(value.at[(mo, slice(None), *second)], sems[5], sems[6].at[1]),
        ]
        return sent + loads

    def onward(self, outputs, sems):
        place = 8
        found = []
        for index, bring in enumerate(self.brings):
            found.append((bring, [sems[4 + index]], [outputs[index]], sems[place : place + len(bring.sems)]))
            place += len(bring.sems)
        return found

    def saves(self, outputs, sems):
        return [pltpu.make_async_copy(sems[4 + k], outputs[k], sems[7].at[k]) for k in range(2)]

    def start(self, inputs, outputs, sems):
        start_all(self.copies(inputs, sems))

    def middle(self, inputs, outputs, sems):
        wait_all(self.copies(inputs, sems))
        for total, landed in ((sems[4], sems[2]), (sems[5], sems[3])):
            depth = total.shape[1]

            def add(index, carry, total=total, landed=landed, depth=depth):
                place, expert = index // depth, lax.rem(index, depth)
                value = total[place, expert].astype(f32)
                for slot in range(landed.shape[0]):
                    value = value + landed[slot, place, expert].astype(f32)
                total[place, expert] = value.astype(bf16)
                return carry

            lax.fori_loop(0, total.shape[0] * depth, add, 0)
        if self.brings:
            for bring, *refs in self.onward(outputs, sems):
                bring.start(*refs)
        else:
            start_all(self.saves(outputs, sems))

    def wait(self, inputs, outputs, sems):
        if self.brings:
            for bring, *refs in self.onward(outputs, sems):
                bring.wait(*refs)
        else:
            wait_all(self.saves(outputs, sems))

    def results(self, outputs):
        return outputs


class DenseSum:
    def __init__(self, value, layer):
        count = lax.axis_size("dp")
        outer, inner = factors(count)
        rows, width = value.shape[2:]
        half = width // 2
        self.half = half
        inside = isinstance(value, jax.ShapeDtypeStruct)
        self.inputs = [] if inside else [value]
        self.outputs = [jax.ShapeDtypeStruct((2, *value.shape), bf16)]

        def buffer(*lead):
            return pltpu.VMEM((*lead, rows, half), bf16)

        self.brings = [
            Bring(layer, "row", jax.ShapeDtypeStruct((outer, rows, half), bf16), True,
                  lambda outputs, core, place: outputs[0].at[core, :, place, :, pl.ds(0, half)]),
            Bring(layer, "column", jax.ShapeDtypeStruct((inner, rows, half), bf16), True,
                  lambda outputs, core, place: outputs[0].at[core, place, :, :, pl.ds(half, half)]),
        ]
        pairs = inner + outer - 2
        self.sems = [
            buffer(inner - 1, outer),
            buffer(outer - 1, inner),
            buffer(outer),
            buffer(inner),
            buffer(outer - 1),
            buffer(inner - 1),
            buffer(outer),
            buffer(inner),
            dma((2,)),
            *[dma((pairs,)) for _ in range(6)],
            *[v for bring in self.brings for v in bring.sems],
        ]

    def numbered(self, found, sems, first):
        return [
            remote(src, dst, sems[first].at[index], sems[first + 1].at[index], device)
            for index, (src, dst, device) in enumerate(found)
        ]

    def sent(self, inputs, sems):
        count = lax.axis_size("dp")
        across, along = near_groups(count)
        _, _, mo, mi = group_place(count)
        value = inputs[0]
        low, high = pl.ds(0, self.half), pl.ds(self.half, self.half)
        found = [
            (value.at[:, place, :, low], sems[0].at[slot], device)
            for slot, (place, device) in enumerate(across)
        ] + [
            (value.at[place, :, :, high], sems[1].at[slot], device)
            for slot, (place, device) in enumerate(along)
        ]
        loads = [
            pltpu.make_async_copy(value.at[:, mi, :, low], sems[2], sems[8].at[0]),
            pltpu.make_async_copy(value.at[mo, :, :, high], sems[3], sems[8].at[1]),
        ]
        return self.numbered(found, sems, 9) + loads

    def sums(self, sems):
        across, along = near_groups(lax.axis_size("dp"))
        found = [
            (sems[2].at[place], sems[4].at[slot], device) for slot, (place, device) in enumerate(along)
        ] + [
            (sems[3].at[place], sems[5].at[slot], device) for slot, (place, device) in enumerate(across)
        ]
        return self.numbered(found, sems, 11)

    def blocks(self, sems):
        count = lax.axis_size("dp")
        across, along = near_groups(count)
        _, _, mo, mi = group_place(count)
        found = [(sems[6].at[mo], sems[6].at[mo], device) for _, device in along]
        found += [(sems[7].at[mi], sems[7].at[mi], device) for _, device in across]
        return self.numbered(found, sems, 13)

    def onward(self, outputs, sems):
        place = 15
        found = []
        for index, bring in enumerate(self.brings):
            found.append((bring, [sems[6 + index]], outputs, sems[place : place + len(bring.sems)]))
            place += len(bring.sems)
        return found

    def start(self, inputs, outputs, sems):
        start_all(self.sent(inputs, sems))

    def middle1(self, inputs, outputs, sems):
        wait_all(self.sent(inputs, sems))
        for total, landed in ((sems[2], sems[0]), (sems[3], sems[1])):
            for place in range(total.shape[0]):
                value = total[place].astype(f32)
                for slot in range(landed.shape[0]):
                    value = value + landed[slot, place].astype(f32)
                total[place] = value.astype(bf16)
        start_all(self.sums(sems))

    def middle2(self, inputs, outputs, sems):
        wait_all(self.sums(sems))
        _, _, mo, mi = group_place(lax.axis_size("dp"))
        for total, landed, whole, mine in (
            (sems[2], sems[4], sems[6], mo),
            (sems[3], sems[5], sems[7], mi),
        ):
            value = total[mine].astype(f32)
            for slot in range(landed.shape[0]):
                value = value + landed[slot].astype(f32)
            whole[mine] = value.astype(bf16)
        start_all(self.blocks(sems))

    def middle3(self, inputs, outputs, sems):
        wait_all(self.blocks(sems))
        for bring, *refs in self.onward(outputs, sems):
            bring.start(*refs)

    def wait(self, inputs, outputs, sems):
        for bring, *refs in self.onward(outputs, sems):
            bring.wait(*refs)

    def results(self, outputs):
        return outputs[0]


class SmallSum:
    def __init__(self, depth, width):
        self.tensor, self.count = lax.axis_size("tensor"), lax.axis_size("dp")
        self.lanes = width // self.tensor
        self.depth = depth
        part = (depth, self.lanes)
        self.sems = [
            pltpu.VMEM((depth, width), f32),
            pltpu.VMEM((self.tensor - 1, *part), f32),
            pltpu.VMEM((self.count - 1, *part), f32),
            *[pltpu.VMEM(part, f32) for _ in range(4)],
            pltpu.VMEM((depth, width), f32),
            dma((2, self.tensor - 1)),
            dma((2, self.tensor - 1)),
            dma((self.count,)),
            dma((self.count,)),
        ]

    def columns(self, place):
        return pl.ds(pl.multiple_of(place * self.lanes, self.lanes), self.lanes)

    def over_tensor(self, sems):
        here = lax.axis_index("tensor")
        found = []
        for step in range(1, self.tensor):
            place = lax.rem(here + step, self.tensor)
            found.append(
                remote(sems[0].at[:, self.columns(place)], sems[1].at[step - 1],
                       sems[8].at[0, step - 1], sems[9].at[0, step - 1], {"tensor": place})
            )
        return found

    def over_groups(self, sems):
        me = lax.axis_index("dp")
        return [
            remote(sems[3], sems[2].at[step - 1], sems[10].at[step - 1], sems[11].at[step - 1],
                   {"dp": lax.rem(me + step, self.count)})
            for step in range(1, self.count)
        ]

    def over_cores(self, sems):
        last = self.count - 1
        return [remote(sems[4], sems[5], sems[10].at[last], sems[11].at[last], core_peer())]

    def back(self, sems):
        here = lax.axis_index("tensor")
        own = sems[7].at[:, self.columns(here)]
        return [
            remote(sems[6], own, sems[8].at[1, step - 1], sems[9].at[1, step - 1],
                   {"tensor": lax.rem(here + step, self.tensor)})
            for step in range(1, self.tensor)
        ]

    def first(self, sems):
        start_all(self.over_tensor(sems))

    def second(self, sems):
        wait_all(self.over_tensor(sems))
        total = sems[0][:, self.columns(lax.axis_index("tensor"))]
        for slot in range(self.tensor - 1):
            total = total + sems[1][slot]
        sems[3][...] = total
        start_all(self.over_groups(sems))

    def third(self, sems):
        wait_all(self.over_groups(sems))
        total = sems[3][...]
        for slot in range(self.count - 1):
            total = total + sems[2][slot]
        sems[4][...] = total
        copies = self.over_cores(sems)
        start_all(copies)
        wait_all(copies)
        sems[6][...] = sems[4][...] + sems[5][...]
        start_all(self.back(sems))
        sems[7][:, self.columns(lax.axis_index("tensor"))] = sems[6][...]

    def last(self, sems, out):
        wait_all(self.back(sems))
        out[...] = sems[7][...]


class Trade:
    def __init__(self, shape):
        self.sems = [pltpu.VMEM((2, *shape), f32), dma((1,)), dma((1,))]

    def copy(self, value, sems):
        core = lax.axis_index("section")
        return remote(value, sems[0].at[core], sems[1].at[0], sems[2].at[0], core_peer())

    def start(self, zero, one, sems):
        core = lax.axis_index("section")

        @pl.when(core == 0)
        def _():
            self.copy(one, sems).start()
            sems[0][0] = zero[...]

        @pl.when(core == 1)
        def _():
            self.copy(zero, sems).start()
            sems[0][1] = one[...]

    def wait(self, zero, out, sems):
        self.copy(zero, sems).wait()
        out[...] = sems[0][...]


def both_cores(groups):
    core = lax.axis_index("section")
    return [{"dp": group, "section": which} for group in groups for which in (core, 1 - core)]


def whole_group():
    count = lax.axis_size("dp")
    me = lax.axis_index("dp")
    return both_cores([lax.rem(me + step, count) for step in range(1, count)])


class Beside:
    def __init__(self, jobs):
        self.jobs = jobs
        self.inputs = [v for job in jobs for v in job.inputs]
        self.outputs = [v for job in jobs for v in job.outputs]
        self.sems = [v for job in jobs for v in job.sems]

    def peers(self):
        count = lax.axis_size("dp")
        if not self.jobs:
            return []
        across, along = near_groups(count)
        return both_cores([device["dp"] for _, device in across + along])

    def each(self, refs, run):
        inputs, outputs, sems = refs
        for job in self.jobs:
            mine, inputs = inputs[: len(job.inputs)], inputs[len(job.inputs) :]
            theirs, outputs = outputs[: len(job.outputs)], outputs[len(job.outputs) :]
            own, sems = sems[: len(job.sems)], sems[len(job.sems) :]
            run(job)(mine, theirs, own)

    def start(self, *refs):
        self.each(refs, lambda job: job.start)

    def middle(self, *refs, step="middle"):
        self.each(refs, lambda job: getattr(job, step, lambda *refs: None))

    def wait(self, *refs):
        self.each(refs, lambda job: job.wait)

    def results(self, outputs):
        found = []
        for job in self.jobs:
            found.append(job.results(outputs[: len(job.outputs)]))
            outputs = outputs[len(job.outputs) :]
        return found


def spread(count, buf, rows, sends, recvs, columns=slice(None)):
    me = lax.axis_index("tensor")
    own = buf.at[pl.ds(pl.multiple_of(me * rows, rows), rows), columns]
    copies = []
    for step in range(1, count):
        copies.append(
            pltpu.make_async_remote_copy(
                src_ref=own,
                dst_ref=own,
                send_sem=sends.at[step - 1],
                recv_sem=recvs.at[step - 1],
                device_id={"tensor": lax.rem(me + step, count)},
                device_id_type=MESH,
            )
        )
    return copies


def deal_out(count, part, rows, columns, landing, sends, recvs):
    me = lax.axis_index("tensor")
    copies = []
    for step in range(1, count):
        peer = lax.rem(me + step, count)
        copies.append(
            pltpu.make_async_remote_copy(
                src_ref=part.at[pl.ds(pl.multiple_of(peer * rows, rows), rows), columns],
                dst_ref=landing.at[step - 1, :, columns],
                send_sem=sends.at[step - 1],
                recv_sem=recvs.at[step - 1],
                device_id={"tensor": peer},
                device_id_type=MESH,
            )
        )
    for copy in copies:
        copy.start()
    return copies


def core_peer():
    return {"section": 1 - lax.axis_index("section")}


def hand_rows(value, pair, sems):
    tokens = value.shape[0]
    return [
        pltpu.make_async_copy(value, pair.at[pl.ds(0, tokens)], sems[0]),
        remote(value, pair.at[pl.ds(tokens, tokens)], sems[1], sems[2], core_peer()),
    ]


def hand_halves(value, pair, sems):
    section = lax.axis_index("section")
    tokens, half = value.shape[0], value.shape[1] // 2
    mine = value.at[:, pl.ds(pl.multiple_of(section * half, half), half)]
    other = value.at[:, pl.ds(pl.multiple_of((1 - section) * half, half), half)]
    return [
        pltpu.make_async_copy(mine, pair.at[pl.ds(0, tokens)], sems[0]),
        remote(other, pair.at[pl.ds(tokens, tokens)], sems[1], sems[2], core_peer()),
    ]


def start_all(copies):
    for copy in copies:
        copy.start()


def wait_all(copies):
    for copy in copies:
        copy.wait()


def either(use_own, own, other, run):
    @pl.when(use_own)
    def _():
        run(own)

    @pl.when(jnp.logical_not(use_own))
    def _():
        run(other)


def weight_copies(refs, scratch, sems, expert):
    gate, up, down = refs
    gu_s, down_s = scratch
    width = gate.shape[2]
    return (
        pltpu.make_async_copy(gate.at[expert], gu_s.at[expert, :, pl.ds(0, width)], sems.at[0, expert]),
        pltpu.make_async_copy(up.at[expert], gu_s.at[expert, :, pl.ds(width, width)], sems.at[1, expert]),
        pltpu.make_async_copy(
            down.at[expert], down_s.at[pl.ds(pl.multiple_of(expert * width, width), width)], sems.at[2, expert]
        ),
    )


def attn_copies(refs, scratch, sems):
    query, key, value, output = refs
    joint_s, output_s = scratch
    qw, kw = query.shape[1], key.shape[1]
    return (
        pltpu.make_async_copy(query, joint_s.at[:, pl.ds(0, qw)], sems.at[0]),
        pltpu.make_async_copy(key, joint_s.at[:, pl.ds(qw, kw)], sems.at[1]),
        pltpu.make_async_copy(value, joint_s.at[:, pl.ds(qw + kw, kw)], sems.at[2]),
        pltpu.make_async_copy(output, output_s, sems.at[3]),
    )


def turned(block):
    lane = lax.broadcasted_iota(jnp.int32, block.shape, 1)
    half = HD // 2
    return jnp.where(
        lane % HD < half, pltpu.roll(block, block.shape[1] - half, 1), pltpu.roll(block, half, 1)
    )


def column(table, index):
    lane = lax.broadcasted_iota(jnp.int32, table.shape, 1)
    return jnp.sum(jnp.where(lane == index, table, 0.0), axis=1, keepdims=True)


def swap_copies(own, other, sems, piece):
    sends, recvs = sems
    names = len(own)
    if isinstance(piece, tuple):
        name, expert = piece
        source, target = own[name].at[expert], other[name].at[expert]
        index = 4 + (name - 4) * own[4].shape[0] + expert
    else:
        source, target, index = own[piece], other[piece], piece
    return pltpu.make_async_remote_copy(
        src_ref=source, dst_ref=target, send_sem=sends.at[index], recv_sem=recvs.at[index],
        device_id=core_peer(), device_id_type=MESH,
    )


def forward_kernel(layer, count, swap, *refs):
    refs = list(refs)

    def take(number):
        taken = refs[:number]
        del refs[:number]
        return taken

    (stream_in, attn_gains, expert_gains, routers, cosine, sine, bias, pickeds, kepts) = take(9)
    attn_gain, expert_gain, router = attn_gains.at[layer], expert_gains.at[layer], routers.at[layer]
    picked, kept = pickeds.at[layer], kepts.at[layer]
    stream = stream_in.at[lax.axis_index("section")] if layer == 0 else stream_in
    own = take(7)
    other = None if swap else take(7)
    (out, mid_out, expert_rows_out, qs_out, keys_out, values_out, probs_out, gate_out,
     attn_in_out, expert_in_out, gated_out, attended_out, pre_out) = take(13)
    if swap:
        other = take(7)
    scratch = take(4)
    joint_s, output_s, gu_s, down_s = scratch
    (ag1, ag2, part, landing1, landing2, pre_s, gated_s, attended_s, send_s, recv_s, attn_sems,
     expert_sems, pre_sems, save_sems) = refs[:14]
    if swap:
        swap_sems = refs[14:]
    rows, width = stream.shape
    tokens = ag1.shape[0]
    experts = gu_s.shape[0]
    hidden_width = gu_s.shape[2] // 2
    kw = keys_out.shape[1]
    qw = attended_s.shape[1]
    heads, key_heads = qw // HD, kw // HD
    group = heads // key_heads
    me = lax.axis_index("tensor")
    own_rows = pl.ds(pl.multiple_of(me * rows, rows), rows)
    use_own = lax.axis_index("section") == layer

    def start_attn(w):
        for copy in attn_copies(w[:4], scratch[:2], attn_sems):
            copy.start()

    def wait_attn(w):
        for copy in attn_copies(w[:4], scratch[:2], attn_sems):
            copy.wait()

    def start_expert(w, expert):
        for copy in weight_copies(w[4:], scratch[2:], expert_sems, expert):
            copy.start()

    def wait_expert(w, expert):
        for copy in weight_copies(w[4:], scratch[2:], expert_sems, expert):
            copy.wait()

    def each_expert(run):
        def step(expert, carry):
            run(expert)
            return carry

        lax.fori_loop(0, experts, step, 0)

    def swap_expert(expert):
        return [swap_copies(own, other, swap_sems, (name, expert)) for name in (4, 5, 6)]

    value = stream[...].astype(bf16).astype(f32)
    ag1[own_rows, :] = (value * norm_scale(value) * attn_gain[...]).astype(bf16)
    greet(tensor_peers(count) + ([core_peer()] if swap else []))
    first = spread(count, ag1, rows, send_s.at[0], recv_s.at[0])
    if swap:
        lead = min(2, experts)
        for piece in range(4):
            swap_copies(own, other, swap_sems, piece).start()
        each_expert(lambda expert: [c.start() for c in swap_expert(expert)] and None)

        @pl.when(use_own)
        def _():
            start_all(first)
            start_attn(own)
            each_expert(lambda expert: start_expert(own, expert))

        @pl.when(jnp.logical_not(use_own))
        def _():
            for piece in range(4):
                swap_copies(own, other, swap_sems, piece).wait_recv()
            start_attn(other)
            for expert in range(lead):
                for copy in swap_expert(expert):
                    copy.wait_recv()
                start_expert(other, expert)
            start_all(first)
    else:
        start_all(first)
        either(use_own, own, other, start_attn)
        either(use_own, own, other, lambda w: each_expert(lambda expert: start_expert(w, expert)))
    wait_all(first)
    saved = [pltpu.make_async_copy(ag1, attn_in_out, save_sems.at[0])]
    saved[0].start()
    either(use_own, own, other, wait_attn)
    proj = dot(ag1[...], joint_s[...], NN)
    for chunk in range(qw // 128):
        block = proj[:, chunk * 128 : chunk * 128 + 128]
        block = (block * cosine[...] + turned(block) * sine[...]).astype(bf16)
        for part_index in range(128 // HD):
            head = chunk * (128 // HD) + part_index
            qs_out[pl.ds(head * tokens, tokens), :] = block[:, part_index * HD : part_index * HD + HD]
    for chunk in range(kw // 128):
        block = proj[:, qw + chunk * 128 : qw + chunk * 128 + 128]
        keys_out[:, pl.ds(chunk * 128, 128)] = (
            block * cosine[...] + turned(block) * sine[...]
        ).astype(bf16)
    values_out[...] = proj[:, qw + kw :].astype(bf16)
    for g in range(key_heads):
        lanes = pl.ds(g * HD, HD)
        span = pl.ds(g * group * tokens, group * tokens)
        scores = dot(qs_out[span, :], keys_out[:, lanes], NT) * 0.125
        scores = (scores.reshape(group, tokens, tokens) + bias[...][None]).reshape(
            group * tokens, tokens
        )
        top = jnp.max(scores, axis=1, keepdims=True)
        weighed = jnp.exp(scores - top)
        probs = (weighed / jnp.sum(weighed, axis=1, keepdims=True)).astype(bf16)
        probs_out[span, :] = probs
        attended = dot(probs, values_out[:, lanes], NN).astype(bf16)
        for h in range(group):
            attended_s[:, pl.ds((g * group + h) * HD, HD)] = attended[h * tokens : (h + 1) * tokens]
    saved.append(pltpu.make_async_copy(attended_s, attended_out, save_sems.at[1]))
    saved[1].start()
    part[...] = dot(attended_s[...], output_s[...], NN).astype(bf16)
    dealt = deal_out(count, part, rows, slice(None), landing1, send_s.at[1], recv_s.at[1])
    wait_all(dealt)
    mid = value + part[own_rows, :].astype(f32)
    for step in range(count - 1):
        mid = mid + landing1[step].astype(f32)
    mid_out[...] = mid
    expert_rows = (mid * norm_scale(mid) * expert_gain[...]).astype(bf16)
    expert_rows_out[...] = expert_rows
    ag2[own_rows, :] = expert_rows
    split = width // 2
    columns = pl.ds(0, split), pl.ds(split, split)
    early, late = [
        spread(count, ag2, rows, send_s.at[index], recv_s.at[index], lanes)
        for index, lanes in zip((2, 7), columns)
    ]
    start_all(early)
    start_all(late)
    wait_all(early)

    def first_step(expert, carry):
        if swap:

            @pl.when(jnp.logical_not(use_own) & (expert + lead < experts))
            def _():
                for copy in swap_expert(expert + lead):
                    copy.wait_recv()
                start_expert(other, expert + lead)

        either(use_own, own, other, lambda w: wait_expert(w, expert))
        pre_s[expert] = dot(ag2[:, columns[0]], gu_s[expert, columns[0], :], NN)
        return carry

    lax.fori_loop(0, experts, first_step, 0)
    wait_all(late)
    saved.append(pltpu.make_async_copy(ag2, expert_in_out, save_sems.at[2]))
    saved[2].start()
    logits = dot(ag2[...], router[...], NT)
    chosen = picked[...] > 0
    top = jnp.max(jnp.where(chosen, logits, masked_score), axis=1, keepdims=True)
    weighed = jnp.where(chosen, jnp.exp(logits - top), 0.0)
    gate_out[...] = weighed / jnp.sum(weighed, axis=1, keepdims=True)

    def expert_step(expert, carry):
        pre = pre_s[expert] + dot(ag2[:, columns[1]], gu_s[expert, columns[1], :], NN)
        pre_s[expert] = pre
        pltpu.make_async_copy(pre_s.at[expert], pre_out.at[expert], pre_sems.at[expert]).start()
        gate_pre, up_pre = pre[:, :hidden_width], pre[:, hidden_width:]
        hidden = (gate_pre / (1.0 + jnp.exp(-gate_pre)) * up_pre).astype(bf16).astype(f32)
        weight = column(gate_out[...] * kept[...], expert)
        gated_s[:, pl.ds(pl.multiple_of(expert * hidden_width, hidden_width), hidden_width)] = (
            hidden * weight
        ).astype(bf16)
        return carry

    lax.fori_loop(0, experts, expert_step, 0)
    saved.append(pltpu.make_async_copy(gated_s, gated_out, save_sems.at[3]))
    saved[3].start()
    copies = []
    tile = width // 4
    for t in range(4):
        columns = pl.ds(t * tile, tile)
        part[:, columns] = dot(gated_s[...], down_s[:, columns], NN).astype(bf16)
        copies += deal_out(count, part, rows, columns, landing2, send_s.at[3 + t], recv_s.at[3 + t])
    wait_all(copies)
    total = mid_out[...] + part[own_rows, :].astype(f32)
    for step in range(count - 1):
        total = total + landing2[step].astype(f32)
    out[...] = total
    wait_all(saved)
    if swap:
        for piece in range(4):
            swap_copies(own, other, swap_sems, piece).wait_send()
        each_expert(lambda expert: [c.wait_send() for c in swap_expert(expert)] and None)

        @pl.when(use_own)
        def _():
            for piece in range(4):
                swap_copies(own, other, swap_sems, piece).wait_recv()
            each_expert(lambda expert: [c.wait_recv() for c in swap_expert(expert)] and None)

    def finish(expert, carry):
        pltpu.make_async_copy(pre_s.at[expert], pre_out.at[expert], pre_sems.at[expert]).wait()
        return carry

    lax.fori_loop(0, experts, finish, 0)


def weight_scratch(own):
    query, key, value, output, gate, up, down = own
    depth = query.shape[0]
    experts, _, hidden_width = gate.shape
    return [
        pltpu.VMEM((depth, query.shape[1] + 2 * key.shape[1]), bf16),
        pltpu.VMEM(output.shape, bf16),
        pltpu.VMEM((experts, depth, 2 * hidden_width), bf16),
        pltpu.VMEM((experts * hidden_width, depth), bf16),
    ]


def layer_forward(layer, gains, own, other, stream, tables, masks):
    count = lax.axis_size("tensor")
    rows, width = stream.shape[-2:]
    tokens = tables[2].shape[0]
    qw, kw = own[0].shape[1], own[1].shape[1]
    experts, _, hidden_width = own[4].shape
    heads = qw // HD
    swap = other is None
    vmem = pl.BlockSpec(memory_space=pltpu.VMEM)
    hbm = pl.BlockSpec(memory_space=pl.ANY)
    shape = jax.ShapeDtypeStruct
    pieces = 4 + 3 * experts
    found = pl.pallas_call(
        functools.partial(forward_kernel, layer, count, swap),
        name=f"layer_forward_{layer}",
        out_shape=(
            shape((rows, width), f32),
            shape((rows, width), f32),
            shape((rows, width), bf16),
            shape((heads * tokens, HD), bf16),
            shape((tokens, kw), bf16),
            shape((tokens, kw), bf16),
            shape((heads * tokens, tokens), bf16),
            shape((tokens, experts), f32),
            shape((tokens, width), bf16),
            shape((tokens, width), bf16),
            shape((tokens, experts * hidden_width), bf16),
            shape((tokens, qw), bf16),
            shape((experts, tokens, 2 * hidden_width), f32),
        )
        + (tuple(shape(w.shape, w.dtype) for w in own) if swap else ()),
        in_specs=[vmem] * 9 + [hbm] * (7 if swap else 14),
        out_specs=(vmem,) * 8 + (hbm,) * (12 if swap else 5),
        scratch_shapes=weight_scratch(own)
        + [
            pltpu.VMEM((tokens, width), bf16),
            pltpu.VMEM((tokens, width), bf16),
            pltpu.VMEM((tokens, width), bf16),
            pltpu.VMEM((count - 1, rows, width), bf16),
            pltpu.VMEM((count - 1, rows, width), bf16),
            pltpu.VMEM((experts, tokens, 2 * hidden_width), f32),
            pltpu.VMEM((tokens, experts * hidden_width), bf16),
            pltpu.VMEM((tokens, qw), bf16),
            dma((8, count - 1)),
            dma((8, count - 1)),
            dma((4,)),
            dma((3, experts)),
            dma((experts,)),
            dma((4,)),
        ]
        + ([dma((pieces,)), dma((pieces,))] if swap else []),
        compiler_params=params(1 + layer),
    )(stream, *gains, *tables, *masks, *own,
      *(() if swap else other))
    return found[:13], found[13:]


def norm_back(value, gain, out_grad):
    scale = norm_scale(value)
    scaled = value * scale
    gain_grad = jnp.sum(out_grad * scaled, axis=0, keepdims=True)
    inner = out_grad * gain
    value_grad = scale * (inner - scaled * jnp.mean(inner * scaled, axis=-1, keepdims=True))
    return value_grad, gain_grad


def experts_back_kernel(layer, count, trade, stage, beside, *refs):
    refs = list(refs)

    def take(number):
        taken = refs[:number]
        del refs[:number]
        return taken

    out_grad, mid, expert_gains, routers, kepts, gate, expert_rows, pre_in = take(8)
    expert_gain, router, kept = expert_gains.at[layer], routers.at[layer], kepts.at[layer]
    x_in, gated_in = take(2)
    own, other = take(3), take(3)
    traded = take(2 if trade else 0)
    beside_in = take(len(beside.inputs))
    mid_grad_out, router_out, expert_gain_out, pair_out = take(4)
    traded_out = take(1 if trade else 0)
    stage_out = take(len(stage.outputs))
    beside_out = take(len(beside.outputs))
    scratch = take(2)
    gu_s, down_s = scratch
    (ag1, part, landing1, pre_s, gpu_s, acc, gate_part, gate_land, og_s, gpu_peer, x_s, turned_x,
     gated_s, hidden_s, pair_s, down_grad_s, send_s, recv_s, expert_sems, pre_sems, core_send, core_recv,
     local_sems, hand_send, hand_recv, save_sems) = take(26)
    trade_sems = take(len(trade.sems) if trade else 0)
    stage_refs = ([down_grad_s], stage_out, take(len(stage.sems)))
    beside_refs = (beside_in, beside_out, refs)
    rows, width = mid.shape
    tokens = ag1.shape[0]
    experts = gu_s.shape[0]
    hidden_width = gu_s.shape[2] // 2
    me = lax.axis_index("tensor")
    own_rows = pl.ds(pl.multiple_of(me * rows, rows), rows)
    use_own = lax.axis_index("section") == layer

    def start_expert(expert, carry):
        either(use_own, own, other,
               lambda w: [c.start() for c in weight_copies(w, scratch, expert_sems, expert)])
        pltpu.make_async_copy(pre_in.at[expert], pre_s.at[expert], pre_sems.at[expert]).start()
        return carry

    everyone = Beside([*beside.jobs, stage])
    if layer:
        ag1[own_rows, :] = out_grad[lax.axis_index("section")]
        greet(tensor_peers(count) + [core_peer()] + everyone.peers())
        first = spread(count, ag1, rows, send_s.at[0], recv_s.at[0])
        start_all(first)
    else:
        ag1[own_rows, :] = out_grad[...].astype(bf16)
        greet(tensor_peers(count) + [core_peer()] + everyone.peers())
        first = spread(count, ag1, rows, send_s.at[0], recv_s.at[0])
        start_all(first)
    lax.fori_loop(0, experts, start_expert, 0)
    loads = hand_halves(x_in, x_s, [v.at[0] for v in (local_sems, hand_send, hand_recv)])
    loads += hand_rows(gated_in, gated_s, [v.at[1] for v in (local_sems, hand_send, hand_recv)])
    for copy in loads:
        copy.start()
    beside.start(*beside_refs)
    if trade:
        trade.start(*traded, trade_sems)
    gate_part[...] = jnp.zeros_like(gate_part)

    def ready_step(expert, carry):
        pltpu.make_async_copy(pre_in.at[expert], pre_s.at[expert], pre_sems.at[expert]).wait()
        gate_pre = pre_s[expert, :, pl.ds(0, hidden_width)]
        up_pre = pre_s[expert, :, pl.ds(hidden_width, hidden_width)]
        sig = 1.0 / (1.0 + jnp.exp(-gate_pre))
        act = gate_pre * sig
        hidden_s[expert] = (act * up_pre).astype(bf16)
        weight = column(gate[...] * kept[...], expert)
        pre_s[expert, :, pl.ds(0, hidden_width)] = (
            weight * up_pre * (sig * (1.0 + gate_pre * (1.0 - sig)))
        )
        pre_s[expert, :, pl.ds(hidden_width, hidden_width)] = weight * act
        return carry

    lax.fori_loop(0, experts, ready_step, 0)
    wait_all(first)
    core = lax.axis_index("section")
    half = width // 2
    og_s[pl.ds(0, tokens), :] = ag1[:, pl.ds(pl.multiple_of(core * half, half), half)]
    handed = [
        remote(ag1.at[:, pl.ds(pl.multiple_of((1 - core) * half, half), half)],
               og_s.at[pl.ds(tokens, tokens)], core_send.at[0], core_recv.at[0], core_peer())
    ]
    handed[0].start()
    wait_all(loads)
    handed[0].wait()
    _, inner, per_group = stage.blocks[:3]

    def down_step(index, carry):
        lanes = pl.ds(pl.multiple_of(index * 2 * hidden_width, 2 * hidden_width), 2 * hidden_width)
        grads = dot(gated_s[:, lanes], og_s[...], TN).astype(bf16)
        for k in range(2):
            expert = 2 * index + k
            group, place = expert // per_group, lax.rem(expert, per_group)
            down_grad_s[group // inner, lax.rem(group, inner), place] = grads[
                k * hidden_width : (k + 1) * hidden_width
            ]
        return carry

    lax.fori_loop(0, experts // 2, down_step, 0)
    stage.start(*stage_refs)
    beside.middle(*beside_refs, step="middle1")

    def expert_step(index, carry):
        pair = (2 * index, 2 * index + 1)
        for expert in pair:
            either(use_own, own, other,
                   lambda w: [c.wait() for c in weight_copies(w, scratch, expert_sems, expert)])
        lanes = pl.ds(pl.multiple_of(index * 2 * hidden_width, 2 * hidden_width), 2 * hidden_width)
        plain = dot(ag1[...], down_s[lanes, :], NT)
        lane = lax.broadcasted_iota(jnp.int32, gate_part.shape, 1)
        for k, expert in enumerate(pair):
            value = plain[:, k * hidden_width : (k + 1) * hidden_width]
            summed = jnp.sum(hidden_s[expert].astype(f32) * value, axis=1, keepdims=True)
            gate_part[...] += jnp.where(lane == expert, summed, 0.0)
            for cut in (pl.ds(0, hidden_width), pl.ds(hidden_width, hidden_width)):
                gpu_s[expert, :, cut] = (value * pre_s[expert, :, cut]).astype(bf16)
        back = dot(gpu_s[pair[0]], gu_s[pair[0]], NT) + dot(gpu_s[pair[1]], gu_s[pair[1]], NT)

        @pl.when(index == 0)
        def _():
            acc[...] = back

        @pl.when(index > 0)
        def _():
            acc[...] += back

        return carry

    lax.fori_loop(0, experts // 2, expert_step, 0)
    gate_part[:, :experts] = gate_part[:, :experts] * kept[...]
    handed.append(remote(gpu_s, gpu_peer, core_send.at[1], core_recv.at[1], core_peer()))
    handed[1].start()
    part[...] = acc[...].astype(bf16)
    copies = deal_out(count, part, rows, slice(None), landing1, send_s.at[1], recv_s.at[1])
    copies += deal_out(count, gate_part, rows, slice(None), gate_land, send_s.at[2], recv_s.at[2])
    beside.middle(*beside_refs, step="middle2")
    turned_x[...] = x_s[...].T
    wait_all(handed[1:])

    def saves(expert):
        return [pltpu.make_async_copy(pair_s.at[expert], pair_out.at[expert], save_sems.at[expert])]

    def grads_step(expert, carry):
        pair_s[expert] = (
            dot(turned_x[:, :tokens], gpu_s[expert], NN)
            + dot(turned_x[:, tokens:], gpu_peer[expert], NN)
        ).astype(bf16)
        for copy in saves(expert):
            copy.start()
        return carry

    lax.fori_loop(0, experts, grads_step, 0)
    beside.middle(*beside_refs, step="middle3")
    if layer:
        stage.middle(*stage_refs)
    wait_all(copies)
    in_grad = acc[own_rows, :]
    gate_grad = gate_part[own_rows, :]
    for step in range(count - 1):
        in_grad = in_grad + landing1[step].astype(f32)
        gate_grad = gate_grad + gate_land[step]
    gate_grad = gate_grad[:, :experts]
    gate_rows = gate[own_rows, :]
    logits_grad = (
        gate_rows * (gate_grad - jnp.sum(gate_rows * gate_grad, axis=1, keepdims=True))
    ).astype(bf16)
    router_out[...] = dot(logits_grad, expert_rows[...], TN)
    in_grad = in_grad + dot(logits_grad, router[...], NN)
    mid_part, expert_gain_grad = norm_back(mid[...], expert_gain[...], in_grad)
    expert_gain_out[...] = expert_gain_grad
    mid_grad_out[...] = ag1[own_rows, :].astype(f32) + mid_part

    def finish_save(expert, carry):
        for copy in saves(expert):
            copy.wait()
        return carry

    lax.fori_loop(0, experts, finish_save, 0)
    if trade:
        trade.wait(traded[0], traded_out[0], trade_sems)
    if not layer:
        stage.middle(*stage_refs)
    stage.wait(*stage_refs)
    beside.wait(*beside_refs)


def experts_back(layer, gains, own, other, out_grad, state, pairs, masks, traded, beside):
    count = lax.axis_size("tensor")
    mid, gate, expert_rows, pre = state
    rows, width = mid.shape
    tokens = gate.shape[0]
    own, other = own[4:], other[4:]
    trade = Trade((rows, width)) if traded else None
    experts, depth, hidden_width = own[0].shape
    stage = FirstStage(
        jax.ShapeDtypeStruct((experts, hidden_width, width // 2), bf16), 2, layer if layer else None
    )
    vmem = pl.BlockSpec(memory_space=pltpu.VMEM)
    hbm = pl.BlockSpec(memory_space=pl.ANY)
    shape = jax.ShapeDtypeStruct
    found = pl.pallas_call(
        functools.partial(experts_back_kernel, layer, count, trade, stage, beside),
        name=f"experts_back_{layer}",
        out_shape=(
            shape((rows, width), f32),
            shape((experts, width), f32),
            shape((1, width), f32),
            shape((experts, width // 2, 2 * hidden_width), bf16),
            *((shape((2, rows, width), f32),) if traded else ()),
            *stage.outputs,
            *beside.outputs,
        ),
        in_specs=[vmem] * 7 + [hbm] * 9 + [vmem] * len(traded) + [hbm] * len(beside.inputs),
        out_specs=(vmem, vmem, vmem, hbm)
        + (vmem,) * bool(traded)
        + (hbm,) * len(stage.outputs + beside.outputs),
        scratch_shapes=[
            pltpu.VMEM((experts, depth, 2 * hidden_width), bf16),
            pltpu.VMEM((experts * hidden_width, depth), bf16),
            pltpu.VMEM((tokens, width), bf16),
            pltpu.VMEM((tokens, width), bf16),
            pltpu.VMEM((count - 1, rows, width), bf16),
            pltpu.VMEM((experts, tokens, 2 * hidden_width), f32),
            pltpu.VMEM((experts, tokens, 2 * hidden_width), bf16),
            pltpu.VMEM((tokens, width), f32),
            pltpu.VMEM((tokens, 128), f32),
            pltpu.VMEM((count - 1, rows, 128), f32),
            pltpu.VMEM((2 * tokens, width // 2), bf16),
            pltpu.VMEM((experts, tokens, 2 * hidden_width), bf16),
            pltpu.VMEM((2 * tokens, width // 2), bf16),
            pltpu.VMEM((width // 2, 2 * tokens), bf16),
            pltpu.VMEM((2 * tokens, experts * hidden_width), bf16),
            pltpu.VMEM((experts, tokens, hidden_width), bf16),
            pltpu.VMEM((experts, width // 2, 2 * hidden_width), bf16),
            pltpu.VMEM(stage.blocks, bf16),
            pltpu.SemaphoreType.DMA((3, count - 1)),
            pltpu.SemaphoreType.DMA((3, count - 1)),
            pltpu.SemaphoreType.DMA((3, experts)),
            pltpu.SemaphoreType.DMA((experts,)),
            *[pltpu.SemaphoreType.DMA((3,)) for _ in range(5)],
            pltpu.SemaphoreType.DMA((experts,)),
            *(trade.sems if trade else ()),
            *stage.sems,
            *beside.sems,
        ],
        compiler_params=params(3 + layer),
    )(out_grad, mid, *gains[1:], masks[1], gate, expert_rows, pre, *pairs, *own, *other,
      *traded, *beside.inputs)
    kept = 5 if traded else 4
    parts = kept + len(stage.outputs)
    return found[:kept], found[kept:parts], beside.results(found[parts:])


def attention_back_kernel(layer, count, last, beside, *refs):
    refs = list(refs)

    def take(number):
        taken = refs[:number]
        del refs[:number]
        return taken

    mid_grad, stream_in, attn_gains, cosine, sine, qs, keys, values, probs = take(9)
    attn_gain = attn_gains.at[layer]
    stream = stream_in.at[lax.axis_index("section")] if layer == 0 else stream_in
    ai_in, attended_in = take(2)
    own, other = take(4), take(4)
    small_parts = take(5 if last else 0)
    later_grad = take(1 if last else 0)
    beside_in = take(len(beside.inputs))
    if last:
        dense_sum, small_sum, trade = last
        traded_out, small_out, whole_out = take(3)
    else:
        grad_out, attn_gain_out, dense_out = take(3)
    beside_out = take(len(beside.outputs))
    scratch = take(2)
    joint_s, output_s = scratch
    (ag2, part, landing2, ag_stack, dq_s, joint_rows, joint_peer, ao_s, ai_s, turned_ai, attended_s,
     dense_s, send_s, recv_s, attn_sems, core_send, core_recv, local_sems,
     hand_send, hand_recv) = take(20)
    if last:
        grad_s, trade_sems = refs.pop(0), take(len(trade.sems))
        dense_sems, small_sems = take(len(dense_sum.sems)), take(len(small_sum.sems))
        dense_refs = ([dense_s], [whole_out], dense_sems)
    beside_refs = (beside_in, beside_out, refs)
    rows, width = stream.shape
    tokens = ag2.shape[0]
    kw = keys.shape[1]
    qw = output_s.shape[0]
    heads, key_heads = qw // HD, kw // HD
    group = heads // key_heads
    me = lax.axis_index("tensor")
    own_rows = pl.ds(pl.multiple_of(me * rows, rows), rows)
    use_own = lax.axis_index("section") == layer
    ag2[own_rows, :] = mid_grad[...].astype(bf16)
    everyone = Beside([*beside.jobs, dense_sum]) if last else beside
    greet(tensor_peers(count) + [core_peer()] + (whole_group() if last else everyone.peers()))
    first = spread(count, ag2, rows, send_s.at[0], recv_s.at[0])
    start_all(first)
    either(use_own, own, other, lambda w: [c.start() for c in attn_copies(w, scratch, attn_sems)])
    loads = hand_halves(ai_in, ai_s, [v.at[0] for v in (local_sems, hand_send, hand_recv)])
    loads += hand_rows(attended_in, attended_s, [v.at[1] for v in (local_sems, hand_send, hand_recv)])
    for copy in loads:
        copy.start()
    beside.start(*beside_refs)
    wait_all(loads)
    turned_ai[...] = ai_s[...].T
    wait_all(first)
    core = lax.axis_index("section")
    half = width // 2
    ao_s[pl.ds(0, tokens), :] = ag2[:, pl.ds(pl.multiple_of(core * half, half), half)]
    handed = [
        remote(ag2.at[:, pl.ds(pl.multiple_of((1 - core) * half, half), half)],
               ao_s.at[pl.ds(tokens, tokens)], core_send.at[0], core_recv.at[0], core_peer())
    ]
    handed[0].start()
    either(use_own, own, other, lambda w: [c.wait() for c in attn_copies(w, scratch, attn_sems)])
    attended_grad = dot(ag2[...], output_s[...], NT).astype(bf16)
    for h in range(heads):
        ag_stack[pl.ds(h * tokens, tokens), :] = attended_grad[:, h * HD : (h + 1) * HD]
    for g in range(key_heads):
        lanes = pl.ds(g * HD, HD)
        span = pl.ds(g * group * tokens, group * tokens)
        soft_b = probs[span, :]
        soft = soft_b.astype(f32)
        soft_grad = dot(ag_stack[span, :], values[:, lanes], NT)
        inner = jnp.sum(soft * soft_grad, axis=1, keepdims=True)
        score_grad = (soft * (soft_grad - inner)).astype(bf16)
        dq = dot(score_grad, keys[:, lanes], NN) * 0.125
        for h in range(group):
            dq_s[:, pl.ds((g * group + h) * HD, HD)] = dq[h * tokens : (h + 1) * tokens]
        dq_s[:, pl.ds(qw + g * HD, HD)] = dot(score_grad, qs[span, :], TN) * 0.125
        joint_rows[:, pl.ds(qw + kw + g * HD, HD)] = dot(soft_b, ag_stack[span, :], TN).astype(bf16)
    for chunk in range((qw + kw) // 128):
        lanes = pl.ds(chunk * 128, 128)
        block = dq_s[:, lanes]
        joint_rows[:, lanes] = (block * cosine[...] - turned(block) * sine[...]).astype(bf16)
    handed.append(remote(joint_rows, joint_peer, core_send.at[1], core_recv.at[1], core_peer()))
    handed[1].start()
    copies = []
    tile = width // 2
    for t in range(2):
        columns = pl.ds(t * tile, tile)
        part[:, columns] = dot(joint_rows[...], joint_s[columns, :], NT).astype(bf16)
        copies += deal_out(count, part, rows, columns, landing2, send_s.at[1 + t], recv_s.at[1 + t])
    wait_all(handed)
    wide = qw + 2 * kw
    joint_grads = (
        dot(turned_ai[:, :tokens], joint_rows[...], NN) + dot(turned_ai[:, tokens:], joint_peer[...], NN)
    ).astype(bf16)
    output_grads = dot(ao_s[...], attended_s[...], TN).astype(bf16)
    outer, inner, depth = dense_s.shape[:3]
    for block in range(outer * inner):
        cut = slice(block * depth, (block + 1) * depth)
        dense_s[block // inner, block % inner, :, :wide] = joint_grads[cut]
        dense_s[block // inner, block % inner, :, wide:] = output_grads[cut]
    if last:
        dense_sum.start(*dense_refs)
    else:
        save = pltpu.make_async_copy(dense_s, dense_out, local_sems.at[0])
        save.start()
    wait_all(copies)
    in_grad = part[own_rows, :].astype(f32)
    for step in range(count - 1):
        in_grad = in_grad + landing2[step].astype(f32)
    stream_part, attn_gain_grad = norm_back(
        stream[...].astype(bf16).astype(f32), attn_gain[...], in_grad
    )
    grad = mid_grad[...] + stream_part
    if not last:
        attn_gain_out[...] = attn_gain_grad
        grad_out[...] = grad
        save.wait()
        beside.middle(*beside_refs)
        beside.wait(*beside_refs)
        return
    small = small_sems[0]
    router0, gain0, router1, attn_gain1, gain1 = small_parts
    place = 0
    for value in (router0[...], attn_gain_grad, gain0[...]):
        small[pl.ds(place, value.shape[0]), :] = value
        place += value.shape[0]
    place = small.shape[0] // 2
    for value in (router1[...], attn_gain1[...], gain1[...]):
        small[pl.ds(place, value.shape[0]), :] = value
        place += value.shape[0]
    small_sum.first(small_sems)
    grad_s[...] = grad
    trade.start(grad_s, later_grad[0], trade_sems)
    beside.middle(*beside_refs)
    dense_sum.middle1(*dense_refs)
    small_sum.second(small_sems)
    dense_sum.middle2(*dense_refs)
    small_sum.third(small_sems)
    dense_sum.middle3(*dense_refs)
    trade.wait(grad_s, traded_out, trade_sems)
    small_sum.last(small_sems, small_out)
    dense_sum.wait(*dense_refs)
    beside.wait(*beside_refs)


def attention_back(layer, gains, own, other, mid_grad, stream, state, pairs, tables, ending, beside):
    count = lax.axis_size("tensor")
    qs, keys, values, probs = state
    rows, width = mid_grad.shape
    tokens = keys.shape[0]
    own, other = own[:4], other[:4]
    qw, kw = own[0].shape[1], own[1].shape[1]
    heads = qw // HD
    vmem = pl.BlockSpec(memory_space=pltpu.VMEM)
    hbm = pl.BlockSpec(memory_space=pl.ANY)
    shape = jax.ShapeDtypeStruct
    groups = lax.axis_size("dp")
    dense = shape((*factors(groups), width // 2 // groups, 2 * qw + 2 * kw), bf16)
    if ending:
        depth = 2 * (-(-(ending[0].shape[0] + 2) // 8) * 8)
        last = (DenseSum(dense, layer), SmallSum(depth, width), Trade((rows, width)))
        own_outs = (shape((2, rows, width), f32), shape((depth, width), f32), *last[0].outputs)
        more = [pltpu.VMEM((rows, width), f32), *last[2].sems, *last[0].sems, *last[1].sems]
    else:
        last, more = None, []
        own_outs = (shape((rows, width), f32), shape((1, width), f32), dense)
    found = pl.pallas_call(
        functools.partial(attention_back_kernel, layer, count, last, beside),
        name=f"attention_back_{layer}",
        out_shape=(*own_outs, *beside.outputs),
        in_specs=[vmem] * 9 + [hbm] * 10 + [vmem] * len(ending) + [hbm] * len(beside.inputs),
        out_specs=(vmem, vmem, hbm) + (hbm,) * len(beside.outputs),
        scratch_shapes=[
            pltpu.VMEM((width, qw + 2 * kw), bf16),
            pltpu.VMEM((qw, width), bf16),
            pltpu.VMEM((tokens, width), bf16),
            pltpu.VMEM((tokens, width), bf16),
            pltpu.VMEM((count - 1, rows, width), bf16),
            pltpu.VMEM((heads * tokens, HD), bf16),
            pltpu.VMEM((tokens, qw + kw), f32),
            pltpu.VMEM((tokens, qw + 2 * kw), bf16),
            pltpu.VMEM((tokens, qw + 2 * kw), bf16),
            pltpu.VMEM((2 * tokens, width // 2), bf16),
            pltpu.VMEM((2 * tokens, width // 2), bf16),
            pltpu.VMEM((width // 2, 2 * tokens), bf16),
            pltpu.VMEM((2 * tokens, qw), bf16),
            pltpu.VMEM(dense.shape, bf16),
            pltpu.SemaphoreType.DMA((3, count - 1)),
            pltpu.SemaphoreType.DMA((3, count - 1)),
            pltpu.SemaphoreType.DMA((4,)),
            *[pltpu.SemaphoreType.DMA((2,)) for _ in range(5)],
            *more,
            *beside.sems,
        ],
        compiler_params=params(5 + layer),
    )(mid_grad, stream, gains[0], *tables[:2], qs, keys, values, probs, *pairs, *own, *other,
      *ending, *beside.inputs)
    return found[:3], beside.results(found[3:])


def prepare_kernel(lengths, dealing, order, routes, attn_gain, expert_gain, router, freqs,
                   cosine, sine, bias, picked, kept, attn_gains, expert_gains, routers,
                   order_peer, routes_peer, sends, recvs):
    core = lax.axis_index("section")
    attn_gains[core] = attn_gain[...]
    expert_gains[core] = expert_gain[...]
    routers[core] = router[...]
    greet([core_peer()])
    copies = [
        remote(source, target, sends.at[index], recvs.at[index], core_peer())
        for index, (source, target) in enumerate((
            (order.at[1 - core], order_peer),
            (routes.at[1 - core], routes_peer),
            (attn_gain, attn_gains.at[core]),
            (expert_gain, expert_gains.at[core]),
            (router, routers.at[core]),
        ))
    ]
    start_all(copies)
    tokens = bias.shape[0]
    sequences = lengths.shape[1]
    tall = lax.broadcasted_iota(jnp.int32, (tokens, 1), 0)
    wide = lax.broadcasted_iota(jnp.int32, (1, tokens), 1)
    sizes = [lengths[core, index] for index in range(sequences)]
    starts = [sum(sizes[:index], 0) for index in range(sequences)]
    ranks = [
        sum(jnp.where(dealing[core, place] == index, place, 0) for place in range(sequences))
        for index in range(sequences)
    ]
    dealt_starts = [
        sum(jnp.where(ranks[before] < ranks[index], sizes[before], 0) for before in range(sequences))
        for index in range(sequences)
    ]

    def places(token):
        segment = sum((token >= starts[index] + sizes[index]).astype(jnp.int32)
                      for index in range(sequences))
        position, dealt = token, token
        for index in range(sequences):
            inside = segment == index
            position = jnp.where(inside, token - starts[index], position)
            dealt = jnp.where(inside, token - starts[index] + dealt_starts[index], dealt)
        return segment, position, dealt

    segment, position, dealt = places(tall)
    segment_wide, _, dealt_wide = places(wide)
    allowed = (segment == segment_wide) & (wide <= tall)
    bias[...] = jnp.where(allowed, 0.0, masked_score).astype(f32)
    angles = position.astype(f32) * freqs[...]
    cosine[...] = jnp.cos(angles)
    lane = lax.broadcasted_iota(jnp.int32, (1, freqs.shape[1]), 1)
    sine[...] = jnp.sin(angles) * jnp.where(lane % HD < HD // 2, -1.0, 1.0)

    def masks(order_row, route_rows):
        order_wide = order_row.astype(f32)
        order_tall = jnp.sum(jnp.where(tall == wide, order_wide, 0.0), axis=1, keepdims=True)
        first = jnp.sum(jnp.where(dealt == wide, order_wide, 0.0), axis=1, keepdims=True)
        first_wide = jnp.sum(jnp.where(dealt_wide == tall, order_tall, 0.0), axis=0, keepdims=True)
        earlier = jnp.where(first_wide < first, 1.0, 0.0).astype(bf16)
        experts = picked.shape[2]
        index = lax.broadcasted_iota(jnp.int32, (experts, tokens), 0)
        chosen = jnp.zeros((experts, tokens), f32)
        for k in range(route_rows.shape[0]):
            chosen = jnp.where(route_rows[k : k + 1] == index, 1.0, chosen)
        chosen = chosen.T
        rank = dot(earlier, chosen.astype(bf16), NN)
        return chosen, jnp.where(rank < CAP, chosen, 0.0)

    picked[core], kept[core] = masks(order[core], routes[core])
    wait_all(copies)
    picked[1 - core], kept[1 - core] = masks(order_peer[...], routes_peer[...])


def prepare(lengths, dealing, order, routes, attn_gain, expert_gain, router):
    tokens = order.shape[2]
    width = attn_gain.shape[1]
    half = HD // 2
    freqs = jnp.tile(rope_base ** (-2.0 * jnp.arange(half, dtype=f32) / HD), 128 // half)[None]
    vmem = pl.BlockSpec(memory_space=pltpu.VMEM)
    smem = pl.BlockSpec(memory_space=pltpu.SMEM)
    shape = jax.ShapeDtypeStruct
    found = pl.pallas_call(
        prepare_kernel,
        name="prepare",
        out_shape=(
            shape((tokens, 128), f32),
            shape((tokens, 128), f32),
            shape((tokens, tokens), f32),
            shape((2, tokens, E), f32),
            shape((2, tokens, E), f32),
            shape((2, 1, width), f32),
            shape((2, 1, width), f32),
            shape((2, *router.shape), bf16),
        ),
        in_specs=[smem] * 2 + [vmem] * 6,
        out_specs=(vmem,) * 8,
        scratch_shapes=[
            pltpu.VMEM(order.shape[1:], order.dtype),
            pltpu.VMEM(routes.shape[1:], routes.dtype),
            dma((5,)),
            dma((5,)),
        ],
        compiler_params=params(8),
    )(lengths, dealing, order, routes, attn_gain, expert_gain, router, freqs)
    return found[:3], found[3:5], found[5:]


def assemble_kernel(section, *refs):
    expert_refs, dense_refs, outs = (refs[:4], refs[4:8]), refs[8:10], refs[10:]
    query, key, value, output, gate, up, down = outs
    hidden_width = gate.shape[2]
    qw, kw = query.shape[1], key.shape[1]

    def write(parts, dense):
        cores = range(2)
        pair = [[jnp.sum(v[core, :, 0].astype(f32), axis=0) for v in parts[:2]] for core in cores]
        depth = 0
        for block in pair[0] + pair[1]:
            rows = pl.ds(depth, block.shape[0])
            gate[0, rows, :] = block[:, :hidden_width]
            up[0, rows, :] = block[:, hidden_width:]
            depth += block.shape[0]
        depth = 0
        for core in cores:
            for v in parts[2:]:
                block = jnp.sum(v[core, :, 0].astype(f32), axis=0)
                down[0, :, pl.ds(depth, block.shape[1])] = block
                depth += block.shape[1]
        rows = dense[...].astype(f32)
        query[...] = rows[:, :qw]
        key[...] = rows[:, qw : qw + kw]
        value[...] = rows[:, qw + kw : qw + 2 * kw]
        output[...] = rows[:, qw + 2 * kw :].T

    pl.when(section[0] == 0)(lambda: write(expert_refs[0], dense_refs[0]))
    pl.when(section[0] == 1)(lambda: write(expert_refs[1], dense_refs[1]))


def assemble(parts, denses, qw, kw):
    groups = parts[0][0].shape[2]
    hidden_width = parts[0][2].shape[3]
    dense = [v.reshape(-1, v.shape[-1]) for v in denses]
    depth = dense[0].shape[0]
    rows = depth // groups

    def part_spec(layer, shape):
        block = (*shape[:2], 1, *shape[3:])
        return pl.BlockSpec(block, lambda e, s: (0, 0, jnp.where(s[0] == layer, e, 0), 0, 0))

    def dense_spec(layer, width):
        return pl.BlockSpec((rows, width), lambda e, s: (jnp.where(s[0] == layer, e, 0), 0))

    shape = jax.ShapeDtypeStruct
    return pl.pallas_call(
        assemble_kernel,
        name="assemble",
        out_shape=(
            shape((depth, qw), f32),
            shape((depth, kw), f32),
            shape((depth, kw), f32),
            shape((qw, depth), f32),
            shape((groups, depth, hidden_width), f32),
            shape((groups, depth, hidden_width), f32),
            shape((groups, hidden_width, depth), f32),
        ),
        grid_spec=pltpu.PrefetchScalarGridSpec(
            num_scalar_prefetch=1,
            grid=(groups,),
            in_specs=[part_spec(layer, v.shape) for layer in range(2) for v in parts[layer]]
            + [dense_spec(layer, dense[layer].shape[1]) for layer in range(2)],
            out_specs=(
                pl.BlockSpec((rows, qw), lambda e, s: (e, 0)),
                pl.BlockSpec((rows, kw), lambda e, s: (e, 0)),
                pl.BlockSpec((rows, kw), lambda e, s: (e, 0)),
                pl.BlockSpec((qw, rows), lambda e, s: (0, e)),
                pl.BlockSpec((1, depth, hidden_width), lambda e, s: (e, 0, 0)),
                pl.BlockSpec((1, depth, hidden_width), lambda e, s: (e, 0, 0)),
                pl.BlockSpec((1, hidden_width, depth), lambda e, s: (e, 0, 0)),
            ),
        ),
        compiler_params=pltpu.CompilerParams(vmem_limit_bytes=58 * 2**20),
    )(lax.axis_index("section").astype(jnp.int32)[None], *parts[0], *parts[1], *dense)


def shards(
    tokens_in, out_cotangent, attn_gain, query_weight, key_weight, value_weight, output_weight,
    expert_gain, router_weight, gate_weight, up_weight, down_weight, lengths, dealing,
    slot_order, routes,
):
    first = lax.axis_index("section") == 0
    qw, kw = query_weight.shape[2], key_weight.shape[2]
    own = (query_weight[0], key_weight[0], value_weight[0], output_weight[0], gate_weight[0],
           up_weight[0], down_weight[0])
    tables, masks, gains = prepare(lengths[:, 0], dealing[:, 0], slot_order[0],
                                   jnp.swapaxes(routes[0], 1, 2), attn_gain, expert_gain,
                                   router_weight[0].T)
    (out0, *state0), other = layer_forward(0, gains, own, None, tokens_in, tables, masks)
    (out1, *state1), _ = layer_forward(1, gains, own, other, out0, tables, masks)
    saved = (state0, state1)
    streams = (tokens_in, out0)

    def experts(layer, out_grad, traded, jobs):
        mid, expert_rows, qs, keys, values, probs, gate, ai, x, gated, attended, pre = saved[layer]
        return experts_back(
            layer, gains, own, other, out_grad, (mid, gate, expert_rows, pre), (x, gated), masks,
            traded, Beside(jobs)
        )

    def attention(layer, mid_grad, ending, jobs):
        mid, expert_rows, qs, keys, values, probs, gate, ai, x, gated, attended, pre = saved[layer]
        return attention_back(
            layer, gains, own, other, mid_grad, streams[layer], (qs, keys, values, probs),
            (ai, attended), tables, ending, Beside(jobs)
        )

    def bring(layer, sums):
        return [Bring(layer, kind, v) for kind, v in zip(("column", "row"), sums)]

    (mid_grad, router1, gain1, pair, layer_outputs), down1, _ = experts(
        1, out_cotangent, (out0, out1), []
    )
    (grad1, attn_gain1, dense1), (sums,) = attention(1, mid_grad, (), [FirstStage(pair, 1)])
    (mid_grad, router0, gain0, pair), sums0, (*pair1, dense1) = experts(
        0, grad1, (), bring(1, sums) + [DenseSum(dense1, 1)]
    )
    (input_grads, small, dense0), (pair0, *down0) = attention(
        0, mid_grad, (router0, gain0, router1, attn_gain1, gain1, grad1),
        [FirstStage(pair, 1, 0), *bring(0, sums0)]
    )
    parts0, parts1 = [*pair0, *down0], [*pair1, *down1]
    query, key, value, output, gate, up, down = assemble((parts0, parts1), (dense0, dense1), qw, kw)
    small = jnp.where(first, small[: small.shape[0] // 2], small[small.shape[0] // 2 :])
    router_grad, attn_gain_grad, expert_gain_grad = small[:E].T, small[E : E + 1], small[E + 1 : E + 2]
    return (
        layer_outputs[None],
        input_grads[None],
        attn_gain_grad,
        query[None],
        key[None],
        value[None],
        output[None],
        expert_gain_grad,
        router_grad[None],
        gate[None],
        up[None],
        down[None],
    )


def solution(mesh):
    return jax.shard_map(
        shards,
        mesh=mesh,
        in_specs=(
            P(None, ("dp", "tensor"), None),
            P(None, ("dp", "tensor"), None),
            P("section", None),
            P("section", None, "tensor"),
            P("section", None, "tensor"),
            P("section", None, "tensor"),
            P("section", "tensor", None),
            P("section", None),
            P("section", None, None),
            P("section", None, None, "tensor"),
            P("section", None, None, "tensor"),
            P("section", None, "tensor", None),
            P(None, "dp", None),
            P(None, "dp", None),
            P("section", None, "dp", None),
            P("section", None, "dp", None),
        ),
        out_specs=(
            P("section", None, ("dp", "tensor"), None),
            P("section", None, ("dp", "tensor"), None),
            P("section", None),
            P("section", None, "tensor"),
            P("section", None, "tensor"),
            P("section", None, "tensor"),
            P("section", "tensor", None),
            P("section", None),
            P("section", None, None),
            P("section", "dp", None, "tensor"),
            P("section", "dp", None, "tensor"),
            P("section", "dp", "tensor", None),
        ),
        check_vma=False,
    )
```

```python
import functools
import math

import jax
import jax.numpy as jnp
import numpy as np
from jax import lax
from jax.experimental import pallas as pl
from jax.experimental.pallas import tpu as pltpu
from jax.sharding import PartitionSpec as P

H = 24
KV = 8
HD = 64
E = 16
CAP = 160

epsilon = 1e-05
rope_base = 10000.0
masked_score = -1e30
bf16 = jnp.bfloat16
f32 = jnp.float32
MESH = pl.DeviceIdType.MESH


def dot(a, b, dims):
    return lax.dot_general(a, b, (dims, ((), ())), preferred_element_type=f32)


NN = ((1,), (0,))
NT = ((1,), (1,))
TN = ((0,), (0,))


def norm_scale(rows_in):
    return lax.rsqrt(jnp.mean(rows_in * rows_in, axis=-1, keepdims=True) + epsilon)


def params(collective_id):
    return pltpu.CompilerParams(
        collective_id=collective_id, has_side_effects=True, vmem_limit_bytes=56 * 2**20
    )


def tensor_peers(count):
    me = lax.axis_index("tensor")
    return [{"tensor": lax.rem(me + step, count)} for step in range(1, count)]


def greet(peers):
    barrier = pltpu.get_barrier_semaphore()
    for peer in peers:
        pl.semaphore_signal(barrier, inc=1, device_id=peer, device_id_type=MESH)
    pl.semaphore_wait(barrier, len(peers))


def factors(count):
    inner = math.isqrt(count)
    while count % inner:
        inner -= 1
    return count // inner, inner


def group_place(count):
    outer, inner = factors(count)
    me = lax.axis_index("dp")
    return outer, inner, me // inner, lax.rem(me, inner)


def near_groups(count):
    outer, inner, mo, mi = group_place(count)
    across = [lax.rem(mi + step, inner) for step in range(1, inner)]
    along = [lax.rem(mo + step, outer) for step in range(1, outer)]
    return (
        [(place, {"dp": mo * inner + place}) for place in across],
        [(place, {"dp": place * inner + mi}) for place in along],
    )


dma = pltpu.SemaphoreType.DMA


def remote(src, dst, send, recv, device):
    return pltpu.make_async_remote_copy(
        src_ref=src, dst_ref=dst, send_sem=send, recv_sem=recv, device_id=device, device_id_type=MESH
    )


class Bring:
    def __init__(self, layer, kind, value, in_vmem=False, target=None):
        self.layer, self.kind, self.in_vmem = layer, kind, in_vmem
        self.whole = kind == "all" or target is not None
        self.target = target or (lambda outputs, core, place: outputs[0].at[core, place])
        count = lax.axis_size("dp")
        outer, inner = factors(count)
        self.size = {"column": outer, "row": inner, "all": count}[kind]
        block = value.shape if self.whole else value.shape[1:]
        self.inputs = [value]
        self.outputs = [jax.ShapeDtypeStruct((2, self.size, *block), value.dtype)]
        self.sems = [dma((self.size,)), dma((2, self.size)), dma((2,))]
        if not in_vmem:
            self.sems.append(pltpu.VMEM(block, value.dtype))

    def place(self, step):
        count = lax.axis_size("dp")
        outer, inner, mo, mi = group_place(count)
        if self.kind == "column":
            place = lax.rem(mo + step, outer)
            return place, place * inner + mi
        if self.kind == "row":
            place = lax.rem(mi + step, inner)
            return place, mo * inner + place
        place = lax.rem(lax.axis_index("dp") + step, count)
        return place, place

    def parts(self, inputs, outputs, sems):
        core = lax.axis_index("section")
        mine, _ = self.place(0)
        target = self.target(outputs, core, mine)
        recv = sems[1].at[core, mine]

        def source(place):
            return inputs[0] if self.whole else inputs[0].at[place]

        sent = []
        for step in range(1, self.size):
            place, group = self.place(step)
            sent.append(
                remote(source(place), target, sems[0].at[step - 1], recv,
                       {"dp": group, "section": self.layer})
            )
        across = remote(source(mine), target, sems[0].at[self.size - 1], recv, core_peer())
        if self.in_vmem:
            local = [pltpu.make_async_copy(source(mine), target, sems[2].at[0])]
        else:
            local = [
                pltpu.make_async_copy(source(mine), sems[3], sems[2].at[0]),
                pltpu.make_async_copy(sems[3], target, sems[2].at[1]),
            ]
        return sent, across, local

    def start(self, inputs, outputs, sems):
        sent, across, local = self.parts(inputs, outputs, sems)
        for copy in sent:
            copy.start()
        here = lax.axis_index("section") == self.layer

        @pl.when(here)
        def _():
            local[0].start()

        @pl.when(jnp.logical_not(here))
        def _():
            across.start()

    def wait(self, inputs, outputs, sems):
        sent, across, local = self.parts(inputs, outputs, sems)
        core = lax.axis_index("section")
        here = core == self.layer
        block = inputs[0] if self.whole else inputs[0].at[0]

        def arrived(which, place):
            remote(block, self.target(outputs, which, place), sems[0].at[0], sems[1].at[which, place],
                   core_peer()).wait_recv()

        for copy in sent:
            copy.wait_send()

        @pl.when(here)
        def _():
            local[0].wait()
            for copy in local[1:]:
                copy.start()
                copy.wait()
            for step in range(self.size):
                place, _ = self.place(step)
                if step:
                    arrived(core, place)
                arrived(1 - core, place)

        @pl.when(jnp.logical_not(here))
        def _():
            across.wait_send()

    def results(self, outputs):
        return outputs[0]


class FirstStage:
    def __init__(self, value, axis, layer=None):
        self.count = lax.axis_size("dp")
        outer, inner = factors(self.count)
        self.blocks = (outer, inner, value.shape[0] // self.count, *value.shape[1:])
        inside = isinstance(value, jax.ShapeDtypeStruct)
        self.inputs = [] if inside else [value.reshape(self.blocks)]
        self.axis = axis
        shape = list(self.blocks[2:])
        shape[axis] //= 2
        self.shape = shape
        sums = [
            jax.ShapeDtypeStruct((outer, *shape), value.dtype),
            jax.ShapeDtypeStruct((inner, *shape), value.dtype),
        ]
        self.sems = [
            dma((inner + outer - 2,)),
            dma((inner + outer - 2,)),
            pltpu.VMEM((inner - 1, outer, *shape), value.dtype),
            pltpu.VMEM((outer - 1, inner, *shape), value.dtype),
            *[pltpu.VMEM(v.shape, v.dtype) for v in sums],
            dma((2,)),
            dma((2,)),
        ]
        self.outputs = sums
        self.brings = []
        if layer is not None:
            self.brings = [Bring(layer, kind, v, True) for kind, v in zip(("column", "row"), sums)]
            self.outputs = [v for bring in self.brings for v in bring.outputs]
            self.sems += [v for bring in self.brings for v in bring.sems]

    def copies(self, inputs, sems):
        across, along = near_groups(self.count)
        _, _, mo, mi = group_place(self.count)
        value = inputs[0]
        half = self.shape[self.axis]
        cut = [slice(None)] * 3
        first, second = list(cut), list(cut)
        first[self.axis], second[self.axis] = pl.ds(0, half), pl.ds(half, half)
        found = []
        for slot, (place, device) in enumerate(across):
            found.append((value.at[(slice(None), place, *first)], sems[2].at[slot], device))
        for slot, (place, device) in enumerate(along):
            found.append((value.at[(place, slice(None), *second)], sems[3].at[slot], device))
        sent = [
            remote(src, dst, sems[0].at[index], sems[1].at[index], device)
            for index, (src, dst, device) in enumerate(found)
        ]
        loads = [
            pltpu.make_async_copy(value.at[(slice(None), mi, *first)], sems[4], sems[6].at[0]),
            pltpu.make_async_copy(value.at[(mo, slice(None), *second)], sems[5], sems[6].at[1]),
        ]
        return sent + loads

    def onward(self, outputs, sems):
        place = 8
        found = []
        for index, bring in enumerate(self.brings):
            found.append((bring, [sems[4 + index]], [outputs[index]], sems[place : place + len(bring.sems)]))
            place += len(bring.sems)
        return found

    def saves(self, outputs, sems):
        return [pltpu.make_async_copy(sems[4 + k], outputs[k], sems[7].at[k]) for k in range(2)]

    def start(self, inputs, outputs, sems):
        start_all(self.copies(inputs, sems))

    def middle(self, inputs, outputs, sems):
        wait_all(self.copies(inputs, sems))
        for total, landed in ((sems[4], sems[2]), (sems[5], sems[3])):
            depth = total.shape[1]

            def add(index, carry, total=total, landed=landed, depth=depth):
                place, expert = index // depth, lax.rem(index, depth)
                value = total[place, expert].astype(f32)
                for slot in range(landed.shape[0]):
                    value = value + landed[slot, place, expert].astype(f32)
                total[place, expert] = value.astype(bf16)
                return carry

            lax.fori_loop(0, total.shape[0] * depth, add, 0)
        if self.brings:
            for bring, *refs in self.onward(outputs, sems):
                bring.start(*refs)
        else:
            start_all(self.saves(outputs, sems))

    def wait(self, inputs, outputs, sems):
        if self.brings:
            for bring, *refs in self.onward(outputs, sems):
                bring.wait(*refs)
        else:
            wait_all(self.saves(outputs, sems))

    def results(self, outputs):
        return outputs


class DenseSum:
    def __init__(self, value, layer):
        count = lax.axis_size("dp")
        outer, inner = factors(count)
        rows, width = value.shape[2:]
        half = width // 2
        self.half = half
        inside = isinstance(value, jax.ShapeDtypeStruct)
        self.inputs = [] if inside else [value]
        self.outputs = [jax.ShapeDtypeStruct((2, *value.shape), bf16)]

        def buffer(*lead):
            return pltpu.VMEM((*lead, rows, half), bf16)

        self.brings = [
            Bring(layer, "row", jax.ShapeDtypeStruct((outer, rows, half), bf16), True,
                  lambda outputs, core, place: outputs[0].at[core, :, place, :, pl.ds(0, half)]),
            Bring(layer, "column", jax.ShapeDtypeStruct((inner, rows, half), bf16), True,
                  lambda outputs, core, place: outputs[0].at[core, place, :, :, pl.ds(half, half)]),
        ]
        pairs = inner + outer - 2
        self.sems = [
            buffer(inner - 1, outer),
            buffer(outer - 1, inner),
            buffer(outer),
            buffer(inner),
            buffer(outer - 1),
            buffer(inner - 1),
            buffer(outer),
            buffer(inner),
            dma((2,)),
            *[dma((pairs,)) for _ in range(6)],
            *[v for bring in self.brings for v in bring.sems],
        ]

    def numbered(self, found, sems, first):
        return [
            remote(src, dst, sems[first].at[index], sems[first + 1].at[index], device)
            for index, (src, dst, device) in enumerate(found)
        ]

    def sent(self, inputs, sems):
        count = lax.axis_size("dp")
        across, along = near_groups(count)
        _, _, mo, mi = group_place(count)
        value = inputs[0]
        low, high = pl.ds(0, self.half), pl.ds(self.half, self.half)
        found = [
            (value.at[:, place, :, low], sems[0].at[slot], device)
            for slot, (place, device) in enumerate(across)
        ] + [
            (value.at[place, :, :, high], sems[1].at[slot], device)
            for slot, (place, device) in enumerate(along)
        ]
        loads = [
            pltpu.make_async_copy(value.at[:, mi, :, low], sems[2], sems[8].at[0]),
            pltpu.make_async_copy(value.at[mo, :, :, high], sems[3], sems[8].at[1]),
        ]
        return self.numbered(found, sems, 9) + loads

    def sums(self, sems):
        across, along = near_groups(lax.axis_size("dp"))
        found = [
            (sems[2].at[place], sems[4].at[slot], device) for slot, (place, device) in enumerate(along)
        ] + [
            (sems[3].at[place], sems[5].at[slot], device) for slot, (place, device) in enumerate(across)
        ]
        return self.numbered(found, sems, 11)

    def blocks(self, sems):
        count = lax.axis_size("dp")
        across, along = near_groups(count)
        _, _, mo, mi = group_place(count)
        found = [(sems[6].at[mo], sems[6].at[mo], device) for _, device in along]
        found += [(sems[7].at[mi], sems[7].at[mi], device) for _, device in across]
        return self.numbered(found, sems, 13)

    def onward(self, outputs, sems):
        place = 15
        found = []
        for index, bring in enumerate(self.brings):
            found.append((bring, [sems[6 + index]], outputs, sems[place : place + len(bring.sems)]))
            place += len(bring.sems)
        return found

    def start(self, inputs, outputs, sems):
        start_all(self.sent(inputs, sems))

    def middle1(self, inputs, outputs, sems):
        wait_all(self.sent(inputs, sems))
        for total, landed in ((sems[2], sems[0]), (sems[3], sems[1])):
            for place in range(total.shape[0]):
                value = total[place].astype(f32)
                for slot in range(landed.shape[0]):
                    value = value + landed[slot, place].astype(f32)
                total[place] = value.astype(bf16)
        start_all(self.sums(sems))

    def middle2(self, inputs, outputs, sems):
        wait_all(self.sums(sems))
        _, _, mo, mi = group_place(lax.axis_size("dp"))
        for total, landed, whole, mine in (
            (sems[2], sems[4], sems[6], mo),
            (sems[3], sems[5], sems[7], mi),
        ):
            value = total[mine].astype(f32)
            for slot in range(landed.shape[0]):
                value = value + landed[slot].astype(f32)
            whole[mine] = value.astype(bf16)
        start_all(self.blocks(sems))

    def middle3(self, inputs, outputs, sems):
        wait_all(self.blocks(sems))
        for bring, *refs in self.onward(outputs, sems):
            bring.start(*refs)

    def wait(self, inputs, outputs, sems):
        for bring, *refs in self.onward(outputs, sems):
            bring.wait(*refs)

    def results(self, outputs):
        return outputs[0]


class SmallSum:
    def __init__(self, depth, width):
        self.tensor, self.count = lax.axis_size("tensor"), lax.axis_size("dp")
        self.lanes = width // self.tensor
        self.depth = depth
        part = (depth, self.lanes)
        self.sems = [
            pltpu.VMEM((depth, width), f32),
            pltpu.VMEM((self.tensor - 1, *part), f32),
            pltpu.VMEM((self.count - 1, *part), f32),
            *[pltpu.VMEM(part, f32) for _ in range(4)],
            pltpu.VMEM((depth, width), f32),
            dma((2, self.tensor - 1)),
            dma((2, self.tensor - 1)),
            dma((self.count,)),
            dma((self.count,)),
        ]

    def columns(self, place):
        return pl.ds(pl.multiple_of(place * self.lanes, self.lanes), self.lanes)

    def over_tensor(self, sems):
        here = lax.axis_index("tensor")
        found = []
        for step in range(1, self.tensor):
            place = lax.rem(here + step, self.tensor)
            found.append(
                remote(sems[0].at[:, self.columns(place)], sems[1].at[step - 1],
                       sems[8].at[0, step - 1], sems[9].at[0, step - 1], {"tensor": place})
            )
        return found

    def over_groups(self, sems):
        me = lax.axis_index("dp")
        return [
            remote(sems[3], sems[2].at[step - 1], sems[10].at[step - 1], sems[11].at[step - 1],
                   {"dp": lax.rem(me + step, self.count)})
            for step in range(1, self.count)
        ]

    def over_cores(self, sems):
        last = self.count - 1
        return [remote(sems[4], sems[5], sems[10].at[last], sems[11].at[last], core_peer())]

    def back(self, sems):
        here = lax.axis_index("tensor")
        own = sems[7].at[:, self.columns(here)]
        return [
            remote(sems[6], own, sems[8].at[1, step - 1], sems[9].at[1, step - 1],
                   {"tensor": lax.rem(here + step, self.tensor)})
            for step in range(1, self.tensor)
        ]

    def first(self, sems):
        start_all(self.over_tensor(sems))

    def second(self, sems):
        wait_all(self.over_tensor(sems))
        total = sems[0][:, self.columns(lax.axis_index("tensor"))]
        for slot in range(self.tensor - 1):
            total = total + sems[1][slot]
        sems[3][...] = total
        start_all(self.over_groups(sems))

    def third(self, sems):
        wait_all(self.over_groups(sems))
        total = sems[3][...]
        for slot in range(self.count - 1):
            total = total + sems[2][slot]
        sems[4][...] = total
        copies = self.over_cores(sems)
        start_all(copies)
        wait_all(copies)
        sems[6][...] = sems[4][...] + sems[5][...]
        start_all(self.back(sems))
        sems[7][:, self.columns(lax.axis_index("tensor"))] = sems[6][...]

    def last(self, sems, out):
        wait_all(self.back(sems))
        out[...] = sems[7][...]


class Trade:
    def __init__(self, shape):
        self.sems = [pltpu.VMEM((2, *shape), f32), dma((1,)), dma((1,))]

    def copy(self, value, sems):
        core = lax.axis_index("section")
        return remote(value, sems[0].at[core], sems[1].at[0], sems[2].at[0], core_peer())

    def start(self, zero, one, sems):
        core = lax.axis_index("section")

        @pl.when(core == 0)
        def _():
            self.copy(one, sems).start()
            sems[0][0] = zero[...]

        @pl.when(core == 1)
        def _():
            self.copy(zero, sems).start()
            sems[0][1] = one[...]

    def wait(self, zero, out, sems):
        self.copy(zero, sems).wait()
        out[...] = sems[0][...]


def both_cores(groups):
    core = lax.axis_index("section")
    return [{"dp": group, "section": which} for group in groups for which in (core, 1 - core)]


def whole_group():
    count = lax.axis_size("dp")
    me = lax.axis_index("dp")
    return both_cores([lax.rem(me + step, count) for step in range(1, count)])


class Beside:
    def __init__(self, jobs):
        self.jobs = jobs
        self.inputs = [v for job in jobs for v in job.inputs]
        self.outputs = [v for job in jobs for v in job.outputs]
        self.sems = [v for job in jobs for v in job.sems]

    def peers(self):
        count = lax.axis_size("dp")
        if not self.jobs:
            return []
        across, along = near_groups(count)
        return both_cores([device["dp"] for _, device in across + along])

    def each(self, refs, run):
        inputs, outputs, sems = refs
        for job in self.jobs:
            mine, inputs = inputs[: len(job.inputs)], inputs[len(job.inputs) :]
            theirs, outputs = outputs[: len(job.outputs)], outputs[len(job.outputs) :]
            own, sems = sems[: len(job.sems)], sems[len(job.sems) :]
            run(job)(mine, theirs, own)

    def start(self, *refs):
        self.each(refs, lambda job: job.start)

    def middle(self, *refs, step="middle"):
        self.each(refs, lambda job: getattr(job, step, lambda *refs: None))

    def wait(self, *refs):
        self.each(refs, lambda job: job.wait)

    def results(self, outputs):
        found = []
        for job in self.jobs:
            found.append(job.results(outputs[: len(job.outputs)]))
            outputs = outputs[len(job.outputs) :]
        return found


def deal_out(count, part, rows, columns, landing, sends, recvs):
    me = lax.axis_index("tensor")
    copies = []
    for step in range(1, count):
        peer = lax.rem(me + step, count)
        copies.append(
            pltpu.make_async_remote_copy(
                src_ref=part.at[pl.ds(pl.multiple_of(peer * rows, rows), rows), columns],
                dst_ref=landing.at[step - 1, :, columns],
                send_sem=sends.at[step - 1],
                recv_sem=recvs.at[step - 1],
                device_id={"tensor": peer},
                device_id_type=MESH,
            )
        )
    for copy in copies:
        copy.start()
    return copies


class Line:
    def __init__(self, count, rows, passing=True):
        self.count, self.rows = count, rows
        self.passing = passing and count == 4
        self.me = me = lax.axis_index("tensor")
        half = me // 2
        self.partner = me + 1 - 2 * lax.rem(me, 2)
        self.far_inner, self.far_edge = 2 - half, 3 - 3 * half
        self.inner = me == 1 + half

    def cut(self, place):
        return pl.ds(pl.multiple_of(place * self.rows, self.rows), self.rows)

    def shard(self, buf, sems, place, target, index):
        buf, columns = buf if isinstance(buf, tuple) else (buf, slice(None))
        rows = buf.at[self.cut(place), columns]
        return remote(rows, rows, sems[0].at[index], sems[1].at[place], {"tensor": target})

    def gather_start(self, buf, sems):
        if self.passing:
            self.shard(buf, sems, self.me, self.far_inner, 1).start()
            self.shard(buf, sems, self.me, self.partner, 0).start()
        else:
            for step in range(1, self.count):
                self.shard(buf, sems, self.me, lax.rem(self.me + step, self.count), step - 1).start()

    def gather_wait(self, buf, sems):
        def arrived(place):
            self.shard(buf, sems, place, self.partner, 0).wait_recv()

        def left(number):
            for index in range(number):
                self.shard(buf, sems, self.me, self.partner, index).wait_send()

        if not self.passing:
            for step in range(1, self.count):
                arrived(lax.rem(self.me + step, self.count))
            left(self.count - 1)
            return

        @pl.when(self.inner)
        def _():
            arrived(self.far_inner)
            self.shard(buf, sems, self.far_inner, self.partner, 2).start()
            arrived(self.far_edge)
            self.shard(buf, sems, self.far_edge, self.partner, 3).start()
            arrived(self.partner)
            left(4)

        @pl.when(jnp.logical_not(self.inner))
        def _():
            for place in (self.partner, self.far_inner, self.far_edge):
                arrived(place)
            left(2)

    def block(self, part, place, columns, landing, slot, sems, index, target):
        return remote(part.at[self.cut(place), columns], landing.at[slot, :, columns],
                      sems[0].at[index], sems[1].at[slot], {"tensor": target})

    def scatter_start(self, part, columns, landing, sems):
        if not self.passing:
            for step in range(1, self.count):
                peer = lax.rem(self.me + step, self.count)
                self.block(part, peer, columns, landing, step - 1, sems, step - 1, peer).start()
            return

        @pl.when(self.inner)
        def _():
            self.block(part, self.partner, columns, landing, 2, sems, 0, self.partner).start()

        @pl.when(jnp.logical_not(self.inner))
        def _():
            for slot, place in enumerate((self.far_edge, self.far_inner, self.partner)):
                self.block(part, place, columns, landing, slot, sems, slot, self.partner).start()

    def scatter_relay(self, part, columns, landing, sems):
        if not self.passing:
            return

        @pl.when(self.inner)
        def _():
            for slot, place in enumerate((self.far_edge, self.far_inner)):
                self.block(part, place, columns, landing, slot, sems, 0, self.partner).wait_recv()
                landing[slot, :, columns] = (
                    landing[slot, :, columns].astype(f32) + part[self.cut(place), columns].astype(f32)
                ).astype(bf16)
                remote(landing.at[slot, :, columns], landing.at[3, :, columns], sems[0].at[1 + slot],
                       sems[1].at[3], {"tensor": place}).start()

    def scatter_wait(self, part, columns, landing, sems):
        slots = (2, 3) if self.passing else range(self.count - 1)
        for slot in slots:
            self.block(part, self.me, columns, landing, slot, sems, 0, self.partner).wait_recv()
        for index in range(3 if self.passing else self.count - 1):
            self.block(part, self.me, columns, landing, 0, sems, index, self.partner).wait_send()

    def total(self, own, landing):
        for slot in (2, 3) if self.passing else range(self.count - 1):
            own = own + landing[slot].astype(f32)
        return own

    @staticmethod
    def landing(count, rows, width):
        return pltpu.VMEM((4 if count == 4 else count - 1, rows, width), bf16)

    @staticmethod
    def sems(count, number):
        return [dma((number, count)), dma((number, count))]


def core_peer():
    return {"section": 1 - lax.axis_index("section")}


def hand_rows(value, pair, sems):
    tokens = value.shape[0]
    return [
        pltpu.make_async_copy(value, pair.at[pl.ds(0, tokens)], sems[0]),
        remote(value, pair.at[pl.ds(tokens, tokens)], sems[1], sems[2], core_peer()),
    ]


def hand_halves(value, pair, sems):
    section = lax.axis_index("section")
    tokens, half = value.shape[0], value.shape[1] // 2
    mine = value.at[:, pl.ds(pl.multiple_of(section * half, half), half)]
    other = value.at[:, pl.ds(pl.multiple_of((1 - section) * half, half), half)]
    return [
        pltpu.make_async_copy(mine, pair.at[pl.ds(0, tokens)], sems[0]),
        remote(other, pair.at[pl.ds(tokens, tokens)], sems[1], sems[2], core_peer()),
    ]


def start_all(copies):
    for copy in copies:
        copy.start()


def wait_all(copies):
    for copy in copies:
        copy.wait()


def either(use_own, own, other, run):
    @pl.when(use_own)
    def _():
        run(own)

    @pl.when(jnp.logical_not(use_own))
    def _():
        run(other)


def weight_copies(refs, scratch, sems, expert):
    gate, up, down = refs
    gu_s, down_s = scratch
    width = gate.shape[2]
    return (
        pltpu.make_async_copy(gate.at[expert], gu_s.at[expert, :, pl.ds(0, width)], sems.at[0, expert]),
        pltpu.make_async_copy(up.at[expert], gu_s.at[expert, :, pl.ds(width, width)], sems.at[1, expert]),
        pltpu.make_async_copy(
            down.at[expert], down_s.at[pl.ds(pl.multiple_of(expert * width, width), width)], sems.at[2, expert]
        ),
    )


def attn_copies(refs, scratch, sems):
    query, key, value, output = refs
    joint_s, output_s = scratch
    qw, kw = query.shape[1], key.shape[1]
    return (
        pltpu.make_async_copy(query, joint_s.at[:, pl.ds(0, qw)], sems.at[0]),
        pltpu.make_async_copy(key, joint_s.at[:, pl.ds(qw, kw)], sems.at[1]),
        pltpu.make_async_copy(value, joint_s.at[:, pl.ds(qw + kw, kw)], sems.at[2]),
        pltpu.make_async_copy(output, output_s, sems.at[3]),
    )


def turned(block):
    lane = lax.broadcasted_iota(jnp.int32, block.shape, 1)
    half = HD // 2
    return jnp.where(
        lane % HD < half, pltpu.roll(block, block.shape[1] - half, 1), pltpu.roll(block, half, 1)
    )


def column(table, index):
    lane = lax.broadcasted_iota(jnp.int32, table.shape, 1)
    return jnp.sum(jnp.where(lane == index, table, 0.0), axis=1, keepdims=True)


def swap_copies(own, other, sems, piece):
    sends, recvs = sems
    names = len(own)
    if isinstance(piece, tuple):
        name, expert = piece
        source, target = own[name].at[expert], other[name].at[expert]
        index = 4 + (name - 4) * own[4].shape[0] + expert
    else:
        source, target, index = own[piece], other[piece], piece
    return pltpu.make_async_remote_copy(
        src_ref=source, dst_ref=target, send_sem=sends.at[index], recv_sem=recvs.at[index],
        device_id=core_peer(), device_id_type=MESH,
    )


def forward_kernel(layer, count, swap, *refs):
    refs = list(refs)

    def take(number):
        taken = refs[:number]
        del refs[:number]
        return taken

    (stream_in, attn_gains, expert_gains, routers, cosine, sine, bias, pickeds, kepts) = take(9)
    attn_gain, expert_gain, router = attn_gains.at[layer], expert_gains.at[layer], routers.at[layer]
    picked, kept = pickeds.at[layer], kepts.at[layer]
    stream = stream_in.at[lax.axis_index("section")] if layer == 0 else stream_in
    own = take(7)
    other = None if swap else take(7)
    (out, mid_out, expert_rows_out, qs_out, keys_out, values_out, probs_out, gate_out,
     attn_in_out, expert_in_out, gated_out, attended_out, pre_out) = take(13)
    if swap:
        other = take(7)
    scratch = take(4)
    joint_s, output_s, gu_s, down_s = scratch
    (ag1, ag2, part, landing1, landing2, pre_s, gated_s, attended_s, send_s, recv_s, attn_sems,
     expert_sems, pre_sems, save_sems) = refs[:14]
    if swap:
        swap_sems = refs[14:]
    rows, width = stream.shape
    tokens = ag1.shape[0]
    experts = gu_s.shape[0]
    hidden_width = gu_s.shape[2] // 2
    kw = keys_out.shape[1]
    qw = attended_s.shape[1]
    heads, key_heads = qw // HD, kw // HD
    group = heads // key_heads
    me = lax.axis_index("tensor")
    own_rows = pl.ds(pl.multiple_of(me * rows, rows), rows)
    ag1_line, rs1_line, ag2_line, rs2_line = [Line(count, rows, v) for v in (True, True, False, True)]

    def sems(index):
        return send_s.at[index], recv_s.at[index]

    use_own = lax.axis_index("section") == layer

    def start_attn(w):
        for copy in attn_copies(w[:4], scratch[:2], attn_sems):
            copy.start()

    def wait_attn(w):
        for copy in attn_copies(w[:4], scratch[:2], attn_sems):
            copy.wait()

    def start_expert(w, expert):
        for copy in weight_copies(w[4:], scratch[2:], expert_sems, expert):
            copy.start()

    def wait_expert(w, expert):
        for copy in weight_copies(w[4:], scratch[2:], expert_sems, expert):
            copy.wait()

    def each_expert(run):
        def step(expert, carry):
            run(expert)
            return carry

        lax.fori_loop(0, experts, step, 0)

    def swap_expert(expert):
        return [swap_copies(own, other, swap_sems, (name, expert)) for name in (4, 5, 6)]

    value = stream[...].astype(bf16).astype(f32)
    ag1[own_rows, :] = (value * norm_scale(value) * attn_gain[...]).astype(bf16)
    greet(tensor_peers(count) + ([core_peer()] if swap else []))
    if swap:
        lead = min(4, experts)
        for piece in range(4):
            swap_copies(own, other, swap_sems, piece).start()
        each_expert(lambda expert: [c.start() for c in swap_expert(expert)] and None)

        @pl.when(use_own)
        def _():
            ag1_line.gather_start(ag1, sems(0))
            start_attn(own)
            each_expert(lambda expert: start_expert(own, expert))

        @pl.when(jnp.logical_not(use_own))
        def _():
            for piece in range(4):
                swap_copies(own, other, swap_sems, piece).wait_recv()
            start_attn(other)
            for expert in range(lead):
                for copy in swap_expert(expert):
                    copy.wait_recv()
                start_expert(other, expert)
            ag1_line.gather_start(ag1, sems(0))
    else:
        ag1_line.gather_start(ag1, sems(0))
        either(use_own, own, other, start_attn)
        either(use_own, own, other, lambda w: each_expert(lambda expert: start_expert(w, expert)))
    ag1_line.gather_wait(ag1, sems(0))
    saved = [pltpu.make_async_copy(ag1, attn_in_out, save_sems.at[0])]
    saved[0].start()
    either(use_own, own, other, wait_attn)
    proj = dot(ag1[...], joint_s[...], NN)
    for chunk in range(qw // 128):
        block = proj[:, chunk * 128 : chunk * 128 + 128]
        block = (block * cosine[...] + turned(block) * sine[...]).astype(bf16)
        for part_index in range(128 // HD):
            head = chunk * (128 // HD) + part_index
            qs_out[pl.ds(head * tokens, tokens), :] = block[:, part_index * HD : part_index * HD + HD]
    for chunk in range(kw // 128):
        block = proj[:, qw + chunk * 128 : qw + chunk * 128 + 128]
        keys_out[:, pl.ds(chunk * 128, 128)] = (
            block * cosine[...] + turned(block) * sine[...]
        ).astype(bf16)
    values_out[...] = proj[:, qw + kw :].astype(bf16)
    for g in range(key_heads):
        lanes = pl.ds(g * HD, HD)
        span = pl.ds(g * group * tokens, group * tokens)
        scores = dot(qs_out[span, :], keys_out[:, lanes], NT) * 0.125
        scores = (scores.reshape(group, tokens, tokens) + bias[...][None]).reshape(
            group * tokens, tokens
        )
        top = jnp.max(scores, axis=1, keepdims=True)
        weighed = jnp.exp(scores - top)
        probs = (weighed / jnp.sum(weighed, axis=1, keepdims=True)).astype(bf16)
        probs_out[span, :] = probs
        attended = dot(probs, values_out[:, lanes], NN).astype(bf16)
        for h in range(group):
            attended_s[:, pl.ds((g * group + h) * HD, HD)] = attended[h * tokens : (h + 1) * tokens]
    saved.append(pltpu.make_async_copy(attended_s, attended_out, save_sems.at[1]))
    saved[1].start()
    part[...] = dot(attended_s[...], output_s[...], NN).astype(bf16)
    dealt = part, slice(None), landing1, sems(1)
    rs1_line.scatter_start(*dealt)
    rs1_line.scatter_relay(*dealt)
    rs1_line.scatter_wait(*dealt)
    mid = rs1_line.total(value + part[own_rows, :].astype(f32), landing1)
    mid_out[...] = mid
    expert_rows = (mid * norm_scale(mid) * expert_gain[...]).astype(bf16)
    expert_rows_out[...] = expert_rows
    ag2[own_rows, :] = expert_rows
    split = width // 2
    columns = pl.ds(0, split), pl.ds(split, split)
    ag2_line.gather_start((ag2, columns[0]), sems(2))
    ag2_line.gather_start((ag2, columns[1]), sems(8))
    if swap:

        @pl.when(jnp.logical_not(use_own))
        def _():
            def landed(expert, carry):
                for copy in swap_expert(expert):
                    copy.wait_recv()
                start_expert(other, expert)
                return carry

            lax.fori_loop(lead, experts, landed, 0)

    ag2_line.gather_wait((ag2, columns[0]), sems(2))

    def first_step(expert, carry):
        either(use_own, own, other, lambda w: wait_expert(w, expert))
        pre_s[expert] = dot(ag2[:, columns[0]], gu_s[expert, columns[0], :], NN)
        return carry

    lax.fori_loop(0, experts, first_step, 0)
    ag2_line.gather_wait((ag2, columns[1]), sems(8))
    saved.append(pltpu.make_async_copy(ag2, expert_in_out, save_sems.at[2]))
    saved[2].start()
    logits = dot(ag2[...], router[...], NT)
    chosen = picked[...] > 0
    top = jnp.max(jnp.where(chosen, logits, masked_score), axis=1, keepdims=True)
    weighed = jnp.where(chosen, jnp.exp(logits - top), 0.0)
    gate_out[...] = weighed / jnp.sum(weighed, axis=1, keepdims=True)

    def expert_step(expert, carry):
        pre = pre_s[expert] + dot(ag2[:, columns[1]], gu_s[expert, columns[1], :], NN)
        pre_s[expert] = pre
        pltpu.make_async_copy(pre_s.at[expert], pre_out.at[expert], pre_sems.at[expert]).start()
        gate_pre, up_pre = pre[:, :hidden_width], pre[:, hidden_width:]
        hidden = (gate_pre / (1.0 + jnp.exp(-gate_pre)) * up_pre).astype(bf16).astype(f32)
        weight = column(gate_out[...] * kept[...], expert)
        gated_s[:, pl.ds(pl.multiple_of(expert * hidden_width, hidden_width), hidden_width)] = (
            hidden * weight
        ).astype(bf16)
        return carry

    lax.fori_loop(0, experts, expert_step, 0)
    saved.append(pltpu.make_async_copy(gated_s, gated_out, save_sems.at[3]))
    saved[3].start()
    tile = width // 4
    dealt = [(part, pl.ds(t * tile, tile), landing2, sems(3 + t)) for t in range(4)]
    for each in dealt:
        part[:, each[1]] = dot(gated_s[...], down_s[:, each[1]], NN).astype(bf16)
        rs2_line.scatter_start(*each)
    for each in dealt:
        rs2_line.scatter_relay(*each)
    for each in dealt:
        rs2_line.scatter_wait(*each)
    total = rs2_line.total(mid_out[...] + part[own_rows, :].astype(f32), landing2)
    out[...] = total
    wait_all(saved)
    if swap:
        for piece in range(4):
            swap_copies(own, other, swap_sems, piece).wait_send()
        each_expert(lambda expert: [c.wait_send() for c in swap_expert(expert)] and None)

        @pl.when(use_own)
        def _():
            for piece in range(4):
                swap_copies(own, other, swap_sems, piece).wait_recv()
            each_expert(lambda expert: [c.wait_recv() for c in swap_expert(expert)] and None)

    def finish(expert, carry):
        pltpu.make_async_copy(pre_s.at[expert], pre_out.at[expert], pre_sems.at[expert]).wait()
        return carry

    lax.fori_loop(0, experts, finish, 0)


def weight_scratch(own):
    query, key, value, output, gate, up, down = own
    depth = query.shape[0]
    experts, _, hidden_width = gate.shape
    return [
        pltpu.VMEM((depth, query.shape[1] + 2 * key.shape[1]), bf16),
        pltpu.VMEM(output.shape, bf16),
        pltpu.VMEM((experts, depth, 2 * hidden_width), bf16),
        pltpu.VMEM((experts * hidden_width, depth), bf16),
    ]


def layer_forward(layer, gains, own, other, stream, tables, masks):
    count = lax.axis_size("tensor")
    rows, width = stream.shape[-2:]
    tokens = tables[2].shape[0]
    qw, kw = own[0].shape[1], own[1].shape[1]
    experts, _, hidden_width = own[4].shape
    heads = qw // HD
    swap = other is None
    vmem = pl.BlockSpec(memory_space=pltpu.VMEM)
    hbm = pl.BlockSpec(memory_space=pl.ANY)
    shape = jax.ShapeDtypeStruct
    pieces = 4 + 3 * experts
    found = pl.pallas_call(
        functools.partial(forward_kernel, layer, count, swap),
        name=f"layer_forward_{layer}",
        out_shape=(
            shape((rows, width), f32),
            shape((rows, width), f32),
            shape((rows, width), bf16),
            shape((heads * tokens, HD), bf16),
            shape((tokens, kw), bf16),
            shape((tokens, kw), bf16),
            shape((heads * tokens, tokens), bf16),
            shape((tokens, experts), f32),
            shape((tokens, width), bf16),
            shape((tokens, width), bf16),
            shape((tokens, experts * hidden_width), bf16),
            shape((tokens, qw), bf16),
            shape((experts, tokens, 2 * hidden_width), f32),
        )
        + (tuple(shape(w.shape, w.dtype) for w in own) if swap else ()),
        in_specs=[vmem] * 9 + [hbm] * (7 if swap else 14),
        out_specs=(vmem,) * 8 + (hbm,) * (12 if swap else 5),
        scratch_shapes=weight_scratch(own)
        + [
            pltpu.VMEM((tokens, width), bf16),
            pltpu.VMEM((tokens, width), bf16),
            pltpu.VMEM((tokens, width), bf16),
            Line.landing(count, rows, width),
            Line.landing(count, rows, width),
            pltpu.VMEM((experts, tokens, 2 * hidden_width), f32),
            pltpu.VMEM((tokens, experts * hidden_width), bf16),
            pltpu.VMEM((tokens, qw), bf16),
            *Line.sems(count, 9),
            dma((4,)),
            dma((3, experts)),
            dma((experts,)),
            dma((4,)),
        ]
        + ([dma((pieces,)), dma((pieces,))] if swap else []),
        compiler_params=params(1 + layer),
    )(stream, *gains, *tables, *masks, *own,
      *(() if swap else other))
    return found[:13], found[13:]


def norm_back(value, gain, out_grad):
    scale = norm_scale(value)
    scaled = value * scale
    gain_grad = jnp.sum(out_grad * scaled, axis=0, keepdims=True)
    inner = out_grad * gain
    value_grad = scale * (inner - scaled * jnp.mean(inner * scaled, axis=-1, keepdims=True))
    return value_grad, gain_grad


def experts_back_kernel(layer, count, trade, stage, beside, *refs):
    refs = list(refs)

    def take(number):
        taken = refs[:number]
        del refs[:number]
        return taken

    out_grad, mid, expert_gains, routers, kepts, gate, expert_rows, pre_in = take(8)
    expert_gain, router, kept = expert_gains.at[layer], routers.at[layer], kepts.at[layer]
    x_in, gated_in = take(2)
    own, other = take(3), take(3)
    traded = take(2 if trade else 0)
    beside_in = take(len(beside.inputs))
    mid_grad_out, router_out, expert_gain_out, pair_out = take(4)
    traded_out = take(1 if trade else 0)
    stage_out = take(len(stage.outputs))
    beside_out = take(len(beside.outputs))
    scratch = take(2)
    gu_s, down_s = scratch
    (ag1, part, landing1, pre_s, gpu_s, acc, gate_part, gate_land, og_s, gpu_peer, x_s, turned_x,
     gated_s, hidden_s, pair_s, down_grad_s, send_s, recv_s, expert_sems, pre_sems, core_send, core_recv,
     local_sems, hand_send, hand_recv, save_sems) = take(26)
    trade_sems = take(len(trade.sems) if trade else 0)
    stage_refs = ([down_grad_s], stage_out, take(len(stage.sems)))
    beside_refs = (beside_in, beside_out, refs)
    rows, width = mid.shape
    tokens = ag1.shape[0]
    experts = gu_s.shape[0]
    hidden_width = gu_s.shape[2] // 2
    me = lax.axis_index("tensor")
    own_rows = pl.ds(pl.multiple_of(me * rows, rows), rows)
    ag_line, rs_line = [Line(count, rows, v) for v in (False, False)]
    gathering = ag1, (send_s.at[0], recv_s.at[0])
    dealt = part, slice(None), landing1, (send_s.at[1], recv_s.at[1])
    use_own = lax.axis_index("section") == layer

    def start_expert(expert, carry):
        either(use_own, own, other,
               lambda w: [c.start() for c in weight_copies(w, scratch, expert_sems, expert)])
        pltpu.make_async_copy(pre_in.at[expert], pre_s.at[expert], pre_sems.at[expert]).start()
        return carry

    everyone = Beside([*beside.jobs, stage])
    if layer:
        ag1[own_rows, :] = out_grad[lax.axis_index("section")]
        greet(tensor_peers(count) + [core_peer()] + everyone.peers())
        ag_line.gather_start(*gathering)
    else:
        ag1[own_rows, :] = out_grad[...].astype(bf16)
        greet(tensor_peers(count) + [core_peer()] + everyone.peers())
        ag_line.gather_start(*gathering)
    lax.fori_loop(0, experts, start_expert, 0)
    loads = hand_halves(x_in, x_s, [v.at[0] for v in (local_sems, hand_send, hand_recv)])
    loads += hand_rows(gated_in, gated_s, [v.at[1] for v in (local_sems, hand_send, hand_recv)])
    for copy in loads:
        copy.start()
    beside.start(*beside_refs)
    if trade:
        trade.start(*traded, trade_sems)
    gate_part[...] = jnp.zeros_like(gate_part)

    def ready_step(expert, carry):
        pltpu.make_async_copy(pre_in.at[expert], pre_s.at[expert], pre_sems.at[expert]).wait()
        gate_pre = pre_s[expert, :, pl.ds(0, hidden_width)]
        up_pre = pre_s[expert, :, pl.ds(hidden_width, hidden_width)]
        sig = 1.0 / (1.0 + jnp.exp(-gate_pre))
        act = gate_pre * sig
        hidden_s[expert] = (act * up_pre).astype(bf16)
        weight = column(gate[...] * kept[...], expert)
        pre_s[expert, :, pl.ds(0, hidden_width)] = (
            weight * up_pre * (sig * (1.0 + gate_pre * (1.0 - sig)))
        )
        pre_s[expert, :, pl.ds(hidden_width, hidden_width)] = weight * act
        return carry

    lax.fori_loop(0, experts, ready_step, 0)
    ag_line.gather_wait(*gathering)
    core = lax.axis_index("section")
    half = width // 2
    og_s[pl.ds(0, tokens), :] = ag1[:, pl.ds(pl.multiple_of(core * half, half), half)]
    handed = [
        remote(ag1.at[:, pl.ds(pl.multiple_of((1 - core) * half, half), half)],
               og_s.at[pl.ds(tokens, tokens)], core_send.at[0], core_recv.at[0], core_peer())
    ]
    handed[0].start()
    wait_all(loads)
    handed[0].wait()
    _, inner, per_group = stage.blocks[:3]

    def down_step(index, carry):
        lanes = pl.ds(pl.multiple_of(index * 2 * hidden_width, 2 * hidden_width), 2 * hidden_width)
        grads = dot(gated_s[:, lanes], og_s[...], TN).astype(bf16)
        for k in range(2):
            expert = 2 * index + k
            group, place = expert // per_group, lax.rem(expert, per_group)
            down_grad_s[group // inner, lax.rem(group, inner), place] = grads[
                k * hidden_width : (k + 1) * hidden_width
            ]
        return carry

    lax.fori_loop(0, experts // 2, down_step, 0)
    stage.start(*stage_refs)
    beside.middle(*beside_refs, step="middle1")

    def expert_step(index, carry):
        pair = (2 * index, 2 * index + 1)
        for expert in pair:
            either(use_own, own, other,
                   lambda w: [c.wait() for c in weight_copies(w, scratch, expert_sems, expert)])
        lanes = pl.ds(pl.multiple_of(index * 2 * hidden_width, 2 * hidden_width), 2 * hidden_width)
        plain = dot(ag1[...], down_s[lanes, :], NT)
        lane = lax.broadcasted_iota(jnp.int32, gate_part.shape, 1)
        for k, expert in enumerate(pair):
            value = plain[:, k * hidden_width : (k + 1) * hidden_width]
            summed = jnp.sum(hidden_s[expert].astype(f32) * value, axis=1, keepdims=True)
            gate_part[...] += jnp.where(lane == expert, summed, 0.0)
            for cut in (pl.ds(0, hidden_width), pl.ds(hidden_width, hidden_width)):
                gpu_s[expert, :, cut] = (value * pre_s[expert, :, cut]).astype(bf16)
        back = dot(gpu_s[pair[0]], gu_s[pair[0]], NT) + dot(gpu_s[pair[1]], gu_s[pair[1]], NT)

        @pl.when(index == 0)
        def _():
            acc[...] = back

        @pl.when(index > 0)
        def _():
            acc[...] += back

        return carry

    lax.fori_loop(0, experts // 2, expert_step, 0)
    gate_part[:, :experts] = gate_part[:, :experts] * kept[...]
    handed.append(remote(gpu_s, gpu_peer, core_send.at[1], core_recv.at[1], core_peer()))
    handed[1].start()
    part[...] = acc[...].astype(bf16)
    rs_line.scatter_start(*dealt)
    copies = deal_out(count, gate_part, rows, slice(None), gate_land, send_s.at[2], recv_s.at[2])
    rs_line.scatter_relay(*dealt)
    beside.middle(*beside_refs, step="middle2")
    turned_x[...] = x_s[...].T
    wait_all(handed[1:])

    def saves(expert):
        return [pltpu.make_async_copy(pair_s.at[expert], pair_out.at[expert], save_sems.at[expert])]

    def grads_step(expert, carry):
        pair_s[expert] = (
            dot(turned_x[:, :tokens], gpu_s[expert], NN)
            + dot(turned_x[:, tokens:], gpu_peer[expert], NN)
        ).astype(bf16)
        for copy in saves(expert):
            copy.start()
        return carry

    lax.fori_loop(0, experts, grads_step, 0)
    beside.middle(*beside_refs, step="middle3")
    stage.middle(*stage_refs)
    wait_all(copies)
    rs_line.scatter_wait(*dealt)
    in_grad = rs_line.total(acc[own_rows, :], landing1)
    gate_grad = gate_part[own_rows, :]
    for step in range(count - 1):
        gate_grad = gate_grad + gate_land[step]
    gate_grad = gate_grad[:, :experts]
    gate_rows = gate[own_rows, :]
    logits_grad = (
        gate_rows * (gate_grad - jnp.sum(gate_rows * gate_grad, axis=1, keepdims=True))
    ).astype(bf16)
    router_out[...] = dot(logits_grad, expert_rows[...], TN)
    in_grad = in_grad + dot(logits_grad, router[...], NN)
    mid_part, expert_gain_grad = norm_back(mid[...], expert_gain[...], in_grad)
    expert_gain_out[...] = expert_gain_grad
    mid_grad_out[...] = ag1[own_rows, :].astype(f32) + mid_part

    def finish_save(expert, carry):
        for copy in saves(expert):
            copy.wait()
        return carry

    lax.fori_loop(0, experts, finish_save, 0)
    if trade:
        trade.wait(traded[0], traded_out[0], trade_sems)
    stage.wait(*stage_refs)
    beside.wait(*beside_refs)


def experts_back(layer, gains, own, other, out_grad, state, pairs, masks, traded, beside):
    count = lax.axis_size("tensor")
    mid, gate, expert_rows, pre = state
    rows, width = mid.shape
    tokens = gate.shape[0]
    own, other = own[4:], other[4:]
    trade = Trade((rows, width)) if traded else None
    experts, depth, hidden_width = own[0].shape
    stage = FirstStage(
        jax.ShapeDtypeStruct((experts, hidden_width, width // 2), bf16), 2, layer if layer else None
    )
    vmem = pl.BlockSpec(memory_space=pltpu.VMEM)
    hbm = pl.BlockSpec(memory_space=pl.ANY)
    shape = jax.ShapeDtypeStruct
    found = pl.pallas_call(
        functools.partial(experts_back_kernel, layer, count, trade, stage, beside),
        name=f"experts_back_{layer}",
        out_shape=(
            shape((rows, width), f32),
            shape((experts, width), f32),
            shape((1, width), f32),
            shape((experts, width // 2, 2 * hidden_width), bf16),
            *((shape((2, rows, width), f32),) if traded else ()),
            *stage.outputs,
            *beside.outputs,
        ),
        in_specs=[vmem] * 7 + [hbm] * 9 + [vmem] * len(traded) + [hbm] * len(beside.inputs),
        out_specs=(vmem, vmem, vmem, hbm)
        + (vmem,) * bool(traded)
        + (hbm,) * len(stage.outputs + beside.outputs),
        scratch_shapes=[
            pltpu.VMEM((experts, depth, 2 * hidden_width), bf16),
            pltpu.VMEM((experts * hidden_width, depth), bf16),
            pltpu.VMEM((tokens, width), bf16),
            pltpu.VMEM((tokens, width), bf16),
            Line.landing(count, rows, width),
            pltpu.VMEM((experts, tokens, 2 * hidden_width), f32),
            pltpu.VMEM((experts, tokens, 2 * hidden_width), bf16),
            pltpu.VMEM((tokens, width), f32),
            pltpu.VMEM((tokens, 128), f32),
            pltpu.VMEM((count - 1, rows, 128), f32),
            pltpu.VMEM((2 * tokens, width // 2), bf16),
            pltpu.VMEM((experts, tokens, 2 * hidden_width), bf16),
            pltpu.VMEM((2 * tokens, width // 2), bf16),
            pltpu.VMEM((width // 2, 2 * tokens), bf16),
            pltpu.VMEM((2 * tokens, experts * hidden_width), bf16),
            pltpu.VMEM((experts, tokens, hidden_width), bf16),
            pltpu.VMEM((experts, width // 2, 2 * hidden_width), bf16),
            pltpu.VMEM(stage.blocks, bf16),
            *Line.sems(count, 3),
            pltpu.SemaphoreType.DMA((3, experts)),
            pltpu.SemaphoreType.DMA((experts,)),
            *[pltpu.SemaphoreType.DMA((3,)) for _ in range(5)],
            pltpu.SemaphoreType.DMA((experts,)),
            *(trade.sems if trade else ()),
            *stage.sems,
            *beside.sems,
        ],
        compiler_params=params(3 + layer),
    )(out_grad, mid, *gains[1:], masks[1], gate, expert_rows, pre, *pairs, *own, *other,
      *traded, *beside.inputs)
    kept = 5 if traded else 4
    parts = kept + len(stage.outputs)
    return found[:kept], found[kept:parts], beside.results(found[parts:])


def attention_back_kernel(layer, count, last, beside, *refs):
    refs = list(refs)

    def take(number):
        taken = refs[:number]
        del refs[:number]
        return taken

    mid_grad, stream_in, attn_gains, cosine, sine, qs, keys, values, probs = take(9)
    attn_gain = attn_gains.at[layer]
    stream = stream_in.at[lax.axis_index("section")] if layer == 0 else stream_in
    ai_in, attended_in = take(2)
    own, other = take(4), take(4)
    small_parts = take(5 if last else 0)
    later_grad = take(1 if last else 0)
    beside_in = take(len(beside.inputs))
    if last:
        dense_sum, small_sum, trade = last
        traded_out, small_out, whole_out = take(3)
    else:
        grad_out, attn_gain_out, dense_out = take(3)
    beside_out = take(len(beside.outputs))
    scratch = take(2)
    joint_s, output_s = scratch
    (ag2, part, landing2, ag_stack, dq_s, joint_rows, joint_peer, ao_s, ai_s, turned_ai, attended_s,
     dense_s, send_s, recv_s, attn_sems, core_send, core_recv, local_sems,
     hand_send, hand_recv) = take(20)
    if last:
        grad_s, trade_sems = refs.pop(0), take(len(trade.sems))
        dense_sems, small_sems = take(len(dense_sum.sems)), take(len(small_sum.sems))
        dense_refs = ([dense_s], [whole_out], dense_sems)
    beside_refs = (beside_in, beside_out, refs)
    rows, width = stream.shape
    tokens = ag2.shape[0]
    kw = keys.shape[1]
    qw = output_s.shape[0]
    heads, key_heads = qw // HD, kw // HD
    group = heads // key_heads
    me = lax.axis_index("tensor")
    own_rows = pl.ds(pl.multiple_of(me * rows, rows), rows)
    ag_line, rs_line = [Line(count, rows, v) for v in (True, False)]
    gathering = ag2, (send_s.at[0], recv_s.at[0])
    use_own = lax.axis_index("section") == layer
    ag2[own_rows, :] = mid_grad[...].astype(bf16)
    everyone = Beside([*beside.jobs, dense_sum]) if last else beside
    greet(tensor_peers(count) + [core_peer()] + (whole_group() if last else everyone.peers()))
    ag_line.gather_start(*gathering)
    either(use_own, own, other, lambda w: [c.start() for c in attn_copies(w, scratch, attn_sems)])
    loads = hand_halves(ai_in, ai_s, [v.at[0] for v in (local_sems, hand_send, hand_recv)])
    loads += hand_rows(attended_in, attended_s, [v.at[1] for v in (local_sems, hand_send, hand_recv)])
    for copy in loads:
        copy.start()
    beside.start(*beside_refs)
    wait_all(loads)
    turned_ai[...] = ai_s[...].T
    ag_line.gather_wait(*gathering)
    core = lax.axis_index("section")
    half = width // 2
    ao_s[pl.ds(0, tokens), :] = ag2[:, pl.ds(pl.multiple_of(core * half, half), half)]
    handed = [
        remote(ag2.at[:, pl.ds(pl.multiple_of((1 - core) * half, half), half)],
               ao_s.at[pl.ds(tokens, tokens)], core_send.at[0], core_recv.at[0], core_peer())
    ]
    handed[0].start()
    either(use_own, own, other, lambda w: [c.wait() for c in attn_copies(w, scratch, attn_sems)])
    attended_grad = dot(ag2[...], output_s[...], NT).astype(bf16)
    for h in range(heads):
        ag_stack[pl.ds(h * tokens, tokens), :] = attended_grad[:, h * HD : (h + 1) * HD]
    for g in range(key_heads):
        lanes = pl.ds(g * HD, HD)
        span = pl.ds(g * group * tokens, group * tokens)
        soft_b = probs[span, :]
        soft = soft_b.astype(f32)
        soft_grad = dot(ag_stack[span, :], values[:, lanes], NT)
        inner = jnp.sum(soft * soft_grad, axis=1, keepdims=True)
        score_grad = (soft * (soft_grad - inner)).astype(bf16)
        dq = dot(score_grad, keys[:, lanes], NN) * 0.125
        for h in range(group):
            dq_s[:, pl.ds((g * group + h) * HD, HD)] = dq[h * tokens : (h + 1) * tokens]
        dq_s[:, pl.ds(qw + g * HD, HD)] = dot(score_grad, qs[span, :], TN) * 0.125
        joint_rows[:, pl.ds(qw + kw + g * HD, HD)] = dot(soft_b, ag_stack[span, :], TN).astype(bf16)
    for chunk in range((qw + kw) // 128):
        lanes = pl.ds(chunk * 128, 128)
        block = dq_s[:, lanes]
        joint_rows[:, lanes] = (block * cosine[...] - turned(block) * sine[...]).astype(bf16)
    handed.append(remote(joint_rows, joint_peer, core_send.at[1], core_recv.at[1], core_peer()))
    handed[1].start()
    tile = width // 2
    dealt = [
        (part, pl.ds(t * tile, tile), landing2, (send_s.at[1 + t], recv_s.at[1 + t])) for t in range(2)
    ]
    for each in dealt:
        part[:, each[1]] = dot(joint_rows[...], joint_s[each[1], :], NT).astype(bf16)
        rs_line.scatter_start(*each)
    for each in dealt:
        rs_line.scatter_relay(*each)
    wait_all(handed)
    wide = qw + 2 * kw
    joint_grads = (
        dot(turned_ai[:, :tokens], joint_rows[...], NN) + dot(turned_ai[:, tokens:], joint_peer[...], NN)
    ).astype(bf16)
    output_grads = dot(ao_s[...], attended_s[...], TN).astype(bf16)
    outer, inner, depth = dense_s.shape[:3]
    for block in range(outer * inner):
        cut = slice(block * depth, (block + 1) * depth)
        dense_s[block // inner, block % inner, :, :wide] = joint_grads[cut]
        dense_s[block // inner, block % inner, :, wide:] = output_grads[cut]
    if last:
        dense_sum.start(*dense_refs)
    else:
        save = pltpu.make_async_copy(dense_s, dense_out, local_sems.at[0])
        save.start()
    for each in dealt:
        rs_line.scatter_wait(*each)
    in_grad = rs_line.total(part[own_rows, :].astype(f32), landing2)
    stream_part, attn_gain_grad = norm_back(
        stream[...].astype(bf16).astype(f32), attn_gain[...], in_grad
    )
    grad = mid_grad[...] + stream_part
    if not last:
        attn_gain_out[...] = attn_gain_grad
        grad_out[...] = grad
        save.wait()
        beside.middle(*beside_refs)
        beside.wait(*beside_refs)
        return
    small = small_sems[0]
    router0, gain0, router1, attn_gain1, gain1 = small_parts
    place = 0
    for value in (router0[...], attn_gain_grad, gain0[...]):
        small[pl.ds(place, value.shape[0]), :] = value
        place += value.shape[0]
    place = small.shape[0] // 2
    for value in (router1[...], attn_gain1[...], gain1[...]):
        small[pl.ds(place, value.shape[0]), :] = value
        place += value.shape[0]
    small_sum.first(small_sems)
    grad_s[...] = grad
    trade.start(grad_s, later_grad[0], trade_sems)
    beside.middle(*beside_refs)
    dense_sum.middle1(*dense_refs)
    small_sum.second(small_sems)
    dense_sum.middle2(*dense_refs)
    small_sum.third(small_sems)
    dense_sum.middle3(*dense_refs)
    trade.wait(grad_s, traded_out, trade_sems)
    small_sum.last(small_sems, small_out)
    dense_sum.wait(*dense_refs)
    beside.wait(*beside_refs)


def attention_back(layer, gains, own, other, mid_grad, stream, state, pairs, tables, ending, beside):
    count = lax.axis_size("tensor")
    qs, keys, values, probs = state
    rows, width = mid_grad.shape
    tokens = keys.shape[0]
    own, other = own[:4], other[:4]
    qw, kw = own[0].shape[1], own[1].shape[1]
    heads = qw // HD
    vmem = pl.BlockSpec(memory_space=pltpu.VMEM)
    hbm = pl.BlockSpec(memory_space=pl.ANY)
    shape = jax.ShapeDtypeStruct
    groups = lax.axis_size("dp")
    dense = shape((*factors(groups), width // 2 // groups, 2 * qw + 2 * kw), bf16)
    if ending:
        depth = 2 * (-(-(ending[0].shape[0] + 2) // 8) * 8)
        last = (DenseSum(dense, layer), SmallSum(depth, width), Trade((rows, width)))
        own_outs = (shape((2, rows, width), f32), shape((depth, width), f32), *last[0].outputs)
        more = [pltpu.VMEM((rows, width), f32), *last[2].sems, *last[0].sems, *last[1].sems]
    else:
        last, more = None, []
        own_outs = (shape((rows, width), f32), shape((1, width), f32), dense)
    found = pl.pallas_call(
        functools.partial(attention_back_kernel, layer, count, last, beside),
        name=f"attention_back_{layer}",
        out_shape=(*own_outs, *beside.outputs),
        in_specs=[vmem] * 9 + [hbm] * 10 + [vmem] * len(ending) + [hbm] * len(beside.inputs),
        out_specs=(vmem, vmem, hbm) + (hbm,) * len(beside.outputs),
        scratch_shapes=[
            pltpu.VMEM((width, qw + 2 * kw), bf16),
            pltpu.VMEM((qw, width), bf16),
            pltpu.VMEM((tokens, width), bf16),
            pltpu.VMEM((tokens, width), bf16),
            Line.landing(count, rows, width),
            pltpu.VMEM((heads * tokens, HD), bf16),
            pltpu.VMEM((tokens, qw + kw), f32),
            pltpu.VMEM((tokens, qw + 2 * kw), bf16),
            pltpu.VMEM((tokens, qw + 2 * kw), bf16),
            pltpu.VMEM((2 * tokens, width // 2), bf16),
            pltpu.VMEM((2 * tokens, width // 2), bf16),
            pltpu.VMEM((width // 2, 2 * tokens), bf16),
            pltpu.VMEM((2 * tokens, qw), bf16),
            pltpu.VMEM(dense.shape, bf16),
            *Line.sems(count, 3),
            pltpu.SemaphoreType.DMA((4,)),
            *[pltpu.SemaphoreType.DMA((2,)) for _ in range(5)],
            *more,
            *beside.sems,
        ],
        compiler_params=params(5 + layer),
    )(mid_grad, stream, gains[0], *tables[:2], qs, keys, values, probs, *pairs, *own, *other,
      *ending, *beside.inputs)
    return found[:3], beside.results(found[3:])


def prepare_kernel(lengths, dealing, order, routes, attn_gain, expert_gain, router, freqs,
                   cosine, sine, bias, picked, kept, attn_gains, expert_gains, routers,
                   order_peer, routes_peer, sends, recvs):
    core = lax.axis_index("section")
    attn_gains[core] = attn_gain[...]
    expert_gains[core] = expert_gain[...]
    routers[core] = router[...]
    greet([core_peer()])
    copies = [
        remote(source, target, sends.at[index], recvs.at[index], core_peer())
        for index, (source, target) in enumerate((
            (order.at[1 - core], order_peer),
            (routes.at[1 - core], routes_peer),
            (attn_gain, attn_gains.at[core]),
            (expert_gain, expert_gains.at[core]),
            (router, routers.at[core]),
        ))
    ]
    start_all(copies)
    tokens = bias.shape[0]
    sequences = lengths.shape[1]
    tall = lax.broadcasted_iota(jnp.int32, (tokens, 1), 0)
    wide = lax.broadcasted_iota(jnp.int32, (1, tokens), 1)
    sizes = [lengths[core, index] for index in range(sequences)]
    starts = [sum(sizes[:index], 0) for index in range(sequences)]
    ranks = [
        sum(jnp.where(dealing[core, place] == index, place, 0) for place in range(sequences))
        for index in range(sequences)
    ]
    dealt_starts = [
        sum(jnp.where(ranks[before] < ranks[index], sizes[before], 0) for before in range(sequences))
        for index in range(sequences)
    ]

    def places(token):
        segment = sum((token >= starts[index] + sizes[index]).astype(jnp.int32)
                      for index in range(sequences))
        position, dealt = token, token
        for index in range(sequences):
            inside = segment == index
            position = jnp.where(inside, token - starts[index], position)
            dealt = jnp.where(inside, token - starts[index] + dealt_starts[index], dealt)
        return segment, position, dealt

    segment, position, dealt = places(tall)
    segment_wide, _, dealt_wide = places(wide)
    allowed = (segment == segment_wide) & (wide <= tall)
    bias[...] = jnp.where(allowed, 0.0, masked_score).astype(f32)
    angles = position.astype(f32) * freqs[...]
    cosine[...] = jnp.cos(angles)
    lane = lax.broadcasted_iota(jnp.int32, (1, freqs.shape[1]), 1)
    sine[...] = jnp.sin(angles) * jnp.where(lane % HD < HD // 2, -1.0, 1.0)

    def masks(order_row, route_rows):
        order_wide = order_row.astype(f32)
        order_tall = jnp.sum(jnp.where(tall == wide, order_wide, 0.0), axis=1, keepdims=True)
        first = jnp.sum(jnp.where(dealt == wide, order_wide, 0.0), axis=1, keepdims=True)
        first_wide = jnp.sum(jnp.where(dealt_wide == tall, order_tall, 0.0), axis=0, keepdims=True)
        earlier = jnp.where(first_wide < first, 1.0, 0.0).astype(bf16)
        experts = picked.shape[2]
        index = lax.broadcasted_iota(jnp.int32, (experts, tokens), 0)
        chosen = jnp.zeros((experts, tokens), f32)
        for k in range(route_rows.shape[0]):
            chosen = jnp.where(route_rows[k : k + 1] == index, 1.0, chosen)
        chosen = chosen.T
        rank = dot(earlier, chosen.astype(bf16), NN)
        return chosen, jnp.where(rank < CAP, chosen, 0.0)

    picked[core], kept[core] = masks(order[core], routes[core])
    wait_all(copies)
    picked[1 - core], kept[1 - core] = masks(order_peer[...], routes_peer[...])


def prepare(lengths, dealing, order, routes, attn_gain, expert_gain, router):
    tokens = order.shape[2]
    width = attn_gain.shape[1]
    half = HD // 2
    freqs = np.tile(rope_base ** (-2.0 * np.arange(half) / HD), 128 // half)[None].astype(np.float32)
    vmem = pl.BlockSpec(memory_space=pltpu.VMEM)
    smem = pl.BlockSpec(memory_space=pltpu.SMEM)
    shape = jax.ShapeDtypeStruct
    found = pl.pallas_call(
        prepare_kernel,
        name="prepare",
        out_shape=(
            shape((tokens, 128), f32),
            shape((tokens, 128), f32),
            shape((tokens, tokens), f32),
            shape((2, tokens, E), f32),
            shape((2, tokens, E), f32),
            shape((2, 1, width), f32),
            shape((2, 1, width), f32),
            shape((2, *router.shape), bf16),
        ),
        in_specs=[smem] * 2 + [vmem] * 6,
        out_specs=(vmem,) * 8,
        scratch_shapes=[
            pltpu.VMEM(order.shape[1:], order.dtype),
            pltpu.VMEM(routes.shape[1:], routes.dtype),
            dma((5,)),
            dma((5,)),
        ],
        compiler_params=params(8),
    )(lengths, dealing, order, routes, attn_gain, expert_gain, router, freqs)
    return found[:3], found[3:5], found[5:]


def assemble_kernel(section, *refs):
    expert_refs, dense_refs, rows_in, outs = (refs[:4], refs[4:8]), refs[8:10], refs[10:12], refs[12:]
    query, key, value, output, gate, up, down = outs[:7]
    for source, target in zip(rows_in, outs[7:]):
        target[...] = source[...]
    hidden_width = gate.shape[2]
    qw, kw = query.shape[1], key.shape[1]

    def write(parts, dense):
        cores = range(2)
        pair = [[jnp.sum(v[core, :, 0].astype(f32), axis=0) for v in parts[:2]] for core in cores]
        depth = 0
        for block in pair[0] + pair[1]:
            rows = pl.ds(depth, block.shape[0])
            gate[0, rows, :] = block[:, :hidden_width]
            up[0, rows, :] = block[:, hidden_width:]
            depth += block.shape[0]
        depth = 0
        for core in cores:
            for v in parts[2:]:
                block = jnp.sum(v[core, :, 0].astype(f32), axis=0)
                down[0, :, pl.ds(depth, block.shape[1])] = block
                depth += block.shape[1]
        rows = dense[...].astype(f32)
        query[...] = rows[:, :qw]
        key[...] = rows[:, qw : qw + kw]
        value[...] = rows[:, qw + kw : qw + 2 * kw]
        output[...] = rows[:, qw + 2 * kw :].T

    pl.when(section[0] == 0)(lambda: write(expert_refs[0], dense_refs[0]))
    pl.when(section[0] == 1)(lambda: write(expert_refs[1], dense_refs[1]))


def assemble(parts, denses, rows_in, qw, kw):
    groups = parts[0][0].shape[2]
    hidden_width = parts[0][2].shape[3]
    dense = [v.reshape(-1, v.shape[-1]) for v in denses]
    depth = dense[0].shape[0]
    rows = depth // groups

    def part_spec(layer, shape):
        block = (*shape[:2], 1, *shape[3:])
        return pl.BlockSpec(block, lambda e, s: (0, 0, jnp.where(s[0] == layer, e, 0), 0, 0))

    def dense_spec(layer, width):
        return pl.BlockSpec((rows, width), lambda e, s: (jnp.where(s[0] == layer, e, 0), 0))

    _, own_rows, width = rows_in[0].shape
    row_spec = pl.BlockSpec((2, own_rows // groups, width), lambda e, s: (0, e, 0))
    shape = jax.ShapeDtypeStruct
    return pl.pallas_call(
        assemble_kernel,
        name="assemble",
        out_shape=(
            shape((depth, qw), f32),
            shape((depth, kw), f32),
            shape((depth, kw), f32),
            shape((qw, depth), f32),
            shape((groups, depth, hidden_width), f32),
            shape((groups, depth, hidden_width), f32),
            shape((groups, hidden_width, depth), f32),
            *[shape(v.shape, f32) for v in rows_in],
        ),
        grid_spec=pltpu.PrefetchScalarGridSpec(
            num_scalar_prefetch=1,
            grid=(groups,),
            in_specs=[part_spec(layer, v.shape) for layer in range(2) for v in parts[layer]]
            + [dense_spec(layer, dense[layer].shape[1]) for layer in range(2)]
            + [row_spec] * 2,
            out_specs=(
                pl.BlockSpec((rows, qw), lambda e, s: (e, 0)),
                pl.BlockSpec((rows, kw), lambda e, s: (e, 0)),
                pl.BlockSpec((rows, kw), lambda e, s: (e, 0)),
                pl.BlockSpec((qw, rows), lambda e, s: (0, e)),
                pl.BlockSpec((1, depth, hidden_width), lambda e, s: (e, 0, 0)),
                pl.BlockSpec((1, depth, hidden_width), lambda e, s: (e, 0, 0)),
                pl.BlockSpec((1, hidden_width, depth), lambda e, s: (e, 0, 0)),
                row_spec,
                row_spec,
            ),
        ),
        compiler_params=pltpu.CompilerParams(vmem_limit_bytes=58 * 2**20),
    )(lax.axis_index("section").astype(jnp.int32)[None], *parts[0], *parts[1], *dense, *rows_in)


def shards(
    tokens_in, out_cotangent, attn_gain, query_weight, key_weight, value_weight, output_weight,
    expert_gain, router_weight, gate_weight, up_weight, down_weight, lengths, dealing,
    slot_order, routes,
):
    first = lax.axis_index("section") == 0
    qw, kw = query_weight.shape[2], key_weight.shape[2]
    own = (query_weight[0], key_weight[0], value_weight[0], output_weight[0], gate_weight[0],
           up_weight[0], down_weight[0])
    tables, masks, gains = prepare(lengths[:, 0], dealing[:, 0], slot_order[0],
                                   jnp.swapaxes(routes[0], 1, 2), attn_gain, expert_gain,
                                   router_weight[0].T)
    (out0, *state0), other = layer_forward(0, gains, own, None, tokens_in, tables, masks)
    (out1, *state1), _ = layer_forward(1, gains, own, other, out0, tables, masks)
    saved = (state0, state1)
    streams = (tokens_in, out0)

    def experts(layer, out_grad, traded, jobs):
        mid, expert_rows, qs, keys, values, probs, gate, ai, x, gated, attended, pre = saved[layer]
        return experts_back(
            layer, gains, own, other, out_grad, (mid, gate, expert_rows, pre), (x, gated), masks,
            traded, Beside(jobs)
        )

    def attention(layer, mid_grad, ending, jobs):
        mid, expert_rows, qs, keys, values, probs, gate, ai, x, gated, attended, pre = saved[layer]
        return attention_back(
            layer, gains, own, other, mid_grad, streams[layer], (qs, keys, values, probs),
            (ai, attended), tables, ending, Beside(jobs)
        )

    def bring(layer, sums):
        return [Bring(layer, kind, v) for kind, v in zip(("column", "row"), sums)]

    (mid_grad, router1, gain1, pair, layer_outputs), down1, _ = experts(
        1, out_cotangent, (out0, out1), []
    )
    (grad1, attn_gain1, dense1), (sums,) = attention(1, mid_grad, (), [FirstStage(pair, 1)])
    (mid_grad, router0, gain0, pair), sums0, (*pair1, dense1) = experts(
        0, grad1, (), bring(1, sums) + [DenseSum(dense1, 1)]
    )
    (input_grads, small, dense0), (pair0, *down0) = attention(
        0, mid_grad, (router0, gain0, router1, attn_gain1, gain1, grad1),
        [FirstStage(pair, 1, 0), *bring(0, sums0)]
    )
    parts0, parts1 = [*pair0, *down0], [*pair1, *down1]
    query, key, value, output, gate, up, down, layer_outputs, input_grads = assemble(
        (parts0, parts1), (dense0, dense1), (layer_outputs, input_grads), qw, kw
    )
    small = jnp.where(first, small[: small.shape[0] // 2], small[small.shape[0] // 2 :])
    router_grad, attn_gain_grad, expert_gain_grad = small[:E].T, small[E : E + 1], small[E + 1 : E + 2]
    return (
        layer_outputs[None],
        input_grads[None],
        attn_gain_grad,
        query[None],
        key[None],
        value[None],
        output[None],
        expert_gain_grad,
        router_grad[None],
        gate[None],
        up[None],
        down[None],
    )


def solution(mesh):
    return jax.shard_map(
        shards,
        mesh=mesh,
        in_specs=(
            P(None, ("dp", "tensor"), None),
            P(None, ("dp", "tensor"), None),
            P("section", None),
            P("section", None, "tensor"),
            P("section", None, "tensor"),
            P("section", None, "tensor"),
            P("section", "tensor", None),
            P("section", None),
            P("section", None, None),
            P("section", None, None, "tensor"),
            P("section", None, None, "tensor"),
            P("section", None, "tensor", None),
            P(None, "dp", None),
            P(None, "dp", None),
            P("section", None, "dp", None),
            P("section", None, "dp", None),
        ),
        out_specs=(
            P("section", None, ("dp", "tensor"), None),
            P("section", None, ("dp", "tensor"), None),
            P("section", None),
            P("section", None, "tensor"),
            P("section", None, "tensor"),
            P("section", None, "tensor"),
            P("section", "tensor", None),
            P("section", None),
            P("section", None, None),
            P("section", "dp", None, "tensor"),
            P("section", "dp", None, "tensor"),
            P("section", "dp", "tensor", None),
        ),
        check_vma=False,
    )
```

```python
import functools
import math

import jax
import jax.numpy as jnp
import numpy as np
from jax import lax
from jax.experimental import pallas as pl
from jax.experimental.pallas import tpu as pltpu
from jax.sharding import PartitionSpec as P

H = 24
KV = 8
HD = 64
E = 16
CAP = 160

epsilon = 1e-05
rope_base = 10000.0
masked_score = -1e30
bf16 = jnp.bfloat16
f32 = jnp.float32
MESH = pl.DeviceIdType.MESH


def dot(a, b, dims):
    return lax.dot_general(a, b, (dims, ((), ())), preferred_element_type=f32)


NN = ((1,), (0,))
NT = ((1,), (1,))
TN = ((0,), (0,))


def norm_scale(rows_in):
    return lax.rsqrt(jnp.mean(rows_in * rows_in, axis=-1, keepdims=True) + epsilon)


def params(collective_id):
    return pltpu.CompilerParams(
        collective_id=collective_id, has_side_effects=True, vmem_limit_bytes=56 * 2**20
    )


def tensor_peers(count):
    me = lax.axis_index("tensor")
    return [{"tensor": lax.rem(me + step, count)} for step in range(1, count)]


def greet(peers):
    barrier = pltpu.get_barrier_semaphore()
    for peer in peers:
        pl.semaphore_signal(barrier, inc=1, device_id=peer, device_id_type=MESH)
    pl.semaphore_wait(barrier, len(peers))


def factors(count):
    inner = math.isqrt(count)
    while count % inner:
        inner -= 1
    return count // inner, inner


def group_place(count):
    outer, inner = factors(count)
    me = lax.axis_index("dp")
    return outer, inner, me // inner, lax.rem(me, inner)


def near_groups(count):
    outer, inner, mo, mi = group_place(count)
    across = [lax.rem(mi + step, inner) for step in range(1, inner)]
    along = [lax.rem(mo + step, outer) for step in range(1, outer)]
    return (
        [(place, {"dp": mo * inner + place}) for place in across],
        [(place, {"dp": place * inner + mi}) for place in along],
    )


dma = pltpu.SemaphoreType.DMA


def remote(src, dst, send, recv, device):
    return pltpu.make_async_remote_copy(
        src_ref=src, dst_ref=dst, send_sem=send, recv_sem=recv, device_id=device, device_id_type=MESH
    )


class Bring:
    def __init__(self, layer, kind, value, in_vmem=False, target=None):
        self.layer, self.kind, self.in_vmem = layer, kind, in_vmem
        self.whole = kind == "all" or target is not None
        self.target = target or (lambda outputs, core, place: outputs[0].at[core, place])
        count = lax.axis_size("dp")
        outer, inner = factors(count)
        self.size = {"column": outer, "row": inner, "all": count}[kind]
        block = value.shape if self.whole else value.shape[1:]
        self.inputs = [value]
        self.outputs = [jax.ShapeDtypeStruct((2, self.size, *block), value.dtype)]
        self.sems = [dma((self.size,)), dma((2, self.size)), dma((2,))]
        if not in_vmem:
            self.sems.append(pltpu.VMEM(block, value.dtype))

    def place(self, step):
        count = lax.axis_size("dp")
        outer, inner, mo, mi = group_place(count)
        if self.kind == "column":
            place = lax.rem(mo + step, outer)
            return place, place * inner + mi
        if self.kind == "row":
            place = lax.rem(mi + step, inner)
            return place, mo * inner + place
        place = lax.rem(lax.axis_index("dp") + step, count)
        return place, place

    def parts(self, inputs, outputs, sems):
        core = lax.axis_index("section")
        mine, _ = self.place(0)
        target = self.target(outputs, core, mine)
        recv = sems[1].at[core, mine]

        def source(place):
            return inputs[0] if self.whole else inputs[0].at[place]

        sent = []
        for step in range(1, self.size):
            place, group = self.place(step)
            sent.append(
                remote(source(place), target, sems[0].at[step - 1], recv,
                       {"dp": group, "section": self.layer})
            )
        across = remote(source(mine), target, sems[0].at[self.size - 1], recv, core_peer())
        if self.in_vmem:
            local = [pltpu.make_async_copy(source(mine), target, sems[2].at[0])]
        else:
            local = [
                pltpu.make_async_copy(source(mine), sems[3], sems[2].at[0]),
                pltpu.make_async_copy(sems[3], target, sems[2].at[1]),
            ]
        return sent, across, local

    def start(self, inputs, outputs, sems):
        sent, across, local = self.parts(inputs, outputs, sems)
        for copy in sent:
            copy.start()
        here = lax.axis_index("section") == self.layer

        @pl.when(here)
        def _():
            local[0].start()

        @pl.when(jnp.logical_not(here))
        def _():
            across.start()

    def wait(self, inputs, outputs, sems):
        sent, across, local = self.parts(inputs, outputs, sems)
        core = lax.axis_index("section")
        here = core == self.layer
        block = inputs[0] if self.whole else inputs[0].at[0]

        def arrived(which, place):
            remote(block, self.target(outputs, which, place), sems[0].at[0], sems[1].at[which, place],
                   core_peer()).wait_recv()

        for copy in sent:
            copy.wait_send()

        @pl.when(here)
        def _():
            local[0].wait()
            for copy in local[1:]:
                copy.start()
                copy.wait()
            for step in range(self.size):
                place, _ = self.place(step)
                if step:
                    arrived(core, place)
                arrived(1 - core, place)

        @pl.when(jnp.logical_not(here))
        def _():
            across.wait_send()

    def results(self, outputs):
        return outputs[0]


class FirstStage:
    def __init__(self, value, axis, layer=None):
        self.count = lax.axis_size("dp")
        outer, inner = factors(self.count)
        self.blocks = (outer, inner, value.shape[0] // self.count, *value.shape[1:])
        inside = isinstance(value, jax.ShapeDtypeStruct)
        self.inputs = [] if inside else [value.reshape(self.blocks)]
        self.axis = axis
        shape = list(self.blocks[2:])
        shape[axis] //= 2
        self.shape = shape
        sums = [
            jax.ShapeDtypeStruct((outer, *shape), value.dtype),
            jax.ShapeDtypeStruct((inner, *shape), value.dtype),
        ]
        self.sems = [
            dma((inner + outer - 2,)),
            dma((inner + outer - 2,)),
            pltpu.VMEM((inner - 1, outer, *shape), value.dtype),
            pltpu.VMEM((outer - 1, inner, *shape), value.dtype),
            *[pltpu.VMEM(v.shape, v.dtype) for v in sums],
            dma((2,)),
            dma((2,)),
        ]
        self.outputs = sums
        self.brings = []
        if layer is not None:
            self.brings = [Bring(layer, kind, v, True) for kind, v in zip(("column", "row"), sums)]
            self.outputs = [v for bring in self.brings for v in bring.outputs]
            self.sems += [v for bring in self.brings for v in bring.sems]

    def copies(self, inputs, sems):
        across, along = near_groups(self.count)
        _, _, mo, mi = group_place(self.count)
        value = inputs[0]
        half = self.shape[self.axis]
        cut = [slice(None)] * 3
        first, second = list(cut), list(cut)
        first[self.axis], second[self.axis] = pl.ds(0, half), pl.ds(half, half)
        found = []
        for slot, (place, device) in enumerate(across):
            found.append((value.at[(slice(None), place, *first)], sems[2].at[slot], device))
        for slot, (place, device) in enumerate(along):
            found.append((value.at[(place, slice(None), *second)], sems[3].at[slot], device))
        sent = [
            remote(src, dst, sems[0].at[index], sems[1].at[index], device)
            for index, (src, dst, device) in enumerate(found)
        ]
        loads = [
            pltpu.make_async_copy(value.at[(slice(None), mi, *first)], sems[4], sems[6].at[0]),
            pltpu.make_async_copy(value.at[(mo, slice(None), *second)], sems[5], sems[6].at[1]),
        ]
        return sent + loads

    def onward(self, outputs, sems):
        place = 8
        found = []
        for index, bring in enumerate(self.brings):
            found.append((bring, [sems[4 + index]], [outputs[index]], sems[place : place + len(bring.sems)]))
            place += len(bring.sems)
        return found

    def saves(self, outputs, sems):
        return [pltpu.make_async_copy(sems[4 + k], outputs[k], sems[7].at[k]) for k in range(2)]

    def start(self, inputs, outputs, sems):
        start_all(self.copies(inputs, sems))

    def middle(self, inputs, outputs, sems):
        wait_all(self.copies(inputs, sems))
        for total, landed in ((sems[4], sems[2]), (sems[5], sems[3])):
            depth = total.shape[1]

            def add(index, carry, total=total, landed=landed, depth=depth):
                place, expert = index // depth, lax.rem(index, depth)
                value = total[place, expert].astype(f32)
                for slot in range(landed.shape[0]):
                    value = value + landed[slot, place, expert].astype(f32)
                total[place, expert] = value.astype(bf16)
                return carry

            lax.fori_loop(0, total.shape[0] * depth, add, 0)
        if self.brings:
            for bring, *refs in self.onward(outputs, sems):
                bring.start(*refs)
        else:
            start_all(self.saves(outputs, sems))

    def wait(self, inputs, outputs, sems):
        if self.brings:
            for bring, *refs in self.onward(outputs, sems):
                bring.wait(*refs)
        else:
            wait_all(self.saves(outputs, sems))

    def results(self, outputs):
        return outputs


class DenseSum:
    def __init__(self, value, layer):
        count = lax.axis_size("dp")
        outer, inner = factors(count)
        rows, width = value.shape[2:]
        half = width // 2
        self.half = half
        inside = isinstance(value, jax.ShapeDtypeStruct)
        self.inputs = [] if inside else [value]
        self.outputs = [jax.ShapeDtypeStruct((2, *value.shape), bf16)]

        def buffer(*lead):
            return pltpu.VMEM((*lead, rows, half), bf16)

        self.brings = [
            Bring(layer, "row", jax.ShapeDtypeStruct((outer, rows, half), bf16), True,
                  lambda outputs, core, place: outputs[0].at[core, :, place, :, pl.ds(0, half)]),
            Bring(layer, "column", jax.ShapeDtypeStruct((inner, rows, half), bf16), True,
                  lambda outputs, core, place: outputs[0].at[core, place, :, :, pl.ds(half, half)]),
        ]
        pairs = inner + outer - 2
        self.sems = [
            buffer(inner - 1, outer),
            buffer(outer - 1, inner),
            buffer(outer),
            buffer(inner),
            buffer(outer - 1),
            buffer(inner - 1),
            buffer(outer),
            buffer(inner),
            dma((2,)),
            *[dma((pairs,)) for _ in range(6)],
            *[v for bring in self.brings for v in bring.sems],
        ]

    def numbered(self, found, sems, first):
        return [
            remote(src, dst, sems[first].at[index], sems[first + 1].at[index], device)
            for index, (src, dst, device) in enumerate(found)
        ]

    def sent(self, inputs, sems):
        count = lax.axis_size("dp")
        across, along = near_groups(count)
        _, _, mo, mi = group_place(count)
        value = inputs[0]
        low, high = pl.ds(0, self.half), pl.ds(self.half, self.half)
        found = [
            (value.at[:, place, :, low], sems[0].at[slot], device)
            for slot, (place, device) in enumerate(across)
        ] + [
            (value.at[place, :, :, high], sems[1].at[slot], device)
            for slot, (place, device) in enumerate(along)
        ]
        loads = [
            pltpu.make_async_copy(value.at[:, mi, :, low], sems[2], sems[8].at[0]),
            pltpu.make_async_copy(value.at[mo, :, :, high], sems[3], sems[8].at[1]),
        ]
        return self.numbered(found, sems, 9) + loads

    def sums(self, sems):
        across, along = near_groups(lax.axis_size("dp"))
        found = [
            (sems[2].at[place], sems[4].at[slot], device) for slot, (place, device) in enumerate(along)
        ] + [
            (sems[3].at[place], sems[5].at[slot], device) for slot, (place, device) in enumerate(across)
        ]
        return self.numbered(found, sems, 11)

    def blocks(self, sems):
        count = lax.axis_size("dp")
        across, along = near_groups(count)
        _, _, mo, mi = group_place(count)
        found = [(sems[6].at[mo], sems[6].at[mo], device) for _, device in along]
        found += [(sems[7].at[mi], sems[7].at[mi], device) for _, device in across]
        return self.numbered(found, sems, 13)

    def onward(self, outputs, sems):
        place = 15
        found = []
        for index, bring in enumerate(self.brings):
            found.append((bring, [sems[6 + index]], outputs, sems[place : place + len(bring.sems)]))
            place += len(bring.sems)
        return found

    def start(self, inputs, outputs, sems):
        start_all(self.sent(inputs, sems))

    def middle1(self, inputs, outputs, sems):
        wait_all(self.sent(inputs, sems))
        for total, landed in ((sems[2], sems[0]), (sems[3], sems[1])):
            for place in range(total.shape[0]):
                value = total[place].astype(f32)
                for slot in range(landed.shape[0]):
                    value = value + landed[slot, place].astype(f32)
                total[place] = value.astype(bf16)
        start_all(self.sums(sems))

    def middle2(self, inputs, outputs, sems):
        wait_all(self.sums(sems))
        _, _, mo, mi = group_place(lax.axis_size("dp"))
        for total, landed, whole, mine in (
            (sems[2], sems[4], sems[6], mo),
            (sems[3], sems[5], sems[7], mi),
        ):
            value = total[mine].astype(f32)
            for slot in range(landed.shape[0]):
                value = value + landed[slot].astype(f32)
            whole[mine] = value.astype(bf16)
        start_all(self.blocks(sems))

    def middle3(self, inputs, outputs, sems):
        wait_all(self.blocks(sems))
        for bring, *refs in self.onward(outputs, sems):
            bring.start(*refs)

    def wait(self, inputs, outputs, sems):
        for bring, *refs in self.onward(outputs, sems):
            bring.wait(*refs)

    def results(self, outputs):
        return outputs[0]


class SmallSum:
    def __init__(self, depth, width):
        self.tensor, self.count = lax.axis_size("tensor"), lax.axis_size("dp")
        self.lanes = width // self.tensor
        self.depth = depth
        part = (depth, self.lanes)
        self.sems = [
            pltpu.VMEM((depth, width), f32),
            pltpu.VMEM((self.tensor - 1, *part), f32),
            pltpu.VMEM((self.count - 1, *part), f32),
            *[pltpu.VMEM(part, f32) for _ in range(4)],
            pltpu.VMEM((depth, width), f32),
            dma((2, self.tensor - 1)),
            dma((2, self.tensor - 1)),
            dma((self.count,)),
            dma((self.count,)),
        ]

    def columns(self, place):
        return pl.ds(pl.multiple_of(place * self.lanes, self.lanes), self.lanes)

    def over_tensor(self, sems):
        here = lax.axis_index("tensor")
        found = []
        for step in range(1, self.tensor):
            place = lax.rem(here + step, self.tensor)
            found.append(
                remote(sems[0].at[:, self.columns(place)], sems[1].at[step - 1],
                       sems[8].at[0, step - 1], sems[9].at[0, step - 1], {"tensor": place})
            )
        return found

    def over_groups(self, sems):
        me = lax.axis_index("dp")
        return [
            remote(sems[3], sems[2].at[step - 1], sems[10].at[step - 1], sems[11].at[step - 1],
                   {"dp": lax.rem(me + step, self.count)})
            for step in range(1, self.count)
        ]

    def over_cores(self, sems):
        last = self.count - 1
        return [remote(sems[4], sems[5], sems[10].at[last], sems[11].at[last], core_peer())]

    def back(self, sems):
        here = lax.axis_index("tensor")
        own = sems[7].at[:, self.columns(here)]
        return [
            remote(sems[6], own, sems[8].at[1, step - 1], sems[9].at[1, step - 1],
                   {"tensor": lax.rem(here + step, self.tensor)})
            for step in range(1, self.tensor)
        ]

    def first(self, sems):
        start_all(self.over_tensor(sems))

    def second(self, sems):
        wait_all(self.over_tensor(sems))
        total = sems[0][:, self.columns(lax.axis_index("tensor"))]
        for slot in range(self.tensor - 1):
            total = total + sems[1][slot]
        sems[3][...] = total
        start_all(self.over_groups(sems))

    def third(self, sems):
        wait_all(self.over_groups(sems))
        total = sems[3][...]
        for slot in range(self.count - 1):
            total = total + sems[2][slot]
        sems[4][...] = total
        copies = self.over_cores(sems)
        start_all(copies)
        wait_all(copies)
        sems[6][...] = sems[4][...] + sems[5][...]
        start_all(self.back(sems))
        sems[7][:, self.columns(lax.axis_index("tensor"))] = sems[6][...]

    def last(self, sems, out):
        wait_all(self.back(sems))
        out[...] = sems[7][...]


class Trade:
    def __init__(self, shape):
        self.sems = [pltpu.VMEM((2, *shape), f32), dma((1,)), dma((1,))]

    def copy(self, value, sems):
        core = lax.axis_index("section")
        return remote(value, sems[0].at[core], sems[1].at[0], sems[2].at[0], core_peer())

    def start(self, zero, one, sems):
        core = lax.axis_index("section")

        @pl.when(core == 0)
        def _():
            self.copy(one, sems).start()
            sems[0][0] = zero[...]

        @pl.when(core == 1)
        def _():
            self.copy(zero, sems).start()
            sems[0][1] = one[...]

    def wait(self, zero, out, sems):
        self.copy(zero, sems).wait()
        out[...] = sems[0][...]


def both_cores(groups):
    core = lax.axis_index("section")
    return [{"dp": group, "section": which} for group in groups for which in (core, 1 - core)]


def whole_group():
    count = lax.axis_size("dp")
    me = lax.axis_index("dp")
    return both_cores([lax.rem(me + step, count) for step in range(1, count)])


class Beside:
    def __init__(self, jobs):
        self.jobs = jobs
        self.inputs = [v for job in jobs for v in job.inputs]
        self.outputs = [v for job in jobs for v in job.outputs]
        self.sems = [v for job in jobs for v in job.sems]

    def peers(self):
        count = lax.axis_size("dp")
        if not self.jobs:
            return []
        across, along = near_groups(count)
        return both_cores([device["dp"] for _, device in across + along])

    def each(self, refs, run):
        inputs, outputs, sems = refs
        for job in self.jobs:
            mine, inputs = inputs[: len(job.inputs)], inputs[len(job.inputs) :]
            theirs, outputs = outputs[: len(job.outputs)], outputs[len(job.outputs) :]
            own, sems = sems[: len(job.sems)], sems[len(job.sems) :]
            run(job)(mine, theirs, own)

    def start(self, *refs):
        self.each(refs, lambda job: job.start)

    def middle(self, *refs, step="middle"):
        self.each(refs, lambda job: getattr(job, step, lambda *refs: None))

    def wait(self, *refs):
        self.each(refs, lambda job: job.wait)

    def results(self, outputs):
        found = []
        for job in self.jobs:
            found.append(job.results(outputs[: len(job.outputs)]))
            outputs = outputs[len(job.outputs) :]
        return found


def deal_out(count, part, rows, columns, landing, sends, recvs):
    me = lax.axis_index("tensor")
    copies = []
    for step in range(1, count):
        peer = lax.rem(me + step, count)
        copies.append(
            pltpu.make_async_remote_copy(
                src_ref=part.at[pl.ds(pl.multiple_of(peer * rows, rows), rows), columns],
                dst_ref=landing.at[step - 1, :, columns],
                send_sem=sends.at[step - 1],
                recv_sem=recvs.at[step - 1],
                device_id={"tensor": peer},
                device_id_type=MESH,
            )
        )
    for copy in copies:
        copy.start()
    return copies


class Line:
    def __init__(self, count, rows, passing=True):
        self.count, self.rows = count, rows
        self.passing = passing and count == 4
        self.me = me = lax.axis_index("tensor")
        half = me // 2
        self.partner = me + 1 - 2 * lax.rem(me, 2)
        self.far_inner, self.far_edge = 2 - half, 3 - 3 * half
        self.inner = me == 1 + half

    def cut(self, place):
        return pl.ds(pl.multiple_of(place * self.rows, self.rows), self.rows)

    def shard(self, buf, sems, place, target, index):
        buf, columns = buf if isinstance(buf, tuple) else (buf, slice(None))
        rows = buf.at[self.cut(place), columns]
        return remote(rows, rows, sems[0].at[index], sems[1].at[place], {"tensor": target})

    def gather_start(self, buf, sems):
        if self.passing:
            self.shard(buf, sems, self.me, self.far_inner, 1).start()
            self.shard(buf, sems, self.me, self.partner, 0).start()
        else:
            for step in range(1, self.count):
                self.shard(buf, sems, self.me, lax.rem(self.me + step, self.count), step - 1).start()

    def gather_wait(self, buf, sems):
        def arrived(place):
            self.shard(buf, sems, place, self.partner, 0).wait_recv()

        def left(number):
            for index in range(number):
                self.shard(buf, sems, self.me, self.partner, index).wait_send()

        if not self.passing:
            for step in range(1, self.count):
                arrived(lax.rem(self.me + step, self.count))
            left(self.count - 1)
            return

        @pl.when(self.inner)
        def _():
            arrived(self.far_inner)
            self.shard(buf, sems, self.far_inner, self.partner, 2).start()
            arrived(self.far_edge)
            self.shard(buf, sems, self.far_edge, self.partner, 3).start()
            arrived(self.partner)
            left(4)

        @pl.when(jnp.logical_not(self.inner))
        def _():
            for place in (self.partner, self.far_inner, self.far_edge):
                arrived(place)
            left(2)

    def block(self, part, place, columns, landing, slot, sems, index, target):
        return remote(part.at[self.cut(place), columns], landing.at[slot, :, columns],
                      sems[0].at[index], sems[1].at[slot], {"tensor": target})

    def scatter_start(self, part, columns, landing, sems):
        if not self.passing:
            for step in range(1, self.count):
                peer = lax.rem(self.me + step, self.count)
                self.block(part, peer, columns, landing, step - 1, sems, step - 1, peer).start()
            return

        @pl.when(self.inner)
        def _():
            self.block(part, self.partner, columns, landing, 2, sems, 0, self.partner).start()

        @pl.when(jnp.logical_not(self.inner))
        def _():
            for slot, place in enumerate((self.far_edge, self.far_inner, self.partner)):
                self.block(part, place, columns, landing, slot, sems, slot, self.partner).start()

    def scatter_relay(self, part, columns, landing, sems):
        if not self.passing:
            return

        @pl.when(self.inner)
        def _():
            for slot, place in enumerate((self.far_edge, self.far_inner)):
                self.block(part, place, columns, landing, slot, sems, 0, self.partner).wait_recv()
                landing[slot, :, columns] = (
                    landing[slot, :, columns].astype(f32) + part[self.cut(place), columns].astype(f32)
                ).astype(bf16)
                remote(landing.at[slot, :, columns], landing.at[3, :, columns], sems[0].at[1 + slot],
                       sems[1].at[3], {"tensor": place}).start()

    def scatter_wait(self, part, columns, landing, sems):
        slots = (2, 3) if self.passing else range(self.count - 1)
        for slot in slots:
            self.block(part, self.me, columns, landing, slot, sems, 0, self.partner).wait_recv()
        for index in range(3 if self.passing else self.count - 1):
            self.block(part, self.me, columns, landing, 0, sems, index, self.partner).wait_send()

    def total(self, own, landing):
        for slot in (2, 3) if self.passing else range(self.count - 1):
            own = own + landing[slot].astype(f32)
        return own

    @staticmethod
    def landing(count, rows, width):
        return pltpu.VMEM((4 if count == 4 else count - 1, rows, width), bf16)

    @staticmethod
    def sems(count, number):
        return [dma((number, count)), dma((number, count))]


def core_peer():
    return {"section": 1 - lax.axis_index("section")}


def hand_rows(value, pair, sems):
    tokens = value.shape[0]
    return [
        pltpu.make_async_copy(value, pair.at[pl.ds(0, tokens)], sems[0]),
        remote(value, pair.at[pl.ds(tokens, tokens)], sems[1], sems[2], core_peer()),
    ]


def hand_halves(value, pair, sems):
    section = lax.axis_index("section")
    tokens, half = value.shape[0], value.shape[1] // 2
    mine = value.at[:, pl.ds(pl.multiple_of(section * half, half), half)]
    other = value.at[:, pl.ds(pl.multiple_of((1 - section) * half, half), half)]
    return [
        pltpu.make_async_copy(mine, pair.at[pl.ds(0, tokens)], sems[0]),
        remote(other, pair.at[pl.ds(tokens, tokens)], sems[1], sems[2], core_peer()),
    ]


def start_all(copies):
    for copy in copies:
        copy.start()


def wait_all(copies):
    for copy in copies:
        copy.wait()


def either(use_own, own, other, run):
    @pl.when(use_own)
    def _():
        run(own)

    @pl.when(jnp.logical_not(use_own))
    def _():
        run(other)


def weight_copies(refs, scratch, sems, expert):
    gate, up, down = refs
    gu_s, down_s = scratch
    width = gate.shape[2]
    return (
        pltpu.make_async_copy(gate.at[expert], gu_s.at[expert, :, pl.ds(0, width)], sems.at[0, expert]),
        pltpu.make_async_copy(up.at[expert], gu_s.at[expert, :, pl.ds(width, width)], sems.at[1, expert]),
        pltpu.make_async_copy(
            down.at[expert], down_s.at[pl.ds(pl.multiple_of(expert * width, width), width)], sems.at[2, expert]
        ),
    )


def attn_copies(refs, scratch, sems):
    query, key, value, output = refs
    joint_s, output_s = scratch
    qw, kw = query.shape[1], key.shape[1]
    return (
        pltpu.make_async_copy(query, joint_s.at[:, pl.ds(0, qw)], sems.at[0]),
        pltpu.make_async_copy(key, joint_s.at[:, pl.ds(qw, kw)], sems.at[1]),
        pltpu.make_async_copy(value, joint_s.at[:, pl.ds(qw + kw, kw)], sems.at[2]),
        pltpu.make_async_copy(output, output_s, sems.at[3]),
    )


def turned(block):
    lane = lax.broadcasted_iota(jnp.int32, block.shape, 1)
    half = HD // 2
    return jnp.where(
        lane % HD < half, pltpu.roll(block, block.shape[1] - half, 1), pltpu.roll(block, half, 1)
    )


def column(table, index):
    lane = lax.broadcasted_iota(jnp.int32, table.shape, 1)
    return jnp.sum(jnp.where(lane == index, table, 0.0), axis=1, keepdims=True)


def swap_copies(own, other, sems, piece):
    sends, recvs = sems
    names = len(own)
    if isinstance(piece, tuple):
        name, expert = piece
        source, target = own[name].at[expert], other[name].at[expert]
        index = 4 + (name - 4) * own[4].shape[0] + expert
    else:
        source, target, index = own[piece], other[piece], piece
    return pltpu.make_async_remote_copy(
        src_ref=source, dst_ref=target, send_sem=sends.at[index], recv_sem=recvs.at[index],
        device_id=core_peer(), device_id_type=MESH,
    )


def forward_kernel(layer, count, swap, *refs):
    refs = list(refs)

    def take(number):
        taken = refs[:number]
        del refs[:number]
        return taken

    (stream_in, attn_gains, expert_gains, routers, cosine, sine, bias, pickeds, kepts) = take(9)
    attn_gain, expert_gain, router = attn_gains.at[layer], expert_gains.at[layer], routers.at[layer]
    picked, kept = pickeds.at[layer], kepts.at[layer]
    stream = stream_in.at[lax.axis_index("section")] if layer == 0 else stream_in
    own = take(7)
    other = None if swap else take(7)
    (out, mid_out, expert_rows_out, qs_out, keys_out, values_out, probs_out, gate_out,
     attn_in_out, expert_in_out, gated_out, attended_out, pre_out) = take(13)
    if swap:
        other = take(7)
    scratch = take(4)
    joint_s, output_s, gu_s, down_s = scratch
    (ag1, ag2, part, landing1, landing2, pre_s, gated_s, attended_s, send_s, recv_s, attn_sems,
     expert_sems, pre_sems, save_sems) = refs[:14]
    if swap:
        swap_sems = refs[14:]
    rows, width = stream.shape
    tokens = ag1.shape[0]
    experts = gu_s.shape[0]
    hidden_width = gu_s.shape[2] // 2
    kw = keys_out.shape[1]
    qw = attended_s.shape[1]
    heads, key_heads = qw // HD, kw // HD
    group = heads // key_heads
    me = lax.axis_index("tensor")
    own_rows = pl.ds(pl.multiple_of(me * rows, rows), rows)
    ag1_line, rs1_line, ag2_line, rs2_line = [Line(count, rows, v) for v in (True, True, False, True)]

    def sems(index):
        return send_s.at[index], recv_s.at[index]

    use_own = lax.axis_index("section") == layer

    def start_attn(w):
        for copy in attn_copies(w[:4], scratch[:2], attn_sems):
            copy.start()

    def wait_attn(w):
        for copy in attn_copies(w[:4], scratch[:2], attn_sems):
            copy.wait()

    def start_expert(w, expert):
        for copy in weight_copies(w[4:], scratch[2:], expert_sems, expert):
            copy.start()

    def wait_expert(w, expert):
        for copy in weight_copies(w[4:], scratch[2:], expert_sems, expert):
            copy.wait()

    def each_expert(run):
        def step(expert, carry):
            run(expert)
            return carry

        lax.fori_loop(0, experts, step, 0)

    def swap_expert(expert):
        return [swap_copies(own, other, swap_sems, (name, expert)) for name in (4, 5, 6)]

    value = stream[...].astype(bf16).astype(f32)
    ag1[own_rows, :] = (value * norm_scale(value) * attn_gain[...]).astype(bf16)
    greet(tensor_peers(count) + ([core_peer()] if swap else []))
    if swap:
        lead = min(4, experts)
        for piece in range(4):
            swap_copies(own, other, swap_sems, piece).start()
        each_expert(lambda expert: [c.start() for c in swap_expert(expert)] and None)

        @pl.when(use_own)
        def _():
            ag1_line.gather_start(ag1, sems(0))
            start_attn(own)
            each_expert(lambda expert: start_expert(own, expert))

        @pl.when(jnp.logical_not(use_own))
        def _():
            for piece in range(4):
                swap_copies(own, other, swap_sems, piece).wait_recv()
            start_attn(other)
            for expert in range(lead):
                for copy in swap_expert(expert):
                    copy.wait_recv()
                start_expert(other, expert)
            ag1_line.gather_start(ag1, sems(0))
    else:
        ag1_line.gather_start(ag1, sems(0))
        either(use_own, own, other, start_attn)
        either(use_own, own, other, lambda w: each_expert(lambda expert: start_expert(w, expert)))
    ag1_line.gather_wait(ag1, sems(0))
    saved = [pltpu.make_async_copy(ag1, attn_in_out, save_sems.at[0])]
    saved[0].start()
    either(use_own, own, other, wait_attn)
    proj = dot(ag1[...], joint_s[...], NN)
    for chunk in range(qw // 128):
        block = proj[:, chunk * 128 : chunk * 128 + 128]
        block = (block * cosine[...] + turned(block) * sine[...]).astype(bf16)
        for part_index in range(128 // HD):
            head = chunk * (128 // HD) + part_index
            qs_out[pl.ds(head * tokens, tokens), :] = block[:, part_index * HD : part_index * HD + HD]
    for chunk in range(kw // 128):
        block = proj[:, qw + chunk * 128 : qw + chunk * 128 + 128]
        keys_out[:, pl.ds(chunk * 128, 128)] = (
            block * cosine[...] + turned(block) * sine[...]
        ).astype(bf16)
    values_out[...] = proj[:, qw + kw :].astype(bf16)
    for g in range(key_heads):
        lanes = pl.ds(g * HD, HD)
        span = pl.ds(g * group * tokens, group * tokens)
        scores = dot(qs_out[span, :], keys_out[:, lanes], NT) * 0.125
        scores = (scores.reshape(group, tokens, tokens) + bias[...][None]).reshape(
            group * tokens, tokens
        )
        top = jnp.max(scores, axis=1, keepdims=True)
        weighed = jnp.exp(scores - top)
        probs = (weighed / jnp.sum(weighed, axis=1, keepdims=True)).astype(bf16)
        probs_out[span, :] = probs
        attended = dot(probs, values_out[:, lanes], NN).astype(bf16)
        for h in range(group):
            attended_s[:, pl.ds((g * group + h) * HD, HD)] = attended[h * tokens : (h + 1) * tokens]
    saved.append(pltpu.make_async_copy(attended_s, attended_out, save_sems.at[1]))
    saved[1].start()
    part[...] = dot(attended_s[...], output_s[...], NN).astype(bf16)
    dealt = part, slice(None), landing1, sems(1)
    rs1_line.scatter_start(*dealt)
    rs1_line.scatter_relay(*dealt)
    rs1_line.scatter_wait(*dealt)
    mid = rs1_line.total(value + part[own_rows, :].astype(f32), landing1)
    mid_out[...] = mid
    expert_rows = (mid * norm_scale(mid) * expert_gain[...]).astype(bf16)
    expert_rows_out[...] = expert_rows
    ag2[own_rows, :] = expert_rows
    split = width // 2
    columns = pl.ds(0, split), pl.ds(split, split)
    ag2_line.gather_start((ag2, columns[0]), sems(2))
    ag2_line.gather_start((ag2, columns[1]), sems(8))
    if swap:

        @pl.when(jnp.logical_not(use_own))
        def _():
            def landed(expert, carry):
                for copy in swap_expert(expert):
                    copy.wait_recv()
                start_expert(other, expert)
                return carry

            lax.fori_loop(lead, experts, landed, 0)

    ag2_line.gather_wait((ag2, columns[0]), sems(2))

    def first_step(expert, carry):
        either(use_own, own, other, lambda w: wait_expert(w, expert))
        pre_s[expert] = dot(ag2[:, columns[0]], gu_s[expert, columns[0], :], NN)
        return carry

    lax.fori_loop(0, experts, first_step, 0)
    ag2_line.gather_wait((ag2, columns[1]), sems(8))
    saved.append(pltpu.make_async_copy(ag2, expert_in_out, save_sems.at[2]))
    saved[2].start()
    logits = dot(ag2[...], router[...], NT)
    chosen = picked[...] > 0
    top = jnp.max(jnp.where(chosen, logits, masked_score), axis=1, keepdims=True)
    weighed = jnp.where(chosen, jnp.exp(logits - top), 0.0)
    gate_out[...] = weighed / jnp.sum(weighed, axis=1, keepdims=True)

    def expert_step(expert, carry):
        pre = pre_s[expert] + dot(ag2[:, columns[1]], gu_s[expert, columns[1], :], NN)
        pre_s[expert] = pre
        pltpu.make_async_copy(pre_s.at[expert], pre_out.at[expert], pre_sems.at[expert]).start()
        gate_pre, up_pre = pre[:, :hidden_width], pre[:, hidden_width:]
        hidden = (gate_pre / (1.0 + jnp.exp(-gate_pre)) * up_pre).astype(bf16).astype(f32)
        weight = column(gate_out[...] * kept[...], expert)
        gated_s[:, pl.ds(pl.multiple_of(expert * hidden_width, hidden_width), hidden_width)] = (
            hidden * weight
        ).astype(bf16)
        return carry

    lax.fori_loop(0, experts, expert_step, 0)
    saved.append(pltpu.make_async_copy(gated_s, gated_out, save_sems.at[3]))
    saved[3].start()
    tile = width // 4
    dealt = [(part, pl.ds(t * tile, tile), landing2, sems(3 + t)) for t in range(4)]
    for each in dealt:
        part[:, each[1]] = dot(gated_s[...], down_s[:, each[1]], NN).astype(bf16)
        rs2_line.scatter_start(*each)
    for each in dealt:
        rs2_line.scatter_relay(*each)
    for each in dealt:
        rs2_line.scatter_wait(*each)
    total = rs2_line.total(mid_out[...] + part[own_rows, :].astype(f32), landing2)
    out[...] = total
    wait_all(saved)
    if swap:
        for piece in range(4):
            swap_copies(own, other, swap_sems, piece).wait_send()
        each_expert(lambda expert: [c.wait_send() for c in swap_expert(expert)] and None)

        @pl.when(use_own)
        def _():
            for piece in range(4):
                swap_copies(own, other, swap_sems, piece).wait_recv()
            each_expert(lambda expert: [c.wait_recv() for c in swap_expert(expert)] and None)

    def finish(expert, carry):
        pltpu.make_async_copy(pre_s.at[expert], pre_out.at[expert], pre_sems.at[expert]).wait()
        return carry

    lax.fori_loop(0, experts, finish, 0)


def weight_scratch(own):
    query, key, value, output, gate, up, down = own
    depth = query.shape[0]
    experts, _, hidden_width = gate.shape
    return [
        pltpu.VMEM((depth, query.shape[1] + 2 * key.shape[1]), bf16),
        pltpu.VMEM(output.shape, bf16),
        pltpu.VMEM((experts, depth, 2 * hidden_width), bf16),
        pltpu.VMEM((experts * hidden_width, depth), bf16),
    ]


def layer_forward(layer, gains, own, other, stream, tables, masks):
    count = lax.axis_size("tensor")
    rows, width = stream.shape[-2:]
    tokens = tables[2].shape[0]
    qw, kw = own[0].shape[1], own[1].shape[1]
    experts, _, hidden_width = own[4].shape
    heads = qw // HD
    swap = other is None
    vmem = pl.BlockSpec(memory_space=pltpu.VMEM)
    hbm = pl.BlockSpec(memory_space=pl.ANY)
    shape = jax.ShapeDtypeStruct
    pieces = 4 + 3 * experts
    found = pl.pallas_call(
        functools.partial(forward_kernel, layer, count, swap),
        name=f"layer_forward_{layer}",
        out_shape=(
            shape((rows, width), f32),
            shape((rows, width), f32),
            shape((rows, width), bf16),
            shape((heads * tokens, HD), bf16),
            shape((tokens, kw), bf16),
            shape((tokens, kw), bf16),
            shape((heads * tokens, tokens), bf16),
            shape((tokens, experts), f32),
            shape((tokens, width), bf16),
            shape((tokens, width), bf16),
            shape((tokens, experts * hidden_width), bf16),
            shape((tokens, qw), bf16),
            shape((experts, tokens, 2 * hidden_width), f32),
        )
        + (tuple(shape(w.shape, w.dtype) for w in own) if swap else ()),
        in_specs=[vmem] * 9 + [hbm] * (7 if swap else 14),
        out_specs=(vmem,) * 8 + (hbm,) * (12 if swap else 5),
        scratch_shapes=weight_scratch(own)
        + [
            pltpu.VMEM((tokens, width), bf16),
            pltpu.VMEM((tokens, width), bf16),
            pltpu.VMEM((tokens, width), bf16),
            Line.landing(count, rows, width),
            Line.landing(count, rows, width),
            pltpu.VMEM((experts, tokens, 2 * hidden_width), f32),
            pltpu.VMEM((tokens, experts * hidden_width), bf16),
            pltpu.VMEM((tokens, qw), bf16),
            *Line.sems(count, 9),
            dma((4,)),
            dma((3, experts)),
            dma((experts,)),
            dma((4,)),
        ]
        + ([dma((pieces,)), dma((pieces,))] if swap else []),
        compiler_params=params(1 + layer),
    )(stream, *gains, *tables, *masks, *own,
      *(() if swap else other))
    return found[:13], found[13:]


def norm_back(value, gain, out_grad):
    scale = norm_scale(value)
    scaled = value * scale
    gain_grad = jnp.sum(out_grad * scaled, axis=0, keepdims=True)
    inner = out_grad * gain
    value_grad = scale * (inner - scaled * jnp.mean(inner * scaled, axis=-1, keepdims=True))
    return value_grad, gain_grad


def experts_back_kernel(layer, count, trade, stage, beside, *refs):
    refs = list(refs)

    def take(number):
        taken = refs[:number]
        del refs[:number]
        return taken

    out_grad, mid, expert_gains, routers, kepts, gate, expert_rows, pre_in = take(8)
    expert_gain, router, kept = expert_gains.at[layer], routers.at[layer], kepts.at[layer]
    x_in, gated_in = take(2)
    own, other = take(3), take(3)
    traded = take(2 if trade else 0)
    beside_in = take(len(beside.inputs))
    mid_grad_out, router_out, expert_gain_out, pair_out = take(4)
    traded_out = take(1 if trade else 0)
    stage_out = take(len(stage.outputs))
    beside_out = take(len(beside.outputs))
    scratch = take(2)
    gu_s, down_s = scratch
    (ag1, part, landing1, pre_s, gpu_s, acc, gate_part, gate_land, og_s, gpu_peer, x_s, turned_x,
     gated_s, hidden_s, pair_s, down_grad_s, send_s, recv_s, expert_sems, pre_sems, core_send, core_recv,
     local_sems, hand_send, hand_recv, save_sems) = take(26)
    trade_sems = take(len(trade.sems) if trade else 0)
    stage_refs = ([down_grad_s], stage_out, take(len(stage.sems)))
    beside_refs = (beside_in, beside_out, refs)
    rows, width = mid.shape
    tokens = ag1.shape[0]
    experts = gu_s.shape[0]
    hidden_width = gu_s.shape[2] // 2
    me = lax.axis_index("tensor")
    own_rows = pl.ds(pl.multiple_of(me * rows, rows), rows)
    ag_line, rs_line = [Line(count, rows, v) for v in (False, False)]
    gathering = ag1, (send_s.at[0], recv_s.at[0])
    tile = width // 2
    dealt = [
        (part, pl.ds(t * tile, tile), landing1, (send_s.at[3 * t], recv_s.at[3 * t]))
        if t
        else (part, pl.ds(0, tile), landing1, (send_s.at[1], recv_s.at[1]))
        for t in range(2)
    ]
    use_own = lax.axis_index("section") == layer

    def start_expert(expert, carry):
        either(use_own, own, other,
               lambda w: [c.start() for c in weight_copies(w, scratch, expert_sems, expert)])
        pltpu.make_async_copy(pre_in.at[expert], pre_s.at[expert], pre_sems.at[expert]).start()
        return carry

    everyone = Beside([*beside.jobs, stage])
    if layer:
        ag1[own_rows, :] = out_grad[lax.axis_index("section")]
        greet(tensor_peers(count) + [core_peer()] + everyone.peers())
        ag_line.gather_start(*gathering)
    else:
        ag1[own_rows, :] = out_grad[...].astype(bf16)
        greet(tensor_peers(count) + [core_peer()] + everyone.peers())
        ag_line.gather_start(*gathering)
    lax.fori_loop(0, experts, start_expert, 0)
    loads = hand_halves(x_in, x_s, [v.at[0] for v in (local_sems, hand_send, hand_recv)])
    loads += hand_rows(gated_in, gated_s, [v.at[1] for v in (local_sems, hand_send, hand_recv)])
    for copy in loads:
        copy.start()
    beside.start(*beside_refs)
    if trade:
        trade.start(*traded, trade_sems)
    gate_part[...] = jnp.zeros_like(gate_part)

    def ready_step(expert, carry):
        pltpu.make_async_copy(pre_in.at[expert], pre_s.at[expert], pre_sems.at[expert]).wait()
        gate_pre = pre_s[expert, :, pl.ds(0, hidden_width)]
        up_pre = pre_s[expert, :, pl.ds(hidden_width, hidden_width)]
        sig = 1.0 / (1.0 + jnp.exp(-gate_pre))
        act = gate_pre * sig
        hidden_s[expert] = (act * up_pre).astype(bf16)
        weight = column(gate[...] * kept[...], expert)
        pre_s[expert, :, pl.ds(0, hidden_width)] = (
            weight * up_pre * (sig * (1.0 + gate_pre * (1.0 - sig)))
        )
        pre_s[expert, :, pl.ds(hidden_width, hidden_width)] = weight * act
        return carry

    lax.fori_loop(0, experts, ready_step, 0)
    ag_line.gather_wait(*gathering)
    core = lax.axis_index("section")
    half = width // 2
    og_s[pl.ds(0, tokens), :] = ag1[:, pl.ds(pl.multiple_of(core * half, half), half)]
    handed = [
        remote(ag1.at[:, pl.ds(pl.multiple_of((1 - core) * half, half), half)],
               og_s.at[pl.ds(tokens, tokens)], core_send.at[0], core_recv.at[0], core_peer())
    ]
    handed[0].start()
    wait_all(loads)
    handed[0].wait()
    _, inner, per_group = stage.blocks[:3]

    def down_step(index, carry):
        lanes = pl.ds(pl.multiple_of(index * 2 * hidden_width, 2 * hidden_width), 2 * hidden_width)
        grads = dot(gated_s[:, lanes], og_s[...], TN).astype(bf16)
        for k in range(2):
            expert = 2 * index + k
            group, place = expert // per_group, lax.rem(expert, per_group)
            down_grad_s[group // inner, lax.rem(group, inner), place] = grads[
                k * hidden_width : (k + 1) * hidden_width
            ]
        return carry

    lax.fori_loop(0, experts // 2, down_step, 0)
    stage.start(*stage_refs)
    beside.middle(*beside_refs, step="middle1")

    def expert_step(index, carry):
        pair = (2 * index, 2 * index + 1)
        for expert in pair:
            either(use_own, own, other,
                   lambda w: [c.wait() for c in weight_copies(w, scratch, expert_sems, expert)])
        lanes = pl.ds(pl.multiple_of(index * 2 * hidden_width, 2 * hidden_width), 2 * hidden_width)
        plain = dot(ag1[...], down_s[lanes, :], NT)
        lane = lax.broadcasted_iota(jnp.int32, gate_part.shape, 1)
        for k, expert in enumerate(pair):
            value = plain[:, k * hidden_width : (k + 1) * hidden_width]
            summed = jnp.sum(hidden_s[expert].astype(f32) * value, axis=1, keepdims=True)
            gate_part[...] += jnp.where(lane == expert, summed, 0.0)
            for cut in (pl.ds(0, hidden_width), pl.ds(hidden_width, hidden_width)):
                gpu_s[expert, :, cut] = (value * pre_s[expert, :, cut]).astype(bf16)
        return carry

    lax.fori_loop(0, experts // 2, expert_step, 0)
    gate_part[:, :experts] = gate_part[:, :experts] * kept[...]
    copies = deal_out(count, gate_part, rows, slice(None), gate_land, send_s.at[2], recv_s.at[2])
    handed.append(remote(gpu_s, gpu_peer, core_send.at[1], core_recv.at[1], core_peer()))
    handed[1].start()
    for each in dealt:
        columns = each[1]
        acc[...] = jnp.zeros_like(acc)

        def back_step(index, carry, columns=columns):
            pair = (2 * index, 2 * index + 1)
            acc[...] += dot(gpu_s[pair[0]], gu_s[pair[0], columns, :], NT) + dot(
                gpu_s[pair[1]], gu_s[pair[1], columns, :], NT
            )
            return carry

        lax.fori_loop(0, experts // 2, back_step, 0)
        part[:, columns] = acc[...].astype(bf16)
        rs_line.scatter_start(*each)
    beside.middle(*beside_refs, step="middle2")
    turned_x[...] = x_s[...].T
    wait_all(handed[1:])

    def saves(expert):
        return [pltpu.make_async_copy(pair_s.at[expert], pair_out.at[expert], save_sems.at[expert])]

    def grads_step(expert, carry):
        pair_s[expert] = (
            dot(turned_x[:, :tokens], gpu_s[expert], NN)
            + dot(turned_x[:, tokens:], gpu_peer[expert], NN)
        ).astype(bf16)
        for copy in saves(expert):
            copy.start()
        return carry

    lax.fori_loop(0, experts, grads_step, 0)
    beside.middle(*beside_refs, step="middle3")
    stage.middle(*stage_refs)
    wait_all(copies)
    for each in dealt:
        rs_line.scatter_wait(*each)
    in_grad = rs_line.total(part[own_rows, :].astype(f32), landing1)
    gate_grad = gate_part[own_rows, :]
    for step in range(count - 1):
        gate_grad = gate_grad + gate_land[step]
    gate_grad = gate_grad[:, :experts]
    gate_rows = gate[own_rows, :]
    logits_grad = (
        gate_rows * (gate_grad - jnp.sum(gate_rows * gate_grad, axis=1, keepdims=True))
    ).astype(bf16)
    router_out[...] = dot(logits_grad, expert_rows[...], TN)
    in_grad = in_grad + dot(logits_grad, router[...], NN)
    mid_part, expert_gain_grad = norm_back(mid[...], expert_gain[...], in_grad)
    expert_gain_out[...] = expert_gain_grad
    mid_grad_out[...] = ag1[own_rows, :].astype(f32) + mid_part

    def finish_save(expert, carry):
        for copy in saves(expert):
            copy.wait()
        return carry

    lax.fori_loop(0, experts, finish_save, 0)
    if trade:
        trade.wait(traded[0], traded_out[0], trade_sems)
    stage.wait(*stage_refs)
    beside.wait(*beside_refs)


def experts_back(layer, gains, own, other, out_grad, state, pairs, masks, traded, beside):
    count = lax.axis_size("tensor")
    mid, gate, expert_rows, pre = state
    rows, width = mid.shape
    tokens = gate.shape[0]
    own, other = own[4:], other[4:]
    trade = Trade((rows, width)) if traded else None
    experts, depth, hidden_width = own[0].shape
    stage = FirstStage(
        jax.ShapeDtypeStruct((experts, hidden_width, width // 2), bf16), 2, layer
    )
    vmem = pl.BlockSpec(memory_space=pltpu.VMEM)
    hbm = pl.BlockSpec(memory_space=pl.ANY)
    shape = jax.ShapeDtypeStruct
    found = pl.pallas_call(
        functools.partial(experts_back_kernel, layer, count, trade, stage, beside),
        name=f"experts_back_{layer}",
        out_shape=(
            shape((rows, width), f32),
            shape((experts, width), f32),
            shape((1, width), f32),
            shape((experts, width // 2, 2 * hidden_width), bf16),
            *((shape((2, rows, width), f32),) if traded else ()),
            *stage.outputs,
            *beside.outputs,
        ),
        in_specs=[vmem] * 7 + [hbm] * 9 + [vmem] * len(traded) + [hbm] * len(beside.inputs),
        out_specs=(vmem, vmem, vmem, hbm)
        + (vmem,) * bool(traded)
        + (hbm,) * len(stage.outputs + beside.outputs),
        scratch_shapes=[
            pltpu.VMEM((experts, depth, 2 * hidden_width), bf16),
            pltpu.VMEM((experts * hidden_width, depth), bf16),
            pltpu.VMEM((tokens, width), bf16),
            pltpu.VMEM((tokens, width), bf16),
            Line.landing(count, rows, width),
            pltpu.VMEM((experts, tokens, 2 * hidden_width), f32),
            pltpu.VMEM((experts, tokens, 2 * hidden_width), bf16),
            pltpu.VMEM((tokens, width // 2), f32),
            pltpu.VMEM((tokens, 128), f32),
            pltpu.VMEM((count - 1, rows, 128), f32),
            pltpu.VMEM((2 * tokens, width // 2), bf16),
            pltpu.VMEM((experts, tokens, 2 * hidden_width), bf16),
            pltpu.VMEM((2 * tokens, width // 2), bf16),
            pltpu.VMEM((width // 2, 2 * tokens), bf16),
            pltpu.VMEM((2 * tokens, experts * hidden_width), bf16),
            pltpu.VMEM((experts, tokens, hidden_width), bf16),
            pltpu.VMEM((experts, width // 2, 2 * hidden_width), bf16),
            pltpu.VMEM(stage.blocks, bf16),
            *Line.sems(count, 4),
            pltpu.SemaphoreType.DMA((3, experts)),
            pltpu.SemaphoreType.DMA((experts,)),
            *[pltpu.SemaphoreType.DMA((3,)) for _ in range(5)],
            pltpu.SemaphoreType.DMA((experts,)),
            *(trade.sems if trade else ()),
            *stage.sems,
            *beside.sems,
        ],
        compiler_params=params(3 + layer),
    )(out_grad, mid, *gains[1:], masks[1], gate, expert_rows, pre, *pairs, *own, *other,
      *traded, *beside.inputs)
    kept = 5 if traded else 4
    parts = kept + len(stage.outputs)
    return found[:kept], found[kept:parts], beside.results(found[parts:])


def attention_back_kernel(layer, count, last, beside, *refs):
    refs = list(refs)

    def take(number):
        taken = refs[:number]
        del refs[:number]
        return taken

    mid_grad, stream_in, attn_gains, cosine, sine, qs, keys, values, probs = take(9)
    attn_gain = attn_gains.at[layer]
    stream = stream_in.at[lax.axis_index("section")] if layer == 0 else stream_in
    ai_in, attended_in = take(2)
    own, other = take(4), take(4)
    small_parts = take(5 if last else 0)
    later_grad = take(1 if last else 0)
    beside_in = take(len(beside.inputs))
    if last:
        dense_sum, small_sum, trade = last
        traded_out, small_out, whole_out = take(3)
    else:
        grad_out, attn_gain_out, dense_out = take(3)
    beside_out = take(len(beside.outputs))
    scratch = take(2)
    joint_s, output_s = scratch
    (ag2, part, landing2, ag_stack, dq_s, joint_rows, joint_peer, ao_s, ai_s, turned_ai, attended_s,
     dense_s, send_s, recv_s, attn_sems, core_send, core_recv, local_sems,
     hand_send, hand_recv) = take(20)
    if last:
        grad_s, trade_sems = refs.pop(0), take(len(trade.sems))
        dense_sems, small_sems = take(len(dense_sum.sems)), take(len(small_sum.sems))
        dense_refs = ([dense_s], [whole_out], dense_sems)
    beside_refs = (beside_in, beside_out, refs)
    rows, width = stream.shape
    tokens = ag2.shape[0]
    kw = keys.shape[1]
    qw = output_s.shape[0]
    heads, key_heads = qw // HD, kw // HD
    group = heads // key_heads
    me = lax.axis_index("tensor")
    own_rows = pl.ds(pl.multiple_of(me * rows, rows), rows)
    ag_line, rs_line = [Line(count, rows, v) for v in (True, False)]
    gathering = ag2, (send_s.at[0], recv_s.at[0])
    use_own = lax.axis_index("section") == layer
    ag2[own_rows, :] = mid_grad[...].astype(bf16)
    everyone = Beside([*beside.jobs, dense_sum]) if last else beside
    greet(tensor_peers(count) + [core_peer()] + (whole_group() if last else everyone.peers()))
    ag_line.gather_start(*gathering)
    either(use_own, own, other, lambda w: [c.start() for c in attn_copies(w, scratch, attn_sems)])
    loads = hand_halves(ai_in, ai_s, [v.at[0] for v in (local_sems, hand_send, hand_recv)])
    loads += hand_rows(attended_in, attended_s, [v.at[1] for v in (local_sems, hand_send, hand_recv)])
    for copy in loads:
        copy.start()
    beside.start(*beside_refs)
    wait_all(loads)
    turned_ai[...] = ai_s[...].T
    ag_line.gather_wait(*gathering)
    core = lax.axis_index("section")
    half = width // 2
    ao_s[pl.ds(0, tokens), :] = ag2[:, pl.ds(pl.multiple_of(core * half, half), half)]
    handed = [
        remote(ag2.at[:, pl.ds(pl.multiple_of((1 - core) * half, half), half)],
               ao_s.at[pl.ds(tokens, tokens)], core_send.at[0], core_recv.at[0], core_peer())
    ]
    handed[0].start()
    either(use_own, own, other, lambda w: [c.wait() for c in attn_copies(w, scratch, attn_sems)])
    attended_grad = dot(ag2[...], output_s[...], NT).astype(bf16)
    for h in range(heads):
        ag_stack[pl.ds(h * tokens, tokens), :] = attended_grad[:, h * HD : (h + 1) * HD]
    for g in range(key_heads):
        lanes = pl.ds(g * HD, HD)
        span = pl.ds(g * group * tokens, group * tokens)
        soft_b = probs[span, :]
        soft = soft_b.astype(f32)
        soft_grad = dot(ag_stack[span, :], values[:, lanes], NT)
        inner = jnp.sum(soft * soft_grad, axis=1, keepdims=True)
        score_grad = (soft * (soft_grad - inner)).astype(bf16)
        dq = dot(score_grad, keys[:, lanes], NN) * 0.125
        for h in range(group):
            dq_s[:, pl.ds((g * group + h) * HD, HD)] = dq[h * tokens : (h + 1) * tokens]
        dq_s[:, pl.ds(qw + g * HD, HD)] = dot(score_grad, qs[span, :], TN) * 0.125
        joint_rows[:, pl.ds(qw + kw + g * HD, HD)] = dot(soft_b, ag_stack[span, :], TN).astype(bf16)
    for chunk in range((qw + kw) // 128):
        lanes = pl.ds(chunk * 128, 128)
        block = dq_s[:, lanes]
        joint_rows[:, lanes] = (block * cosine[...] - turned(block) * sine[...]).astype(bf16)
    handed.append(remote(joint_rows, joint_peer, core_send.at[1], core_recv.at[1], core_peer()))
    handed[1].start()
    tile = width // 2
    dealt = [
        (part, pl.ds(t * tile, tile), landing2, (send_s.at[1 + t], recv_s.at[1 + t])) for t in range(2)
    ]
    for each in dealt:
        part[:, each[1]] = dot(joint_rows[...], joint_s[each[1], :], NT).astype(bf16)
        rs_line.scatter_start(*each)
    for each in dealt:
        rs_line.scatter_relay(*each)
    wait_all(handed)
    wide = qw + 2 * kw
    joint_grads = (
        dot(turned_ai[:, :tokens], joint_rows[...], NN) + dot(turned_ai[:, tokens:], joint_peer[...], NN)
    ).astype(bf16)
    output_grads = dot(ao_s[...], attended_s[...], TN).astype(bf16)
    outer, inner, depth = dense_s.shape[:3]
    for block in range(outer * inner):
        cut = slice(block * depth, (block + 1) * depth)
        dense_s[block // inner, block % inner, :, :wide] = joint_grads[cut]
        dense_s[block // inner, block % inner, :, wide:] = output_grads[cut]
    if last:
        dense_sum.start(*dense_refs)
    else:
        save = pltpu.make_async_copy(dense_s, dense_out, local_sems.at[0])
        save.start()
    beside.middle(*beside_refs)
    for each in dealt:
        rs_line.scatter_wait(*each)
    in_grad = rs_line.total(part[own_rows, :].astype(f32), landing2)
    stream_part, attn_gain_grad = norm_back(
        stream[...].astype(bf16).astype(f32), attn_gain[...], in_grad
    )
    grad = mid_grad[...] + stream_part
    if not last:
        attn_gain_out[...] = attn_gain_grad
        grad_out[...] = grad
        save.wait()
        beside.wait(*beside_refs)
        return
    small = small_sems[0]
    router0, gain0, router1, attn_gain1, gain1 = small_parts
    place = 0
    for value in (router0[...], attn_gain_grad, gain0[...]):
        small[pl.ds(place, value.shape[0]), :] = value
        place += value.shape[0]
    place = small.shape[0] // 2
    for value in (router1[...], attn_gain1[...], gain1[...]):
        small[pl.ds(place, value.shape[0]), :] = value
        place += value.shape[0]
    small_sum.first(small_sems)
    grad_s[...] = grad
    trade.start(grad_s, later_grad[0], trade_sems)
    dense_sum.middle1(*dense_refs)
    small_sum.second(small_sems)
    dense_sum.middle2(*dense_refs)
    small_sum.third(small_sems)
    dense_sum.middle3(*dense_refs)
    trade.wait(grad_s, traded_out, trade_sems)
    small_sum.last(small_sems, small_out)
    dense_sum.wait(*dense_refs)
    beside.wait(*beside_refs)


def attention_back(layer, gains, own, other, mid_grad, stream, state, pairs, tables, ending, beside):
    count = lax.axis_size("tensor")
    qs, keys, values, probs = state
    rows, width = mid_grad.shape
    tokens = keys.shape[0]
    own, other = own[:4], other[:4]
    qw, kw = own[0].shape[1], own[1].shape[1]
    heads = qw // HD
    vmem = pl.BlockSpec(memory_space=pltpu.VMEM)
    hbm = pl.BlockSpec(memory_space=pl.ANY)
    shape = jax.ShapeDtypeStruct
    groups = lax.axis_size("dp")
    dense = shape((*factors(groups), width // 2 // groups, 2 * qw + 2 * kw), bf16)
    if ending:
        depth = 2 * (-(-(ending[0].shape[0] + 2) // 8) * 8)
        last = (DenseSum(dense, layer), SmallSum(depth, width), Trade((rows, width)))
        own_outs = (shape((2, rows, width), f32), shape((depth, width), f32), *last[0].outputs)
        more = [pltpu.VMEM((rows, width), f32), *last[2].sems, *last[0].sems, *last[1].sems]
    else:
        last, more = None, []
        own_outs = (shape((rows, width), f32), shape((1, width), f32), dense)
    found = pl.pallas_call(
        functools.partial(attention_back_kernel, layer, count, last, beside),
        name=f"attention_back_{layer}",
        out_shape=(*own_outs, *beside.outputs),
        in_specs=[vmem] * 9 + [hbm] * 10 + [vmem] * len(ending) + [hbm] * len(beside.inputs),
        out_specs=(vmem, vmem, hbm) + (hbm,) * len(beside.outputs),
        scratch_shapes=[
            pltpu.VMEM((width, qw + 2 * kw), bf16),
            pltpu.VMEM((qw, width), bf16),
            pltpu.VMEM((tokens, width), bf16),
            pltpu.VMEM((tokens, width), bf16),
            Line.landing(count, rows, width),
            pltpu.VMEM((heads * tokens, HD), bf16),
            pltpu.VMEM((tokens, qw + kw), f32),
            pltpu.VMEM((tokens, qw + 2 * kw), bf16),
            pltpu.VMEM((tokens, qw + 2 * kw), bf16),
            pltpu.VMEM((2 * tokens, width // 2), bf16),
            pltpu.VMEM((2 * tokens, width // 2), bf16),
            pltpu.VMEM((width // 2, 2 * tokens), bf16),
            pltpu.VMEM((2 * tokens, qw), bf16),
            pltpu.VMEM(dense.shape, bf16),
            *Line.sems(count, 3),
            pltpu.SemaphoreType.DMA((4,)),
            *[pltpu.SemaphoreType.DMA((2,)) for _ in range(5)],
            *more,
            *beside.sems,
        ],
        compiler_params=params(5 + layer),
    )(mid_grad, stream, gains[0], *tables[:2], qs, keys, values, probs, *pairs, *own, *other,
      *ending, *beside.inputs)
    return found[:3], beside.results(found[3:])


def prepare_kernel(lengths, dealing, order, routes, attn_gain, expert_gain, router, freqs,
                   cosine, sine, bias, picked, kept, attn_gains, expert_gains, routers,
                   order_peer, routes_peer, sends, recvs):
    core = lax.axis_index("section")
    attn_gains[core] = attn_gain[...]
    expert_gains[core] = expert_gain[...]
    routers[core] = router[...]
    greet([core_peer()])
    copies = [
        remote(source, target, sends.at[index], recvs.at[index], core_peer())
        for index, (source, target) in enumerate((
            (order.at[1 - core], order_peer),
            (routes.at[1 - core], routes_peer),
            (attn_gain, attn_gains.at[core]),
            (expert_gain, expert_gains.at[core]),
            (router, routers.at[core]),
        ))
    ]
    start_all(copies)
    tokens = bias.shape[0]
    sequences = lengths.shape[1]
    tall = lax.broadcasted_iota(jnp.int32, (tokens, 1), 0)
    wide = lax.broadcasted_iota(jnp.int32, (1, tokens), 1)
    sizes = [lengths[core, index] for index in range(sequences)]
    starts = [sum(sizes[:index], 0) for index in range(sequences)]
    ranks = [
        sum(jnp.where(dealing[core, place] == index, place, 0) for place in range(sequences))
        for index in range(sequences)
    ]
    dealt_starts = [
        sum(jnp.where(ranks[before] < ranks[index], sizes[before], 0) for before in range(sequences))
        for index in range(sequences)
    ]

    def places(token):
        segment = sum((token >= starts[index] + sizes[index]).astype(jnp.int32)
                      for index in range(sequences))
        position, dealt = token, token
        for index in range(sequences):
            inside = segment == index
            position = jnp.where(inside, token - starts[index], position)
            dealt = jnp.where(inside, token - starts[index] + dealt_starts[index], dealt)
        return segment, position, dealt

    segment, position, dealt = places(tall)
    segment_wide, _, dealt_wide = places(wide)
    allowed = (segment == segment_wide) & (wide <= tall)
    bias[...] = jnp.where(allowed, 0.0, masked_score).astype(f32)
    angles = position.astype(f32) * freqs[...]
    cosine[...] = jnp.cos(angles)
    lane = lax.broadcasted_iota(jnp.int32, (1, freqs.shape[1]), 1)
    sine[...] = jnp.sin(angles) * jnp.where(lane % HD < HD // 2, -1.0, 1.0)

    def masks(order_row, route_rows):
        order_wide = order_row.astype(f32)
        order_tall = jnp.sum(jnp.where(tall == wide, order_wide, 0.0), axis=1, keepdims=True)
        first = jnp.sum(jnp.where(dealt == wide, order_wide, 0.0), axis=1, keepdims=True)
        first_wide = jnp.sum(jnp.where(dealt_wide == tall, order_tall, 0.0), axis=0, keepdims=True)
        earlier = jnp.where(first_wide < first, 1.0, 0.0).astype(bf16)
        experts = picked.shape[2]
        index = lax.broadcasted_iota(jnp.int32, (experts, tokens), 0)
        chosen = jnp.zeros((experts, tokens), f32)
        for k in range(route_rows.shape[0]):
            chosen = jnp.where(route_rows[k : k + 1] == index, 1.0, chosen)
        chosen = chosen.T
        rank = dot(earlier, chosen.astype(bf16), NN)
        return chosen, jnp.where(rank < CAP, chosen, 0.0)

    picked[core], kept[core] = masks(order[core], routes[core])
    wait_all(copies)
    picked[1 - core], kept[1 - core] = masks(order_peer[...], routes_peer[...])


def prepare(lengths, dealing, order, routes, attn_gain, expert_gain, router):
    tokens = order.shape[2]
    width = attn_gain.shape[1]
    half = HD // 2
    freqs = np.tile(rope_base ** (-2.0 * np.arange(half) / HD), 128 // half)[None].astype(np.float32)
    vmem = pl.BlockSpec(memory_space=pltpu.VMEM)
    smem = pl.BlockSpec(memory_space=pltpu.SMEM)
    shape = jax.ShapeDtypeStruct
    found = pl.pallas_call(
        prepare_kernel,
        name="prepare",
        out_shape=(
            shape((tokens, 128), f32),
            shape((tokens, 128), f32),
            shape((tokens, tokens), f32),
            shape((2, tokens, E), f32),
            shape((2, tokens, E), f32),
            shape((2, 1, width), f32),
            shape((2, 1, width), f32),
            shape((2, *router.shape), bf16),
        ),
        in_specs=[smem] * 2 + [vmem] * 6,
        out_specs=(vmem,) * 8,
        scratch_shapes=[
            pltpu.VMEM(order.shape[1:], order.dtype),
            pltpu.VMEM(routes.shape[1:], routes.dtype),
            dma((5,)),
            dma((5,)),
        ],
        compiler_params=params(8),
    )(lengths, dealing, order, routes, attn_gain, expert_gain, router, freqs)
    return found[:3], found[3:5], found[5:]


def assemble_kernel(section, *refs):
    expert_refs, dense_refs, rows_in, outs = (refs[:4], refs[4:8]), refs[8:10], refs[10:12], refs[12:]
    query, key, value, output, gate, up, down = outs[:7]
    for source, target in zip(rows_in, outs[7:]):
        target[...] = source[...]
    hidden_width = gate.shape[2]
    qw, kw = query.shape[1], key.shape[1]

    def write(parts, dense):
        cores = range(2)
        pair = [[jnp.sum(v[core, :, 0].astype(f32), axis=0) for v in parts[:2]] for core in cores]
        depth = 0
        for block in pair[0] + pair[1]:
            rows = pl.ds(depth, block.shape[0])
            gate[0, rows, :] = block[:, :hidden_width]
            up[0, rows, :] = block[:, hidden_width:]
            depth += block.shape[0]
        depth = 0
        for core in cores:
            for v in parts[2:]:
                block = jnp.sum(v[core, :, 0].astype(f32), axis=0)
                down[0, :, pl.ds(depth, block.shape[1])] = block
                depth += block.shape[1]
        rows = dense[...].astype(f32)
        query[...] = rows[:, :qw]
        key[...] = rows[:, qw : qw + kw]
        value[...] = rows[:, qw + kw : qw + 2 * kw]
        output[...] = rows[:, qw + 2 * kw :].T

    pl.when(section[0] == 0)(lambda: write(expert_refs[0], dense_refs[0]))
    pl.when(section[0] == 1)(lambda: write(expert_refs[1], dense_refs[1]))


def assemble(parts, denses, rows_in, qw, kw):
    groups = parts[0][0].shape[2]
    hidden_width = parts[0][2].shape[3]
    dense = [v.reshape(-1, v.shape[-1]) for v in denses]
    depth = dense[0].shape[0]
    rows = depth // groups

    def part_spec(layer, shape):
        block = (*shape[:2], 1, *shape[3:])
        return pl.BlockSpec(block, lambda e, s: (0, 0, jnp.where(s[0] == layer, e, 0), 0, 0))

    def dense_spec(layer, width):
        return pl.BlockSpec((rows, width), lambda e, s: (jnp.where(s[0] == layer, e, 0), 0))

    _, own_rows, width = rows_in[0].shape
    row_spec = pl.BlockSpec((2, own_rows // groups, width), lambda e, s: (0, e, 0))
    shape = jax.ShapeDtypeStruct
    return pl.pallas_call(
        assemble_kernel,
        name="assemble",
        out_shape=(
            shape((depth, qw), f32),
            shape((depth, kw), f32),
            shape((depth, kw), f32),
            shape((qw, depth), f32),
            shape((groups, depth, hidden_width), f32),
            shape((groups, depth, hidden_width), f32),
            shape((groups, hidden_width, depth), f32),
            *[shape(v.shape, f32) for v in rows_in],
        ),
        grid_spec=pltpu.PrefetchScalarGridSpec(
            num_scalar_prefetch=1,
            grid=(groups,),
            in_specs=[part_spec(layer, v.shape) for layer in range(2) for v in parts[layer]]
            + [dense_spec(layer, dense[layer].shape[1]) for layer in range(2)]
            + [row_spec] * 2,
            out_specs=(
                pl.BlockSpec((rows, qw), lambda e, s: (e, 0)),
                pl.BlockSpec((rows, kw), lambda e, s: (e, 0)),
                pl.BlockSpec((rows, kw), lambda e, s: (e, 0)),
                pl.BlockSpec((qw, rows), lambda e, s: (0, e)),
                pl.BlockSpec((1, depth, hidden_width), lambda e, s: (e, 0, 0)),
                pl.BlockSpec((1, depth, hidden_width), lambda e, s: (e, 0, 0)),
                pl.BlockSpec((1, hidden_width, depth), lambda e, s: (e, 0, 0)),
                row_spec,
                row_spec,
            ),
        ),
        compiler_params=pltpu.CompilerParams(vmem_limit_bytes=58 * 2**20),
    )(lax.axis_index("section").astype(jnp.int32)[None], *parts[0], *parts[1], *dense, *rows_in)


def shards(
    tokens_in, out_cotangent, attn_gain, query_weight, key_weight, value_weight, output_weight,
    expert_gain, router_weight, gate_weight, up_weight, down_weight, lengths, dealing,
    slot_order, routes,
):
    first = lax.axis_index("section") == 0
    qw, kw = query_weight.shape[2], key_weight.shape[2]
    own = (query_weight[0], key_weight[0], value_weight[0], output_weight[0], gate_weight[0],
           up_weight[0], down_weight[0])
    tables, masks, gains = prepare(lengths[:, 0], dealing[:, 0], slot_order[0],
                                   jnp.swapaxes(routes[0], 1, 2), attn_gain, expert_gain,
                                   router_weight[0].T)
    (out0, *state0), other = layer_forward(0, gains, own, None, tokens_in, tables, masks)
    (out1, *state1), _ = layer_forward(1, gains, own, other, out0, tables, masks)
    saved = (state0, state1)
    streams = (tokens_in, out0)

    def experts(layer, out_grad, traded, jobs):
        mid, expert_rows, qs, keys, values, probs, gate, ai, x, gated, attended, pre = saved[layer]
        return experts_back(
            layer, gains, own, other, out_grad, (mid, gate, expert_rows, pre), (x, gated), masks,
            traded, Beside(jobs)
        )

    def attention(layer, mid_grad, ending, jobs):
        mid, expert_rows, qs, keys, values, probs, gate, ai, x, gated, attended, pre = saved[layer]
        return attention_back(
            layer, gains, own, other, mid_grad, streams[layer], (qs, keys, values, probs),
            (ai, attended), tables, ending, Beside(jobs)
        )

    def bring(layer, sums):
        return [Bring(layer, kind, v) for kind, v in zip(("column", "row"), sums)]

    (mid_grad, router1, gain1, pair, layer_outputs), down1, _ = experts(
        1, out_cotangent, (out0, out1), []
    )
    (grad1, attn_gain1, dense1), (sums,) = attention(1, mid_grad, (), [FirstStage(pair, 1)])
    (mid_grad, router0, gain0, pair), down0, (*pair1, dense1) = experts(
        0, grad1, (), bring(1, sums) + [DenseSum(dense1, 1)]
    )
    (input_grads, small, dense0), (pair0,) = attention(
        0, mid_grad, (router0, gain0, router1, attn_gain1, gain1, grad1),
        [FirstStage(pair, 1, 0)]
    )
    parts0, parts1 = [*pair0, *down0], [*pair1, *down1]
    query, key, value, output, gate, up, down, layer_outputs, input_grads = assemble(
        (parts0, parts1), (dense0, dense1), (layer_outputs, input_grads), qw, kw
    )
    small = jnp.where(first, small[: small.shape[0] // 2], small[small.shape[0] // 2 :])
    router_grad, attn_gain_grad, expert_gain_grad = small[:E].T, small[E : E + 1], small[E + 1 : E + 2]
    return (
        layer_outputs[None],
        input_grads[None],
        attn_gain_grad,
        query[None],
        key[None],
        value[None],
        output[None],
        expert_gain_grad,
        router_grad[None],
        gate[None],
        up[None],
        down[None],
    )


def solution(mesh):
    return jax.shard_map(
        shards,
        mesh=mesh,
        in_specs=(
            P(None, ("dp", "tensor"), None),
            P(None, ("dp", "tensor"), None),
            P("section", None),
            P("section", None, "tensor"),
            P("section", None, "tensor"),
            P("section", None, "tensor"),
            P("section", "tensor", None),
            P("section", None),
            P("section", None, None),
            P("section", None, None, "tensor"),
            P("section", None, None, "tensor"),
            P("section", None, "tensor", None),
            P(None, "dp", None),
            P(None, "dp", None),
            P("section", None, "dp", None),
            P("section", None, "dp", None),
        ),
        out_specs=(
            P("section", None, ("dp", "tensor"), None),
            P("section", None, ("dp", "tensor"), None),
            P("section", None),
            P("section", None, "tensor"),
            P("section", None, "tensor"),
            P("section", None, "tensor"),
            P("section", "tensor", None),
            P("section", None),
            P("section", None, None),
            P("section", "dp", None, "tensor"),
            P("section", "dp", None, "tensor"),
            P("section", "dp", "tensor", None),
        ),
        check_vma=False,
    )
```

```python
import functools
import math

import jax
import jax.numpy as jnp
import numpy as np
from jax import lax
from jax.experimental import pallas as pl
from jax.experimental.pallas import tpu as pltpu
from jax.sharding import PartitionSpec as P

H = 24
KV = 8
HD = 64
E = 16
CAP = 160

epsilon = 1e-05
rope_base = 10000.0
masked_score = -1e30
bf16 = jnp.bfloat16
f32 = jnp.float32
MESH = pl.DeviceIdType.MESH


def dot(a, b, dims):
    return lax.dot_general(a, b, (dims, ((), ())), preferred_element_type=f32)


NN = ((1,), (0,))
NT = ((1,), (1,))
TN = ((0,), (0,))


def norm_scale(rows_in):
    return lax.rsqrt(jnp.mean(rows_in * rows_in, axis=-1, keepdims=True) + epsilon)


def params(collective_id):
    return pltpu.CompilerParams(
        collective_id=collective_id, has_side_effects=True, vmem_limit_bytes=56 * 2**20
    )


def tensor_peers(count):
    me = lax.axis_index("tensor")
    return [{"tensor": lax.rem(me + step, count)} for step in range(1, count)]


def greet(peers):
    barrier = pltpu.get_barrier_semaphore()
    for peer in peers:
        pl.semaphore_signal(barrier, inc=1, device_id=peer, device_id_type=MESH)
    pl.semaphore_wait(barrier, len(peers))


def factors(count):
    inner = math.isqrt(count)
    while count % inner:
        inner -= 1
    return count // inner, inner


def group_place(count):
    outer, inner = factors(count)
    me = lax.axis_index("dp")
    return outer, inner, me // inner, lax.rem(me, inner)


def near_groups(count):
    outer, inner, mo, mi = group_place(count)
    across = [lax.rem(mi + step, inner) for step in range(1, inner)]
    along = [lax.rem(mo + step, outer) for step in range(1, outer)]
    return (
        [(place, {"dp": mo * inner + place}) for place in across],
        [(place, {"dp": place * inner + mi}) for place in along],
    )


dma = pltpu.SemaphoreType.DMA


def remote(src, dst, send, recv, device):
    return pltpu.make_async_remote_copy(
        src_ref=src, dst_ref=dst, send_sem=send, recv_sem=recv, device_id=device, device_id_type=MESH
    )


class Bring:
    def __init__(self, layer, kind, value, in_vmem=False, target=None):
        self.layer, self.kind, self.in_vmem = layer, kind, in_vmem
        self.whole = kind == "all" or target is not None
        self.target = target or (lambda outputs, core, place: outputs[0].at[core, place])
        count = lax.axis_size("dp")
        outer, inner = factors(count)
        self.size = {"column": outer, "row": inner, "all": count}[kind]
        block = value.shape if self.whole else value.shape[1:]
        self.inputs = [value]
        self.outputs = [jax.ShapeDtypeStruct((2, self.size, *block), value.dtype)]
        self.sems = [dma((self.size,)), dma((2, self.size)), dma((2,))]
        if not in_vmem:
            self.sems.append(pltpu.VMEM(block, value.dtype))

    def place(self, step):
        count = lax.axis_size("dp")
        outer, inner, mo, mi = group_place(count)
        if self.kind == "column":
            place = lax.rem(mo + step, outer)
            return place, place * inner + mi
        if self.kind == "row":
            place = lax.rem(mi + step, inner)
            return place, mo * inner + place
        place = lax.rem(lax.axis_index("dp") + step, count)
        return place, place

    def parts(self, inputs, outputs, sems):
        core = lax.axis_index("section")
        mine, _ = self.place(0)
        target = self.target(outputs, core, mine)
        recv = sems[1].at[core, mine]

        def source(place):
            return inputs[0] if self.whole else inputs[0].at[place]

        sent = []
        for step in range(1, self.size):
            place, group = self.place(step)
            sent.append(
                remote(source(place), target, sems[0].at[step - 1], recv,
                       {"dp": group, "section": self.layer})
            )
        across = remote(source(mine), target, sems[0].at[self.size - 1], recv, core_peer())
        if self.in_vmem:
            local = [pltpu.make_async_copy(source(mine), target, sems[2].at[0])]
        else:
            local = [
                pltpu.make_async_copy(source(mine), sems[3], sems[2].at[0]),
                pltpu.make_async_copy(sems[3], target, sems[2].at[1]),
            ]
        return sent, across, local

    def start(self, inputs, outputs, sems):
        sent, across, local = self.parts(inputs, outputs, sems)
        for copy in sent:
            copy.start()
        here = lax.axis_index("section") == self.layer

        @pl.when(here)
        def _():
            local[0].start()

        @pl.when(jnp.logical_not(here))
        def _():
            across.start()

    def wait(self, inputs, outputs, sems):
        sent, across, local = self.parts(inputs, outputs, sems)
        core = lax.axis_index("section")
        here = core == self.layer
        block = inputs[0] if self.whole else inputs[0].at[0]

        def arrived(which, place):
            remote(block, self.target(outputs, which, place), sems[0].at[0], sems[1].at[which, place],
                   core_peer()).wait_recv()

        for copy in sent:
            copy.wait_send()

        @pl.when(here)
        def _():
            local[0].wait()
            for copy in local[1:]:
                copy.start()
                copy.wait()
            for step in range(self.size):
                place, _ = self.place(step)
                if step:
                    arrived(core, place)
                arrived(1 - core, place)

        @pl.when(jnp.logical_not(here))
        def _():
            across.wait_send()

    def results(self, outputs):
        return outputs[0]


class FirstStage:
    def __init__(self, value, axis, layer=None):
        self.count = lax.axis_size("dp")
        outer, inner = factors(self.count)
        self.blocks = (outer, inner, value.shape[0] // self.count, *value.shape[1:])
        inside = isinstance(value, jax.ShapeDtypeStruct)
        self.inputs = [] if inside else [value.reshape(self.blocks)]
        self.axis = axis
        shape = list(self.blocks[2:])
        shape[axis] //= 2
        self.shape = shape
        sums = [
            jax.ShapeDtypeStruct((outer, *shape), value.dtype),
            jax.ShapeDtypeStruct((inner, *shape), value.dtype),
        ]
        self.sems = [
            dma((inner + outer - 2,)),
            dma((inner + outer - 2,)),
            pltpu.VMEM((inner - 1, outer, *shape), value.dtype),
            pltpu.VMEM((outer - 1, inner, *shape), value.dtype),
            *[pltpu.VMEM(v.shape, v.dtype) for v in sums],
            dma((2,)),
            dma((2,)),
        ]
        self.outputs = sums
        self.brings = []
        if layer is not None:
            self.brings = [Bring(layer, kind, v, True) for kind, v in zip(("column", "row"), sums)]
            self.outputs = [v for bring in self.brings for v in bring.outputs]
            self.sems += [v for bring in self.brings for v in bring.sems]

    def copies(self, inputs, sems):
        across, along = near_groups(self.count)
        _, _, mo, mi = group_place(self.count)
        value = inputs[0]
        half = self.shape[self.axis]
        cut = [slice(None)] * 3
        first, second = list(cut), list(cut)
        first[self.axis], second[self.axis] = pl.ds(0, half), pl.ds(half, half)
        found = []
        for slot, (place, device) in enumerate(across):
            found.append((value.at[(slice(None), place, *first)], sems[2].at[slot], device))
        for slot, (place, device) in enumerate(along):
            found.append((value.at[(place, slice(None), *second)], sems[3].at[slot], device))
        sent = [
            remote(src, dst, sems[0].at[index], sems[1].at[index], device)
            for index, (src, dst, device) in enumerate(found)
        ]
        loads = [
            pltpu.make_async_copy(value.at[(slice(None), mi, *first)], sems[4], sems[6].at[0]),
            pltpu.make_async_copy(value.at[(mo, slice(None), *second)], sems[5], sems[6].at[1]),
        ]
        return sent + loads

    def onward(self, outputs, sems):
        place = 8
        found = []
        for index, bring in enumerate(self.brings):
            found.append((bring, [sems[4 + index]], [outputs[index]], sems[place : place + len(bring.sems)]))
            place += len(bring.sems)
        return found

    def saves(self, outputs, sems):
        return [pltpu.make_async_copy(sems[4 + k], outputs[k], sems[7].at[k]) for k in range(2)]

    def start(self, inputs, outputs, sems):
        start_all(self.copies(inputs, sems))

    def middle(self, inputs, outputs, sems):
        wait_all(self.copies(inputs, sems))
        going = self.onward(outputs, sems) if self.brings else self.saves(outputs, sems)
        for index, (total, landed) in enumerate(((sems[4], sems[2]), (sems[5], sems[3]))):
            depth = total.shape[1]

            def add(index, carry, total=total, landed=landed, depth=depth):
                place, expert = index // depth, lax.rem(index, depth)
                value = total[place, expert].astype(f32)
                for slot in range(landed.shape[0]):
                    value = value + landed[slot, place, expert].astype(f32)
                total[place, expert] = value.astype(bf16)
                return carry

            lax.fori_loop(0, total.shape[0] * depth, add, 0)
            if self.brings:
                bring, *refs = going[index]
                bring.start(*refs)
            else:
                going[index].start()

    def wait(self, inputs, outputs, sems):
        if self.brings:
            for bring, *refs in self.onward(outputs, sems):
                bring.wait(*refs)
        else:
            wait_all(self.saves(outputs, sems))

    def results(self, outputs):
        return outputs


class DenseSum:
    def __init__(self, value, layer):
        count = lax.axis_size("dp")
        outer, inner = factors(count)
        rows, width = value.shape[2:]
        half = width // 2
        self.half = half
        inside = isinstance(value, jax.ShapeDtypeStruct)
        self.inputs = [] if inside else [value]
        self.outputs = [jax.ShapeDtypeStruct((2, *value.shape), bf16)]

        def buffer(*lead):
            return pltpu.VMEM((*lead, rows, half), bf16)

        self.brings = [
            Bring(layer, "row", jax.ShapeDtypeStruct((outer, rows, half), bf16), True,
                  lambda outputs, core, place: outputs[0].at[core, :, place, :, pl.ds(0, half)]),
            Bring(layer, "column", jax.ShapeDtypeStruct((inner, rows, half), bf16), True,
                  lambda outputs, core, place: outputs[0].at[core, place, :, :, pl.ds(half, half)]),
        ]
        pairs = inner + outer - 2
        self.sems = [
            buffer(inner - 1, outer),
            buffer(outer - 1, inner),
            buffer(outer),
            buffer(inner),
            buffer(outer - 1),
            buffer(inner - 1),
            buffer(outer),
            buffer(inner),
            dma((2,)),
            *[dma((pairs,)) for _ in range(6)],
            *[v for bring in self.brings for v in bring.sems],
        ]

    def numbered(self, found, sems, first):
        return [
            remote(src, dst, sems[first].at[index], sems[first + 1].at[index], device)
            for index, (src, dst, device) in enumerate(found)
        ]

    def sent(self, inputs, sems):
        count = lax.axis_size("dp")
        across, along = near_groups(count)
        _, _, mo, mi = group_place(count)
        value = inputs[0]
        low, high = pl.ds(0, self.half), pl.ds(self.half, self.half)
        found = [
            (value.at[:, place, :, low], sems[0].at[slot], device)
            for slot, (place, device) in enumerate(across)
        ] + [
            (value.at[place, :, :, high], sems[1].at[slot], device)
            for slot, (place, device) in enumerate(along)
        ]
        loads = [
            pltpu.make_async_copy(value.at[:, mi, :, low], sems[2], sems[8].at[0]),
            pltpu.make_async_copy(value.at[mo, :, :, high], sems[3], sems[8].at[1]),
        ]
        return self.numbered(found, sems, 9) + loads

    def sums(self, sems):
        across, along = near_groups(lax.axis_size("dp"))
        found = [
            (sems[2].at[place], sems[4].at[slot], device) for slot, (place, device) in enumerate(along)
        ] + [
            (sems[3].at[place], sems[5].at[slot], device) for slot, (place, device) in enumerate(across)
        ]
        return self.numbered(found, sems, 11)

    def blocks(self, sems):
        count = lax.axis_size("dp")
        across, along = near_groups(count)
        _, _, mo, mi = group_place(count)
        found = [(sems[6].at[mo], sems[6].at[mo], device) for _, device in along]
        found += [(sems[7].at[mi], sems[7].at[mi], device) for _, device in across]
        return self.numbered(found, sems, 13)

    def onward(self, outputs, sems):
        place = 15
        found = []
        for index, bring in enumerate(self.brings):
            found.append((bring, [sems[6 + index]], outputs, sems[place : place + len(bring.sems)]))
            place += len(bring.sems)
        return found

    def start(self, inputs, outputs, sems):
        start_all(self.sent(inputs, sems))

    def middle1(self, inputs, outputs, sems):
        wait_all(self.sent(inputs, sems))
        for total, landed in ((sems[2], sems[0]), (sems[3], sems[1])):
            for place in range(total.shape[0]):
                value = total[place].astype(f32)
                for slot in range(landed.shape[0]):
                    value = value + landed[slot, place].astype(f32)
                total[place] = value.astype(bf16)
        start_all(self.sums(sems))

    def middle2(self, inputs, outputs, sems):
        wait_all(self.sums(sems))
        _, _, mo, mi = group_place(lax.axis_size("dp"))
        for total, landed, whole, mine in (
            (sems[2], sems[4], sems[6], mo),
            (sems[3], sems[5], sems[7], mi),
        ):
            value = total[mine].astype(f32)
            for slot in range(landed.shape[0]):
                value = value + landed[slot].astype(f32)
            whole[mine] = value.astype(bf16)
        start_all(self.blocks(sems))

    def middle3(self, inputs, outputs, sems):
        wait_all(self.blocks(sems))
        for bring, *refs in self.onward(outputs, sems):
            bring.start(*refs)

    def wait(self, inputs, outputs, sems):
        for bring, *refs in self.onward(outputs, sems):
            bring.wait(*refs)

    def results(self, outputs):
        return outputs[0]


class SmallSum:
    def __init__(self, depth, width):
        self.tensor, self.count = lax.axis_size("tensor"), lax.axis_size("dp")
        self.lanes = width // self.tensor
        self.depth = depth
        part = (depth, self.lanes)
        self.sems = [
            pltpu.VMEM((depth, width), f32),
            pltpu.VMEM((self.tensor - 1, *part), f32),
            pltpu.VMEM((self.count - 1, *part), f32),
            *[pltpu.VMEM(part, f32) for _ in range(4)],
            pltpu.VMEM((depth, width), f32),
            dma((2, self.tensor - 1)),
            dma((2, self.tensor - 1)),
            dma((self.count,)),
            dma((self.count,)),
        ]

    def columns(self, place):
        return pl.ds(pl.multiple_of(place * self.lanes, self.lanes), self.lanes)

    def over_tensor(self, sems):
        here = lax.axis_index("tensor")
        found = []
        for step in range(1, self.tensor):
            place = lax.rem(here + step, self.tensor)
            found.append(
                remote(sems[0].at[:, self.columns(place)], sems[1].at[step - 1],
                       sems[8].at[0, step - 1], sems[9].at[0, step - 1], {"tensor": place})
            )
        return found

    def over_groups(self, sems):
        me = lax.axis_index("dp")
        return [
            remote(sems[3], sems[2].at[step - 1], sems[10].at[step - 1], sems[11].at[step - 1],
                   {"dp": lax.rem(me + step, self.count)})
            for step in range(1, self.count)
        ]

    def over_cores(self, sems):
        last = self.count - 1
        return [remote(sems[4], sems[5], sems[10].at[last], sems[11].at[last], core_peer())]

    def back(self, sems):
        here = lax.axis_index("tensor")
        own = sems[7].at[:, self.columns(here)]
        return [
            remote(sems[6], own, sems[8].at[1, step - 1], sems[9].at[1, step - 1],
                   {"tensor": lax.rem(here + step, self.tensor)})
            for step in range(1, self.tensor)
        ]

    def first(self, sems):
        start_all(self.over_tensor(sems))

    def second(self, sems):
        wait_all(self.over_tensor(sems))
        total = sems[0][:, self.columns(lax.axis_index("tensor"))]
        for slot in range(self.tensor - 1):
            total = total + sems[1][slot]
        sems[3][...] = total
        start_all(self.over_groups(sems))

    def third(self, sems):
        wait_all(self.over_groups(sems))
        total = sems[3][...]
        for slot in range(self.count - 1):
            total = total + sems[2][slot]
        sems[4][...] = total
        copies = self.over_cores(sems)
        start_all(copies)
        wait_all(copies)
        sems[6][...] = sems[4][...] + sems[5][...]
        start_all(self.back(sems))
        sems[7][:, self.columns(lax.axis_index("tensor"))] = sems[6][...]

    def last(self, sems, out):
        wait_all(self.back(sems))
        out[...] = sems[7][...]


class Trade:
    def __init__(self, shape):
        self.sems = [pltpu.VMEM((2, *shape), f32), dma((1,)), dma((1,))]

    def copy(self, value, sems):
        core = lax.axis_index("section")
        return remote(value, sems[0].at[core], sems[1].at[0], sems[2].at[0], core_peer())

    def start(self, zero, one, sems):
        core = lax.axis_index("section")

        @pl.when(core == 0)
        def _():
            self.copy(one, sems).start()
            sems[0][0] = zero[...]

        @pl.when(core == 1)
        def _():
            self.copy(zero, sems).start()
            sems[0][1] = one[...]

    def wait(self, zero, out, sems):
        self.copy(zero, sems).wait()
        out[...] = sems[0][...]


def both_cores(groups):
    core = lax.axis_index("section")
    return [{"dp": group, "section": which} for group in groups for which in (core, 1 - core)]


def whole_group():
    count = lax.axis_size("dp")
    me = lax.axis_index("dp")
    return both_cores([lax.rem(me + step, count) for step in range(1, count)])


class Beside:
    def __init__(self, jobs):
        self.jobs = jobs
        self.inputs = [v for job in jobs for v in job.inputs]
        self.outputs = [v for job in jobs for v in job.outputs]
        self.sems = [v for job in jobs for v in job.sems]

    def peers(self):
        count = lax.axis_size("dp")
        if not self.jobs:
            return []
        across, along = near_groups(count)
        return both_cores([device["dp"] for _, device in across + along])

    def each(self, refs, run):
        inputs, outputs, sems = refs
        for job in self.jobs:
            mine, inputs = inputs[: len(job.inputs)], inputs[len(job.inputs) :]
            theirs, outputs = outputs[: len(job.outputs)], outputs[len(job.outputs) :]
            own, sems = sems[: len(job.sems)], sems[len(job.sems) :]
            run(job)(mine, theirs, own)

    def start(self, *refs):
        self.each(refs, lambda job: job.start)

    def middle(self, *refs, step="middle"):
        self.each(refs, lambda job: getattr(job, step, lambda *refs: None))

    def wait(self, *refs):
        self.each(refs, lambda job: job.wait)

    def results(self, outputs):
        found = []
        for job in self.jobs:
            found.append(job.results(outputs[: len(job.outputs)]))
            outputs = outputs[len(job.outputs) :]
        return found


def deal_out(count, part, rows, columns, landing, sends, recvs):
    me = lax.axis_index("tensor")
    copies = []
    for step in range(1, count):
        peer = lax.rem(me + step, count)
        copies.append(
            pltpu.make_async_remote_copy(
                src_ref=part.at[pl.ds(pl.multiple_of(peer * rows, rows), rows), columns],
                dst_ref=landing.at[step - 1, :, columns],
                send_sem=sends.at[step - 1],
                recv_sem=recvs.at[step - 1],
                device_id={"tensor": peer},
                device_id_type=MESH,
            )
        )
    for copy in copies:
        copy.start()
    return copies


class Line:
    def __init__(self, count, rows, passing=True):
        self.count, self.rows = count, rows
        self.passing = passing and count == 4
        self.me = me = lax.axis_index("tensor")
        half = me // 2
        self.partner = me + 1 - 2 * lax.rem(me, 2)
        self.far_inner, self.far_edge = 2 - half, 3 - 3 * half
        self.inner = me == 1 + half

    def cut(self, place):
        return pl.ds(pl.multiple_of(place * self.rows, self.rows), self.rows)

    def shard(self, buf, sems, place, target, index):
        buf, columns = buf if isinstance(buf, tuple) else (buf, slice(None))
        rows = buf.at[self.cut(place), columns]
        return remote(rows, rows, sems[0].at[index], sems[1].at[place], {"tensor": target})

    def gather_start(self, buf, sems):
        if self.passing:
            self.shard(buf, sems, self.me, self.far_inner, 1).start()
            self.shard(buf, sems, self.me, self.partner, 0).start()
        else:
            for step in range(1, self.count):
                self.shard(buf, sems, self.me, lax.rem(self.me + step, self.count), step - 1).start()

    def gather_wait(self, buf, sems):
        def arrived(place):
            self.shard(buf, sems, place, self.partner, 0).wait_recv()

        def left(number):
            for index in range(number):
                self.shard(buf, sems, self.me, self.partner, index).wait_send()

        if not self.passing:
            for step in range(1, self.count):
                arrived(lax.rem(self.me + step, self.count))
            left(self.count - 1)
            return

        @pl.when(self.inner)
        def _():
            arrived(self.far_inner)
            self.shard(buf, sems, self.far_inner, self.partner, 2).start()
            arrived(self.far_edge)
            self.shard(buf, sems, self.far_edge, self.partner, 3).start()
            arrived(self.partner)
            left(4)

        @pl.when(jnp.logical_not(self.inner))
        def _():
            for place in (self.partner, self.far_inner, self.far_edge):
                arrived(place)
            left(2)

    def block(self, part, place, columns, landing, slot, sems, index, target):
        return remote(part.at[self.cut(place), columns], landing.at[slot, :, columns],
                      sems[0].at[index], sems[1].at[slot], {"tensor": target})

    def scatter_start(self, part, columns, landing, sems):
        if not self.passing:
            for step in range(1, self.count):
                peer = lax.rem(self.me + step, self.count)
                self.block(part, peer, columns, landing, step - 1, sems, step - 1, peer).start()
            return

        @pl.when(self.inner)
        def _():
            self.block(part, self.partner, columns, landing, 2, sems, 0, self.partner).start()

        @pl.when(jnp.logical_not(self.inner))
        def _():
            for slot, place in enumerate((self.far_edge, self.far_inner, self.partner)):
                self.block(part, place, columns, landing, slot, sems, slot, self.partner).start()

    def scatter_relay(self, part, columns, landing, sems):
        if not self.passing:
            return

        @pl.when(self.inner)
        def _():
            for slot, place in enumerate((self.far_edge, self.far_inner)):
                self.block(part, place, columns, landing, slot, sems, 0, self.partner).wait_recv()
                landing[slot, :, columns] = (
                    landing[slot, :, columns].astype(f32) + part[self.cut(place), columns].astype(f32)
                ).astype(bf16)
                remote(landing.at[slot, :, columns], landing.at[3, :, columns], sems[0].at[1 + slot],
                       sems[1].at[3], {"tensor": place}).start()

    def scatter_wait(self, part, columns, landing, sems):
        slots = (2, 3) if self.passing else range(self.count - 1)
        for slot in slots:
            self.block(part, self.me, columns, landing, slot, sems, 0, self.partner).wait_recv()
        for index in range(3 if self.passing else self.count - 1):
            self.block(part, self.me, columns, landing, 0, sems, index, self.partner).wait_send()

    def total(self, own, landing):
        for slot in (2, 3) if self.passing else range(self.count - 1):
            own = own + landing[slot].astype(f32)
        return own

    @staticmethod
    def landing(count, rows, width):
        return pltpu.VMEM((4 if count == 4 else count - 1, rows, width), bf16)

    @staticmethod
    def sems(count, number):
        return [dma((number, count)), dma((number, count))]


def core_peer():
    return {"section": 1 - lax.axis_index("section")}


def hand_rows(value, pair, sems):
    tokens = value.shape[0]
    return [
        pltpu.make_async_copy(value, pair.at[pl.ds(0, tokens)], sems[0]),
        remote(value, pair.at[pl.ds(tokens, tokens)], sems[1], sems[2], core_peer()),
    ]


def hand_halves(value, pair, sems):
    section = lax.axis_index("section")
    tokens, half = value.shape[0], value.shape[1] // 2
    mine = value.at[:, pl.ds(pl.multiple_of(section * half, half), half)]
    other = value.at[:, pl.ds(pl.multiple_of((1 - section) * half, half), half)]
    return [
        pltpu.make_async_copy(mine, pair.at[pl.ds(0, tokens)], sems[0]),
        remote(other, pair.at[pl.ds(tokens, tokens)], sems[1], sems[2], core_peer()),
    ]


def start_all(copies):
    for copy in copies:
        copy.start()


def wait_all(copies):
    for copy in copies:
        copy.wait()


def either(use_own, own, other, run):
    @pl.when(use_own)
    def _():
        run(own)

    @pl.when(jnp.logical_not(use_own))
    def _():
        run(other)


def weight_copies(refs, scratch, sems, expert):
    gate, up, down = refs
    gu_s, down_s = scratch
    width = gate.shape[2]
    return (
        pltpu.make_async_copy(gate.at[expert], gu_s.at[expert, :, pl.ds(0, width)], sems.at[0, expert]),
        pltpu.make_async_copy(up.at[expert], gu_s.at[expert, :, pl.ds(width, width)], sems.at[1, expert]),
        pltpu.make_async_copy(
            down.at[expert], down_s.at[pl.ds(pl.multiple_of(expert * width, width), width)], sems.at[2, expert]
        ),
    )


def attn_copies(refs, scratch, sems):
    query, key, value, output = refs
    joint_s, output_s = scratch
    qw, kw = query.shape[1], key.shape[1]
    return (
        pltpu.make_async_copy(query, joint_s.at[:, pl.ds(0, qw)], sems.at[0]),
        pltpu.make_async_copy(key, joint_s.at[:, pl.ds(qw, kw)], sems.at[1]),
        pltpu.make_async_copy(value, joint_s.at[:, pl.ds(qw + kw, kw)], sems.at[2]),
        pltpu.make_async_copy(output, output_s, sems.at[3]),
    )


def turned(block):
    lane = lax.broadcasted_iota(jnp.int32, block.shape, 1)
    half = HD // 2
    return jnp.where(
        lane % HD < half, pltpu.roll(block, block.shape[1] - half, 1), pltpu.roll(block, half, 1)
    )


def column(table, index):
    lane = lax.broadcasted_iota(jnp.int32, table.shape, 1)
    return jnp.sum(jnp.where(lane == index, table, 0.0), axis=1, keepdims=True)


def swap_copies(own, other, sems, piece):
    sends, recvs = sems
    names = len(own)
    if isinstance(piece, tuple):
        name, expert = piece
        source, target = own[name].at[expert], other[name].at[expert]
        index = 4 + (name - 4) * own[4].shape[0] + expert
    else:
        source, target, index = own[piece], other[piece], piece
    return pltpu.make_async_remote_copy(
        src_ref=source, dst_ref=target, send_sem=sends.at[index], recv_sem=recvs.at[index],
        device_id=core_peer(), device_id_type=MESH,
    )


def forward_kernel(layer, count, swap, *refs):
    refs = list(refs)

    def take(number):
        taken = refs[:number]
        del refs[:number]
        return taken

    (stream_in, attn_gains, expert_gains, routers, cosine, sine, bias, pickeds, kepts) = take(9)
    attn_gain, expert_gain, router = attn_gains.at[layer], expert_gains.at[layer], routers.at[layer]
    picked, kept = pickeds.at[layer], kepts.at[layer]
    stream = stream_in.at[lax.axis_index("section")] if layer == 0 else stream_in
    own = take(7)
    other = None if swap else take(7)
    (out, mid_out, expert_rows_out, qs_out, keys_out, values_out, probs_out, gate_out,
     attn_in_out, expert_in_out, gated_out, attended_out, pre_out) = take(13)
    if swap:
        other = take(7)
    scratch = take(4)
    joint_s, output_s, gu_s, down_s = scratch
    (ag1, ag2, part, landing1, landing2, pre_s, gated_s, attended_s, send_s, recv_s, attn_sems,
     expert_sems, pre_sems, save_sems) = refs[:14]
    if swap:
        swap_sems = refs[14:]
    rows, width = stream.shape
    tokens = ag1.shape[0]
    experts = gu_s.shape[0]
    hidden_width = gu_s.shape[2] // 2
    kw = keys_out.shape[1]
    qw = attended_s.shape[1]
    heads, key_heads = qw // HD, kw // HD
    group = heads // key_heads
    me = lax.axis_index("tensor")
    own_rows = pl.ds(pl.multiple_of(me * rows, rows), rows)
    ag1_line, rs1_line, ag2_line, rs2_line = [Line(count, rows, v) for v in (True, True, False, True)]

    def sems(index):
        return send_s.at[index], recv_s.at[index]

    use_own = lax.axis_index("section") == layer
    middle = width // 2
    gathering = [((ag1, pl.ds(0, middle)), sems(0)), ((ag1, pl.ds(middle, middle)), sems(7))]

    def start_attn(w):
        for copy in attn_copies(w[:4], scratch[:2], attn_sems):
            copy.start()

    def wait_attn(w):
        for copy in attn_copies(w[:4], scratch[:2], attn_sems):
            copy.wait()

    def start_expert(w, expert):
        for copy in weight_copies(w[4:], scratch[2:], expert_sems, expert):
            copy.start()

    def wait_expert(w, expert):
        for copy in weight_copies(w[4:], scratch[2:], expert_sems, expert):
            copy.wait()

    def each_expert(run):
        def step(expert, carry):
            run(expert)
            return carry

        lax.fori_loop(0, experts, step, 0)

    def swap_expert(expert):
        return [swap_copies(own, other, swap_sems, (name, expert)) for name in (4, 5, 6)]

    value = stream[...].astype(bf16).astype(f32)
    ag1[own_rows, :] = (value * norm_scale(value) * attn_gain[...]).astype(bf16)
    greet(tensor_peers(count) + ([core_peer()] if swap else []))
    if swap:
        lead = min(4, experts)
        for piece in range(4):
            swap_copies(own, other, swap_sems, piece).start()
        each_expert(lambda expert: [c.start() for c in swap_expert(expert)] and None)

        @pl.when(use_own)
        def _():
            [ag1_line.gather_start(*each) for each in gathering]
            start_attn(own)
            each_expert(lambda expert: start_expert(own, expert))

        @pl.when(jnp.logical_not(use_own))
        def _():
            for piece in range(4):
                swap_copies(own, other, swap_sems, piece).wait_recv()
            start_attn(other)
            for expert in range(lead):
                for copy in swap_expert(expert):
                    copy.wait_recv()
                start_expert(other, expert)
            [ag1_line.gather_start(*each) for each in gathering]
    else:
        [ag1_line.gather_start(*each) for each in gathering]
        either(use_own, own, other, start_attn)
        either(use_own, own, other, lambda w: each_expert(lambda expert: start_expert(w, expert)))
    for each in gathering:
        ag1_line.gather_wait(*each)
    saved = [pltpu.make_async_copy(ag1, attn_in_out, save_sems.at[0])]
    saved[0].start()
    either(use_own, own, other, wait_attn)
    proj = dot(ag1[...], joint_s[...], NN)
    for chunk in range(qw // 128):
        block = proj[:, chunk * 128 : chunk * 128 + 128]
        block = (block * cosine[...] + turned(block) * sine[...]).astype(bf16)
        for part_index in range(128 // HD):
            head = chunk * (128 // HD) + part_index
            qs_out[pl.ds(head * tokens, tokens), :] = block[:, part_index * HD : part_index * HD + HD]
    for chunk in range(kw // 128):
        block = proj[:, qw + chunk * 128 : qw + chunk * 128 + 128]
        keys_out[:, pl.ds(chunk * 128, 128)] = (
            block * cosine[...] + turned(block) * sine[...]
        ).astype(bf16)
    values_out[...] = proj[:, qw + kw :].astype(bf16)
    for g in range(key_heads):
        lanes = pl.ds(g * HD, HD)
        span = pl.ds(g * group * tokens, group * tokens)
        scores = dot(qs_out[span, :], keys_out[:, lanes], NT) * 0.125
        scores = (scores.reshape(group, tokens, tokens) + bias[...][None]).reshape(
            group * tokens, tokens
        )
        top = jnp.max(scores, axis=1, keepdims=True)
        weighed = jnp.exp(scores - top)
        probs = (weighed / jnp.sum(weighed, axis=1, keepdims=True)).astype(bf16)
        probs_out[span, :] = probs
        attended = dot(probs, values_out[:, lanes], NN).astype(bf16)
        for h in range(group):
            attended_s[:, pl.ds((g * group + h) * HD, HD)] = attended[h * tokens : (h + 1) * tokens]
    saved.append(pltpu.make_async_copy(attended_s, attended_out, save_sems.at[1]))
    saved[1].start()
    half = width // 2
    dealt = [(part, pl.ds(t * half, half), landing1, sems(1 + 8 * t)) for t in range(2)]
    for each in dealt:
        part[:, each[1]] = dot(attended_s[...], output_s[:, each[1]], NN).astype(bf16)
        rs1_line.scatter_start(*each)
    for each in dealt:
        rs1_line.scatter_relay(*each)
    for each in dealt:
        rs1_line.scatter_wait(*each)
    mid = rs1_line.total(value + part[own_rows, :].astype(f32), landing1)
    mid_out[...] = mid
    expert_rows = (mid * norm_scale(mid) * expert_gain[...]).astype(bf16)
    expert_rows_out[...] = expert_rows
    ag2[own_rows, :] = expert_rows
    split = width // 2
    columns = pl.ds(0, split), pl.ds(split, split)
    ag2_line.gather_start((ag2, columns[0]), sems(2))
    ag2_line.gather_start((ag2, columns[1]), sems(8))
    if swap:

        @pl.when(jnp.logical_not(use_own))
        def _():
            def landed(expert, carry):
                for copy in swap_expert(expert):
                    copy.wait_recv()
                start_expert(other, expert)
                return carry

            lax.fori_loop(lead, experts, landed, 0)

    ag2_line.gather_wait((ag2, columns[0]), sems(2))

    def first_step(expert, carry):
        either(use_own, own, other, lambda w: wait_expert(w, expert))
        pre_s[expert] = dot(ag2[:, columns[0]], gu_s[expert, columns[0], :], NN)
        return carry

    lax.fori_loop(0, experts, first_step, 0)
    ag2_line.gather_wait((ag2, columns[1]), sems(8))
    saved.append(pltpu.make_async_copy(ag2, expert_in_out, save_sems.at[2]))
    saved[2].start()
    logits = dot(ag2[...], router[...], NT)
    chosen = picked[...] > 0
    top = jnp.max(jnp.where(chosen, logits, masked_score), axis=1, keepdims=True)
    weighed = jnp.where(chosen, jnp.exp(logits - top), 0.0)
    gate_out[...] = weighed / jnp.sum(weighed, axis=1, keepdims=True)

    def expert_step(expert, carry):
        pre = pre_s[expert] + dot(ag2[:, columns[1]], gu_s[expert, columns[1], :], NN)
        pre_s[expert] = pre
        pltpu.make_async_copy(pre_s.at[expert], pre_out.at[expert], pre_sems.at[expert]).start()
        gate_pre, up_pre = pre[:, :hidden_width], pre[:, hidden_width:]
        hidden = (gate_pre / (1.0 + jnp.exp(-gate_pre)) * up_pre).astype(bf16).astype(f32)
        weight = column(gate_out[...] * kept[...], expert)
        gated_s[:, pl.ds(pl.multiple_of(expert * hidden_width, hidden_width), hidden_width)] = (
            hidden * weight
        ).astype(bf16)
        return carry

    lax.fori_loop(0, experts, expert_step, 0)
    saved.append(pltpu.make_async_copy(gated_s, gated_out, save_sems.at[3]))
    saved[3].start()
    tile = width // 4
    dealt = [(part, pl.ds(t * tile, tile), landing2, sems(3 + t)) for t in range(4)]
    for each in dealt:
        part[:, each[1]] = dot(gated_s[...], down_s[:, each[1]], NN).astype(bf16)
        rs2_line.scatter_start(*each)
    for each in dealt:
        rs2_line.scatter_relay(*each)
    for each in dealt:
        rs2_line.scatter_wait(*each)
    total = rs2_line.total(mid_out[...] + part[own_rows, :].astype(f32), landing2)
    out[...] = total
    wait_all(saved)
    if swap:
        for piece in range(4):
            swap_copies(own, other, swap_sems, piece).wait_send()
        each_expert(lambda expert: [c.wait_send() for c in swap_expert(expert)] and None)

        @pl.when(use_own)
        def _():
            for piece in range(4):
                swap_copies(own, other, swap_sems, piece).wait_recv()
            each_expert(lambda expert: [c.wait_recv() for c in swap_expert(expert)] and None)

    def finish(expert, carry):
        pltpu.make_async_copy(pre_s.at[expert], pre_out.at[expert], pre_sems.at[expert]).wait()
        return carry

    lax.fori_loop(0, experts, finish, 0)


def weight_scratch(own):
    query, key, value, output, gate, up, down = own
    depth = query.shape[0]
    experts, _, hidden_width = gate.shape
    return [
        pltpu.VMEM((depth, query.shape[1] + 2 * key.shape[1]), bf16),
        pltpu.VMEM(output.shape, bf16),
        pltpu.VMEM((experts, depth, 2 * hidden_width), bf16),
        pltpu.VMEM((experts * hidden_width, depth), bf16),
    ]


def layer_forward(layer, gains, own, other, stream, tables, masks):
    count = lax.axis_size("tensor")
    rows, width = stream.shape[-2:]
    tokens = tables[2].shape[0]
    qw, kw = own[0].shape[1], own[1].shape[1]
    experts, _, hidden_width = own[4].shape
    heads = qw // HD
    swap = other is None
    vmem = pl.BlockSpec(memory_space=pltpu.VMEM)
    hbm = pl.BlockSpec(memory_space=pl.ANY)
    shape = jax.ShapeDtypeStruct
    pieces = 4 + 3 * experts
    found = pl.pallas_call(
        functools.partial(forward_kernel, layer, count, swap),
        name=f"layer_forward_{layer}",
        out_shape=(
            shape((rows, width), f32),
            shape((rows, width), f32),
            shape((rows, width), bf16),
            shape((heads * tokens, HD), bf16),
            shape((tokens, kw), bf16),
            shape((tokens, kw), bf16),
            shape((heads * tokens, tokens), bf16),
            shape((tokens, experts), f32),
            shape((tokens, width), bf16),
            shape((tokens, width), bf16),
            shape((tokens, experts * hidden_width), bf16),
            shape((tokens, qw), bf16),
            shape((experts, tokens, 2 * hidden_width), f32),
        )
        + (tuple(shape(w.shape, w.dtype) for w in own) if swap else ()),
        in_specs=[vmem] * 9 + [hbm] * (7 if swap else 14),
        out_specs=(vmem,) * 8 + (hbm,) * (12 if swap else 5),
        scratch_shapes=weight_scratch(own)
        + [
            pltpu.VMEM((tokens, width), bf16),
            pltpu.VMEM((tokens, width), bf16),
            pltpu.VMEM((tokens, width), bf16),
            Line.landing(count, rows, width),
            Line.landing(count, rows, width),
            pltpu.VMEM((experts, tokens, 2 * hidden_width), f32),
            pltpu.VMEM((tokens, experts * hidden_width), bf16),
            pltpu.VMEM((tokens, qw), bf16),
            *Line.sems(count, 10),
            dma((4,)),
            dma((3, experts)),
            dma((experts,)),
            dma((4,)),
        ]
        + ([dma((pieces,)), dma((pieces,))] if swap else []),
        compiler_params=params(1 + layer),
    )(stream, *gains, *tables, *masks, *own,
      *(() if swap else other))
    return found[:13], found[13:]


def norm_back(value, gain, out_grad):
    scale = norm_scale(value)
    scaled = value * scale
    gain_grad = jnp.sum(out_grad * scaled, axis=0, keepdims=True)
    inner = out_grad * gain
    value_grad = scale * (inner - scaled * jnp.mean(inner * scaled, axis=-1, keepdims=True))
    return value_grad, gain_grad


def experts_back_kernel(layer, count, trade, stage, beside, *refs):
    refs = list(refs)

    def take(number):
        taken = refs[:number]
        del refs[:number]
        return taken

    out_grad, mid, expert_gains, routers, kepts, gate, expert_rows, pre_in = take(8)
    expert_gain, router, kept = expert_gains.at[layer], routers.at[layer], kepts.at[layer]
    x_in, gated_in = take(2)
    own, other = take(3), take(3)
    traded = take(2 if trade else 0)
    beside_in = take(len(beside.inputs))
    mid_grad_out, router_out, expert_gain_out, pair_out = take(4)
    traded_out = take(1 if trade else 0)
    stage_out = take(len(stage.outputs))
    beside_out = take(len(beside.outputs))
    scratch = take(2)
    gu_s, down_s = scratch
    (ag1, part, landing1, pre_s, gpu_s, acc, gate_part, gate_land, og_s, gpu_peer, x_s, turned_x,
     gated_s, hidden_s, pair_s, down_grad_s, send_s, recv_s, expert_sems, pre_sems, core_send, core_recv,
     local_sems, hand_send, hand_recv, save_sems) = take(26)
    trade_sems = take(len(trade.sems) if trade else 0)
    stage_refs = ([down_grad_s], stage_out, take(len(stage.sems)))
    beside_refs = (beside_in, beside_out, refs)
    rows, width = mid.shape
    tokens = ag1.shape[0]
    experts = gu_s.shape[0]
    hidden_width = gu_s.shape[2] // 2
    me = lax.axis_index("tensor")
    own_rows = pl.ds(pl.multiple_of(me * rows, rows), rows)
    ag_line, rs_line = [Line(count, rows, v) for v in (False, False)]
    gathering = ag1, (send_s.at[0], recv_s.at[0])
    tile = width // 2
    dealt = [
        (part, pl.ds(t * tile, tile), landing1, (send_s.at[3 * t], recv_s.at[3 * t]))
        if t
        else (part, pl.ds(0, tile), landing1, (send_s.at[1], recv_s.at[1]))
        for t in range(2)
    ]
    use_own = lax.axis_index("section") == layer

    def start_expert(expert, carry):
        either(use_own, own, other,
               lambda w: [c.start() for c in weight_copies(w, scratch, expert_sems, expert)])
        pltpu.make_async_copy(pre_in.at[expert], pre_s.at[expert], pre_sems.at[expert]).start()
        return carry

    everyone = Beside([*beside.jobs, stage])
    if layer:
        ag1[own_rows, :] = out_grad[lax.axis_index("section")]
        greet(tensor_peers(count) + [core_peer()] + everyone.peers())
        ag_line.gather_start(*gathering)
    else:
        ag1[own_rows, :] = out_grad[...].astype(bf16)
        greet(tensor_peers(count) + [core_peer()] + everyone.peers())
        ag_line.gather_start(*gathering)
    lax.fori_loop(0, experts, start_expert, 0)
    loads = hand_halves(x_in, x_s, [v.at[0] for v in (local_sems, hand_send, hand_recv)])
    loads += hand_rows(gated_in, gated_s, [v.at[1] for v in (local_sems, hand_send, hand_recv)])
    for copy in loads:
        copy.start()
    beside.start(*beside_refs)
    if trade:
        trade.start(*traded, trade_sems)
    gate_part[...] = jnp.zeros_like(gate_part)

    def ready_step(expert, carry):
        pltpu.make_async_copy(pre_in.at[expert], pre_s.at[expert], pre_sems.at[expert]).wait()
        gate_pre = pre_s[expert, :, pl.ds(0, hidden_width)]
        up_pre = pre_s[expert, :, pl.ds(hidden_width, hidden_width)]
        sig = 1.0 / (1.0 + jnp.exp(-gate_pre))
        act = gate_pre * sig
        hidden_s[expert] = (act * up_pre).astype(bf16)
        weight = column(gate[...] * kept[...], expert)
        pre_s[expert, :, pl.ds(0, hidden_width)] = (
            weight * up_pre * (sig * (1.0 + gate_pre * (1.0 - sig)))
        )
        pre_s[expert, :, pl.ds(hidden_width, hidden_width)] = weight * act
        return carry

    lax.fori_loop(0, experts, ready_step, 0)
    ag_line.gather_wait(*gathering)
    core = lax.axis_index("section")
    half = width // 2
    og_s[pl.ds(0, tokens), :] = ag1[:, pl.ds(pl.multiple_of(core * half, half), half)]
    handed = [
        remote(ag1.at[:, pl.ds(pl.multiple_of((1 - core) * half, half), half)],
               og_s.at[pl.ds(tokens, tokens)], core_send.at[0], core_recv.at[0], core_peer())
    ]
    handed[0].start()
    wait_all(loads)
    handed[0].wait()
    _, inner, per_group = stage.blocks[:3]

    def down_step(index, carry):
        lanes = pl.ds(pl.multiple_of(index * 2 * hidden_width, 2 * hidden_width), 2 * hidden_width)
        grads = dot(gated_s[:, lanes], og_s[...], TN).astype(bf16)
        for k in range(2):
            expert = 2 * index + k
            group, place = expert // per_group, lax.rem(expert, per_group)
            down_grad_s[group // inner, lax.rem(group, inner), place] = grads[
                k * hidden_width : (k + 1) * hidden_width
            ]
        return carry

    lax.fori_loop(0, experts // 2, down_step, 0)
    stage.start(*stage_refs)
    beside.middle(*beside_refs, step="middle1")

    def expert_step(index, carry):
        pair = (2 * index, 2 * index + 1)
        for expert in pair:
            either(use_own, own, other,
                   lambda w: [c.wait() for c in weight_copies(w, scratch, expert_sems, expert)])
        lanes = pl.ds(pl.multiple_of(index * 2 * hidden_width, 2 * hidden_width), 2 * hidden_width)
        plain = dot(ag1[...], down_s[lanes, :], NT)
        lane = lax.broadcasted_iota(jnp.int32, gate_part.shape, 1)
        for k, expert in enumerate(pair):
            value = plain[:, k * hidden_width : (k + 1) * hidden_width]
            summed = jnp.sum(hidden_s[expert].astype(f32) * value, axis=1, keepdims=True)
            gate_part[...] += jnp.where(lane == expert, summed, 0.0)
            for cut in (pl.ds(0, hidden_width), pl.ds(hidden_width, hidden_width)):
                gpu_s[expert, :, cut] = (value * pre_s[expert, :, cut]).astype(bf16)
        return carry

    lax.fori_loop(0, experts // 2, expert_step, 0)
    gate_part[:, :experts] = gate_part[:, :experts] * kept[...]
    copies = deal_out(count, gate_part, rows, slice(None), gate_land, send_s.at[2], recv_s.at[2])
    handed.append(remote(gpu_s, gpu_peer, core_send.at[1], core_recv.at[1], core_peer()))
    handed[1].start()
    for each in dealt:
        columns = each[1]
        acc[...] = jnp.zeros_like(acc)

        def back_step(index, carry, columns=columns):
            pair = (2 * index, 2 * index + 1)
            acc[...] += dot(gpu_s[pair[0]], gu_s[pair[0], columns, :], NT) + dot(
                gpu_s[pair[1]], gu_s[pair[1], columns, :], NT
            )
            return carry

        lax.fori_loop(0, experts // 2, back_step, 0)
        part[:, columns] = acc[...].astype(bf16)
        rs_line.scatter_start(*each)
    beside.middle(*beside_refs, step="middle2")
    turned_x[...] = x_s[...].T
    wait_all(handed[1:])

    def saves(expert):
        return [pltpu.make_async_copy(pair_s.at[expert], pair_out.at[expert], save_sems.at[expert])]

    def grads_step(expert, carry):
        pair_s[expert] = (
            dot(turned_x[:, :tokens], gpu_s[expert], NN)
            + dot(turned_x[:, tokens:], gpu_peer[expert], NN)
        ).astype(bf16)
        for copy in saves(expert):
            copy.start()
        return carry

    lax.fori_loop(0, experts, grads_step, 0)
    beside.middle(*beside_refs, step="middle3")
    stage.middle(*stage_refs)
    wait_all(copies)
    for each in dealt:
        rs_line.scatter_wait(*each)
    in_grad = rs_line.total(part[own_rows, :].astype(f32), landing1)
    gate_grad = gate_part[own_rows, :]
    for step in range(count - 1):
        gate_grad = gate_grad + gate_land[step]
    gate_grad = gate_grad[:, :experts]
    gate_rows = gate[own_rows, :]
    logits_grad = (
        gate_rows * (gate_grad - jnp.sum(gate_rows * gate_grad, axis=1, keepdims=True))
    ).astype(bf16)
    router_out[...] = dot(logits_grad, expert_rows[...], TN)
    in_grad = in_grad + dot(logits_grad, router[...], NN)
    mid_part, expert_gain_grad = norm_back(mid[...], expert_gain[...], in_grad)
    expert_gain_out[...] = expert_gain_grad
    mid_grad_out[...] = ag1[own_rows, :].astype(f32) + mid_part

    def finish_save(expert, carry):
        for copy in saves(expert):
            copy.wait()
        return carry

    lax.fori_loop(0, experts, finish_save, 0)
    if trade:
        trade.wait(traded[0], traded_out[0], trade_sems)
    stage.wait(*stage_refs)
    beside.wait(*beside_refs)


def experts_back(layer, gains, own, other, out_grad, state, pairs, masks, traded, beside):
    count = lax.axis_size("tensor")
    mid, gate, expert_rows, pre = state
    rows, width = mid.shape
    tokens = gate.shape[0]
    own, other = own[4:], other[4:]
    trade = Trade((rows, width)) if traded else None
    experts, depth, hidden_width = own[0].shape
    stage = FirstStage(
        jax.ShapeDtypeStruct((experts, hidden_width, width // 2), bf16), 2, layer
    )
    vmem = pl.BlockSpec(memory_space=pltpu.VMEM)
    hbm = pl.BlockSpec(memory_space=pl.ANY)
    shape = jax.ShapeDtypeStruct
    found = pl.pallas_call(
        functools.partial(experts_back_kernel, layer, count, trade, stage, beside),
        name=f"experts_back_{layer}",
        out_shape=(
            shape((rows, width), f32),
            shape((experts, width), f32),
            shape((1, width), f32),
            shape((experts, width // 2, 2 * hidden_width), bf16),
            *((shape((2, rows, width), f32),) if traded else ()),
            *stage.outputs,
            *beside.outputs,
        ),
        in_specs=[vmem] * 7 + [hbm] * 9 + [vmem] * len(traded) + [hbm] * len(beside.inputs),
        out_specs=(vmem, vmem, vmem, hbm)
        + (vmem,) * bool(traded)
        + (hbm,) * len(stage.outputs + beside.outputs),
        scratch_shapes=[
            pltpu.VMEM((experts, depth, 2 * hidden_width), bf16),
            pltpu.VMEM((experts * hidden_width, depth), bf16),
            pltpu.VMEM((tokens, width), bf16),
            pltpu.VMEM((tokens, width), bf16),
            Line.landing(count, rows, width),
            pltpu.VMEM((experts, tokens, 2 * hidden_width), f32),
            pltpu.VMEM((experts, tokens, 2 * hidden_width), bf16),
            pltpu.VMEM((tokens, width // 2), f32),
            pltpu.VMEM((tokens, 128), f32),
            pltpu.VMEM((count - 1, rows, 128), f32),
            pltpu.VMEM((2 * tokens, width // 2), bf16),
            pltpu.VMEM((experts, tokens, 2 * hidden_width), bf16),
            pltpu.VMEM((2 * tokens, width // 2), bf16),
            pltpu.VMEM((width // 2, 2 * tokens), bf16),
            pltpu.VMEM((2 * tokens, experts * hidden_width), bf16),
            pltpu.VMEM((experts, tokens, hidden_width), bf16),
            pltpu.VMEM((experts, width // 2, 2 * hidden_width), bf16),
            pltpu.VMEM(stage.blocks, bf16),
            *Line.sems(count, 4),
            pltpu.SemaphoreType.DMA((3, experts)),
            pltpu.SemaphoreType.DMA((experts,)),
            *[pltpu.SemaphoreType.DMA((3,)) for _ in range(5)],
            pltpu.SemaphoreType.DMA((experts,)),
            *(trade.sems if trade else ()),
            *stage.sems,
            *beside.sems,
        ],
        compiler_params=params(3 + layer),
    )(out_grad, mid, *gains[1:], masks[1], gate, expert_rows, pre, *pairs, *own, *other,
      *traded, *beside.inputs)
    kept = 5 if traded else 4
    parts = kept + len(stage.outputs)
    return found[:kept], found[kept:parts], beside.results(found[parts:])


def attention_back_kernel(layer, count, last, beside, *refs):
    refs = list(refs)

    def take(number):
        taken = refs[:number]
        del refs[:number]
        return taken

    mid_grad, stream_in, attn_gains, cosine, sine, qs, keys, values, probs = take(9)
    attn_gain = attn_gains.at[layer]
    stream = stream_in.at[lax.axis_index("section")] if layer == 0 else stream_in
    ai_in, attended_in = take(2)
    own, other = take(4), take(4)
    small_parts = take(5 if last else 0)
    later_grad = take(1 if last else 0)
    beside_in = take(len(beside.inputs))
    if last:
        dense_sum, small_sum, trade = last
        traded_out, small_out, whole_out = take(3)
    else:
        grad_out, attn_gain_out, dense_out = take(3)
    beside_out = take(len(beside.outputs))
    scratch = take(2)
    joint_s, output_s = scratch
    (ag2, part, landing2, ag_stack, dq_s, joint_rows, joint_peer, ao_s, ai_s, turned_ai, attended_s,
     dense_s, send_s, recv_s, attn_sems, core_send, core_recv, local_sems,
     hand_send, hand_recv) = take(20)
    if last:
        grad_s, trade_sems = refs.pop(0), take(len(trade.sems))
        dense_sems, small_sems = take(len(dense_sum.sems)), take(len(small_sum.sems))
        dense_refs = ([dense_s], [whole_out], dense_sems)
    beside_refs = (beside_in, beside_out, refs)
    rows, width = stream.shape
    tokens = ag2.shape[0]
    kw = keys.shape[1]
    qw = output_s.shape[0]
    heads, key_heads = qw // HD, kw // HD
    group = heads // key_heads
    me = lax.axis_index("tensor")
    own_rows = pl.ds(pl.multiple_of(me * rows, rows), rows)
    ag_line, rs_line = [Line(count, rows, v) for v in (True, False)]
    gathering = ag2, (send_s.at[0], recv_s.at[0])
    use_own = lax.axis_index("section") == layer
    ag2[own_rows, :] = mid_grad[...].astype(bf16)
    everyone = Beside([*beside.jobs, dense_sum]) if last else beside
    greet(tensor_peers(count) + [core_peer()] + (whole_group() if last else everyone.peers()))
    ag_line.gather_start(*gathering)
    either(use_own, own, other, lambda w: [c.start() for c in attn_copies(w, scratch, attn_sems)])
    loads = hand_halves(ai_in, ai_s, [v.at[0] for v in (local_sems, hand_send, hand_recv)])
    loads += hand_rows(attended_in, attended_s, [v.at[1] for v in (local_sems, hand_send, hand_recv)])
    for copy in loads:
        copy.start()
    beside.start(*beside_refs)
    wait_all(loads)
    turned_ai[...] = ai_s[...].T
    ag_line.gather_wait(*gathering)
    core = lax.axis_index("section")
    half = width // 2
    ao_s[pl.ds(0, tokens), :] = ag2[:, pl.ds(pl.multiple_of(core * half, half), half)]
    handed = [
        remote(ag2.at[:, pl.ds(pl.multiple_of((1 - core) * half, half), half)],
               ao_s.at[pl.ds(tokens, tokens)], core_send.at[0], core_recv.at[0], core_peer())
    ]
    handed[0].start()
    either(use_own, own, other, lambda w: [c.wait() for c in attn_copies(w, scratch, attn_sems)])
    attended_grad = dot(ag2[...], output_s[...], NT).astype(bf16)
    for h in range(heads):
        ag_stack[pl.ds(h * tokens, tokens), :] = attended_grad[:, h * HD : (h + 1) * HD]
    for g in range(key_heads):
        lanes = pl.ds(g * HD, HD)
        span = pl.ds(g * group * tokens, group * tokens)
        soft_b = probs[span, :]
        soft = soft_b.astype(f32)
        soft_grad = dot(ag_stack[span, :], values[:, lanes], NT)
        inner = jnp.sum(soft * soft_grad, axis=1, keepdims=True)
        score_grad = (soft * (soft_grad - inner)).astype(bf16)
        dq = dot(score_grad, keys[:, lanes], NN) * 0.125
        for h in range(group):
            dq_s[:, pl.ds((g * group + h) * HD, HD)] = dq[h * tokens : (h + 1) * tokens]
        dq_s[:, pl.ds(qw + g * HD, HD)] = dot(score_grad, qs[span, :], TN) * 0.125
        joint_rows[:, pl.ds(qw + kw + g * HD, HD)] = dot(soft_b, ag_stack[span, :], TN).astype(bf16)
    for chunk in range((qw + kw) // 128):
        lanes = pl.ds(chunk * 128, 128)
        block = dq_s[:, lanes]
        joint_rows[:, lanes] = (block * cosine[...] - turned(block) * sine[...]).astype(bf16)
    handed.append(remote(joint_rows, joint_peer, core_send.at[1], core_recv.at[1], core_peer()))
    handed[1].start()
    tile = width // 2
    dealt = [
        (part, pl.ds(t * tile, tile), landing2, (send_s.at[1 + t], recv_s.at[1 + t])) for t in range(2)
    ]
    for each in dealt:
        part[:, each[1]] = dot(joint_rows[...], joint_s[each[1], :], NT).astype(bf16)
        rs_line.scatter_start(*each)
    for each in dealt:
        rs_line.scatter_relay(*each)
    wait_all(handed)
    wide = qw + 2 * kw
    joint_grads = (
        dot(turned_ai[:, :tokens], joint_rows[...], NN) + dot(turned_ai[:, tokens:], joint_peer[...], NN)
    ).astype(bf16)
    output_grads = dot(ao_s[...], attended_s[...], TN).astype(bf16)
    outer, inner, depth = dense_s.shape[:3]
    for block in range(outer * inner):
        cut = slice(block * depth, (block + 1) * depth)
        dense_s[block // inner, block % inner, :, :wide] = joint_grads[cut]
        dense_s[block // inner, block % inner, :, wide:] = output_grads[cut]
    if last:
        dense_sum.start(*dense_refs)
    else:
        save = pltpu.make_async_copy(dense_s, dense_out, local_sems.at[0])
        save.start()
    beside.middle(*beside_refs)
    for each in dealt:
        rs_line.scatter_wait(*each)
    in_grad = rs_line.total(part[own_rows, :].astype(f32), landing2)
    stream_part, attn_gain_grad = norm_back(
        stream[...].astype(bf16).astype(f32), attn_gain[...], in_grad
    )
    grad = mid_grad[...] + stream_part
    if not last:
        attn_gain_out[...] = attn_gain_grad
        grad_out[...] = grad
        save.wait()
        beside.wait(*beside_refs)
        return
    small = small_sems[0]
    router0, gain0, router1, attn_gain1, gain1 = small_parts
    place = 0
    for value in (router0[...], attn_gain_grad, gain0[...]):
        small[pl.ds(place, value.shape[0]), :] = value
        place += value.shape[0]
    place = small.shape[0] // 2
    for value in (router1[...], attn_gain1[...], gain1[...]):
        small[pl.ds(place, value.shape[0]), :] = value
        place += value.shape[0]
    small_sum.first(small_sems)
    grad_s[...] = grad
    trade.start(grad_s, later_grad[0], trade_sems)
    dense_sum.middle1(*dense_refs)
    small_sum.second(small_sems)
    dense_sum.middle2(*dense_refs)
    small_sum.third(small_sems)
    dense_sum.middle3(*dense_refs)
    trade.wait(grad_s, traded_out, trade_sems)
    small_sum.last(small_sems, small_out)
    dense_sum.wait(*dense_refs)
    beside.wait(*beside_refs)


def attention_back(layer, gains, own, other, mid_grad, stream, state, pairs, tables, ending, beside):
    count = lax.axis_size("tensor")
    qs, keys, values, probs = state
    rows, width = mid_grad.shape
    tokens = keys.shape[0]
    own, other = own[:4], other[:4]
    qw, kw = own[0].shape[1], own[1].shape[1]
    heads = qw // HD
    vmem = pl.BlockSpec(memory_space=pltpu.VMEM)
    hbm = pl.BlockSpec(memory_space=pl.ANY)
    shape = jax.ShapeDtypeStruct
    groups = lax.axis_size("dp")
    dense = shape((*factors(groups), width // 2 // groups, 2 * qw + 2 * kw), bf16)
    if ending:
        depth = 2 * (-(-(ending[0].shape[0] + 2) // 8) * 8)
        last = (DenseSum(dense, layer), SmallSum(depth, width), Trade((rows, width)))
        own_outs = (shape((2, rows, width), f32), shape((depth, width), f32), *last[0].outputs)
        more = [pltpu.VMEM((rows, width), f32), *last[2].sems, *last[0].sems, *last[1].sems]
    else:
        last, more = None, []
        own_outs = (shape((rows, width), f32), shape((1, width), f32), dense)
    found = pl.pallas_call(
        functools.partial(attention_back_kernel, layer, count, last, beside),
        name=f"attention_back_{layer}",
        out_shape=(*own_outs, *beside.outputs),
        in_specs=[vmem] * 9 + [hbm] * 10 + [vmem] * len(ending) + [hbm] * len(beside.inputs),
        out_specs=(vmem, vmem, hbm) + (hbm,) * len(beside.outputs),
        scratch_shapes=[
            pltpu.VMEM((width, qw + 2 * kw), bf16),
            pltpu.VMEM((qw, width), bf16),
            pltpu.VMEM((tokens, width), bf16),
            pltpu.VMEM((tokens, width), bf16),
            Line.landing(count, rows, width),
            pltpu.VMEM((heads * tokens, HD), bf16),
            pltpu.VMEM((tokens, qw + kw), f32),
            pltpu.VMEM((tokens, qw + 2 * kw), bf16),
            pltpu.VMEM((tokens, qw + 2 * kw), bf16),
            pltpu.VMEM((2 * tokens, width // 2), bf16),
            pltpu.VMEM((2 * tokens, width // 2), bf16),
            pltpu.VMEM((width // 2, 2 * tokens), bf16),
            pltpu.VMEM((2 * tokens, qw), bf16),
            pltpu.VMEM(dense.shape, bf16),
            *Line.sems(count, 3),
            pltpu.SemaphoreType.DMA((4,)),
            *[pltpu.SemaphoreType.DMA((2,)) for _ in range(5)],
            *more,
            *beside.sems,
        ],
        compiler_params=params(5 + layer),
    )(mid_grad, stream, gains[0], *tables[:2], qs, keys, values, probs, *pairs, *own, *other,
      *ending, *beside.inputs)
    return found[:3], beside.results(found[3:])


def prepare_kernel(lengths, dealing, order, routes, attn_gain, expert_gain, router, freqs,
                   cosine, sine, bias, picked, kept, attn_gains, expert_gains, routers,
                   order_peer, routes_peer, sends, recvs):
    core = lax.axis_index("section")
    attn_gains[core] = attn_gain[...]
    expert_gains[core] = expert_gain[...]
    routers[core] = router[...]
    greet([core_peer()])
    copies = [
        remote(source, target, sends.at[index], recvs.at[index], core_peer())
        for index, (source, target) in enumerate((
            (order.at[1 - core], order_peer),
            (routes.at[1 - core], routes_peer),
            (attn_gain, attn_gains.at[core]),
            (expert_gain, expert_gains.at[core]),
            (router, routers.at[core]),
        ))
    ]
    start_all(copies)
    tokens = bias.shape[0]
    sequences = lengths.shape[1]
    tall = lax.broadcasted_iota(jnp.int32, (tokens, 1), 0)
    wide = lax.broadcasted_iota(jnp.int32, (1, tokens), 1)
    sizes = [lengths[core, index] for index in range(sequences)]
    starts = [sum(sizes[:index], 0) for index in range(sequences)]
    ranks = [
        sum(jnp.where(dealing[core, place] == index, place, 0) for place in range(sequences))
        for index in range(sequences)
    ]
    dealt_starts = [
        sum(jnp.where(ranks[before] < ranks[index], sizes[before], 0) for before in range(sequences))
        for index in range(sequences)
    ]

    def places(token):
        segment = sum((token >= starts[index] + sizes[index]).astype(jnp.int32)
                      for index in range(sequences))
        position, dealt = token, token
        for index in range(sequences):
            inside = segment == index
            position = jnp.where(inside, token - starts[index], position)
            dealt = jnp.where(inside, token - starts[index] + dealt_starts[index], dealt)
        return segment, position, dealt

    segment, position, dealt = places(tall)
    segment_wide, _, dealt_wide = places(wide)
    allowed = (segment == segment_wide) & (wide <= tall)
    bias[...] = jnp.where(allowed, 0.0, masked_score).astype(f32)
    angles = position.astype(f32) * freqs[...]
    cosine[...] = jnp.cos(angles)
    lane = lax.broadcasted_iota(jnp.int32, (1, freqs.shape[1]), 1)
    sine[...] = jnp.sin(angles) * jnp.where(lane % HD < HD // 2, -1.0, 1.0)

    def masks(order_row, route_rows):
        order_wide = order_row.astype(f32)
        order_tall = jnp.sum(jnp.where(tall == wide, order_wide, 0.0), axis=1, keepdims=True)
        first = jnp.sum(jnp.where(dealt == wide, order_wide, 0.0), axis=1, keepdims=True)
        first_wide = jnp.sum(jnp.where(dealt_wide == tall, order_tall, 0.0), axis=0, keepdims=True)
        earlier = jnp.where(first_wide < first, 1.0, 0.0).astype(bf16)
        experts = picked.shape[2]
        index = lax.broadcasted_iota(jnp.int32, (experts, tokens), 0)
        chosen = jnp.zeros((experts, tokens), f32)
        for k in range(route_rows.shape[0]):
            chosen = jnp.where(route_rows[k : k + 1] == index, 1.0, chosen)
        chosen = chosen.T
        rank = dot(earlier, chosen.astype(bf16), NN)
        return chosen, jnp.where(rank < CAP, chosen, 0.0)

    picked[core], kept[core] = masks(order[core], routes[core])
    wait_all(copies)
    picked[1 - core], kept[1 - core] = masks(order_peer[...], routes_peer[...])


def prepare(lengths, dealing, order, routes, attn_gain, expert_gain, router):
    tokens = order.shape[2]
    width = attn_gain.shape[1]
    half = HD // 2
    freqs = np.tile(rope_base ** (-2.0 * np.arange(half) / HD), 128 // half)[None].astype(np.float32)
    vmem = pl.BlockSpec(memory_space=pltpu.VMEM)
    smem = pl.BlockSpec(memory_space=pltpu.SMEM)
    shape = jax.ShapeDtypeStruct
    found = pl.pallas_call(
        prepare_kernel,
        name="prepare",
        out_shape=(
            shape((tokens, 128), f32),
            shape((tokens, 128), f32),
            shape((tokens, tokens), f32),
            shape((2, tokens, E), f32),
            shape((2, tokens, E), f32),
            shape((2, 1, width), f32),
            shape((2, 1, width), f32),
            shape((2, *router.shape), bf16),
        ),
        in_specs=[smem] * 2 + [vmem] * 6,
        out_specs=(vmem,) * 8,
        scratch_shapes=[
            pltpu.VMEM(order.shape[1:], order.dtype),
            pltpu.VMEM(routes.shape[1:], routes.dtype),
            dma((5,)),
            dma((5,)),
        ],
        compiler_params=params(8),
    )(lengths, dealing, order, routes, attn_gain, expert_gain, router, freqs)
    return found[:3], found[3:5], found[5:]


def assemble_kernel(section, *refs):
    expert_refs, dense_refs, rows_in, outs = (refs[:4], refs[4:8]), refs[8:10], refs[10:12], refs[12:]
    query, key, value, output, gate, up, down = outs[:7]
    for source, target in zip(rows_in, outs[7:]):
        target[...] = source[...]
    hidden_width = gate.shape[2]
    qw, kw = query.shape[1], key.shape[1]

    def write(parts, dense):
        cores = range(2)
        pair = [[jnp.sum(v[core, :, 0].astype(f32), axis=0) for v in parts[:2]] for core in cores]
        depth = 0
        for block in pair[0] + pair[1]:
            rows = pl.ds(depth, block.shape[0])
            gate[0, rows, :] = block[:, :hidden_width]
            up[0, rows, :] = block[:, hidden_width:]
            depth += block.shape[0]
        depth = 0
        for core in cores:
            for v in parts[2:]:
                block = jnp.sum(v[core, :, 0].astype(f32), axis=0)
                down[0, :, pl.ds(depth, block.shape[1])] = block
                depth += block.shape[1]
        rows = dense[...].astype(f32)
        query[...] = rows[:, :qw]
        key[...] = rows[:, qw : qw + kw]
        value[...] = rows[:, qw + kw : qw + 2 * kw]
        output[...] = rows[:, qw + 2 * kw :].T

    pl.when(section[0] == 0)(lambda: write(expert_refs[0], dense_refs[0]))
    pl.when(section[0] == 1)(lambda: write(expert_refs[1], dense_refs[1]))


def assemble(parts, denses, rows_in, qw, kw):
    groups = parts[0][0].shape[2]
    hidden_width = parts[0][2].shape[3]
    dense = [v.reshape(-1, v.shape[-1]) for v in denses]
    depth = dense[0].shape[0]
    rows = depth // groups

    def part_spec(layer, shape):
        block = (*shape[:2], 1, *shape[3:])
        return pl.BlockSpec(block, lambda e, s: (0, 0, jnp.where(s[0] == layer, e, 0), 0, 0))

    def dense_spec(layer, width):
        return pl.BlockSpec((rows, width), lambda e, s: (jnp.where(s[0] == layer, e, 0), 0))

    _, own_rows, width = rows_in[0].shape
    row_spec = pl.BlockSpec((2, own_rows // groups, width), lambda e, s: (0, e, 0))
    shape = jax.ShapeDtypeStruct
    return pl.pallas_call(
        assemble_kernel,
        name="assemble",
        out_shape=(
            shape((depth, qw), f32),
            shape((depth, kw), f32),
            shape((depth, kw), f32),
            shape((qw, depth), f32),
            shape((groups, depth, hidden_width), f32),
            shape((groups, depth, hidden_width), f32),
            shape((groups, hidden_width, depth), f32),
            *[shape(v.shape, f32) for v in rows_in],
        ),
        grid_spec=pltpu.PrefetchScalarGridSpec(
            num_scalar_prefetch=1,
            grid=(groups,),
            in_specs=[part_spec(layer, v.shape) for layer in range(2) for v in parts[layer]]
            + [dense_spec(layer, dense[layer].shape[1]) for layer in range(2)]
            + [row_spec] * 2,
            out_specs=(
                pl.BlockSpec((rows, qw), lambda e, s: (e, 0)),
                pl.BlockSpec((rows, kw), lambda e, s: (e, 0)),
                pl.BlockSpec((rows, kw), lambda e, s: (e, 0)),
                pl.BlockSpec((qw, rows), lambda e, s: (0, e)),
                pl.BlockSpec((1, depth, hidden_width), lambda e, s: (e, 0, 0)),
                pl.BlockSpec((1, depth, hidden_width), lambda e, s: (e, 0, 0)),
                pl.BlockSpec((1, hidden_width, depth), lambda e, s: (e, 0, 0)),
                row_spec,
                row_spec,
            ),
        ),
        compiler_params=pltpu.CompilerParams(vmem_limit_bytes=58 * 2**20),
    )(lax.axis_index("section").astype(jnp.int32)[None], *parts[0], *parts[1], *dense, *rows_in)


def shards(
    tokens_in, out_cotangent, attn_gain, query_weight, key_weight, value_weight, output_weight,
    expert_gain, router_weight, gate_weight, up_weight, down_weight, lengths, dealing,
    slot_order, routes,
):
    first = lax.axis_index("section") == 0
    qw, kw = query_weight.shape[2], key_weight.shape[2]
    own = (query_weight[0], key_weight[0], value_weight[0], output_weight[0], gate_weight[0],
           up_weight[0], down_weight[0])
    tables, masks, gains = prepare(lengths[:, 0], dealing[:, 0], slot_order[0],
                                   jnp.swapaxes(routes[0], 1, 2), attn_gain, expert_gain,
                                   router_weight[0].T)
    (out0, *state0), other = layer_forward(0, gains, own, None, tokens_in, tables, masks)
    (out1, *state1), _ = layer_forward(1, gains, own, other, out0, tables, masks)
    saved = (state0, state1)
    streams = (tokens_in, out0)

    def experts(layer, out_grad, traded, jobs):
        mid, expert_rows, qs, keys, values, probs, gate, ai, x, gated, attended, pre = saved[layer]
        return experts_back(
            layer, gains, own, other, out_grad, (mid, gate, expert_rows, pre), (x, gated), masks,
            traded, Beside(jobs)
        )

    def attention(layer, mid_grad, ending, jobs):
        mid, expert_rows, qs, keys, values, probs, gate, ai, x, gated, attended, pre = saved[layer]
        return attention_back(
            layer, gains, own, other, mid_grad, streams[layer], (qs, keys, values, probs),
            (ai, attended), tables, ending, Beside(jobs)
        )

    def bring(layer, sums):
        return [Bring(layer, kind, v) for kind, v in zip(("column", "row"), sums)]

    (mid_grad, router1, gain1, pair, layer_outputs), down1, _ = experts(
        1, out_cotangent, (out0, out1), []
    )
    (grad1, attn_gain1, dense1), (sums,) = attention(1, mid_grad, (), [FirstStage(pair, 1)])
    (mid_grad, router0, gain0, pair), down0, (*pair1, dense1) = experts(
        0, grad1, (), bring(1, sums) + [DenseSum(dense1, 1)]
    )
    (input_grads, small, dense0), (pair0,) = attention(
        0, mid_grad, (router0, gain0, router1, attn_gain1, gain1, grad1),
        [FirstStage(pair, 1, 0)]
    )
    parts0, parts1 = [*pair0, *down0], [*pair1, *down1]
    query, key, value, output, gate, up, down, layer_outputs, input_grads = assemble(
        (parts0, parts1), (dense0, dense1), (layer_outputs, input_grads), qw, kw
    )
    small = jnp.where(first, small[: small.shape[0] // 2], small[small.shape[0] // 2 :])
    router_grad, attn_gain_grad, expert_gain_grad = small[:E].T, small[E : E + 1], small[E + 1 : E + 2]
    return (
        layer_outputs[None],
        input_grads[None],
        attn_gain_grad,
        query[None],
        key[None],
        value[None],
        output[None],
        expert_gain_grad,
        router_grad[None],
        gate[None],
        up[None],
        down[None],
    )


def solution(mesh):
    return jax.shard_map(
        shards,
        mesh=mesh,
        in_specs=(
            P(None, ("dp", "tensor"), None),
            P(None, ("dp", "tensor"), None),
            P("section", None),
            P("section", None, "tensor"),
            P("section", None, "tensor"),
            P("section", None, "tensor"),
            P("section", "tensor", None),
            P("section", None),
            P("section", None, None),
            P("section", None, None, "tensor"),
            P("section", None, None, "tensor"),
            P("section", None, "tensor", None),
            P(None, "dp", None),
            P(None, "dp", None),
            P("section", None, "dp", None),
            P("section", None, "dp", None),
        ),
        out_specs=(
            P("section", None, ("dp", "tensor"), None),
            P("section", None, ("dp", "tensor"), None),
            P("section", None),
            P("section", None, "tensor"),
            P("section", None, "tensor"),
            P("section", None, "tensor"),
            P("section", "tensor", None),
            P("section", None),
            P("section", None, None),
            P("section", "dp", None, "tensor"),
            P("section", "dp", None, "tensor"),
            P("section", "dp", "tensor", None),
        ),
        check_vma=False,
    )
```

```python
import functools
import math

import jax
import jax.numpy as jnp
import numpy as np
from jax import lax
from jax.experimental import pallas as pl
from jax.experimental.pallas import tpu as pltpu
from jax.sharding import PartitionSpec as P

H = 24
KV = 8
HD = 64
E = 16
CAP = 160

epsilon = 1e-05
rope_base = 10000.0
masked_score = -1e30
bf16 = jnp.bfloat16
f32 = jnp.float32
MESH = pl.DeviceIdType.MESH


def dot(a, b, dims):
    return lax.dot_general(a, b, (dims, ((), ())), preferred_element_type=f32)


NN = ((1,), (0,))
NT = ((1,), (1,))
TN = ((0,), (0,))


def norm_scale(rows_in):
    return lax.rsqrt(jnp.mean(rows_in * rows_in, axis=-1, keepdims=True) + epsilon)


def params(collective_id):
    return pltpu.CompilerParams(
        collective_id=collective_id, has_side_effects=True, vmem_limit_bytes=56 * 2**20
    )


def tensor_peers(count):
    me = lax.axis_index("tensor")
    return [{"tensor": lax.rem(me + step, count)} for step in range(1, count)]


def greet(peers):
    barrier = pltpu.get_barrier_semaphore()
    for peer in peers:
        pl.semaphore_signal(barrier, inc=1, device_id=peer, device_id_type=MESH)
    pl.semaphore_wait(barrier, len(peers))


def factors(count):
    inner = math.isqrt(count)
    while count % inner:
        inner -= 1
    return count // inner, inner


def group_place(count):
    outer, inner = factors(count)
    me = lax.axis_index("dp")
    return outer, inner, me // inner, lax.rem(me, inner)


def near_groups(count):
    outer, inner, mo, mi = group_place(count)
    across = [lax.rem(mi + step, inner) for step in range(1, inner)]
    along = [lax.rem(mo + step, outer) for step in range(1, outer)]
    return (
        [(place, {"dp": mo * inner + place}) for place in across],
        [(place, {"dp": place * inner + mi}) for place in along],
    )


dma = pltpu.SemaphoreType.DMA


def remote(src, dst, send, recv, device):
    return pltpu.make_async_remote_copy(
        src_ref=src, dst_ref=dst, send_sem=send, recv_sem=recv, device_id=device, device_id_type=MESH
    )


class Bring:
    def __init__(self, layer, kind, value, in_vmem=False, target=None):
        self.layer, self.kind, self.in_vmem = layer, kind, in_vmem
        self.whole = kind == "all" or target is not None
        self.target = target or (lambda outputs, core, place: outputs[0].at[core, place])
        count = lax.axis_size("dp")
        outer, inner = factors(count)
        self.size = {"column": outer, "row": inner, "all": count}[kind]
        block = value.shape if self.whole else value.shape[1:]
        self.inputs = [value]
        self.outputs = [jax.ShapeDtypeStruct((2, self.size, *block), value.dtype)]
        self.sems = [dma((self.size,)), dma((2, self.size)), dma((2,))]
        if not in_vmem:
            self.sems.append(pltpu.VMEM(block, value.dtype))

    def place(self, step):
        count = lax.axis_size("dp")
        outer, inner, mo, mi = group_place(count)
        if self.kind == "column":
            place = lax.rem(mo + step, outer)
            return place, place * inner + mi
        if self.kind == "row":
            place = lax.rem(mi + step, inner)
            return place, mo * inner + place
        place = lax.rem(lax.axis_index("dp") + step, count)
        return place, place

    def parts(self, inputs, outputs, sems):
        core = lax.axis_index("section")
        mine, _ = self.place(0)
        target = self.target(outputs, core, mine)
        recv = sems[1].at[core, mine]

        def source(place):
            return inputs[0] if self.whole else inputs[0].at[place]

        sent = []
        for step in range(1, self.size):
            place, group = self.place(step)
            sent.append(
                remote(source(place), target, sems[0].at[step - 1], recv,
                       {"dp": group, "section": self.layer})
            )
        across = remote(source(mine), target, sems[0].at[self.size - 1], recv, core_peer())
        if self.in_vmem:
            local = [pltpu.make_async_copy(source(mine), target, sems[2].at[0])]
        else:
            local = [
                pltpu.make_async_copy(source(mine), sems[3], sems[2].at[0]),
                pltpu.make_async_copy(sems[3], target, sems[2].at[1]),
            ]
        return sent, across, local

    def start(self, inputs, outputs, sems):
        sent, across, local = self.parts(inputs, outputs, sems)
        for copy in sent:
            copy.start()
        here = lax.axis_index("section") == self.layer

        @pl.when(here)
        def _():
            local[0].start()

        @pl.when(jnp.logical_not(here))
        def _():
            across.start()

    def wait(self, inputs, outputs, sems):
        sent, across, local = self.parts(inputs, outputs, sems)
        core = lax.axis_index("section")
        here = core == self.layer
        block = inputs[0] if self.whole else inputs[0].at[0]

        def arrived(which, place):
            remote(block, self.target(outputs, which, place), sems[0].at[0], sems[1].at[which, place],
                   core_peer()).wait_recv()

        for copy in sent:
            copy.wait_send()

        @pl.when(here)
        def _():
            local[0].wait()
            for copy in local[1:]:
                copy.start()
                copy.wait()
            for step in range(self.size):
                place, _ = self.place(step)
                if step:
                    arrived(core, place)
                arrived(1 - core, place)

        @pl.when(jnp.logical_not(here))
        def _():
            across.wait_send()

    def results(self, outputs):
        return outputs[0]


class FirstStage:
    def __init__(self, value, axis, layer=None):
        self.count = lax.axis_size("dp")
        outer, inner = factors(self.count)
        self.blocks = (outer, inner, value.shape[0] // self.count, *value.shape[1:])
        inside = isinstance(value, jax.ShapeDtypeStruct)
        self.inputs = [] if inside else [value.reshape(self.blocks)]
        self.axis = axis
        shape = list(self.blocks[2:])
        shape[axis] //= 2
        self.shape = shape
        sums = [
            jax.ShapeDtypeStruct((outer, *shape), value.dtype),
            jax.ShapeDtypeStruct((inner, *shape), value.dtype),
        ]
        self.sems = [
            dma((inner + outer - 2,)),
            dma((inner + outer - 2,)),
            pltpu.VMEM((inner - 1, outer, *shape), value.dtype),
            pltpu.VMEM((outer - 1, inner, *shape), value.dtype),
            *[pltpu.VMEM(v.shape, v.dtype) for v in sums],
            dma((2,)),
            dma((2,)),
        ]
        self.outputs = sums
        self.brings = []
        if layer is not None:
            self.brings = [Bring(layer, kind, v, True) for kind, v in zip(("column", "row"), sums)]
            self.outputs = [v for bring in self.brings for v in bring.outputs]
            self.sems += [v for bring in self.brings for v in bring.sems]

    def copies(self, inputs, sems):
        across, along = near_groups(self.count)
        _, _, mo, mi = group_place(self.count)
        value = inputs[0]
        half = self.shape[self.axis]
        cut = [slice(None)] * 3
        first, second = list(cut), list(cut)
        first[self.axis], second[self.axis] = pl.ds(0, half), pl.ds(half, half)
        found = []
        for slot, (place, device) in enumerate(across):
            found.append((value.at[(slice(None), place, *first)], sems[2].at[slot], device))
        for slot, (place, device) in enumerate(along):
            found.append((value.at[(place, slice(None), *second)], sems[3].at[slot], device))
        sent = [
            remote(src, dst, sems[0].at[index], sems[1].at[index], device)
            for index, (src, dst, device) in enumerate(found)
        ]
        loads = [
            pltpu.make_async_copy(value.at[(slice(None), mi, *first)], sems[4], sems[6].at[0]),
            pltpu.make_async_copy(value.at[(mo, slice(None), *second)], sems[5], sems[6].at[1]),
        ]
        return sent + loads

    def onward(self, outputs, sems):
        place = 8
        found = []
        for index, bring in enumerate(self.brings):
            found.append((bring, [sems[4 + index]], [outputs[index]], sems[place : place + len(bring.sems)]))
            place += len(bring.sems)
        return found

    def saves(self, outputs, sems):
        return [pltpu.make_async_copy(sems[4 + k], outputs[k], sems[7].at[k]) for k in range(2)]

    def start(self, inputs, outputs, sems):
        start_all(self.copies(inputs, sems))

    def middle(self, inputs, outputs, sems):
        wait_all(self.copies(inputs, sems))
        going = self.onward(outputs, sems) if self.brings else self.saves(outputs, sems)
        for index, (total, landed) in enumerate(((sems[4], sems[2]), (sems[5], sems[3]))):
            depth = total.shape[1]

            def add(index, carry, total=total, landed=landed, depth=depth):
                place, expert = index // depth, lax.rem(index, depth)
                value = total[place, expert].astype(f32)
                for slot in range(landed.shape[0]):
                    value = value + landed[slot, place, expert].astype(f32)
                total[place, expert] = value.astype(bf16)
                return carry

            lax.fori_loop(0, total.shape[0] * depth, add, 0)
            if self.brings:
                bring, *refs = going[index]
                bring.start(*refs)
            else:
                going[index].start()

    def wait(self, inputs, outputs, sems):
        if self.brings:
            for bring, *refs in self.onward(outputs, sems):
                bring.wait(*refs)
        else:
            wait_all(self.saves(outputs, sems))

    def results(self, outputs):
        return outputs


class DenseSum:
    def __init__(self, value, layer):
        count = lax.axis_size("dp")
        outer, inner = factors(count)
        rows, width = value.shape[2:]
        half = width // 2
        self.half = half
        inside = isinstance(value, jax.ShapeDtypeStruct)
        self.inputs = [] if inside else [value]
        self.outputs = [jax.ShapeDtypeStruct((2, *value.shape), bf16)]

        def buffer(*lead):
            return pltpu.VMEM((*lead, rows, half), bf16)

        self.brings = [
            Bring(layer, "row", jax.ShapeDtypeStruct((outer, rows, half), bf16), True,
                  lambda outputs, core, place: outputs[0].at[core, :, place, :, pl.ds(0, half)]),
            Bring(layer, "column", jax.ShapeDtypeStruct((inner, rows, half), bf16), True,
                  lambda outputs, core, place: outputs[0].at[core, place, :, :, pl.ds(half, half)]),
        ]
        pairs = inner + outer - 2
        self.sems = [
            buffer(inner - 1, outer),
            buffer(outer - 1, inner),
            buffer(outer),
            buffer(inner),
            buffer(outer - 1),
            buffer(inner - 1),
            buffer(outer),
            buffer(inner),
            dma((2,)),
            *[dma((pairs,)) for _ in range(6)],
            *[v for bring in self.brings for v in bring.sems],
        ]

    def numbered(self, found, sems, first):
        return [
            remote(src, dst, sems[first].at[index], sems[first + 1].at[index], device)
            for index, (src, dst, device) in enumerate(found)
        ]

    def sent(self, inputs, sems):
        count = lax.axis_size("dp")
        across, along = near_groups(count)
        _, _, mo, mi = group_place(count)
        value = inputs[0]
        low, high = pl.ds(0, self.half), pl.ds(self.half, self.half)
        found = [
            (value.at[:, place, :, low], sems[0].at[slot], device)
            for slot, (place, device) in enumerate(across)
        ] + [
            (value.at[place, :, :, high], sems[1].at[slot], device)
            for slot, (place, device) in enumerate(along)
        ]
        loads = [
            pltpu.make_async_copy(value.at[:, mi, :, low], sems[2], sems[8].at[0]),
            pltpu.make_async_copy(value.at[mo, :, :, high], sems[3], sems[8].at[1]),
        ]
        return self.numbered(found, sems, 9) + loads

    def sums(self, sems):
        across, along = near_groups(lax.axis_size("dp"))
        found = [
            (sems[2].at[place], sems[4].at[slot], device) for slot, (place, device) in enumerate(along)
        ] + [
            (sems[3].at[place], sems[5].at[slot], device) for slot, (place, device) in enumerate(across)
        ]
        return self.numbered(found, sems, 11)

    def blocks(self, sems):
        count = lax.axis_size("dp")
        across, along = near_groups(count)
        _, _, mo, mi = group_place(count)
        found = [(sems[6].at[mo], sems[6].at[mo], device) for _, device in along]
        found += [(sems[7].at[mi], sems[7].at[mi], device) for _, device in across]
        return self.numbered(found, sems, 13)

    def onward(self, outputs, sems):
        place = 15
        found = []
        for index, bring in enumerate(self.brings):
            found.append((bring, [sems[6 + index]], outputs, sems[place : place + len(bring.sems)]))
            place += len(bring.sems)
        return found

    def start(self, inputs, outputs, sems):
        start_all(self.sent(inputs, sems))

    def middle1(self, inputs, outputs, sems):
        wait_all(self.sent(inputs, sems))
        for total, landed in ((sems[2], sems[0]), (sems[3], sems[1])):
            for place in range(total.shape[0]):
                value = total[place].astype(f32)
                for slot in range(landed.shape[0]):
                    value = value + landed[slot, place].astype(f32)
                total[place] = value.astype(bf16)
        start_all(self.sums(sems))

    def middle2(self, inputs, outputs, sems):
        wait_all(self.sums(sems))
        _, _, mo, mi = group_place(lax.axis_size("dp"))
        for total, landed, whole, mine in (
            (sems[2], sems[4], sems[6], mo),
            (sems[3], sems[5], sems[7], mi),
        ):
            value = total[mine].astype(f32)
            for slot in range(landed.shape[0]):
                value = value + landed[slot].astype(f32)
            whole[mine] = value.astype(bf16)
        start_all(self.blocks(sems))

    def middle3(self, inputs, outputs, sems):
        wait_all(self.blocks(sems))
        for bring, *refs in self.onward(outputs, sems):
            bring.start(*refs)

    def wait(self, inputs, outputs, sems):
        for bring, *refs in self.onward(outputs, sems):
            bring.wait(*refs)

    def results(self, outputs):
        return outputs[0]


class SmallSum:
    def __init__(self, depth, width):
        self.tensor, self.count = lax.axis_size("tensor"), lax.axis_size("dp")
        self.lanes = width // self.tensor
        self.depth = depth
        part = (depth, self.lanes)
        self.sems = [
            pltpu.VMEM((depth, width), f32),
            pltpu.VMEM((self.tensor - 1, *part), f32),
            pltpu.VMEM((self.count - 1, *part), f32),
            *[pltpu.VMEM(part, f32) for _ in range(4)],
            pltpu.VMEM((depth, width), f32),
            dma((2, self.tensor - 1)),
            dma((2, self.tensor - 1)),
            dma((self.count,)),
            dma((self.count,)),
        ]

    def columns(self, place):
        return pl.ds(pl.multiple_of(place * self.lanes, self.lanes), self.lanes)

    def over_tensor(self, sems):
        here = lax.axis_index("tensor")
        found = []
        for step in range(1, self.tensor):
            place = lax.rem(here + step, self.tensor)
            found.append(
                remote(sems[0].at[:, self.columns(place)], sems[1].at[step - 1],
                       sems[8].at[0, step - 1], sems[9].at[0, step - 1], {"tensor": place})
            )
        return found

    def over_groups(self, sems):
        me = lax.axis_index("dp")
        return [
            remote(sems[3], sems[2].at[step - 1], sems[10].at[step - 1], sems[11].at[step - 1],
                   {"dp": lax.rem(me + step, self.count)})
            for step in range(1, self.count)
        ]

    def over_cores(self, sems):
        last = self.count - 1
        return [remote(sems[4], sems[5], sems[10].at[last], sems[11].at[last], core_peer())]

    def back(self, sems):
        here = lax.axis_index("tensor")
        own = sems[7].at[:, self.columns(here)]
        return [
            remote(sems[6], own, sems[8].at[1, step - 1], sems[9].at[1, step - 1],
                   {"tensor": lax.rem(here + step, self.tensor)})
            for step in range(1, self.tensor)
        ]

    def first(self, sems):
        start_all(self.over_tensor(sems))

    def second(self, sems):
        wait_all(self.over_tensor(sems))
        total = sems[0][:, self.columns(lax.axis_index("tensor"))]
        for slot in range(self.tensor - 1):
            total = total + sems[1][slot]
        sems[3][...] = total
        start_all(self.over_groups(sems))

    def third(self, sems):
        wait_all(self.over_groups(sems))
        total = sems[3][...]
        for slot in range(self.count - 1):
            total = total + sems[2][slot]
        sems[4][...] = total
        copies = self.over_cores(sems)
        start_all(copies)
        wait_all(copies)
        sems[6][...] = sems[4][...] + sems[5][...]
        start_all(self.back(sems))
        sems[7][:, self.columns(lax.axis_index("tensor"))] = sems[6][...]

    def last(self, sems, out):
        wait_all(self.back(sems))
        out[...] = sems[7][...]


class Trade:
    def __init__(self, shape):
        self.sems = [pltpu.VMEM((2, *shape), f32), dma((1,)), dma((1,))]

    def copy(self, value, sems):
        core = lax.axis_index("section")
        return remote(value, sems[0].at[core], sems[1].at[0], sems[2].at[0], core_peer())

    def start(self, zero, one, sems):
        core = lax.axis_index("section")

        @pl.when(core == 0)
        def _():
            self.copy(one, sems).start()
            sems[0][0] = zero[...]

        @pl.when(core == 1)
        def _():
            self.copy(zero, sems).start()
            sems[0][1] = one[...]

    def wait(self, zero, out, sems):
        self.copy(zero, sems).wait()
        out[...] = sems[0][...]


def both_cores(groups):
    core = lax.axis_index("section")
    return [{"dp": group, "section": which} for group in groups for which in (core, 1 - core)]


def whole_group():
    count = lax.axis_size("dp")
    me = lax.axis_index("dp")
    return both_cores([lax.rem(me + step, count) for step in range(1, count)])


class Beside:
    def __init__(self, jobs):
        self.jobs = jobs
        self.inputs = [v for job in jobs for v in job.inputs]
        self.outputs = [v for job in jobs for v in job.outputs]
        self.sems = [v for job in jobs for v in job.sems]

    def peers(self):
        count = lax.axis_size("dp")
        if not self.jobs:
            return []
        across, along = near_groups(count)
        return both_cores([device["dp"] for _, device in across + along])

    def each(self, refs, run):
        inputs, outputs, sems = refs
        for job in self.jobs:
            mine, inputs = inputs[: len(job.inputs)], inputs[len(job.inputs) :]
            theirs, outputs = outputs[: len(job.outputs)], outputs[len(job.outputs) :]
            own, sems = sems[: len(job.sems)], sems[len(job.sems) :]
            run(job)(mine, theirs, own)

    def start(self, *refs):
        self.each(refs, lambda job: job.start)

    def middle(self, *refs, step="middle"):
        self.each(refs, lambda job: getattr(job, step, lambda *refs: None))

    def wait(self, *refs):
        self.each(refs, lambda job: job.wait)

    def results(self, outputs):
        found = []
        for job in self.jobs:
            found.append(job.results(outputs[: len(job.outputs)]))
            outputs = outputs[len(job.outputs) :]
        return found


def deal_out(count, part, rows, columns, landing, sends, recvs):
    me = lax.axis_index("tensor")
    copies = []
    for step in range(1, count):
        peer = lax.rem(me + step, count)
        copies.append(
            pltpu.make_async_remote_copy(
                src_ref=part.at[pl.ds(pl.multiple_of(peer * rows, rows), rows), columns],
                dst_ref=landing.at[step - 1, :, columns],
                send_sem=sends.at[step - 1],
                recv_sem=recvs.at[step - 1],
                device_id={"tensor": peer},
                device_id_type=MESH,
            )
        )
    for copy in copies:
        copy.start()
    return copies


class Line:
    def __init__(self, count, rows, passing=True):
        self.count, self.rows = count, rows
        self.passing = passing and count == 4
        self.me = me = lax.axis_index("tensor")
        half = me // 2
        self.partner = me + 1 - 2 * lax.rem(me, 2)
        self.far_inner, self.far_edge = 2 - half, 3 - 3 * half
        self.inner = me == 1 + half

    def cut(self, place):
        return pl.ds(pl.multiple_of(place * self.rows, self.rows), self.rows)

    def shard(self, buf, sems, place, target, index):
        buf, columns = buf if isinstance(buf, tuple) else (buf, slice(None))
        rows = buf.at[self.cut(place), columns]
        return remote(rows, rows, sems[0].at[index], sems[1].at[place], {"tensor": target})

    def gather_start(self, buf, sems):
        if self.passing:
            self.shard(buf, sems, self.me, self.far_inner, 1).start()
            self.shard(buf, sems, self.me, self.partner, 0).start()
        else:
            for step in range(1, self.count):
                self.shard(buf, sems, self.me, lax.rem(self.me + step, self.count), step - 1).start()

    def gather_wait(self, buf, sems):
        def arrived(place):
            self.shard(buf, sems, place, self.partner, 0).wait_recv()

        def left(number):
            for index in range(number):
                self.shard(buf, sems, self.me, self.partner, index).wait_send()

        if not self.passing:
            for step in range(1, self.count):
                arrived(lax.rem(self.me + step, self.count))
            left(self.count - 1)
            return

        @pl.when(self.inner)
        def _():
            arrived(self.far_inner)
            self.shard(buf, sems, self.far_inner, self.partner, 2).start()
            arrived(self.far_edge)
            self.shard(buf, sems, self.far_edge, self.partner, 3).start()
            arrived(self.partner)
            left(4)

        @pl.when(jnp.logical_not(self.inner))
        def _():
            for place in (self.partner, self.far_inner, self.far_edge):
                arrived(place)
            left(2)

    def block(self, part, place, columns, landing, slot, sems, index, target):
        return remote(part.at[self.cut(place), columns], landing.at[slot, :, columns],
                      sems[0].at[index], sems[1].at[slot], {"tensor": target})

    def scatter_start(self, part, columns, landing, sems):
        if not self.passing:
            for step in range(1, self.count):
                peer = lax.rem(self.me + step, self.count)
                self.block(part, peer, columns, landing, step - 1, sems, step - 1, peer).start()
            return

        @pl.when(self.inner)
        def _():
            self.block(part, self.partner, columns, landing, 2, sems, 0, self.partner).start()

        @pl.when(jnp.logical_not(self.inner))
        def _():
            for slot, place in enumerate((self.far_edge, self.far_inner, self.partner)):
                self.block(part, place, columns, landing, slot, sems, slot, self.partner).start()

    def scatter_relay(self, part, columns, landing, sems):
        if not self.passing:
            return

        @pl.when(self.inner)
        def _():
            for slot, place in enumerate((self.far_edge, self.far_inner)):
                self.block(part, place, columns, landing, slot, sems, 0, self.partner).wait_recv()
                landing[slot, :, columns] = (
                    landing[slot, :, columns].astype(f32) + part[self.cut(place), columns].astype(f32)
                ).astype(bf16)
                remote(landing.at[slot, :, columns], landing.at[3, :, columns], sems[0].at[1 + slot],
                       sems[1].at[3], {"tensor": place}).start()

    def scatter_wait(self, part, columns, landing, sems):
        slots = (2, 3) if self.passing else range(self.count - 1)
        for slot in slots:
            self.block(part, self.me, columns, landing, slot, sems, 0, self.partner).wait_recv()
        for index in range(3 if self.passing else self.count - 1):
            self.block(part, self.me, columns, landing, 0, sems, index, self.partner).wait_send()

    def total(self, own, landing):
        for slot in (2, 3) if self.passing else range(self.count - 1):
            own = own + landing[slot].astype(f32)
        return own

    @staticmethod
    def landing(count, rows, width):
        return pltpu.VMEM((4 if count == 4 else count - 1, rows, width), bf16)

    @staticmethod
    def sems(count, number):
        return [dma((number, count)), dma((number, count))]


def core_peer():
    return {"section": 1 - lax.axis_index("section")}


def hand_rows(value, pair, sems):
    tokens = value.shape[0]
    return [
        pltpu.make_async_copy(value, pair.at[pl.ds(0, tokens)], sems[0]),
        remote(value, pair.at[pl.ds(tokens, tokens)], sems[1], sems[2], core_peer()),
    ]


def hand_halves(value, pair, sems):
    section = lax.axis_index("section")
    tokens, half = value.shape[0], value.shape[1] // 2
    mine = value.at[:, pl.ds(pl.multiple_of(section * half, half), half)]
    other = value.at[:, pl.ds(pl.multiple_of((1 - section) * half, half), half)]
    return [
        pltpu.make_async_copy(mine, pair.at[pl.ds(0, tokens)], sems[0]),
        remote(other, pair.at[pl.ds(tokens, tokens)], sems[1], sems[2], core_peer()),
    ]


def start_all(copies):
    for copy in copies:
        copy.start()


def wait_all(copies):
    for copy in copies:
        copy.wait()


def either(use_own, own, other, run):
    @pl.when(use_own)
    def _():
        run(own)

    @pl.when(jnp.logical_not(use_own))
    def _():
        run(other)


def weight_copies(refs, scratch, sems, expert):
    gate, up, down = refs
    gu_s, down_s = scratch
    width = gate.shape[2]
    return (
        pltpu.make_async_copy(gate.at[expert], gu_s.at[expert, :, pl.ds(0, width)], sems.at[0, expert]),
        pltpu.make_async_copy(up.at[expert], gu_s.at[expert, :, pl.ds(width, width)], sems.at[1, expert]),
        pltpu.make_async_copy(
            down.at[expert], down_s.at[pl.ds(pl.multiple_of(expert * width, width), width)], sems.at[2, expert]
        ),
    )


def attn_copies(refs, scratch, sems):
    query, key, value, output = refs
    joint_s, output_s = scratch
    qw, kw = query.shape[1], key.shape[1]
    return (
        pltpu.make_async_copy(query, joint_s.at[:, pl.ds(0, qw)], sems.at[0]),
        pltpu.make_async_copy(key, joint_s.at[:, pl.ds(qw, kw)], sems.at[1]),
        pltpu.make_async_copy(value, joint_s.at[:, pl.ds(qw + kw, kw)], sems.at[2]),
        pltpu.make_async_copy(output, output_s, sems.at[3]),
    )


def turned(block):
    lane = lax.broadcasted_iota(jnp.int32, block.shape, 1)
    half = HD // 2
    return jnp.where(
        lane % HD < half, pltpu.roll(block, block.shape[1] - half, 1), pltpu.roll(block, half, 1)
    )


def column(table, index):
    lane = lax.broadcasted_iota(jnp.int32, table.shape, 1)
    return jnp.sum(jnp.where(lane == index, table, 0.0), axis=1, keepdims=True)


def swap_copies(own, other, sems, piece):
    sends, recvs = sems
    names = len(own)
    if isinstance(piece, tuple):
        name, expert = piece
        source, target = own[name].at[expert], other[name].at[expert]
        index = 4 + (name - 4) * own[4].shape[0] + expert
    else:
        source, target, index = own[piece], other[piece], piece
    return pltpu.make_async_remote_copy(
        src_ref=source, dst_ref=target, send_sem=sends.at[index], recv_sem=recvs.at[index],
        device_id=core_peer(), device_id_type=MESH,
    )


def forward_kernel(layer, count, swap, *refs):
    refs = list(refs)

    def take(number):
        taken = refs[:number]
        del refs[:number]
        return taken

    (stream_in, attn_gains, expert_gains, routers, cosine, sine, bias, pickeds, kepts) = take(9)
    attn_gain, expert_gain, router = attn_gains.at[layer], expert_gains.at[layer], routers.at[layer]
    picked, kept = pickeds.at[layer], kepts.at[layer]
    stream = stream_in.at[lax.axis_index("section")] if layer == 0 else stream_in
    own = take(7)
    other = None if swap else take(7)
    (out, mid_out, expert_rows_out, qs_out, keys_out, values_out, probs_out, gate_out,
     attn_in_out, expert_in_out, gated_out, attended_out, pre_out) = take(13)
    if swap:
        other = take(7)
    scratch = take(4)
    joint_s, output_s, gu_s, down_s = scratch
    (ag1, ag2, part, landing1, landing2, pre_s, gated_s, attended_s, send_s, recv_s, attn_sems,
     expert_sems, pre_sems, save_sems) = refs[:14]
    if swap:
        swap_sems = refs[14:]
    rows, width = stream.shape
    tokens = ag1.shape[0]
    experts = gu_s.shape[0]
    hidden_width = gu_s.shape[2] // 2
    kw = keys_out.shape[1]
    qw = attended_s.shape[1]
    heads, key_heads = qw // HD, kw // HD
    group = heads // key_heads
    me = lax.axis_index("tensor")
    own_rows = pl.ds(pl.multiple_of(me * rows, rows), rows)
    ag1_line, rs1_line, ag2_line, rs2_line = [Line(count, rows, v) for v in (True, True, False, True)]

    def sems(index):
        return send_s.at[index], recv_s.at[index]

    use_own = lax.axis_index("section") == layer
    middle = width // 2
    gathering = [((ag1, pl.ds(0, middle)), sems(0)), ((ag1, pl.ds(middle, middle)), sems(7))]

    def start_attn(w):
        for copy in attn_copies(w[:4], scratch[:2], attn_sems):
            copy.start()

    def wait_attn(w):
        for copy in attn_copies(w[:4], scratch[:2], attn_sems):
            copy.wait()

    def start_expert(w, expert):
        for copy in weight_copies(w[4:], scratch[2:], expert_sems, expert):
            copy.start()

    def wait_expert(w, expert):
        for copy in weight_copies(w[4:], scratch[2:], expert_sems, expert):
            copy.wait()

    def each_expert(run):
        def step(expert, carry):
            run(expert)
            return carry

        lax.fori_loop(0, experts, step, 0)

    def swap_expert(expert):
        return [swap_copies(own, other, swap_sems, (name, expert)) for name in (4, 5, 6)]

    value = stream[...].astype(bf16).astype(f32)
    ag1[own_rows, :] = (value * norm_scale(value) * attn_gain[...]).astype(bf16)
    greet(tensor_peers(count) + ([core_peer()] if swap else []))
    if swap:
        lead = min(4, experts)
        for piece in range(4):
            swap_copies(own, other, swap_sems, piece).start()
        each_expert(lambda expert: [c.start() for c in swap_expert(expert)] and None)

        @pl.when(use_own)
        def _():
            [ag1_line.gather_start(*each) for each in gathering]
            start_attn(own)
            each_expert(lambda expert: start_expert(own, expert))

        @pl.when(jnp.logical_not(use_own))
        def _():
            for piece in range(4):
                swap_copies(own, other, swap_sems, piece).wait_recv()
            start_attn(other)
            for expert in range(lead):
                for copy in swap_expert(expert):
                    copy.wait_recv()
                start_expert(other, expert)
            [ag1_line.gather_start(*each) for each in gathering]
    else:
        [ag1_line.gather_start(*each) for each in gathering]
        either(use_own, own, other, start_attn)
        either(use_own, own, other, lambda w: each_expert(lambda expert: start_expert(w, expert)))
    for each in gathering:
        ag1_line.gather_wait(*each)
    saved = [pltpu.make_async_copy(ag1, attn_in_out, save_sems.at[0])]
    saved[0].start()
    either(use_own, own, other, wait_attn)
    proj = dot(ag1[...], joint_s[...], NN)
    for chunk in range(qw // 128):
        block = proj[:, chunk * 128 : chunk * 128 + 128]
        block = (block * cosine[...] + turned(block) * sine[...]).astype(bf16)
        for part_index in range(128 // HD):
            head = chunk * (128 // HD) + part_index
            qs_out[pl.ds(head * tokens, tokens), :] = block[:, part_index * HD : part_index * HD + HD]
    for chunk in range(kw // 128):
        block = proj[:, qw + chunk * 128 : qw + chunk * 128 + 128]
        keys_out[:, pl.ds(chunk * 128, 128)] = (
            block * cosine[...] + turned(block) * sine[...]
        ).astype(bf16)
    values_out[...] = proj[:, qw + kw :].astype(bf16)
    for g in range(key_heads):
        lanes = pl.ds(g * HD, HD)
        span = pl.ds(g * group * tokens, group * tokens)
        scores = dot(qs_out[span, :], keys_out[:, lanes], NT) * 0.125
        scores = (scores.reshape(group, tokens, tokens) + bias[...][None]).reshape(
            group * tokens, tokens
        )
        top = jnp.max(scores, axis=1, keepdims=True)
        weighed = jnp.exp(scores - top)
        probs = (weighed / jnp.sum(weighed, axis=1, keepdims=True)).astype(bf16)
        probs_out[span, :] = probs
        attended = dot(probs, values_out[:, lanes], NN).astype(bf16)
        for h in range(group):
            attended_s[:, pl.ds((g * group + h) * HD, HD)] = attended[h * tokens : (h + 1) * tokens]
    saved.append(pltpu.make_async_copy(attended_s, attended_out, save_sems.at[1]))
    saved[1].start()
    half = width // 2
    dealt = [(part, pl.ds(t * half, half), landing1, sems(1 + 8 * t)) for t in range(2)]
    for each in dealt:
        part[:, each[1]] = dot(attended_s[...], output_s[:, each[1]], NN).astype(bf16)
        rs1_line.scatter_start(*each)
    for each in dealt:
        rs1_line.scatter_relay(*each)
    for each in dealt:
        rs1_line.scatter_wait(*each)
    mid = rs1_line.total(value + part[own_rows, :].astype(f32), landing1)
    mid_out[...] = mid
    expert_rows = (mid * norm_scale(mid) * expert_gain[...]).astype(bf16)
    expert_rows_out[...] = expert_rows
    ag2[own_rows, :] = expert_rows
    split = width // 2
    columns = pl.ds(0, split), pl.ds(split, split)
    ag2_line.gather_start((ag2, columns[0]), sems(2))
    ag2_line.gather_start((ag2, columns[1]), sems(8))
    if swap:

        @pl.when(jnp.logical_not(use_own))
        def _():
            def landed(expert, carry):
                for copy in swap_expert(expert):
                    copy.wait_recv()
                start_expert(other, expert)
                return carry

            lax.fori_loop(lead, experts, landed, 0)

    ag2_line.gather_wait((ag2, columns[0]), sems(2))

    def first_step(expert, carry):
        either(use_own, own, other, lambda w: wait_expert(w, expert))
        pre_s[expert] = dot(ag2[:, columns[0]], gu_s[expert, columns[0], :], NN)
        return carry

    lax.fori_loop(0, experts, first_step, 0)
    ag2_line.gather_wait((ag2, columns[1]), sems(8))
    saved.append(pltpu.make_async_copy(ag2, expert_in_out, save_sems.at[2]))
    saved[2].start()
    logits = dot(ag2[...], router[...], NT)
    chosen = picked[...] > 0
    top = jnp.max(jnp.where(chosen, logits, masked_score), axis=1, keepdims=True)
    weighed = jnp.where(chosen, jnp.exp(logits - top), 0.0)
    gate_out[...] = weighed / jnp.sum(weighed, axis=1, keepdims=True)

    def expert_step(expert, carry):
        pre = pre_s[expert] + dot(ag2[:, columns[1]], gu_s[expert, columns[1], :], NN)
        pre_s[expert] = pre
        pltpu.make_async_copy(pre_s.at[expert], pre_out.at[expert], pre_sems.at[expert]).start()
        gate_pre, up_pre = pre[:, :hidden_width], pre[:, hidden_width:]
        hidden = (gate_pre / (1.0 + jnp.exp(-gate_pre)) * up_pre).astype(bf16).astype(f32)
        weight = column(gate_out[...] * kept[...], expert)
        gated_s[:, pl.ds(pl.multiple_of(expert * hidden_width, hidden_width), hidden_width)] = (
            hidden * weight
        ).astype(bf16)
        return carry

    lax.fori_loop(0, experts, expert_step, 0)
    saved.append(pltpu.make_async_copy(gated_s, gated_out, save_sems.at[3]))
    saved[3].start()
    tile = width // 4
    dealt = [(part, pl.ds(t * tile, tile), landing2, sems(3 + t)) for t in range(4)]
    for each in dealt:
        part[:, each[1]] = dot(gated_s[...], down_s[:, each[1]], NN).astype(bf16)
        rs2_line.scatter_start(*each)
    for each in dealt:
        rs2_line.scatter_relay(*each)
    for each in dealt:
        rs2_line.scatter_wait(*each)
    total = rs2_line.total(mid_out[...] + part[own_rows, :].astype(f32), landing2)
    out[...] = total
    wait_all(saved)
    if swap:
        for piece in range(4):
            swap_copies(own, other, swap_sems, piece).wait_send()
        each_expert(lambda expert: [c.wait_send() for c in swap_expert(expert)] and None)

        @pl.when(use_own)
        def _():
            for piece in range(4):
                swap_copies(own, other, swap_sems, piece).wait_recv()
            each_expert(lambda expert: [c.wait_recv() for c in swap_expert(expert)] and None)

    def finish(expert, carry):
        pltpu.make_async_copy(pre_s.at[expert], pre_out.at[expert], pre_sems.at[expert]).wait()
        return carry

    lax.fori_loop(0, experts, finish, 0)


def weight_scratch(own):
    query, key, value, output, gate, up, down = own
    depth = query.shape[0]
    experts, _, hidden_width = gate.shape
    return [
        pltpu.VMEM((depth, query.shape[1] + 2 * key.shape[1]), bf16),
        pltpu.VMEM(output.shape, bf16),
        pltpu.VMEM((experts, depth, 2 * hidden_width), bf16),
        pltpu.VMEM((experts * hidden_width, depth), bf16),
    ]


def layer_forward(layer, gains, own, other, stream, tables, masks):
    count = lax.axis_size("tensor")
    rows, width = stream.shape[-2:]
    tokens = tables[2].shape[0]
    qw, kw = own[0].shape[1], own[1].shape[1]
    experts, _, hidden_width = own[4].shape
    heads = qw // HD
    swap = other is None
    vmem = pl.BlockSpec(memory_space=pltpu.VMEM)
    hbm = pl.BlockSpec(memory_space=pl.ANY)
    shape = jax.ShapeDtypeStruct
    pieces = 4 + 3 * experts
    found = pl.pallas_call(
        functools.partial(forward_kernel, layer, count, swap),
        name=f"layer_forward_{layer}",
        out_shape=(
            shape((rows, width), f32),
            shape((rows, width), f32),
            shape((rows, width), bf16),
            shape((heads * tokens, HD), bf16),
            shape((tokens, kw), bf16),
            shape((tokens, kw), bf16),
            shape((heads * tokens, tokens), bf16),
            shape((tokens, experts), f32),
            shape((tokens, width), bf16),
            shape((tokens, width), bf16),
            shape((tokens, experts * hidden_width), bf16),
            shape((tokens, qw), bf16),
            shape((experts, tokens, 2 * hidden_width), f32),
        )
        + (tuple(shape(w.shape, w.dtype) for w in own) if swap else ()),
        in_specs=[vmem] * 9 + [hbm] * (7 if swap else 14),
        out_specs=(vmem,) * 8 + (hbm,) * (12 if swap else 5),
        scratch_shapes=weight_scratch(own)
        + [
            pltpu.VMEM((tokens, width), bf16),
            pltpu.VMEM((tokens, width), bf16),
            pltpu.VMEM((tokens, width), bf16),
            Line.landing(count, rows, width),
            Line.landing(count, rows, width),
            pltpu.VMEM((experts, tokens, 2 * hidden_width), f32),
            pltpu.VMEM((tokens, experts * hidden_width), bf16),
            pltpu.VMEM((tokens, qw), bf16),
            *Line.sems(count, 10),
            dma((4,)),
            dma((3, experts)),
            dma((experts,)),
            dma((4,)),
        ]
        + ([dma((pieces,)), dma((pieces,))] if swap else []),
        compiler_params=params(1 + layer),
    )(stream, *gains, *tables, *masks, *own,
      *(() if swap else other))
    return found[:13], found[13:]


def norm_back(value, gain, out_grad):
    scale = norm_scale(value)
    scaled = value * scale
    gain_grad = jnp.sum(out_grad * scaled, axis=0, keepdims=True)
    inner = out_grad * gain
    value_grad = scale * (inner - scaled * jnp.mean(inner * scaled, axis=-1, keepdims=True))
    return value_grad, gain_grad


def experts_back_kernel(layer, count, trade, stage, beside, *refs):
    refs = list(refs)

    def take(number):
        taken = refs[:number]
        del refs[:number]
        return taken

    out_grad, mid, expert_gains, routers, kepts, gate, expert_rows, pre_in = take(8)
    expert_gain, router, kept = expert_gains.at[layer], routers.at[layer], kepts.at[layer]
    x_in, gated_in = take(2)
    own, other = take(3), take(3)
    traded = take(2 if trade else 0)
    beside_in = take(len(beside.inputs))
    mid_grad_out, router_out, expert_gain_out, pair_out = take(4)
    traded_out = take(1 if trade else 0)
    stage_out = take(len(stage.outputs))
    beside_out = take(len(beside.outputs))
    scratch = take(2)
    gu_s, down_s = scratch
    (ag1, part, landing1, pre_s, gpu_s, acc, gate_part, gate_land, og_s, gpu_peer, x_s, turned_x,
     gated_s, hidden_s, pair_s, down_grad_s, send_s, recv_s, expert_sems, pre_sems, core_send, core_recv,
     local_sems, hand_send, hand_recv, save_sems) = take(26)
    trade_sems = take(len(trade.sems) if trade else 0)
    stage_refs = ([down_grad_s], stage_out, take(len(stage.sems)))
    beside_refs = (beside_in, beside_out, refs)
    rows, width = mid.shape
    tokens = ag1.shape[0]
    experts = gu_s.shape[0]
    hidden_width = gu_s.shape[2] // 2
    me = lax.axis_index("tensor")
    own_rows = pl.ds(pl.multiple_of(me * rows, rows), rows)
    ag_line, rs_line = [Line(count, rows, v) for v in (False, False)]
    gathering = ag1, (send_s.at[0], recv_s.at[0])
    tile = width // 2
    dealt = [
        (part, pl.ds(t * tile, tile), landing1, (send_s.at[3 * t], recv_s.at[3 * t]))
        if t
        else (part, pl.ds(0, tile), landing1, (send_s.at[1], recv_s.at[1]))
        for t in range(2)
    ]
    use_own = lax.axis_index("section") == layer

    def start_expert(expert, carry):
        either(use_own, own, other,
               lambda w: [c.start() for c in weight_copies(w, scratch, expert_sems, expert)])
        pltpu.make_async_copy(pre_in.at[expert], pre_s.at[expert], pre_sems.at[expert]).start()
        return carry

    everyone = Beside([*beside.jobs, stage])
    if layer:
        ag1[own_rows, :] = out_grad[lax.axis_index("section")]
        greet(tensor_peers(count) + [core_peer()] + everyone.peers())
        ag_line.gather_start(*gathering)
    else:
        ag1[own_rows, :] = out_grad[...].astype(bf16)
        greet(tensor_peers(count) + [core_peer()] + everyone.peers())
        ag_line.gather_start(*gathering)
    lax.fori_loop(0, experts, start_expert, 0)
    loads = hand_halves(x_in, x_s, [v.at[0] for v in (local_sems, hand_send, hand_recv)])
    loads += hand_rows(gated_in, gated_s, [v.at[1] for v in (local_sems, hand_send, hand_recv)])
    for copy in loads:
        copy.start()
    beside.start(*beside_refs)
    if trade:
        trade.start(*traded, trade_sems)
    gate_part[...] = jnp.zeros_like(gate_part)

    def ready_step(expert, carry):
        pltpu.make_async_copy(pre_in.at[expert], pre_s.at[expert], pre_sems.at[expert]).wait()
        gate_pre = pre_s[expert, :, pl.ds(0, hidden_width)]
        up_pre = pre_s[expert, :, pl.ds(hidden_width, hidden_width)]
        sig = 1.0 / (1.0 + jnp.exp(-gate_pre))
        act = gate_pre * sig
        hidden_s[expert] = (act * up_pre).astype(bf16)
        weight = column(gate[...] * kept[...], expert)
        pre_s[expert, :, pl.ds(0, hidden_width)] = (
            weight * up_pre * (sig * (1.0 + gate_pre * (1.0 - sig)))
        )
        pre_s[expert, :, pl.ds(hidden_width, hidden_width)] = weight * act
        return carry

    lax.fori_loop(0, experts, ready_step, 0)
    wait_all(loads)
    turned_x[...] = x_s[...].T
    ag_line.gather_wait(*gathering)
    core = lax.axis_index("section")
    half = width // 2
    og_s[pl.ds(0, tokens), :] = ag1[:, pl.ds(pl.multiple_of(core * half, half), half)]
    handed = [
        remote(ag1.at[:, pl.ds(pl.multiple_of((1 - core) * half, half), half)],
               og_s.at[pl.ds(tokens, tokens)], core_send.at[0], core_recv.at[0], core_peer())
    ]
    handed[0].start()
    handed[0].wait()
    _, inner, per_group = stage.blocks[:3]

    def down_step(index, carry):
        lanes = pl.ds(pl.multiple_of(index * 2 * hidden_width, 2 * hidden_width), 2 * hidden_width)
        grads = dot(gated_s[:, lanes], og_s[...], TN).astype(bf16)
        for k in range(2):
            expert = 2 * index + k
            group, place = expert // per_group, lax.rem(expert, per_group)
            down_grad_s[group // inner, lax.rem(group, inner), place] = grads[
                k * hidden_width : (k + 1) * hidden_width
            ]
        return carry

    lax.fori_loop(0, experts // 2, down_step, 0)
    stage.start(*stage_refs)
    beside.middle(*beside_refs, step="middle1")

    def expert_step(index, carry):
        pair = (2 * index, 2 * index + 1)
        for expert in pair:
            either(use_own, own, other,
                   lambda w: [c.wait() for c in weight_copies(w, scratch, expert_sems, expert)])
        lanes = pl.ds(pl.multiple_of(index * 2 * hidden_width, 2 * hidden_width), 2 * hidden_width)
        plain = dot(ag1[...], down_s[lanes, :], NT)
        lane = lax.broadcasted_iota(jnp.int32, gate_part.shape, 1)
        for k, expert in enumerate(pair):
            value = plain[:, k * hidden_width : (k + 1) * hidden_width]
            summed = jnp.sum(hidden_s[expert].astype(f32) * value, axis=1, keepdims=True)
            gate_part[...] += jnp.where(lane == expert, summed, 0.0)
            for cut in (pl.ds(0, hidden_width), pl.ds(hidden_width, hidden_width)):
                gpu_s[expert, :, cut] = (value * pre_s[expert, :, cut]).astype(bf16)
        return carry

    lax.fori_loop(0, experts // 2, expert_step, 0)
    gate_part[:, :experts] = gate_part[:, :experts] * kept[...]
    copies = deal_out(count, gate_part, rows, slice(None), gate_land, send_s.at[2], recv_s.at[2])
    handed.append(remote(gpu_s, gpu_peer, core_send.at[1], core_recv.at[1], core_peer()))
    handed[1].start()
    for each in dealt:
        columns = each[1]
        acc[...] = jnp.zeros_like(acc)

        def back_step(index, carry, columns=columns):
            pair = (2 * index, 2 * index + 1)
            acc[...] += dot(gpu_s[pair[0]], gu_s[pair[0], columns, :], NT) + dot(
                gpu_s[pair[1]], gu_s[pair[1], columns, :], NT
            )
            return carry

        lax.fori_loop(0, experts // 2, back_step, 0)
        part[:, columns] = acc[...].astype(bf16)
        rs_line.scatter_start(*each)
    beside.middle(*beside_refs, step="middle2")
    wait_all(handed[1:])

    def saves(expert):
        return [pltpu.make_async_copy(pair_s.at[expert], pair_out.at[expert], save_sems.at[expert])]

    def grads_step(expert, carry):
        pair_s[expert] = (
            dot(turned_x[:, :tokens], gpu_s[expert], NN)
            + dot(turned_x[:, tokens:], gpu_peer[expert], NN)
        ).astype(bf16)
        for copy in saves(expert):
            copy.start()
        return carry

    lax.fori_loop(0, experts, grads_step, 0)
    beside.middle(*beside_refs, step="middle3")
    stage.middle(*stage_refs)
    wait_all(copies)
    for each in dealt:
        rs_line.scatter_wait(*each)
    in_grad = rs_line.total(part[own_rows, :].astype(f32), landing1)
    gate_grad = gate_part[own_rows, :]
    for step in range(count - 1):
        gate_grad = gate_grad + gate_land[step]
    gate_grad = gate_grad[:, :experts]
    gate_rows = gate[own_rows, :]
    logits_grad = (
        gate_rows * (gate_grad - jnp.sum(gate_rows * gate_grad, axis=1, keepdims=True))
    ).astype(bf16)
    router_out[...] = dot(logits_grad, expert_rows[...], TN)
    in_grad = in_grad + dot(logits_grad, router[...], NN)
    mid_part, expert_gain_grad = norm_back(mid[...], expert_gain[...], in_grad)
    expert_gain_out[...] = expert_gain_grad
    mid_grad_out[...] = ag1[own_rows, :].astype(f32) + mid_part

    def finish_save(expert, carry):
        for copy in saves(expert):
            copy.wait()
        return carry

    lax.fori_loop(0, experts, finish_save, 0)
    if trade:
        trade.wait(traded[0], traded_out[0], trade_sems)
    stage.wait(*stage_refs)
    beside.wait(*beside_refs)


def experts_back(layer, gains, own, other, out_grad, state, pairs, masks, traded, beside):
    count = lax.axis_size("tensor")
    mid, gate, expert_rows, pre = state
    rows, width = mid.shape
    tokens = gate.shape[0]
    own, other = own[4:], other[4:]
    trade = Trade((rows, width)) if traded else None
    experts, depth, hidden_width = own[0].shape
    stage = FirstStage(
        jax.ShapeDtypeStruct((experts, hidden_width, width // 2), bf16), 2, layer
    )
    vmem = pl.BlockSpec(memory_space=pltpu.VMEM)
    hbm = pl.BlockSpec(memory_space=pl.ANY)
    shape = jax.ShapeDtypeStruct
    found = pl.pallas_call(
        functools.partial(experts_back_kernel, layer, count, trade, stage, beside),
        name=f"experts_back_{layer}",
        out_shape=(
            shape((rows, width), f32),
            shape((experts, width), f32),
            shape((1, width), f32),
            shape((experts, width // 2, 2 * hidden_width), bf16),
            *((shape((2, rows, width), f32),) if traded else ()),
            *stage.outputs,
            *beside.outputs,
        ),
        in_specs=[vmem] * 7 + [hbm] * 9 + [vmem] * len(traded) + [hbm] * len(beside.inputs),
        out_specs=(vmem, vmem, vmem, hbm)
        + (vmem,) * bool(traded)
        + (hbm,) * len(stage.outputs + beside.outputs),
        scratch_shapes=[
            pltpu.VMEM((experts, depth, 2 * hidden_width), bf16),
            pltpu.VMEM((experts * hidden_width, depth), bf16),
            pltpu.VMEM((tokens, width), bf16),
            pltpu.VMEM((tokens, width), bf16),
            Line.landing(count, rows, width),
            pltpu.VMEM((experts, tokens, 2 * hidden_width), f32),
            pltpu.VMEM((experts, tokens, 2 * hidden_width), bf16),
            pltpu.VMEM((tokens, width // 2), f32),
            pltpu.VMEM((tokens, 128), f32),
            pltpu.VMEM((count - 1, rows, 128), f32),
            pltpu.VMEM((2 * tokens, width // 2), bf16),
            pltpu.VMEM((experts, tokens, 2 * hidden_width), bf16),
            pltpu.VMEM((2 * tokens, width // 2), bf16),
            pltpu.VMEM((width // 2, 2 * tokens), bf16),
            pltpu.VMEM((2 * tokens, experts * hidden_width), bf16),
            pltpu.VMEM((experts, tokens, hidden_width), bf16),
            pltpu.VMEM((experts, width // 2, 2 * hidden_width), bf16),
            pltpu.VMEM(stage.blocks, bf16),
            *Line.sems(count, 4),
            pltpu.SemaphoreType.DMA((3, experts)),
            pltpu.SemaphoreType.DMA((experts,)),
            *[pltpu.SemaphoreType.DMA((3,)) for _ in range(5)],
            pltpu.SemaphoreType.DMA((experts,)),
            *(trade.sems if trade else ()),
            *stage.sems,
            *beside.sems,
        ],
        compiler_params=params(3 + layer),
    )(out_grad, mid, *gains[1:], masks[1], gate, expert_rows, pre, *pairs, *own, *other,
      *traded, *beside.inputs)
    kept = 5 if traded else 4
    parts = kept + len(stage.outputs)
    return found[:kept], found[kept:parts], beside.results(found[parts:])


def attention_back_kernel(layer, count, last, beside, *refs):
    refs = list(refs)

    def take(number):
        taken = refs[:number]
        del refs[:number]
        return taken

    mid_grad, stream_in, attn_gains, cosine, sine, qs, keys, values, probs = take(9)
    attn_gain = attn_gains.at[layer]
    stream = stream_in.at[lax.axis_index("section")] if layer == 0 else stream_in
    ai_in, attended_in = take(2)
    own, other = take(4), take(4)
    small_parts = take(5 if last else 0)
    later_grad = take(1 if last else 0)
    beside_in = take(len(beside.inputs))
    if last:
        dense_sum, small_sum, trade = last
        traded_out, small_out, whole_out = take(3)
    else:
        grad_out, attn_gain_out, dense_out = take(3)
    beside_out = take(len(beside.outputs))
    scratch = take(2)
    joint_s, output_s = scratch
    (ag2, part, landing2, ag_stack, dq_s, joint_rows, joint_peer, ao_s, ai_s, turned_ai, attended_s,
     dense_s, send_s, recv_s, attn_sems, core_send, core_recv, local_sems,
     hand_send, hand_recv) = take(20)
    if last:
        grad_s, trade_sems = refs.pop(0), take(len(trade.sems))
        dense_sems, small_sems = take(len(dense_sum.sems)), take(len(small_sum.sems))
        dense_refs = ([dense_s], [whole_out], dense_sems)
    beside_refs = (beside_in, beside_out, refs)
    rows, width = stream.shape
    tokens = ag2.shape[0]
    kw = keys.shape[1]
    qw = output_s.shape[0]
    heads, key_heads = qw // HD, kw // HD
    group = heads // key_heads
    me = lax.axis_index("tensor")
    own_rows = pl.ds(pl.multiple_of(me * rows, rows), rows)
    ag_line, rs_line = [Line(count, rows, v) for v in (True, False)]
    gathering = ag2, (send_s.at[0], recv_s.at[0])
    use_own = lax.axis_index("section") == layer
    ag2[own_rows, :] = mid_grad[...].astype(bf16)
    everyone = Beside([*beside.jobs, dense_sum]) if last else beside
    greet(tensor_peers(count) + [core_peer()] + (whole_group() if last else everyone.peers()))
    ag_line.gather_start(*gathering)
    either(use_own, own, other, lambda w: [c.start() for c in attn_copies(w, scratch, attn_sems)])
    loads = hand_halves(ai_in, ai_s, [v.at[0] for v in (local_sems, hand_send, hand_recv)])
    loads += hand_rows(attended_in, attended_s, [v.at[1] for v in (local_sems, hand_send, hand_recv)])
    for copy in loads:
        copy.start()
    beside.start(*beside_refs)
    wait_all(loads)
    turned_ai[...] = ai_s[...].T
    ag_line.gather_wait(*gathering)
    core = lax.axis_index("section")
    half = width // 2
    ao_s[pl.ds(0, tokens), :] = ag2[:, pl.ds(pl.multiple_of(core * half, half), half)]
    handed = [
        remote(ag2.at[:, pl.ds(pl.multiple_of((1 - core) * half, half), half)],
               ao_s.at[pl.ds(tokens, tokens)], core_send.at[0], core_recv.at[0], core_peer())
    ]
    handed[0].start()
    either(use_own, own, other, lambda w: [c.wait() for c in attn_copies(w, scratch, attn_sems)])
    attended_grad = dot(ag2[...], output_s[...], NT).astype(bf16)
    for h in range(heads):
        ag_stack[pl.ds(h * tokens, tokens), :] = attended_grad[:, h * HD : (h + 1) * HD]
    for g in range(key_heads):
        lanes = pl.ds(g * HD, HD)
        span = pl.ds(g * group * tokens, group * tokens)
        soft_b = probs[span, :]
        soft = soft_b.astype(f32)
        soft_grad = dot(ag_stack[span, :], values[:, lanes], NT)
        inner = jnp.sum(soft * soft_grad, axis=1, keepdims=True)
        score_grad = (soft * (soft_grad - inner)).astype(bf16)
        dq = dot(score_grad, keys[:, lanes], NN) * 0.125
        for h in range(group):
            dq_s[:, pl.ds((g * group + h) * HD, HD)] = dq[h * tokens : (h + 1) * tokens]
        dq_s[:, pl.ds(qw + g * HD, HD)] = dot(score_grad, qs[span, :], TN) * 0.125
        joint_rows[:, pl.ds(qw + kw + g * HD, HD)] = dot(soft_b, ag_stack[span, :], TN).astype(bf16)
    for chunk in range((qw + kw) // 128):
        lanes = pl.ds(chunk * 128, 128)
        block = dq_s[:, lanes]
        joint_rows[:, lanes] = (block * cosine[...] - turned(block) * sine[...]).astype(bf16)
    handed.append(remote(joint_rows, joint_peer, core_send.at[1], core_recv.at[1], core_peer()))
    handed[1].start()
    tile = width // 2
    dealt = [
        (part, pl.ds(t * tile, tile), landing2, (send_s.at[1 + t], recv_s.at[1 + t])) for t in range(2)
    ]
    for each in dealt:
        part[:, each[1]] = dot(joint_rows[...], joint_s[each[1], :], NT).astype(bf16)
        rs_line.scatter_start(*each)
    for each in dealt:
        rs_line.scatter_relay(*each)
    wait_all(handed)
    wide = qw + 2 * kw
    joint_grads = (
        dot(turned_ai[:, :tokens], joint_rows[...], NN) + dot(turned_ai[:, tokens:], joint_peer[...], NN)
    ).astype(bf16)
    output_grads = dot(ao_s[...], attended_s[...], TN).astype(bf16)
    outer, inner, depth = dense_s.shape[:3]
    for block in range(outer * inner):
        cut = slice(block * depth, (block + 1) * depth)
        dense_s[block // inner, block % inner, :, :wide] = joint_grads[cut]
        dense_s[block // inner, block % inner, :, wide:] = output_grads[cut]
    if last:
        dense_sum.start(*dense_refs)
    else:
        save = pltpu.make_async_copy(dense_s, dense_out, local_sems.at[0])
        save.start()
    beside.middle(*beside_refs)
    for each in dealt:
        rs_line.scatter_wait(*each)
    in_grad = rs_line.total(part[own_rows, :].astype(f32), landing2)
    stream_part, attn_gain_grad = norm_back(
        stream[...].astype(bf16).astype(f32), attn_gain[...], in_grad
    )
    grad = mid_grad[...] + stream_part
    if not last:
        attn_gain_out[...] = attn_gain_grad
        grad_out[...] = grad
        save.wait()
        beside.wait(*beside_refs)
        return
    small = small_sems[0]
    router0, gain0, router1, attn_gain1, gain1 = small_parts
    place = 0
    for value in (router0[...], attn_gain_grad, gain0[...]):
        small[pl.ds(place, value.shape[0]), :] = value
        place += value.shape[0]
    place = small.shape[0] // 2
    for value in (router1[...], attn_gain1[...], gain1[...]):
        small[pl.ds(place, value.shape[0]), :] = value
        place += value.shape[0]
    small_sum.first(small_sems)
    grad_s[...] = grad
    trade.start(grad_s, later_grad[0], trade_sems)
    dense_sum.middle1(*dense_refs)
    small_sum.second(small_sems)
    dense_sum.middle2(*dense_refs)
    small_sum.third(small_sems)
    dense_sum.middle3(*dense_refs)
    trade.wait(grad_s, traded_out, trade_sems)
    small_sum.last(small_sems, small_out)
    dense_sum.wait(*dense_refs)
    beside.wait(*beside_refs)


def attention_back(layer, gains, own, other, mid_grad, stream, state, pairs, tables, ending, beside):
    count = lax.axis_size("tensor")
    qs, keys, values, probs = state
    rows, width = mid_grad.shape
    tokens = keys.shape[0]
    own, other = own[:4], other[:4]
    qw, kw = own[0].shape[1], own[1].shape[1]
    heads = qw // HD
    vmem = pl.BlockSpec(memory_space=pltpu.VMEM)
    hbm = pl.BlockSpec(memory_space=pl.ANY)
    shape = jax.ShapeDtypeStruct
    groups = lax.axis_size("dp")
    dense = shape((*factors(groups), width // 2 // groups, 2 * qw + 2 * kw), bf16)
    if ending:
        depth = 2 * (-(-(ending[0].shape[0] + 2) // 8) * 8)
        last = (DenseSum(dense, layer), SmallSum(depth, width), Trade((rows, width)))
        own_outs = (shape((2, rows, width), f32), shape((depth, width), f32), *last[0].outputs)
        more = [pltpu.VMEM((rows, width), f32), *last[2].sems, *last[0].sems, *last[1].sems]
    else:
        last, more = None, []
        own_outs = (shape((rows, width), f32), shape((1, width), f32), dense)
    found = pl.pallas_call(
        functools.partial(attention_back_kernel, layer, count, last, beside),
        name=f"attention_back_{layer}",
        out_shape=(*own_outs, *beside.outputs),
        in_specs=[vmem] * 9 + [hbm] * 10 + [vmem] * len(ending) + [hbm] * len(beside.inputs),
        out_specs=(vmem, vmem, hbm) + (hbm,) * len(beside.outputs),
        scratch_shapes=[
            pltpu.VMEM((width, qw + 2 * kw), bf16),
            pltpu.VMEM((qw, width), bf16),
            pltpu.VMEM((tokens, width), bf16),
            pltpu.VMEM((tokens, width), bf16),
            Line.landing(count, rows, width),
            pltpu.VMEM((heads * tokens, HD), bf16),
            pltpu.VMEM((tokens, qw + kw), f32),
            pltpu.VMEM((tokens, qw + 2 * kw), bf16),
            pltpu.VMEM((tokens, qw + 2 * kw), bf16),
            pltpu.VMEM((2 * tokens, width // 2), bf16),
            pltpu.VMEM((2 * tokens, width // 2), bf16),
            pltpu.VMEM((width // 2, 2 * tokens), bf16),
            pltpu.VMEM((2 * tokens, qw), bf16),
            pltpu.VMEM(dense.shape, bf16),
            *Line.sems(count, 3),
            pltpu.SemaphoreType.DMA((4,)),
            *[pltpu.SemaphoreType.DMA((2,)) for _ in range(5)],
            *more,
            *beside.sems,
        ],
        compiler_params=params(5 + layer),
    )(mid_grad, stream, gains[0], *tables[:2], qs, keys, values, probs, *pairs, *own, *other,
      *ending, *beside.inputs)
    return found[:3], beside.results(found[3:])


def prepare_kernel(lengths, dealing, order, routes, attn_gain, expert_gain, router, freqs,
                   cosine, sine, bias, picked, kept, attn_gains, expert_gains, routers,
                   order_peer, routes_peer, sends, recvs):
    core = lax.axis_index("section")
    attn_gains[core] = attn_gain[...]
    expert_gains[core] = expert_gain[...]
    routers[core] = router[...]
    greet([core_peer()])
    copies = [
        remote(source, target, sends.at[index], recvs.at[index], core_peer())
        for index, (source, target) in enumerate((
            (order.at[1 - core], order_peer),
            (routes.at[1 - core], routes_peer),
            (attn_gain, attn_gains.at[core]),
            (expert_gain, expert_gains.at[core]),
            (router, routers.at[core]),
        ))
    ]
    start_all(copies)
    tokens = bias.shape[0]
    sequences = lengths.shape[1]
    tall = lax.broadcasted_iota(jnp.int32, (tokens, 1), 0)
    wide = lax.broadcasted_iota(jnp.int32, (1, tokens), 1)
    sizes = [lengths[core, index] for index in range(sequences)]
    starts = [sum(sizes[:index], 0) for index in range(sequences)]
    ranks = [
        sum(jnp.where(dealing[core, place] == index, place, 0) for place in range(sequences))
        for index in range(sequences)
    ]
    dealt_starts = [
        sum(jnp.where(ranks[before] < ranks[index], sizes[before], 0) for before in range(sequences))
        for index in range(sequences)
    ]

    def places(token):
        segment = sum((token >= starts[index] + sizes[index]).astype(jnp.int32)
                      for index in range(sequences))
        position, dealt = token, token
        for index in range(sequences):
            inside = segment == index
            position = jnp.where(inside, token - starts[index], position)
            dealt = jnp.where(inside, token - starts[index] + dealt_starts[index], dealt)
        return segment, position, dealt

    segment, position, dealt = places(tall)
    segment_wide, _, dealt_wide = places(wide)
    allowed = (segment == segment_wide) & (wide <= tall)
    bias[...] = jnp.where(allowed, 0.0, masked_score).astype(f32)
    angles = position.astype(f32) * freqs[...]
    cosine[...] = jnp.cos(angles)
    lane = lax.broadcasted_iota(jnp.int32, (1, freqs.shape[1]), 1)
    sine[...] = jnp.sin(angles) * jnp.where(lane % HD < HD // 2, -1.0, 1.0)

    def masks(order_row, route_rows):
        order_wide = order_row.astype(f32)
        order_tall = jnp.sum(jnp.where(tall == wide, order_wide, 0.0), axis=1, keepdims=True)
        first = jnp.sum(jnp.where(dealt == wide, order_wide, 0.0), axis=1, keepdims=True)
        first_wide = jnp.sum(jnp.where(dealt_wide == tall, order_tall, 0.0), axis=0, keepdims=True)
        earlier = jnp.where(first_wide < first, 1.0, 0.0).astype(bf16)
        experts = picked.shape[2]
        index = lax.broadcasted_iota(jnp.int32, (experts, tokens), 0)
        chosen = jnp.zeros((experts, tokens), f32)
        for k in range(route_rows.shape[0]):
            chosen = jnp.where(route_rows[k : k + 1] == index, 1.0, chosen)
        chosen = chosen.T
        rank = dot(earlier, chosen.astype(bf16), NN)
        return chosen, jnp.where(rank < CAP, chosen, 0.0)

    picked[core], kept[core] = masks(order[core], routes[core])
    wait_all(copies)
    picked[1 - core], kept[1 - core] = masks(order_peer[...], routes_peer[...])


def prepare(lengths, dealing, order, routes, attn_gain, expert_gain, router):
    tokens = order.shape[2]
    width = attn_gain.shape[1]
    half = HD // 2
    freqs = np.tile(rope_base ** (-2.0 * np.arange(half) / HD), 128 // half)[None].astype(np.float32)
    vmem = pl.BlockSpec(memory_space=pltpu.VMEM)
    smem = pl.BlockSpec(memory_space=pltpu.SMEM)
    shape = jax.ShapeDtypeStruct
    found = pl.pallas_call(
        prepare_kernel,
        name="prepare",
        out_shape=(
            shape((tokens, 128), f32),
            shape((tokens, 128), f32),
            shape((tokens, tokens), f32),
            shape((2, tokens, E), f32),
            shape((2, tokens, E), f32),
            shape((2, 1, width), f32),
            shape((2, 1, width), f32),
            shape((2, *router.shape), bf16),
        ),
        in_specs=[smem] * 2 + [vmem] * 6,
        out_specs=(vmem,) * 8,
        scratch_shapes=[
            pltpu.VMEM(order.shape[1:], order.dtype),
            pltpu.VMEM(routes.shape[1:], routes.dtype),
            dma((5,)),
            dma((5,)),
        ],
        compiler_params=params(8),
    )(lengths, dealing, order, routes, attn_gain, expert_gain, router, freqs)
    return found[:3], found[3:5], found[5:]


def assemble_kernel(section, *refs):
    expert_refs, dense_refs, rows_in, outs = (refs[:4], refs[4:8]), refs[8:10], refs[10:12], refs[12:]
    query, key, value, output, gate, up, down = outs[:7]
    for source, target in zip(rows_in, outs[7:]):
        target[...] = source[...]
    hidden_width = gate.shape[2]
    qw, kw = query.shape[1], key.shape[1]

    def write(parts, dense):
        cores = range(2)
        pair = [[jnp.sum(v[core, :, 0].astype(f32), axis=0) for v in parts[:2]] for core in cores]
        depth = 0
        for block in pair[0] + pair[1]:
            rows = pl.ds(depth, block.shape[0])
            gate[0, rows, :] = block[:, :hidden_width]
            up[0, rows, :] = block[:, hidden_width:]
            depth += block.shape[0]
        depth = 0
        for core in cores:
            for v in parts[2:]:
                block = jnp.sum(v[core, :, 0].astype(f32), axis=0)
                down[0, :, pl.ds(depth, block.shape[1])] = block
                depth += block.shape[1]
        rows = dense[...].astype(f32)
        query[...] = rows[:, :qw]
        key[...] = rows[:, qw : qw + kw]
        value[...] = rows[:, qw + kw : qw + 2 * kw]
        output[...] = rows[:, qw + 2 * kw :].T

    pl.when(section[0] == 0)(lambda: write(expert_refs[0], dense_refs[0]))
    pl.when(section[0] == 1)(lambda: write(expert_refs[1], dense_refs[1]))


def assemble(parts, denses, rows_in, qw, kw):
    groups = parts[0][0].shape[2]
    hidden_width = parts[0][2].shape[3]
    dense = [v.reshape(-1, v.shape[-1]) for v in denses]
    depth = dense[0].shape[0]
    rows = depth // groups

    def part_spec(layer, shape):
        block = (*shape[:2], 1, *shape[3:])
        return pl.BlockSpec(block, lambda e, s: (0, 0, jnp.where(s[0] == layer, e, 0), 0, 0))

    def dense_spec(layer, width):
        return pl.BlockSpec((rows, width), lambda e, s: (jnp.where(s[0] == layer, e, 0), 0))

    _, own_rows, width = rows_in[0].shape
    row_spec = pl.BlockSpec((2, own_rows // groups, width), lambda e, s: (0, e, 0))
    shape = jax.ShapeDtypeStruct
    return pl.pallas_call(
        assemble_kernel,
        name="assemble",
        out_shape=(
            shape((depth, qw), f32),
            shape((depth, kw), f32),
            shape((depth, kw), f32),
            shape((qw, depth), f32),
            shape((groups, depth, hidden_width), f32),
            shape((groups, depth, hidden_width), f32),
            shape((groups, hidden_width, depth), f32),
            *[shape(v.shape, f32) for v in rows_in],
        ),
        grid_spec=pltpu.PrefetchScalarGridSpec(
            num_scalar_prefetch=1,
            grid=(groups,),
            in_specs=[part_spec(layer, v.shape) for layer in range(2) for v in parts[layer]]
            + [dense_spec(layer, dense[layer].shape[1]) for layer in range(2)]
            + [row_spec] * 2,
            out_specs=(
                pl.BlockSpec((rows, qw), lambda e, s: (e, 0)),
                pl.BlockSpec((rows, kw), lambda e, s: (e, 0)),
                pl.BlockSpec((rows, kw), lambda e, s: (e, 0)),
                pl.BlockSpec((qw, rows), lambda e, s: (0, e)),
                pl.BlockSpec((1, depth, hidden_width), lambda e, s: (e, 0, 0)),
                pl.BlockSpec((1, depth, hidden_width), lambda e, s: (e, 0, 0)),
                pl.BlockSpec((1, hidden_width, depth), lambda e, s: (e, 0, 0)),
                row_spec,
                row_spec,
            ),
        ),
        compiler_params=pltpu.CompilerParams(vmem_limit_bytes=58 * 2**20),
    )(lax.axis_index("section").astype(jnp.int32)[None], *parts[0], *parts[1], *dense, *rows_in)


def shards(
    tokens_in, out_cotangent, attn_gain, query_weight, key_weight, value_weight, output_weight,
    expert_gain, router_weight, gate_weight, up_weight, down_weight, lengths, dealing,
    slot_order, routes,
):
    first = lax.axis_index("section") == 0
    qw, kw = query_weight.shape[2], key_weight.shape[2]
    own = (query_weight[0], key_weight[0], value_weight[0], output_weight[0], gate_weight[0],
           up_weight[0], down_weight[0])
    tables, masks, gains = prepare(lengths[:, 0], dealing[:, 0], slot_order[0],
                                   jnp.swapaxes(routes[0], 1, 2), attn_gain, expert_gain,
                                   router_weight[0].T)
    (out0, *state0), other = layer_forward(0, gains, own, None, tokens_in, tables, masks)
    (out1, *state1), _ = layer_forward(1, gains, own, other, out0, tables, masks)
    saved = (state0, state1)
    streams = (tokens_in, out0)

    def experts(layer, out_grad, traded, jobs):
        mid, expert_rows, qs, keys, values, probs, gate, ai, x, gated, attended, pre = saved[layer]
        return experts_back(
            layer, gains, own, other, out_grad, (mid, gate, expert_rows, pre), (x, gated), masks,
            traded, Beside(jobs)
        )

    def attention(layer, mid_grad, ending, jobs):
        mid, expert_rows, qs, keys, values, probs, gate, ai, x, gated, attended, pre = saved[layer]
        return attention_back(
            layer, gains, own, other, mid_grad, streams[layer], (qs, keys, values, probs),
            (ai, attended), tables, ending, Beside(jobs)
        )

    def bring(layer, sums):
        return [Bring(layer, kind, v) for kind, v in zip(("column", "row"), sums)]

    (mid_grad, router1, gain1, pair, layer_outputs), down1, _ = experts(
        1, out_cotangent, (out0, out1), []
    )
    (grad1, attn_gain1, dense1), (sums,) = attention(1, mid_grad, (), [FirstStage(pair, 1)])
    (mid_grad, router0, gain0, pair), down0, (*pair1, dense1) = experts(
        0, grad1, (), bring(1, sums) + [DenseSum(dense1, 1)]
    )
    (input_grads, small, dense0), (pair0,) = attention(
        0, mid_grad, (router0, gain0, router1, attn_gain1, gain1, grad1),
        [FirstStage(pair, 1, 0)]
    )
    parts0, parts1 = [*pair0, *down0], [*pair1, *down1]
    query, key, value, output, gate, up, down, layer_outputs, input_grads = assemble(
        (parts0, parts1), (dense0, dense1), (layer_outputs, input_grads), qw, kw
    )
    small = jnp.where(first, small[: small.shape[0] // 2], small[small.shape[0] // 2 :])
    router_grad, attn_gain_grad, expert_gain_grad = small[:E].T, small[E : E + 1], small[E + 1 : E + 2]
    return (
        layer_outputs[None],
        input_grads[None],
        attn_gain_grad,
        query[None],
        key[None],
        value[None],
        output[None],
        expert_gain_grad,
        router_grad[None],
        gate[None],
        up[None],
        down[None],
    )


def solution(mesh):
    return jax.shard_map(
        shards,
        mesh=mesh,
        in_specs=(
            P(None, ("dp", "tensor"), None),
            P(None, ("dp", "tensor"), None),
            P("section", None),
            P("section", None, "tensor"),
            P("section", None, "tensor"),
            P("section", None, "tensor"),
            P("section", "tensor", None),
            P("section", None),
            P("section", None, None),
            P("section", None, None, "tensor"),
            P("section", None, None, "tensor"),
            P("section", None, "tensor", None),
            P(None, "dp", None),
            P(None, "dp", None),
            P("section", None, "dp", None),
            P("section", None, "dp", None),
        ),
        out_specs=(
            P("section", None, ("dp", "tensor"), None),
            P("section", None, ("dp", "tensor"), None),
            P("section", None),
            P("section", None, "tensor"),
            P("section", None, "tensor"),
            P("section", None, "tensor"),
            P("section", "tensor", None),
            P("section", None),
            P("section", None, None),
            P("section", "dp", None, "tensor"),
            P("section", "dp", None, "tensor"),
            P("section", "dp", "tensor", None),
        ),
        check_vma=False,
    )
```
